32 devices in a mesh: dp: 8 (over z, x), opt: 4 (over y, core).
Axes of the slice: x: 2, y: 2, z: 4, core: 2. Of those that a mesh axis runs over, the one named last changes fastest.
Arguments:
- patches: bfloat16 [4, 8, 64, 49, 512], P('opt', 'dp'), may hold values from -6 to 6
- regions: bfloat16 [4, 8, 64, 512], P('opt', None, 'dp'), may hold values from -6 to 6
- image_ids: int32 [4, 8, 64], P('opt'), may hold values from 0 to 15, as said below
- attn_w: float32 [4, 512, 512], P('opt')
- mlp_in: float32 [512, 2048], P(None, 'opt'), may hold values from -0.25 to 0.25
- mlp_out: float32 [2048, 512], P('opt'), may hold values from -0.125 to 0.125
- vec_params: float32 [12, 512], replicated
- patch_cot: bfloat16 [4, 8, 64, 49, 512], P('opt', None, 'dp'), may hold values from -6 to 6
- region_cot: bfloat16 [4, 8, 64, 512], P('opt', None, 'dp'), may hold values from -6 to 6
- attn_mom: float32 [4, 512, 512], P('opt'), may hold values from -0.0078125 to 0.0078125
- mlp_in_mom: float32 [512, 2048], P(None, 'opt'), may hold values from -0.0078125 to 0.0078125
- mlp_out_mom: float32 [2048, 512], P('opt'), may hold values from -0.0078125 to 0.0078125
- adam_first: float32 [12, 512], replicated, may hold values from -0.001953125 to 0.001953125
- adam_second: float32 [12, 512], replicated, may hold values from 6.357829e-08 to 2.5431316e-07
Outputs:
- out_patches: bfloat16 [4, 8, 64, 49, 512], P('opt', None, 'dp')
- out_regions: bfloat16 [4, 8, 64, 512], P('opt', None, 'dp')
- d_patches: bfloat16 [4, 8, 64, 49, 512], P('opt', 'dp')
- d_regions: float32 [4, 8, 64, 512], P('opt', None, 'dp')
- new_attn_w: float32 [4, 512, 512], P('opt')
- new_attn_mom: float32 [4, 512, 512], P('opt')
- new_mlp_in: float32 [512, 2048], P(None, 'opt')
- new_mlp_in_mom: float32 [512, 2048], P(None, 'opt')
- new_mlp_out: float32 [2048, 512], P('opt')
- new_mlp_out_mom: float32 [2048, 512], P('opt')
- new_vec_params: float32 [12, 512], replicated
- new_adam_first: float32 [12, 512], replicated
- new_adam_second: float32 [12, 512], replicated
- grad_norm: float32 [], replicated
The draws below stay inside these ranges and needn't reach their ends.
Inputs may be any that keep to these rules, and one draw needn't show every extreme that they name: `image_ids`: equal ids within one canvas mark one image; an image is a band of whole canvas rows or the left or right part of such a band; in every canvas some image covers all 64 window columns.
All inputs are finite; a program needn't handle non-finite values.
Results may differ from the reference program's by a relative error of at most 0.018.
Values may be sent and summed in bfloat16 or wider, within the bound.
No kernel may reach another device: no remote copies, remote signals or barrier semaphores. Data moves between devices by JAX's collectives and lax.ppermute only.
A program may use at most 384 MiB of HBM per device.

```python
import math
import jax
import jax.numpy as jnp
from jax import lax

D = 512
HEADS = 16
HEAD_DIM = 32
FF = 2048
PATCH = 49
GW = 64
OPT_STEP = 10
GH = 8
GROUPS = 4
VEC_ROWS = 12


def draw_image_ids(key, part):
    key = jax.random.fold_in(key, 11)

    def one_group(group_key):
        start_key, cut_key, side_key, pick_key = jax.random.split(group_key, 4)
        row_index = jnp.arange(GH)
        starts = jax.random.randint(start_key, (GH,), 0, 3) == 0
        starts = jnp.where(row_index == 0, True, starts)
        starts = jnp.where(row_index == GH - 1, True, starts)
        strip = jnp.cumsum(starts.astype(jnp.int32)) - 1
        strips = strip[GH - 1] + 1
        cuts = jax.random.randint(cut_key, (GH,), 1, GW)
        cut_on = jax.random.randint(side_key, (GH,), 0, 2)
        whole = jax.random.randint(pick_key, (), 0, GH) % strips
        cut_on = jnp.where(row_index == whole, 0, cut_on)
        row_cut = cuts[strip]
        row_on = cut_on[strip]
        columns = jnp.arange(GW)
        side = ((columns[None, :] >= row_cut[:, None]) & (row_on[:, None] == 1)).astype(jnp.int32)
        labels = (strip[:, None] * 2 + side).astype(jnp.int32)
        top_label = jnp.max(labels)
        return jnp.where(labels == top_label, 2 * GH - 1, labels).astype(jnp.int32)
    group_keys = jax.random.split(key, GROUPS)
    return jax.vmap(one_group)(group_keys)


def draw_attn_w(key, part):
    key = jax.random.fold_in(key, 5)
    noise = jax.random.normal(key, (4, D, D), jnp.float32)
    factors = jnp.array([1.0, 1.0, 1.0, 4.0], jnp.float32)
    return noise * factors[:, None, None] * D ** (-0.5)


def draw_vec_params(key, part):
    key = jax.random.fold_in(key, 7)
    noise = jax.random.normal(key, (VEC_ROWS, D), jnp.float32)
    rows = jnp.arange(VEC_ROWS)
    is_gain = (rows == 0) | (rows == 2)
    return jnp.where(is_gain[:, None], 1.0 + 0.1 * noise, 0.2 * noise)


def block_levels(stream_key, extent, cuts, smallest, high):
    loudness, own = 1.0, jax.random.fold_in(stream_key, 6)
    for position, parts in cuts:
        draws = jnp.exp(jax.random.uniform(jax.random.fold_in(own, position), (parts,), jnp.float32, smallest / len(cuts), high / len(cuts)))
        loudness = loudness * jnp.repeat(draws, extent[position] // parts).reshape([-1 if axis == position else 1 for axis in range(len(extent))])
    return loudness


def gaussian(own_key, dims, scale, most, cuts=(), held_as=jnp.bfloat16):
    drawn = jax.random.normal(own_key, dims, jnp.float32) * scale
    if len(cuts) > 0:
        drawn = block_levels(own_key, dims, cuts, -0.22, 0.18) * drawn
    return jnp.clip(drawn, min=-most, max=most).astype(held_as)


def setup_inputs(seed: int = 0) -> dict:
    keys = jax.random.split(jax.random.key(seed), 15)
    patches = gaussian(keys[0], (GROUPS, GH, GW, PATCH, D), 1.0, 6.0, ((0, 4), (1, 8)))
    regions = gaussian(keys[1], (GROUPS, GH, GW, D), 1.0, 6.0, ((0, 4), (2, 8)))
    image_ids = draw_image_ids(jax.random.fold_in(keys[14], 71), 0)
    attn_w = draw_attn_w(jax.random.fold_in(keys[14], 71), 0)
    mlp_in = gaussian(keys[4], (D, FF), D ** -0.5, 0.25, ((1, 4),), jnp.float32)
    mlp_out = gaussian(keys[5], (FF, D), FF ** -0.5, 0.125, ((0, 4),), jnp.float32)
    vec_params = draw_vec_params(jax.random.fold_in(keys[14], 71), 0)
    patch_cot = gaussian(keys[7], (GROUPS, GH, GW, PATCH, D), 1.0, 6.0, ((0, 4), (2, 8)))
    region_cot = gaussian(keys[8], (GROUPS, GH, GW, D), 1.0, 6.0, ((0, 4), (2, 8)))
    attn_mom = gaussian(keys[9], (4, D, D), ((4 * D * D + 2 * D * FF) ** -0.5), 0.0078125, ((0, 4),), jnp.float32)
    mlp_in_mom = gaussian(keys[10], (D, FF), ((4 * D * D + 2 * D * FF) ** -0.5), 0.0078125, ((1, 4),), jnp.float32)
    mlp_out_mom = gaussian(keys[11], (FF, D), ((4 * D * D + 2 * D * FF) ** -0.5), 0.0078125, ((0, 4),), jnp.float32)
    adam_first = gaussian(keys[12], (VEC_ROWS, D), (0.22 * (4 * D * D + 2 * D * FF) ** -0.5), 0.001953125, (), jnp.float32)
    adam_second = jnp.clip(jnp.exp(jax.random.uniform(keys[13], (VEC_ROWS, D), jnp.float32, math.log(6.357829107628277e-08), math.log(2.5431316430513107e-07))), 6.357829107628277e-08, 2.5431316430513107e-07)
    return dict(patches=patches, regions=regions, image_ids=image_ids, attn_w=attn_w, mlp_in=mlp_in, mlp_out=mlp_out, vec_params=vec_params, patch_cot=patch_cot, region_cot=region_cot, attn_mom=attn_mom, mlp_in_mom=mlp_in_mom, mlp_out_mom=mlp_out_mom, adam_first=adam_first, adam_second=adam_second)


NORM_EPS = 1e-05
MASKED = -1e+30
NS_FIRST = 3.4445
NS_SECOND = -4.775
NS_THIRD = 2.0315
MUON_RATE = 0.5
MUON_MOMENTUM = 0.5
MUON_DECAY = 0.01
ADAM_RATE = 0.5
BETA_FIRST = 0.9
BETA_SECOND = 0.95
ADAM_EPS = 1e-08
CLIP_LIMIT = 1.0

@jax.custom_vjp
def low(v):
    return lax.optimization_barrier(v.astype(jnp.bfloat16)).astype(jnp.float32)

@jax.custom_vjp
def low_back(v):
    return v

def low_keep(v):
    return (low(v), None)

def low_pass(kept, grad):
    return (grad,)

def back_keep(v):
    return (v, None)

def back_low(kept, grad):
    return (low(grad),)
low.defvjp(low_keep, low_pass)
low_back.defvjp(back_keep, back_low)

def matmul_high(left, right):
    return jnp.matmul(left, right, precision=lax.Precision.HIGHEST)

def layer_norm(values, gain, offset):
    centre = values - lax.optimization_barrier(jnp.mean(values, axis=-1, keepdims=True))
    spread = lax.optimization_barrier(jnp.mean(centre * centre, axis=-1, keepdims=True))
    return centre * lax.rsqrt(spread + NORM_EPS) * gain + offset

def split_heads(values):
    return values.reshape(values.shape[:-1] + (HEADS, HEAD_DIM))

def attention_branch(normed, weights, same_image):
    w_query, w_key, w_value, w_output, bias_query, bias_value, bias_output = weights
    queries = split_heads(low_back(low(matmul_high(normed, w_query) + bias_query)))
    keys_all = split_heads(low_back(low(matmul_high(normed, w_key))))
    values_all = split_heads(low_back(low(matmul_high(normed, w_value) + bias_value)))
    scores = jnp.einsum('...qhd,...khd->...hqk', queries, keys_all, precision=lax.Precision.HIGHEST)
    scores = low_back(scores * HEAD_DIM ** (-0.5))
    if same_image is not None:
        scores = jnp.where(same_image, scores, MASKED)
    soft_weights = low(jax.nn.softmax(scores, axis=-1))
    mixed = jnp.einsum('...hqk,...khd->...qhd', soft_weights, values_all, precision=lax.Precision.HIGHEST)
    mixed = low_back(low(mixed.reshape(normed.shape)))
    return low_back(matmul_high(mixed, w_output) + bias_output)

def orthogonalize(matrix):
    current = matrix / (jnp.sqrt(jnp.sum(matrix * matrix)) + 1e-07)
    for sweep_index in range(5):
        gram = matmul_high(current, current.T)
        poly = NS_SECOND * gram + NS_THIRD * matmul_high(gram, gram)
        current = NS_FIRST * current + matmul_high(poly, current)
    return current

def reference(patches, regions, image_ids, attn_w, mlp_in, mlp_out, vec_params, patch_cot, region_cot, attn_mom, mlp_in_mom, mlp_out_mom, adam_first, adam_second):

    def forward(patch_vals, region_vals, attn_vals, in_vals, out_vals, vec_vals):
        patch_vals = low_back(patch_vals)
        attn_low = low(attn_vals)
        in_low = low(in_vals)
        out_low = low(out_vals)
        attn_weights = (attn_low[0], attn_low[1], attn_low[2], attn_low[3], vec_vals[4], vec_vals[5], vec_vals[6])
        bias_first = vec_vals[8:].reshape(FF)

        def one_group(items):
            patch_group, region_group, ids_group = items
            flat_regions = region_group.reshape(GH * GW, D)
            flat_ids = ids_group.reshape(GH * GW)
            same_image = (flat_ids[:, None] == flat_ids[None, :])[None]
            normed = low(layer_norm(flat_regions, vec_vals[0], vec_vals[1]))
            regional = flat_regions + attention_branch(normed, attn_weights, same_image)
            window_rows = jnp.concatenate([regional.reshape(GH, GW, 1, D), patch_group], axis=2)
            normed_rows = low(layer_norm(window_rows, vec_vals[0], vec_vals[1]))
            after_attention = window_rows + attention_branch(normed_rows, attn_weights, None)
            hidden = low(layer_norm(after_attention, vec_vals[2], vec_vals[3]))
            active = low_back(matmul_high(hidden, in_low) + bias_first)
            gelu_rows = low(jax.nn.gelu(active, approximate=False))
            result = after_attention + low_back(matmul_high(gelu_rows, out_low) + vec_vals[7])
            return (result[:, :, 1:], result[:, :, 0])
        return lax.map(jax.checkpoint(one_group), (patch_vals, region_vals, image_ids))
    outputs, pullback = jax.vjp(forward, patches.astype(jnp.float32), regions.astype(jnp.float32), attn_w, mlp_in, mlp_out, vec_params)
    d_patch, d_region, grad_attn, grad_in, grad_out, grad_vec = pullback((patch_cot.astype(jnp.float32), region_cot.astype(jnp.float32)))
    total = jnp.sum(grad_attn * grad_attn) + jnp.sum(grad_in * grad_in) + jnp.sum(grad_out * grad_out) + jnp.sum(grad_vec * grad_vec)
    grad_norm = jnp.sqrt(total)
    clip = jnp.minimum(1.0, CLIP_LIMIT / (grad_norm + 1e-06))
    decay_keep = 1.0 - MUON_RATE * MUON_DECAY
    attn_mom_new = MUON_MOMENTUM * attn_mom + clip * grad_attn
    new_attn = attn_w * decay_keep - MUON_RATE * jax.vmap(orthogonalize)(attn_mom_new)
    in_mom_new = MUON_MOMENTUM * mlp_in_mom + clip * grad_in
    new_in = mlp_in * decay_keep - MUON_RATE * orthogonalize(in_mom_new)
    out_mom_new = MUON_MOMENTUM * mlp_out_mom + clip * grad_out
    tall_scale = max(1.0, FF / D) ** 0.5
    new_out = mlp_out * decay_keep - MUON_RATE * tall_scale * orthogonalize(out_mom_new.T).T
    clipped = clip * grad_vec
    first = BETA_FIRST * adam_first + (1.0 - BETA_FIRST) * clipped
    second = BETA_SECOND * adam_second + (1.0 - BETA_SECOND) * clipped * clipped
    first_hat = first / (1.0 - BETA_FIRST ** OPT_STEP)
    second_hat = second / (1.0 - BETA_SECOND ** OPT_STEP)
    new_vec = vec_params - ADAM_RATE * first_hat / (jnp.sqrt(second_hat) + ADAM_EPS)
    out_patches, out_regions = outputs
    return (out_patches.astype(jnp.bfloat16), out_regions.astype(jnp.bfloat16), d_patch.astype(jnp.bfloat16), d_region, new_attn, attn_mom_new, new_in, in_mom_new, new_out, out_mom_new, new_vec, first, second, grad_norm)
```

```python
from functools import partial

import jax
import jax.numpy as jnp
from jax import lax
from jax.experimental import pallas as pl
from jax.experimental.pallas import tpu as pltpu
from jax.sharding import PartitionSpec as P

BF = jnp.bfloat16
F32 = jnp.float32

D = 512
HEADS = 16
HEAD_DIM = 32
FF = 2048
PATCH = 49
LIVE = 50
ROWS = 56
GROUP = 128
STACK = 4 * ROWS
OPT_STEP = 10
OPT = 4

SCALE = HEAD_DIM ** (-0.5)
NORM_EPS = 1e-05
MASKED = -1e30
NS_FIRST = 3.4445
NS_SECOND = -4.775
NS_THIRD = 2.0315
MUON_RATE = 0.5
MUON_MOMENTUM = 0.5
MUON_DECAY = 0.01
ADAM_RATE = 0.5
BETA_FIRST = 0.9
BETA_SECOND = 0.95
ADAM_EPS = 1e-08
CLIP_LIMIT = 1.0
DECAY_KEEP = 1.0 - MUON_RATE * MUON_DECAY
VMEM = 60 * 2**20

ERF_P = 0.3275911 * 0.5**0.5
ERF = tuple(0.5 * c for c in (0.254829592, -0.284496736, 1.421413741, -1.453152027, 1.061405429))
INV_SQRT_2PI = 0.3989422804014327
LOG2E = 1.4426950408889634


def nn(a, b):
    return lax.dot_general(a, b, (((1,), (0,)), ((), ())), preferred_element_type=F32)


def nt(a, b):
    return lax.dot_general(a, b, (((1,), (1,)), ((), ())), preferred_element_type=F32)


def tn(a, b):
    return lax.dot_general(a, b, (((0,), (0,)), ((), ())), preferred_element_type=F32)


def full(shape):
    return pl.BlockSpec(shape, lambda i: (0,) * len(shape))


def block(shape):
    return pl.BlockSpec(shape, lambda i: (i,) + (0,) * (len(shape) - 1))


def norm_parts(x):
    centre = x - jnp.mean(x, axis=-1, keepdims=True)
    scale = lax.rsqrt(jnp.mean(centre * centre, axis=-1, keepdims=True) + NORM_EPS)
    return centre * scale, scale


def norm_back(grad, xhat, scale, gain):
    inner = grad * gain
    first = jnp.mean(inner, axis=-1, keepdims=True)
    second = jnp.mean(inner * xhat, axis=-1, keepdims=True)
    return scale * (inner - first - xhat * second)


def head_masks():
    lane = lax.broadcasted_iota(jnp.int32, (1, GROUP), 1) // HEAD_DIM
    return [lane == h for h in range(4)]


def spread(rows, masks):
    return jnp.concatenate([jnp.where(m, rows, 0.0) for m in masks], axis=0).astype(BF)


def collect(stacked, masks, rows):
    out = stacked[:rows]
    for h in range(1, 4):
        out = jnp.where(masks[h], stacked[h * rows : (h + 1) * rows], out)
    return out


def fill_rows(held, patches, regions):
    count = held.shape[0]
    held[:, 0:PATCH, :] = patches.astype(F32)
    held[:, PATCH:LIVE, :] = regions.astype(F32)
    held[:, LIVE:ROWS, :] = jnp.zeros((count, ROWS - LIVE, D), F32)


def fold(x):
    return jnp.sum(x.reshape(x.shape[0] // 8, 8, x.shape[1]), axis=0)


def gelu_parts(a):
    bell = jnp.exp2(a * a * (-0.5 * LOG2E))
    t = 1.0 / (1.0 + ERF_P * jnp.abs(a))
    tail = ((((ERF[4] * t + ERF[3]) * t + ERF[2]) * t + ERF[1]) * t + ERF[0]) * t * bell
    share = jnp.where(a < 0, tail, 1.0 - tail)
    return a * share, share + a * bell * INV_SQRT_2PI


def attn_fwd_kernel(count, batch, p_ref, r_ref, wq_ref, wk_ref, wv_ref, wo_ref, vec_ref,
                    x1_ref, q_ref, k_ref, v_ref, o_ref, pt_ref, held):
    total = count * ROWS
    fill_rows(held, p_ref[...], r_ref[...])
    x = held[...].reshape(total, D)
    vec = vec_ref[...]
    xhat, _ = norm_parts(x)
    xn = (xhat * vec[0:1] + vec[1:2]).astype(BF)
    shape = (count, ROWS, D)
    q_ref[...] = (nn(xn, wq_ref[...]) + vec[4:5]).reshape(shape).astype(BF)
    k_ref[...] = nn(xn, wk_ref[...]).reshape(shape).astype(BF)
    v_ref[...] = (nn(xn, wv_ref[...]) + vec[5:6]).reshape(shape).astype(BF)
    masks = head_masks()
    live = lax.broadcasted_iota(jnp.int32, (ROWS, 1), 0) < LIVE

    def body(step, carry):
        units = [(step * batch + w, g) for w in range(batch) for g in range(4)]
        scores, probs = [], []
        for w, g in units:
            lanes = slice(GROUP * g, GROUP * (g + 1))
            scores.append(nt(k_ref[w, :, lanes], spread(q_ref[w, :, lanes].astype(F32), masks)))
        for (w, g), s in zip(units, scores):
            s = jnp.where(live, s, MASKED)
            e = jnp.exp((s - jnp.max(s, axis=0, keepdims=True)) * SCALE)
            p = (e * (1.0 / jnp.sum(e, axis=0, keepdims=True))).astype(BF)
            pt_ref[w, g] = p
            probs.append(p)
        for (w, g), p in zip(units, probs):
            lanes = slice(GROUP * g, GROUP * (g + 1))
            o_ref[w, :, lanes] = collect(tn(p, v_ref[w, :, lanes]), masks, ROWS).astype(BF)
        return carry

    lax.fori_loop(0, count // batch, body, 0)
    mixed = o_ref[...].astype(F32).reshape(total, D).astype(BF)
    x1_ref[...] = (x + nn(mixed, wo_ref[...]) + vec[6:7]).reshape(shape)


def attn_fwd(patches, region_rows, weights, vec, count=8, batch=4):
    windows = patches.shape[0]
    rows = lambda dtype: jax.ShapeDtypeStruct((windows, ROWS, D), dtype)
    return pl.pallas_call(
        partial(attn_fwd_kernel, count, batch),
        grid=(windows // count,),
        in_specs=[block((count, PATCH, D)), block((count, 1, D))] + [full((D, D))] * 4 + [full(vec.shape)],
        out_specs=[block((count, ROWS, D))] * 5 + [block((count, 4, ROWS, STACK))],
        out_shape=[rows(F32), rows(BF), rows(BF), rows(BF), rows(BF),
                   jax.ShapeDtypeStruct((windows, 4, ROWS, STACK), BF)],
        scratch_shapes=[pltpu.VMEM((count, ROWS, D), F32)],
        compiler_params=pltpu.CompilerParams(vmem_limit_bytes=VMEM),
        cost_estimate=pl.CostEstimate(flops=3 * 10**10, bytes_accessed=3 * 10**7, transcendentals=0),
        name="window_attention_forward",
    )(patches, region_rows, *weights, vec)


def mlp_kernel(count, steps, cols, x1_ref, pc_ref, rc_ref, w1a, w1b, w1c, w1d, w2a, w2b, w2c, w2d,
               vec_ref, b1_ref, op_ref, or_ref, dx1_ref, dw1_ref, dw2_ref, dv_ref, db1_ref,
               held, acc1, acc2):
    total = count * ROWS
    step = pl.program_id(0)

    @pl.when(step == 0)
    def _():
        for ref in (acc1, acc2, dv_ref, db1_ref):
            ref[...] = jnp.zeros_like(ref)

    vec = vec_ref[...]
    gain = vec[2:3]
    x1 = x1_ref[...].reshape(total, D)
    xhat, scale = norm_parts(x1)
    h = (xhat * gain + vec[3:4]).astype(BF)
    fill_rows(held, pc_ref[...].reshape(count, PATCH, D), rc_ref[...].reshape(count, 1, D))
    dy = held[...].reshape(total, D)
    dm = dy.astype(BF)
    ht = h.T
    dmt = dm.T
    w1s, w2s = (w1a, w1b, w1c, w1d), (w2a, w2b, w2c, w2d)
    y = x1 + vec[7:8]
    dh = jnp.zeros((total, D), F32)
    parts = [(j, slice(c, c + cols)) for j in range(4) for c in range(0, D, cols)]

    def activate(j, s):
        u, slope = gelu_parts(nn(h, w1s[j][:, s]) + b1_ref[j : j + 1, s])
        da = slope * nt(dm, w2s[j][s, :])
        db1_ref[j, :, s] += fold(da)
        return u.astype(BF), da.astype(BF)

    def apply(j, s, u, da):
        acc1[j, :, s] += nn(ht, da)
        acc2[j, :, s] += nn(dmt, u)
        return nn(u, w2s[j][s, :]), nt(da, w1s[j][:, s])

    held_pair = activate(*parts[0])
    for n in range(1, len(parts) + 1):
        later = activate(*parts[n]) if n < len(parts) else None
        up, down = apply(*parts[n - 1], *held_pair)
        y, dh = y + up, dh + down
        held_pair = later
    y = y.reshape(count, ROWS, D)
    op_ref[...] = y[:, :PATCH].astype(BF).reshape(op_ref.shape)
    or_ref[...] = y[:, PATCH:LIVE].astype(BF).reshape(or_ref.shape)
    dx1_ref[...] = (dy + norm_back(dh, xhat, scale, gain)).reshape(dx1_ref.shape)
    dv_ref[0] += fold(dh * xhat)
    dv_ref[1] += fold(dh)
    dv_ref[2] += fold(dy)

    @pl.when(step == steps - 1)
    def _():
        dw1_ref[...] = acc1[...].astype(BF)
        dw2_ref[...] = acc2[...].astype(BF)


def mlp(x1, chunk, patch_cot, region_cot, first, second, vec, bias_first, count=8, cols=256):
    sources, _, per, _, _ = x1.shape
    many = count // per
    steps = sources // many
    some = lambda rows: pl.BlockSpec((many, per, rows, D), lambda i: (i, 0, 0, 0))
    array = jax.ShapeDtypeStruct
    return pl.pallas_call(
        partial(mlp_kernel, count, steps, cols),
        grid=(steps,),
        in_specs=[pl.BlockSpec((many, 1, per, ROWS, D), lambda i: (i, chunk, 0, 0, 0)), some(PATCH), some(1)]
        + [full((D, D))] * 8 + [full(vec.shape), full((4, D))],
        out_specs=[some(PATCH), some(1), some(ROWS), full((4, D, D)), full((4, D, D)), full((3, 8, D)), full((4, 8, D))],
        out_shape=[array((sources, per, PATCH, D), BF), array((sources, per, 1, D), BF),
                   array((sources, per, ROWS, D), F32), array((4, D, D), BF), array((4, D, D), BF),
                   array((3, 8, D), F32), array((4, 8, D), F32)],
        scratch_shapes=[pltpu.VMEM((count, ROWS, D), F32), pltpu.VMEM((4, D, D), F32), pltpu.VMEM((4, D, D), F32)],
        compiler_params=pltpu.CompilerParams(vmem_limit_bytes=VMEM),
        cost_estimate=pl.CostEstimate(flops=4 * 10**10, bytes_accessed=3 * 10**7, transcendentals=0),
        name="mlp_forward_backward",
    )(x1, patch_cot, region_cot, *first, *second, vec, bias_first)


def attn_bwd_kernel(count, batch, chunks, *refs):
    p_ref, r_ref = refs[:2]
    dx1_refs = refs[2 : 2 + chunks]
    (q_ref, k_ref, v_ref, o_ref, pt_ref, wq_ref, wk_ref, wv_ref, wo_ref, vec_ref,
     dp_ref, dr_ref, dw_ref, dv_ref, held, dq_held, dk_held, dvv_held, do_held) = refs[2 + chunks :]
    total = count * ROWS
    shape = (count, ROWS, D)

    @pl.when(pl.program_id(0) == 0)
    def _():
        dw_ref[...] = jnp.zeros_like(dw_ref)
        dv_ref[...] = jnp.zeros_like(dv_ref)

    vec = vec_ref[...]
    gain = vec[0:1]
    dx1 = jnp.concatenate([ref[...] for ref in dx1_refs], axis=1).reshape(total, D)
    gb = dx1.astype(BF)
    do_held[...] = nt(gb, wo_ref[...]).astype(BF).astype(F32).reshape(shape)
    masks = head_masks()

    def body(step, carry):
        units = [(step * batch + w, g) for w in range(batch) for g in range(4)]
        grads, scores = [], []
        for w, g in units:
            lanes = slice(GROUP * g, GROUP * (g + 1))
            do_wide = spread(do_held[w, :, lanes], masks)
            dvv_held[w, :, lanes] = nn(pt_ref[w, g], do_wide)
            grads.append(nt(v_ref[w, :, lanes], do_wide))
        for (w, g), grad in zip(units, grads):
            p = pt_ref[w, g].astype(F32)
            both = p * grad
            scores.append((both - p * jnp.sum(both, axis=0, keepdims=True)).astype(BF))
        for (w, g), ds in zip(units, scores):
            lanes = slice(GROUP * g, GROUP * (g + 1))
            dk_held[w, :, lanes] = nn(ds, spread(q_ref[w, :, lanes].astype(F32), masks)) * SCALE
            dq_held[w, :, lanes] = collect(tn(ds, k_ref[w, :, lanes]), masks, ROWS) * SCALE
        return carry

    lax.fori_loop(0, count // batch, body, 0)
    fill_rows(held, p_ref[...], r_ref[...])
    xhat, scale = norm_parts(held[...].reshape(total, D))
    xn = (xhat * gain + vec[1:2]).astype(BF)
    dq_wide = dq_held[...].reshape(total, D)
    dv_wide = dvv_held[...].reshape(total, D)
    dq = dq_wide.astype(BF)
    dk = dk_held[...].reshape(total, D).astype(BF)
    dv = dv_wide.astype(BF)
    dn = nt(dq, wq_ref[...]) + nt(dk, wk_ref[...]) + nt(dv, wv_ref[...])
    dx = (dx1 + norm_back(dn, xhat, scale, gain)).reshape(shape)
    dp_ref[...] = dx[:, :PATCH].astype(BF)
    dr_ref[...] = dx[:, PATCH:LIVE]
    xt = xn.T
    dw_ref[0] += nn(xt, dq)
    dw_ref[1] += nn(xt, dk)
    dw_ref[2] += nn(xt, dv)
    mixed = o_ref[...].astype(F32).reshape(total, D).astype(BF)
    dw_ref[3] += nn(mixed.T, gb)
    dv_ref[0] += fold(dn * xhat)
    dv_ref[1] += fold(dn)
    dv_ref[2] += fold(dq_wide)
    dv_ref[3] += fold(dv_wide)
    dv_ref[4] += fold(dx1)


def attn_bwd(patches, region_rows, dx1_parts, saved, weights, vec, count=8, batch=4):
    windows = patches.shape[0]
    per = dx1_parts[0].shape[1]
    chunks = len(dx1_parts)
    many = count // (per * chunks)
    array = jax.ShapeDtypeStruct
    return pl.pallas_call(
        partial(attn_bwd_kernel, count, batch, chunks),
        grid=(windows // count,),
        in_specs=[block((count, PATCH, D)), block((count, 1, D))] + [block((many, per, ROWS, D))] * chunks
        + [block((count, ROWS, D))] * 4 + [block((count, 4, ROWS, STACK))] + [full((D, D))] * 4 + [full(vec.shape)],
        out_specs=[block((count, PATCH, D)), block((count, 1, D)), full((4, D, D)), full((5, 8, D))],
        out_shape=[array((windows, PATCH, D), BF), array((windows, 1, D), F32),
                   array((4, D, D), F32), array((5, 8, D), F32)],
        scratch_shapes=[pltpu.VMEM((count, ROWS, D), F32)] * 5,
        compiler_params=pltpu.CompilerParams(vmem_limit_bytes=VMEM),
        cost_estimate=pl.CostEstimate(flops=4 * 10**10, bytes_accessed=5 * 10**7, transcendentals=0),
        name="window_attention_backward",
    )(patches, region_rows, *dx1_parts, *saved, *weights, vec)


def halves(a):
    high = a.astype(BF)
    return high, (a - high.astype(F32)).astype(BF)


def product(a, b, passes, dot=nn):
    if passes == 1:
        return dot(a.astype(BF), b.astype(BF))
    (ah, al), (bh, bl) = halves(a), halves(b)
    return dot(ah, bh) + (dot(ah, bl) + dot(al, bh))


DIRECT_STEPS = (1, 1, 1, -1, -1)
GRAM_STEPS = (3, 3, 3, 3, -1)
NEAR_ZERO = NS_FIRST + NS_SECOND + NS_THIRD
NEAR_ONE = NS_SECOND + 2.0 * NS_THIRD


def identity():
    rows = lax.broadcasted_iota(jnp.int32, (D, D), 0)
    return rows == lax.broadcasted_iota(jnp.int32, (D, D), 1)


def polynomial(gram, eye, step):
    if step > 0:
        return NS_FIRST, NS_SECOND * gram + NS_THIRD * product(gram, gram, step)
    rest = gram - jnp.where(eye, 1.0, 0.0)
    return NEAR_ZERO, NEAR_ONE * rest + NS_THIRD * product(rest, rest, -step)


def moments_kernel(clip_ref, g1_ref, g2_ref, m1_ref, m2_ref, n1_ref, n2_ref, gram1_ref, gram2_ref):
    clip = clip_ref[0, 0]
    first = MUON_MOMENTUM * m1_ref[...] + clip * g1_ref[...].astype(F32)
    n1_ref[...] = first
    gram1_ref[...] = product(first, first, 3, nt)
    second = MUON_MOMENTUM * m2_ref[...] + clip * g2_ref[...].astype(F32).T
    n2_ref[...] = second
    gram2_ref[...] = product(second, second, 3, tn)


def square_kernel(clip_ref, g_ref, m_ref, w_ref, n_ref, new_ref):
    moment = MUON_MOMENTUM * m_ref[...] + clip_ref[0, 0] * g_ref[...].astype(F32)
    n_ref[...] = moment
    z = moment * (1.0 / (jnp.sqrt(jnp.sum(moment * moment)) + 1e-07))
    eye = identity()
    for step in DIRECT_STEPS:
        scale, poly = polynomial(product(z, z, abs(step), nt), eye, step)
        z = scale * z + product(poly, z, abs(step))
    new_ref[...] = w_ref[...] * DECAY_KEEP - MUON_RATE * z


def gram_steps(gram):
    eye = identity()
    factor = 1.0 / (jnp.sqrt(jnp.sum(jnp.where(eye, gram, 0.0))) + 1e-07)
    gram = gram * (factor * factor)
    steps = None
    for n, step in enumerate(GRAM_STEPS):
        scale, poly = polynomial(gram, eye, step)
        if steps is None:
            steps = jnp.where(eye, scale, 0.0) + poly
        else:
            steps = scale * steps + product(poly, steps, abs(step))
        if n < len(GRAM_STEPS) - 1:
            half = scale * gram + product(poly, gram, step)
            gram = scale * half + product(poly, half, step)
    return steps * factor


def sharded_kernel(gram1_ref, gram2_ref, n1_ref, n2_ref, w1_ref, w2_ref, new1_ref, new2_ref):
    z = product(gram_steps(gram1_ref[...]), n1_ref[...], 3)
    new1_ref[...] = w1_ref[...] * DECAY_KEEP - MUON_RATE * z
    z = product(n2_ref[...], gram_steps(gram2_ref[...]), 3)
    new2_ref[...] = w2_ref[...] * DECAY_KEEP - (MUON_RATE * max(1.0, FF / D) ** 0.5) * z


def whole_call(kernel, outs, name, *args):
    in_specs = [pl.BlockSpec(memory_space=pltpu.VMEM) for _ in args]
    if args[0].shape == (1, 1):
        in_specs[0] = pl.BlockSpec(memory_space=pltpu.SMEM)
    return pl.pallas_call(
        kernel,
        in_specs=in_specs,
        out_specs=[pl.BlockSpec(memory_space=pltpu.VMEM) for _ in outs],
        out_shape=[jax.ShapeDtypeStruct((D, D), dtype) for dtype in outs],
        compiler_params=pltpu.CompilerParams(vmem_limit_bytes=VMEM),
        cost_estimate=pl.CostEstimate(flops=10**10, bytes_accessed=10**7, transcendentals=0),
        name=name,
    )(*args)


def pair(values, bit):
    return lax.ppermute(values, "opt", [(i, i ^ bit) for i in range(OPT)])


def pieces_of_owners(own):
    mate = pair(own, 1)
    across = pair(own, 2)
    return [own, mate, across, pair(across, 1)]


def sum_at_owner(pieces):
    near = pair(jnp.stack([pieces[1], pieces[3]]), 1).astype(F32)
    far = (pieces[2].astype(F32) + near[1]).astype(BF)
    return pieces[0].astype(F32) + near[0] + pair(far, 2).astype(F32)


def share(x):
    copies = jnp.broadcast_to(x[None], (lax.axis_size("dp"),) + x.shape)
    return lax.all_to_all(copies, "dp", 0, 0, tiled=True)


def sum_over_dp(x):
    parts = x.reshape((lax.axis_size("dp"), -1) + x.shape[1:])
    parts = lax.all_to_all(parts, "dp", 0, 0, tiled=True)
    return share(jnp.sum(parts.astype(F32), axis=0).astype(BF)).reshape(x.shape)


def split_heads(x):
    return x.reshape(x.shape[0], HEADS, HEAD_DIM)


def regional_forward(queries, keys, values, same_image):
    scores = jnp.einsum("qhd,khd->hqk", split_heads(queries), split_heads(keys), preferred_element_type=F32)
    scores = jnp.where(same_image[None], scores * SCALE, MASKED)
    peak = jnp.max(scores, axis=-1, keepdims=True)
    raised = jnp.exp(scores - peak)
    sums = jnp.sum(raised, axis=-1, keepdims=True)
    low = (raised / sums).astype(BF)
    mixed = jnp.einsum("hqk,khd->qhd", low, split_heads(values), preferred_element_type=F32)
    return mixed.reshape(queries.shape), (peak + jnp.log(sums))[:, :, 0]


def regional_terms(queries, keys, values, grad_mixed, same_image, level, delta):
    scores = jnp.einsum("qhd,khd->hqk", split_heads(queries), split_heads(keys), preferred_element_type=F32)
    probs = jnp.where(same_image[None], jnp.exp(scores * SCALE - level[:, :, None]), 0.0)
    grads = jnp.einsum("qhd,khd->hqk", split_heads(grad_mixed), split_heads(values), preferred_element_type=F32)
    return probs.astype(BF), (probs * (grads - delta[:, :, None])).astype(BF)


def regional_backward(tokens, start, columns, same_rows, same_columns, weights, grads, level, delta):
    queries, keys, values = tokens
    grad_mixed = nt(grads, weights[3]).astype(BF)
    own = partial(columns, start=start)
    _, scores = regional_terms(own(queries), keys, values, own(grad_mixed), same_columns.T,
                               own(level.T).T, own(delta.T).T)
    dq = jnp.einsum("hqk,khd->qhd", scores, split_heads(keys), preferred_element_type=F32)
    probs, scores = regional_terms(queries, own(keys), own(values), grad_mixed, same_columns, level, delta)
    dk = jnp.einsum("hqk,qhd->khd", scores, split_heads(queries), preferred_element_type=F32)
    dv = jnp.einsum("hqk,qhd->khd", probs, split_heads(grad_mixed), preferred_element_type=F32)
    flat = lambda x: x.reshape(-1, D)
    return flat(dq) * SCALE, flat(dk) * SCALE, flat(dv)


def per_device(patches, regions, image_ids, attn_w, mlp_in, mlp_out, vec_params, patch_cot, region_cot,
               attn_mom, mlp_in_mom, mlp_out_mom, adam_first, adam_second):
    dp_size = lax.axis_size("dp")
    dp_index = lax.axis_index("dp")
    opt_index = lax.axis_index("opt")
    _, grid_rows, cols, _, _ = patch_cot.shape
    grid_cols = patches.shape[2]
    tokens = grid_rows * grid_cols
    chunks = 2 if cols % 2 == 0 else 1
    per = cols // chunks
    vec = vec_params
    order = opt_index ^ jnp.arange(OPT)

    attn_pieces = jnp.stack(pieces_of_owners(attn_w[0].astype(BF)))
    weights = [lax.dynamic_index_in_dim(attn_pieces, opt_index ^ j, 0, keepdims=False) for j in range(OPT)]
    canvas = share(regions[0]).transpose(1, 0, 2, 3).reshape(tokens, D)
    first = pieces_of_owners(mlp_in.astype(BF))
    second = pieces_of_owners(mlp_out.astype(BF))
    bias_first = jnp.take(vec[8:], order, axis=0)
    cots = []
    for c in range(chunks):
        part = slice(c * per, (c + 1) * per)
        moved = lax.all_to_all(patch_cot[0, :, part], "dp", 0, 0, tiled=True)
        moved_regions = lax.all_to_all(region_cot[0, :, part, None], "dp", 0, 0, tiled=True)
        cots.append((moved, moved_regions))

    def columns(x, start):
        wide = x.reshape((grid_rows, grid_cols) + x.shape[1:])
        return lax.dynamic_slice_in_dim(wide, start, cols, 1).reshape((grid_rows * cols,) + x.shape[1:])

    band = lambda x: lax.dynamic_slice_in_dim(x, dp_index * grid_cols, grid_cols, 0)
    start = dp_index * cols
    ids = image_ids[0].reshape(tokens)
    same_rows = band(ids)[:, None] == ids[None, :]
    same_columns = ids[:, None] == columns(ids, start)[None, :]
    canvas_hat, _ = norm_parts(canvas.astype(F32))
    canvas_low = (canvas_hat * vec[0] + vec[1]).astype(BF)
    reg_q = (nn(canvas_low, weights[0]) + vec[4]).astype(BF)
    reg_k = nn(canvas_low, weights[1]).astype(BF)
    reg_v = (nn(canvas_low, weights[2]) + vec[5]).astype(BF)
    reg_mixed, reg_level = regional_forward(band(reg_q), reg_k, reg_v, same_rows)
    reg_low = reg_mixed.astype(BF)
    region_rows = band(canvas).astype(F32) + nn(reg_low, weights[3]) + vec[6]
    region_rows = region_rows[:, None, :]
    level_all = share(reg_level.T).reshape(tokens, HEADS).T

    windows = patches.reshape(grid_cols, PATCH, D)
    x1, *saved = attn_fwd(windows, region_rows, weights, vec)
    x1 = x1.reshape(dp_size, chunks, per, ROWS, D)
    outs = [mlp(x1, c, *cots[c], first, second, vec, bias_first) for c in range(chunks)]
    moved = [lax.all_to_all(o[0], "dp", 0, 0, tiled=True) for o in outs]
    out_patches = jnp.concatenate(moved, axis=1)[None]
    moved = [lax.all_to_all(o[1], "dp", 0, 0, tiled=True) for o in outs]
    out_regions = jnp.concatenate(moved, axis=1)[None, :, :, 0]
    d_patches, d_region, d_attn, d_vec_attn = attn_bwd(windows, region_rows, [o[2] for o in outs], saved, weights, vec)
    d_patches = d_patches.reshape(patches.shape)

    add = lambda n, j: sum(o[n][j].astype(F32) for o in outs).astype(BF) if chunks > 1 else outs[0][n][j]
    own_first = sum_at_owner([add(3, j) for j in range(OPT)])
    own_second = sum_at_owner([add(4, j) for j in range(OPT)])
    own_mlp = sum_over_dp(jnp.concatenate([own_first, own_second], axis=1).astype(BF))

    grad_low = d_region[:, 0].astype(BF)
    mixed_grad = nt(grad_low, weights[3]).astype(BF).astype(F32)
    delta = jnp.sum(split_heads(mixed_grad * reg_mixed), axis=-1)
    grads_all = share(grad_low).reshape(tokens, D)
    delta_all = share(delta).reshape(tokens, HEADS).T
    dq, dk, dv = regional_backward((reg_q, reg_k, reg_v), start, columns, same_rows, same_columns,
                                   weights, grads_all, level_all, delta_all)
    dq_low, dk_low, dv_low = dq.astype(BF), dk.astype(BF), dv.astype(BF)
    d_normed = nt(dq_low, weights[0]) + nt(dk_low, weights[1]) + nt(dv_low, weights[2])
    own_hat, own_scale = norm_parts(columns(canvas, start).astype(F32))
    d_regions = columns(grads_all, start).astype(F32) + norm_back(d_normed, own_hat, own_scale, vec[0])
    d_regions = d_regions.reshape(regions.shape)
    own_low = columns(canvas_low, start)

    grad_attn = jnp.stack([
        (d_attn[0] + tn(own_low, dq_low)).astype(BF),
        (d_attn[1] + tn(own_low, dk_low)).astype(BF),
        (d_attn[2] + tn(own_low, dv_low)).astype(BF),
        (d_attn[3] + tn(reg_low, grad_low)).astype(BF),
    ])
    pieces = [lax.dynamic_index_in_dim(grad_attn, opt_index ^ j, 0, keepdims=False) for j in range(OPT)]
    own_attn = sum_over_dp(sum_at_owner(pieces).astype(BF))

    d_vec_attn = jnp.sum(d_vec_attn, axis=1)
    d_vec_mlp = sum(jnp.sum(o[5], axis=1) for o in outs)
    d_bias_first = jnp.take(sum(jnp.sum(o[6], axis=1) for o in outs), order, axis=0)
    sums = lambda x: jnp.sum(x, axis=0)
    grad_vec = jnp.concatenate([
        jnp.stack([
            d_vec_attn[0] + sums(d_normed * own_hat),
            d_vec_attn[1] + sums(d_normed),
            d_vec_mlp[0],
            d_vec_mlp[1],
            d_vec_attn[2] + sums(dq),
            d_vec_attn[3] + sums(dv),
            d_vec_attn[4] + sums(d_region[:, 0]),
            d_vec_mlp[2],
        ]),
        d_bias_first,
    ])
    grad_vec = grad_vec + pair(grad_vec, 1)
    grad_vec = grad_vec + pair(grad_vec, 2)
    grad_vec = jnp.sum(share(grad_vec), axis=0)

    squares = lambda x: jnp.sum(x.astype(F32) ** 2)
    total = jnp.full((8, 128), squares(own_attn) + squares(own_mlp))
    total = total + pair(total, 1)
    total = total + pair(total, 2)
    grad_norm = jnp.sqrt(total[0, 0] + squares(grad_vec))
    clip = jnp.minimum(1.0, CLIP_LIMIT / (grad_norm + 1e-06))
    clip_cell = clip.reshape(1, 1)
    first_mom, second_mom, gram_first, gram_second = whole_call(
        moments_kernel, [F32, F32, F32, F32], "mlp_moments", clip_cell,
        own_mlp[:, :D], own_mlp[:, D:], mlp_in_mom, mlp_out_mom)
    grams = jnp.stack([gram_first, gram_second])
    grams = grams + pair(grams, 1)
    grams = grams + pair(grams, 2)
    attn_mom_new, new_attn = whole_call(
        square_kernel, [F32, F32], "attention_update", clip_cell, own_attn, attn_mom[0], attn_w[0])
    new_first, new_second = whole_call(
        sharded_kernel, [F32, F32], "mlp_update", grams[0], grams[1], first_mom, second_mom, mlp_in, mlp_out)
    clipped = clip * grad_vec
    moment_one = BETA_FIRST * adam_first + (1.0 - BETA_FIRST) * clipped
    moment_two = BETA_SECOND * adam_second + (1.0 - BETA_SECOND) * clipped * clipped
    first_hat = moment_one / (1.0 - BETA_FIRST**OPT_STEP)
    second_hat = moment_two / (1.0 - BETA_SECOND**OPT_STEP)
    new_vec = vec_params - ADAM_RATE * first_hat / (jnp.sqrt(second_hat) + ADAM_EPS)
    return (out_patches, out_regions, d_patches, d_regions, new_attn[None], attn_mom_new[None], new_first, first_mom,
            new_second, second_mom, new_vec, moment_one, moment_two, grad_norm)


def solution(mesh):
    canvas = P("opt", None, "dp", None)
    wide = P("opt", None, "dp", None, None)
    bands = P("opt", "dp", None, None, None)
    square, right, down = P("opt", None, None), P(None, "opt"), P("opt", None)
    return jax.shard_map(
        per_device,
        mesh=mesh,
        in_specs=(bands, canvas, square, square, right, down, P(), wide, canvas, square, right, down, P(), P()),
        out_specs=(wide, canvas, bands, canvas, square, square, right, right, down, down, P(), P(), P(), P()),
        check_vma=False,
    )
```

```python
from functools import partial

import jax
import jax.numpy as jnp
from jax import lax
from jax.experimental import pallas as pl
from jax.experimental.pallas import tpu as pltpu
from jax.sharding import PartitionSpec as P

BF = jnp.bfloat16
F32 = jnp.float32

D = 512
HEADS = 16
HEAD_DIM = 32
FF = 2048
PATCH = 49
LIVE = 50
ROWS = 56
GROUP = 128
STACK = 4 * ROWS
OPT_STEP = 10
OPT = 4

SCALE = HEAD_DIM ** (-0.5)
NORM_EPS = 1e-05
MASKED = -1e30
NS_FIRST = 3.4445
NS_SECOND = -4.775
NS_THIRD = 2.0315
MUON_RATE = 0.5
MUON_MOMENTUM = 0.5
MUON_DECAY = 0.01
ADAM_RATE = 0.5
BETA_FIRST = 0.9
BETA_SECOND = 0.95
ADAM_EPS = 1e-08
CLIP_LIMIT = 1.0
DECAY_KEEP = 1.0 - MUON_RATE * MUON_DECAY
VMEM = 60 * 2**20

ERF_P = 0.3275911 * 0.5**0.5
ERF = tuple(0.5 * c for c in (0.254829592, -0.284496736, 1.421413741, -1.453152027, 1.061405429))
INV_SQRT_2PI = 0.3989422804014327
LOG2E = 1.4426950408889634


def nn(a, b):
    return lax.dot_general(a, b, (((1,), (0,)), ((), ())), preferred_element_type=F32)


def nt(a, b):
    return lax.dot_general(a, b, (((1,), (1,)), ((), ())), preferred_element_type=F32)


def tn(a, b):
    return lax.dot_general(a, b, (((0,), (0,)), ((), ())), preferred_element_type=F32)


def full(shape):
    return pl.BlockSpec(shape, lambda i: (0,) * len(shape))


def block(shape):
    return pl.BlockSpec(shape, lambda i: (i,) + (0,) * (len(shape) - 1))


def norm_parts(x):
    centre = x - jnp.mean(x, axis=-1, keepdims=True)
    scale = lax.rsqrt(jnp.mean(centre * centre, axis=-1, keepdims=True) + NORM_EPS)
    return centre * scale, scale


def norm_back(grad, xhat, scale, gain):
    inner = grad * gain
    first = jnp.mean(inner, axis=-1, keepdims=True)
    second = jnp.mean(inner * xhat, axis=-1, keepdims=True)
    return scale * (inner - first - xhat * second)


def head_masks():
    lane = lax.broadcasted_iota(jnp.int32, (1, GROUP), 1) // HEAD_DIM
    return [lane == h for h in range(4)]


def spread(rows, masks):
    return jnp.concatenate([jnp.where(m, rows, 0.0) for m in masks], axis=0).astype(BF)


def collect(stacked, masks, rows):
    out = stacked[:rows]
    for h in range(1, 4):
        out = jnp.where(masks[h], stacked[h * rows : (h + 1) * rows], out)
    return out


def lane_groups(x):
    return [x[:, GROUP * g : GROUP * (g + 1)] for g in range(4)]


def hold(ref, total, x):
    for g, part in enumerate(lane_groups(x)):
        ref[g, :total] = part


def held_rows(ref, total):
    return jnp.concatenate([ref[g, :total] for g in range(4)], axis=1)


def fold(x):
    return jnp.sum(x.reshape(x.shape[0] // 8, 8, x.shape[1]), axis=0)


def gelu_parts(a):
    bell = jnp.exp2(a * a * (-0.5 * LOG2E))
    t = 1.0 / (1.0 + ERF_P * jnp.abs(a))
    tail = ((((ERF[4] * t + ERF[3]) * t + ERF[2]) * t + ERF[1]) * t + ERF[0]) * t * bell
    share = jnp.where(a < 0, tail, 1.0 - tail)
    return a * share, share + a * bell * INV_SQRT_2PI


def attn_fwd_kernel(count, batch, p_ref, r_ref, wq_ref, wk_ref, wv_ref, wo_ref, vec_ref,
                    x1_ref, q_ref, k_ref, v_ref, o_ref, pt_ref, q_held, k_held, v_held, o_held):
    total = count * LIVE

    @pl.when(pl.program_id(0) == 0)
    def _():
        for ref in (q_held, k_held, v_held):
            ref[:, total:] = jnp.zeros((4, count * (ROWS - LIVE), GROUP), F32)

    x = jnp.concatenate([p_ref[...].astype(F32), r_ref[...][None]], axis=0).reshape(total, D)
    vec = vec_ref[...]
    xhat, _ = norm_parts(x)
    xn = (xhat * vec[0:1] + vec[1:2]).astype(BF)
    hold(q_held, total, nn(xn, wq_ref[...]) + vec[4:5])
    hold(k_held, total, nn(xn, wk_ref[...]))
    hold(v_held, total, nn(xn, wv_ref[...]) + vec[5:6])
    masks = head_masks()
    live = lax.broadcasted_iota(jnp.int32, (ROWS, 1), 0) < LIVE

    def body(step, carry):
        units = [(step * batch + w, g) for w in range(batch) for g in range(4)]
        scores, probs = [], []
        for w, g in units:
            lanes = slice(GROUP * g, GROUP * (g + 1))
            rows = pl.ds(w, ROWS, stride=count)
            q = q_held[g, rows, :]
            q_ref[w, :, lanes] = q.astype(BF)
            k = k_held[g, rows, :].astype(BF)
            k_ref[w, :, lanes] = k
            scores.append(nt(k, spread(q, masks)))
        for (w, g), s in zip(units, scores):
            s = jnp.where(live, s, MASKED)
            e = jnp.exp((s - jnp.max(s, axis=0, keepdims=True)) * SCALE)
            p = (e * (1.0 / jnp.sum(e, axis=0, keepdims=True))).astype(BF)
            pt_ref[w, g] = p
            probs.append(p)
        for (w, g), p in zip(units, probs):
            lanes = slice(GROUP * g, GROUP * (g + 1))
            rows = pl.ds(w, ROWS, stride=count)
            v = v_held[g, rows, :].astype(BF)
            v_ref[w, :, lanes] = v
            o_held[g, rows, :] = collect(tn(p, v), masks, ROWS)
        return carry

    lax.fori_loop(0, count // batch, body, 0)
    mixed = held_rows(o_held, total).astype(BF)
    o_ref[...] = mixed.reshape(LIVE, count, D)
    x1_ref[...] = (x + nn(mixed, wo_ref[...]) + vec[6:7]).reshape(LIVE, count, D)


def middle(rows, count):
    return pl.BlockSpec((rows, count, D), lambda i: (0, i, 0))


def attn_fwd(patches, region_rows, weights, vec, count=16, batch=4):
    windows = patches.shape[1]
    array = jax.ShapeDtypeStruct
    return pl.pallas_call(
        partial(attn_fwd_kernel, count, batch),
        grid=(windows // count,),
        in_specs=[middle(PATCH, count), block((count, D))] + [full((D, D))] * 4 + [full(vec.shape)],
        out_specs=[middle(LIVE, count)] + [block((count, ROWS, D))] * 3
        + [middle(LIVE, count), block((count, 4, ROWS, STACK))],
        out_shape=[array((LIVE, windows, D), F32)] + [array((windows, ROWS, D), BF)] * 3
        + [array((LIVE, windows, D), BF), array((windows, 4, ROWS, STACK), BF)],
        scratch_shapes=[pltpu.VMEM((4, count * ROWS, GROUP), F32)] * 4,
        compiler_params=pltpu.CompilerParams(vmem_limit_bytes=VMEM),
        cost_estimate=pl.CostEstimate(flops=3 * 10**10, bytes_accessed=3 * 10**7, transcendentals=0),
        name="window_attention_forward",
    )(patches, region_rows, *weights, vec)


def mlp_kernel(many, sources, cols, steps, lanes, x1_ref, pc_ref, w1a, w1b, w1c, w1d, w2a, w2b, w2c, w2d,
               vec_ref, b1_ref, op_ref, dx1_ref, dw1_ref, dw2_ref, dv_ref, db1_ref, acc1, acc2):
    total = many * sources * cols
    step = pl.program_id(0)

    @pl.when(step == 0)
    def _():
        for ref in (acc1, acc2, dv_ref, db1_ref):
            ref[...] = jnp.zeros_like(ref)

    vec = vec_ref[...]
    gain = vec[2:3]
    x1 = x1_ref[...].reshape(total, D)
    xhat, scale = norm_parts(x1)
    h = (xhat * gain + vec[3:4]).astype(BF)
    for s in range(sources):
        dx1_ref[:, s * cols : (s + 1) * cols] = pc_ref[s].astype(F32)
    dy = dx1_ref[...].reshape(total, D)
    dm = dy.astype(BF)
    ht = h.T
    dmt = dm.T
    w1s, w2s = (w1a, w1b, w1c, w1d), (w2a, w2b, w2c, w2d)
    y = x1 + vec[7:8]
    dh = jnp.zeros((total, D), F32)
    parts = [(j, slice(c, c + lanes)) for j in range(4) for c in range(0, D, lanes)]

    def activate(j, s):
        u, slope = gelu_parts(nn(h, w1s[j][:, s]) + b1_ref[j : j + 1, s])
        da = slope * nt(dm, w2s[j][s, :])
        db1_ref[j, :, s] += fold(da)
        return u.astype(BF), da.astype(BF)

    def apply(j, s, u, da):
        acc1[j, :, s] += nn(ht, da)
        acc2[j, :, s] += nn(dmt, u)
        return nn(u, w2s[j][s, :]), nt(da, w1s[j][:, s])

    held_pair = activate(*parts[0])
    for n in range(1, len(parts) + 1):
        later = activate(*parts[n]) if n < len(parts) else None
        up, down = apply(*parts[n - 1], *held_pair)
        y, dh = y + up, dh + down
        held_pair = later
    y = y.reshape(many, sources * cols, D)
    for s in range(sources):
        op_ref[s] = y[:, s * cols : (s + 1) * cols].astype(BF)
    dy = dx1_ref[...].reshape(total, D)
    dx1_ref[...] = (dy + norm_back(dh, xhat, scale, gain)).reshape(dx1_ref.shape)
    dv_ref[0] += fold(dh * xhat)
    dv_ref[1] += fold(dh)
    dv_ref[2] += fold(dy)

    @pl.when(step == steps - 1)
    def _():
        dw1_ref[...] = acc1[...].astype(BF)
        dw2_ref[...] = acc2[...].astype(BF)


def mlp(x1, first_position, cot, first, second, vec, bias_first, many=10, lanes=256):
    sources, positions, cols, _ = cot.shape
    windows = x1.shape[1]
    steps = positions // many
    skip = first_position // many
    some = pl.BlockSpec((sources, many, cols, D), lambda i: (0, i, 0, 0))
    array = jax.ShapeDtypeStruct
    return pl.pallas_call(
        partial(mlp_kernel, many, sources, cols, steps, lanes),
        grid=(steps,),
        in_specs=[pl.BlockSpec((many, windows, D), lambda i: (i + skip, 0, 0)), some]
        + [full((D, D))] * 8 + [full(vec.shape), full((4, D))],
        out_specs=[some, block((many, windows, D)), full((4, D, D)), full((4, D, D)), full((3, 8, D)), full((4, 8, D))],
        out_shape=[array(cot.shape, BF), array((positions, windows, D), F32), array((4, D, D), BF),
                   array((4, D, D), BF), array((3, 8, D), F32), array((4, 8, D), F32)],
        scratch_shapes=[pltpu.VMEM((4, D, D), F32), pltpu.VMEM((4, D, D), F32)],
        compiler_params=pltpu.CompilerParams(vmem_limit_bytes=VMEM),
        cost_estimate=pl.CostEstimate(flops=4 * 10**10, bytes_accessed=3 * 10**7, transcendentals=0),
        name="mlp_forward_backward",
    )(x1, cot, *first, *second, vec, bias_first)


def attn_bwd_kernel(count, batch, chunks, *refs):
    p_ref, r_ref = refs[:2]
    dx1_refs = refs[2 : 2 + chunks]
    (q_ref, k_ref, v_ref, o_ref, pt_ref, wq_ref, wk_ref, wv_ref, wo_ref, vec_ref,
     dp_ref, dr_ref, dw_ref, dv_ref, dq_held, dk_held, dvv_held, do_held) = refs[2 + chunks :]
    total = count * LIVE

    @pl.when(pl.program_id(0) == 0)
    def _():
        dw_ref[...] = jnp.zeros_like(dw_ref)
        dv_ref[...] = jnp.zeros_like(dv_ref)
        do_held[:, total:] = jnp.zeros((4, count * (ROWS - LIVE), GROUP), F32)

    vec = vec_ref[...]
    gain = vec[0:1]
    dx1 = jnp.concatenate([ref[...] for ref in dx1_refs], axis=0).reshape(total, D)
    gb = dx1.astype(BF)
    hold(do_held, total, nt(gb, wo_ref[...]))
    masks = head_masks()

    def body(step, carry):
        units = [(step * batch + w, g) for w in range(batch) for g in range(4)]
        grads, scores = [], []
        for w, g in units:
            lanes = slice(GROUP * g, GROUP * (g + 1))
            rows = pl.ds(w, ROWS, stride=count)
            do_wide = spread(do_held[g, rows, :], masks)
            dvv_held[g, rows, :] = nn(pt_ref[w, g], do_wide)
            grads.append(nt(v_ref[w, :, lanes], do_wide))
        for (w, g), grad in zip(units, grads):
            p = pt_ref[w, g].astype(F32)
            both = p * grad
            scores.append((both - p * jnp.sum(both, axis=0, keepdims=True)).astype(BF))
        for (w, g), ds in zip(units, scores):
            lanes = slice(GROUP * g, GROUP * (g + 1))
            rows = pl.ds(w, ROWS, stride=count)
            dk_held[g, rows, :] = nn(ds, spread(q_ref[w, :, lanes].astype(F32), masks)) * SCALE
            dq_held[g, rows, :] = collect(tn(ds, k_ref[w, :, lanes]), masks, ROWS) * SCALE
        return carry

    lax.fori_loop(0, count // batch, body, 0)
    x = jnp.concatenate([p_ref[...].astype(F32), r_ref[...][None]], axis=0).reshape(total, D)
    xhat, scale = norm_parts(x)
    xn = (xhat * gain + vec[1:2]).astype(BF)
    dq_wide = held_rows(dq_held, total)
    dv_wide = held_rows(dvv_held, total)
    dq = dq_wide.astype(BF)
    dk = held_rows(dk_held, total).astype(BF)
    dv = dv_wide.astype(BF)
    dn = nt(dq, wq_ref[...]) + nt(dk, wk_ref[...]) + nt(dv, wv_ref[...])
    dx = (dx1 + norm_back(dn, xhat, scale, gain)).reshape(LIVE, count, D)
    dp_ref[...] = dx[:PATCH].astype(BF)
    dr_ref[...] = dx[PATCH]
    xt = xn.T
    dw_ref[0] += nn(xt, dq)
    dw_ref[1] += nn(xt, dk)
    dw_ref[2] += nn(xt, dv)
    dw_ref[3] += nn(o_ref[...].reshape(total, D).T, gb)
    dv_ref[0] += fold(dn * xhat)
    dv_ref[1] += fold(dn)
    dv_ref[2] += fold(dq_wide)
    dv_ref[3] += fold(dv_wide)
    dv_ref[4] += fold(dx1)


def attn_bwd(patches, region_rows, dx1_parts, saved, weights, vec, count=16, batch=4):
    windows = patches.shape[1]
    array = jax.ShapeDtypeStruct
    return pl.pallas_call(
        partial(attn_bwd_kernel, count, batch, len(dx1_parts)),
        grid=(windows // count,),
        in_specs=[middle(PATCH, count), block((count, D))] + [middle(part.shape[0], count) for part in dx1_parts]
        + [block((count, ROWS, D))] * 3 + [middle(LIVE, count), block((count, 4, ROWS, STACK))]
        + [full((D, D))] * 4 + [full(vec.shape)],
        out_specs=[middle(PATCH, count), block((count, D)), full((4, D, D)), full((5, 8, D))],
        out_shape=[array((PATCH, windows, D), BF), array((windows, D), F32),
                   array((4, D, D), F32), array((5, 8, D), F32)],
        scratch_shapes=[pltpu.VMEM((4, count * ROWS, GROUP), F32)] * 4,
        compiler_params=pltpu.CompilerParams(vmem_limit_bytes=VMEM),
        cost_estimate=pl.CostEstimate(flops=4 * 10**10, bytes_accessed=5 * 10**7, transcendentals=0),
        name="window_attention_backward",
    )(patches, region_rows, *dx1_parts, *saved, *weights, vec)


def regional_fwd_kernel(canvas_ref, band_ref, ids_ref, band_ids_ref, wq_ref, wk_ref, wv_ref, wo_ref, vec_ref,
                        r1_ref, mixed_ref, level_ref, q_ref, k_ref, v_ref):
    vec = vec_ref[...]
    xhat, _ = norm_parts(canvas_ref[...].astype(F32))
    low = (xhat * vec[0:1] + vec[1:2]).astype(BF)
    q_ref[...] = (nn(low, wq_ref[...]) + vec[4:5]).astype(BF)
    k_ref[...] = nn(low, wk_ref[...]).astype(BF)
    v_ref[...] = (nn(low, wv_ref[...]) + vec[5:6]).astype(BF)
    band = band_ref[...].astype(F32)
    rows = band.shape[0]
    xhat, _ = norm_parts(band)
    q = nn((xhat * vec[0:1] + vec[1:2]).astype(BF), wq_ref[...]) + vec[4:5]
    masks = head_masks()
    same = ids_ref[...] == band_ids_ref[...]
    scores, probs = [], []
    for g in range(4):
        lanes = slice(GROUP * g, GROUP * (g + 1))
        scores.append(nt(k_ref[:, lanes], spread(q[:, lanes], masks)))
    for g, s in enumerate(scores):
        s = jnp.where(same, s, MASKED)
        peak = jnp.max(s, axis=0, keepdims=True)
        e = jnp.exp((s - peak) * SCALE)
        sums = jnp.sum(e, axis=0, keepdims=True)
        level_ref[g : g + 1] = peak * SCALE + jnp.log(sums)
        probs.append((e * (1.0 / sums)).astype(BF))
    for g, p in enumerate(probs):
        lanes = slice(GROUP * g, GROUP * (g + 1))
        mixed_ref[:, lanes] = collect(tn(p, v_ref[:, lanes]), masks, rows)
    r1_ref[...] = band + nn(mixed_ref[...].astype(BF), wo_ref[...]) + vec[6:7]


def in_vmem(kernel, outs, name, *args):
    return pl.pallas_call(
        kernel,
        in_specs=[pl.BlockSpec(memory_space=pltpu.VMEM) for _ in args],
        out_specs=[pl.BlockSpec(memory_space=pltpu.VMEM) for _ in outs],
        out_shape=[jax.ShapeDtypeStruct(*out) for out in outs],
        compiler_params=pltpu.CompilerParams(vmem_limit_bytes=VMEM),
        cost_estimate=pl.CostEstimate(flops=10**10, bytes_accessed=10**7, transcendentals=0),
        name=name,
    )(*args)


def payload_kernel(dr_ref, mixed_ref, level_ref, wo_ref, grad_ref, extra_ref):
    low = dr_ref[...].astype(BF)
    grad_ref[...] = low
    both = nt(low, wo_ref[...]).astype(BF).astype(F32) * mixed_ref[...]
    head = lax.broadcasted_iota(jnp.int32, (D, GROUP), 0) // HEAD_DIM
    lane = lax.broadcasted_iota(jnp.int32, (D, GROUP), 1)
    pick = ((head == lane) | (head + HEADS == lane)).astype(BF)
    high, low_part = halves(both)
    rest = (both - high.astype(F32) - low_part.astype(F32)).astype(BF)
    delta = nn(high, pick) + (nn(low_part, pick) + nn(rest, pick))
    top = delta.astype(BF).astype(F32)
    lane = lax.broadcasted_iota(jnp.int32, (1, GROUP), 1)
    extra = jnp.where(lane < HEADS, top, jnp.where(lane < 2 * HEADS, delta - top, level_ref[...]))
    extra_ref[...] = extra.astype(BF)


def regional_bwd_kernel(own_rows, q_ref, k_ref, v_ref, grads_ref, qo_ref, ko_ref, vo_ref, own_ref, ids_ref, ids_row_ref,
                        ids_own_ref, ids_own_row_ref, level_ref, delta_ref, level_own_ref, delta_own_ref,
                        grads_own_ref, mixed_ref, band_grad_ref, dw_ref, wq_ref, wk_ref, wv_ref, wo_ref, vec_ref,
                        dr_ref, gw_ref, gv_ref):
    vec = vec_ref[...]
    masks = head_masks()
    do = nt(grads_ref[...], wo_ref[...]).astype(BF).astype(F32)
    do_own = nt(grads_own_ref[...], wo_ref[...]).astype(BF).astype(F32)
    same_own = ids_ref[...] == ids_own_row_ref[...]
    same = ids_own_ref[...] == ids_row_ref[...]
    lanes = [slice(GROUP * g, GROUP * (g + 1)) for g in range(4)]
    first, second = [], []
    dqs, dks, dvs = [], [], []
    for g in range(4):
        q_wide = spread(qo_ref[:, lanes[g]].astype(F32), masks)
        do_wide = spread(do_own[:, lanes[g]], masks)
        first.append((nt(k_ref[:, lanes[g]], q_wide), nt(v_ref[:, lanes[g]], do_wide)))
        q_wide = spread(q_ref[:, lanes[g]].astype(F32), masks)
        do_wide = spread(do[:, lanes[g]], masks)
        second.append((nt(ko_ref[:, lanes[g]], q_wide), nt(vo_ref[:, lanes[g]], do_wide), q_wide, do_wide))
    for g in range(4):
        s, dp = first[g]
        p = jnp.where(same_own, jnp.exp(s * SCALE - level_own_ref[g : g + 1]), 0.0)
        ds = (p * (dp - delta_own_ref[g : g + 1])).astype(BF)
        dqs.append(collect(tn(ds, k_ref[:, lanes[g]]), masks, own_rows) * SCALE)
        s, dp, q_wide, do_wide = second[g]
        p = jnp.where(same, jnp.exp(s * SCALE - level_ref[g : g + 1]), 0.0)
        ds = (p * (dp - delta_ref[g : g + 1])).astype(BF)
        dvs.append(nn(p.astype(BF), do_wide))
        dks.append(nn(ds, q_wide) * SCALE)
    xhat, scale = norm_parts(own_ref[...].astype(F32))
    low = (xhat * vec[0:1] + vec[1:2]).astype(BF)
    dq_wide, dk_wide, dv_wide = (jnp.concatenate(x, axis=1) for x in (dqs, dks, dvs))
    dq, dk, dv = dq_wide.astype(BF), dk_wide.astype(BF), dv_wide.astype(BF)
    dn = nt(dq, wq_ref[...]) + nt(dk, wk_ref[...]) + nt(dv, wv_ref[...])
    dr_ref[...] = grads_own_ref[...].astype(F32) + norm_back(dn, xhat, scale, vec[0:1])
    gw_ref[0] = (dw_ref[0] + tn(low, dq)).astype(BF)
    gw_ref[1] = (dw_ref[1] + tn(low, dk)).astype(BF)
    gw_ref[2] = (dw_ref[2] + tn(low, dv)).astype(BF)
    gw_ref[3] = (dw_ref[3] + tn(mixed_ref[...].astype(BF), band_grad_ref[...])).astype(BF)
    gv_ref[0] = fold(dn * xhat)
    gv_ref[1] = fold(dn)
    gv_ref[2] = fold(dq_wide)
    gv_ref[3] = fold(dv_wide)
    gv_ref[4] = fold(band_grad_ref[...].astype(F32))


def halves(a):
    high = a.astype(BF)
    return high, (a - high.astype(F32)).astype(BF)


def product(a, b, passes, dot=nn):
    if passes == 1:
        return dot(a.astype(BF), b.astype(BF))
    (ah, al), (bh, bl) = halves(a), halves(b)
    return dot(ah, bh) + (dot(ah, bl) + dot(al, bh))


DIRECT_STEPS = (1, 1, 1, -1, -1)
GRAM_STEPS = (3, 3, 3, 3, -1)
NEAR_ZERO = NS_FIRST + NS_SECOND + NS_THIRD
NEAR_ONE = NS_SECOND + 2.0 * NS_THIRD


def identity():
    rows = lax.broadcasted_iota(jnp.int32, (D, D), 0)
    return rows == lax.broadcasted_iota(jnp.int32, (D, D), 1)


def polynomial(gram, eye, step):
    if step > 0:
        return NS_FIRST, NS_SECOND * gram + NS_THIRD * product(gram, gram, step)
    rest = gram - jnp.where(eye, 1.0, 0.0)
    return NEAR_ZERO, NEAR_ONE * rest + NS_THIRD * product(rest, rest, -step)


def moments_kernel(clip_ref, g1_ref, g2_ref, m1_ref, m2_ref, n1_ref, n2_ref, gram1_ref, gram2_ref):
    clip = clip_ref[0, 0]
    first = MUON_MOMENTUM * m1_ref[...] + clip * g1_ref[...].astype(F32)
    n1_ref[...] = first
    gram1_ref[...] = product(first, first, 3, nt)
    second = MUON_MOMENTUM * m2_ref[...] + clip * g2_ref[...].astype(F32).T
    n2_ref[...] = second
    gram2_ref[...] = product(second, second, 3, tn)


def square_kernel(clip_ref, g_ref, m_ref, w_ref, n_ref, new_ref):
    moment = MUON_MOMENTUM * m_ref[...] + clip_ref[0, 0] * g_ref[...].astype(F32)
    n_ref[...] = moment
    z = moment * (1.0 / (jnp.sqrt(jnp.sum(moment * moment)) + 1e-07))
    eye = identity()
    for step in DIRECT_STEPS:
        scale, poly = polynomial(product(z, z, abs(step), nt), eye, step)
        z = scale * z + product(poly, z, abs(step))
    new_ref[...] = w_ref[...] * DECAY_KEEP - MUON_RATE * z


def gram_steps(gram):
    eye = identity()
    factor = 1.0 / (jnp.sqrt(jnp.sum(jnp.where(eye, gram, 0.0))) + 1e-07)
    gram = gram * (factor * factor)
    steps = None
    for n, step in enumerate(GRAM_STEPS):
        scale, poly = polynomial(gram, eye, step)
        if steps is None:
            steps = jnp.where(eye, scale, 0.0) + poly
        else:
            steps = scale * steps + product(poly, steps, abs(step))
        if n < len(GRAM_STEPS) - 1:
            half = scale * gram + product(poly, gram, step)
            gram = scale * half + product(poly, half, step)
    return steps * factor


def sharded_kernel(gram1_ref, gram2_ref, n1_ref, n2_ref, w1_ref, w2_ref, new1_ref, new2_ref):
    z = product(gram_steps(gram1_ref[...]), n1_ref[...], 3)
    new1_ref[...] = w1_ref[...] * DECAY_KEEP - MUON_RATE * z
    z = product(n2_ref[...], gram_steps(gram2_ref[...]), 3)
    new2_ref[...] = w2_ref[...] * DECAY_KEEP - (MUON_RATE * max(1.0, FF / D) ** 0.5) * z


def whole_call(kernel, outs, name, *args):
    in_specs = [pl.BlockSpec(memory_space=pltpu.VMEM) for _ in args]
    if args[0].shape == (1, 1):
        in_specs[0] = pl.BlockSpec(memory_space=pltpu.SMEM)
    return pl.pallas_call(
        kernel,
        in_specs=in_specs,
        out_specs=[pl.BlockSpec(memory_space=pltpu.VMEM) for _ in outs],
        out_shape=[jax.ShapeDtypeStruct((D, D), dtype) for dtype in outs],
        compiler_params=pltpu.CompilerParams(vmem_limit_bytes=VMEM),
        cost_estimate=pl.CostEstimate(flops=10**10, bytes_accessed=10**7, transcendentals=0),
        name=name,
    )(*args)


def pair(values, bit):
    return lax.ppermute(values, "opt", [(i, i ^ bit) for i in range(OPT)])


def pieces_of_owners(own):
    mate = pair(own, 1)
    across = pair(own, 2)
    return [own, mate, across, pair(across, 1)]


def sum_at_owner(pieces):
    near = pair(jnp.stack([pieces[1], pieces[3]]), 1).astype(F32)
    far = (pieces[2].astype(F32) + near[1]).astype(BF)
    return pieces[0].astype(F32) + near[0] + pair(far, 2).astype(F32)


def share(x):
    copies = jnp.broadcast_to(x[None], (lax.axis_size("dp"),) + x.shape)
    return lax.all_to_all(copies, "dp", 0, 0, tiled=True)


def sum_over_dp(x):
    parts = x.reshape((lax.axis_size("dp"), -1) + x.shape[1:])
    parts = lax.all_to_all(parts, "dp", 0, 0, tiled=True)
    return share(jnp.sum(parts.astype(F32), axis=0).astype(BF)).reshape(x.shape)


def split_heads(x):
    return x.reshape(x.shape[0], HEADS, HEAD_DIM)


def regional_forward(canvas, band, same, weights, vec):
    low = lambda x: (norm_parts(x.astype(F32))[0] * vec[0] + vec[1]).astype(BF)
    normed = low(canvas)
    queries = (nn(normed, weights[0]) + vec[4]).astype(BF)
    keys = nn(normed, weights[1]).astype(BF)
    values = (nn(normed, weights[2]) + vec[5]).astype(BF)
    own = (nn(low(band), weights[0]) + vec[4]).astype(BF)
    scores = jnp.einsum("qhd,khd->hqk", split_heads(own), split_heads(keys), preferred_element_type=F32)
    scores = jnp.where(same[None], scores * SCALE, MASKED)
    peak = jnp.max(scores, axis=-1, keepdims=True)
    raised = jnp.exp(scores - peak)
    sums = jnp.sum(raised, axis=-1, keepdims=True)
    probs = (raised / sums).astype(BF)
    mixed = jnp.einsum("hqk,khd->qhd", probs, split_heads(values), preferred_element_type=F32).reshape(own.shape)
    region_rows = band.astype(F32) + nn(mixed.astype(BF), weights[3]) + vec[6]
    return region_rows, mixed, (peak + jnp.log(sums))[:, :, 0], queries, keys, values


def regional_terms(queries, keys, values, grad_mixed, same, level, delta):
    scores = jnp.einsum("qhd,khd->hqk", split_heads(queries), split_heads(keys), preferred_element_type=F32)
    probs = jnp.where(same[None], jnp.exp(scores * SCALE - level[:, :, None]), 0.0)
    grads = jnp.einsum("qhd,khd->hqk", split_heads(grad_mixed), split_heads(values), preferred_element_type=F32)
    return probs.astype(BF), (probs * (grads - delta[:, :, None])).astype(BF)


def regional_backward(queries, keys, values, grads, own, rows, same, level, delta, weights, vec, mixed, band_grad, dw):
    grad_mixed = nt(grads, weights[3]).astype(BF)
    level_own, delta_own = own(level.T).T, own(delta.T).T
    _, scores = regional_terms(own(queries), keys, values, own(grad_mixed), same.T, level_own, delta_own)
    dq = jnp.einsum("hqk,khd->qhd", scores, split_heads(keys), preferred_element_type=F32)
    probs, scores = regional_terms(queries, own(keys), own(values), grad_mixed, same, level, delta)
    dk = jnp.einsum("hqk,qhd->khd", scores, split_heads(queries), preferred_element_type=F32)
    dv = jnp.einsum("hqk,qhd->khd", probs, split_heads(grad_mixed), preferred_element_type=F32)
    flat = lambda x: x.reshape(-1, D)
    dq, dk, dv = flat(dq) * SCALE, flat(dk) * SCALE, flat(dv)
    lows = [x.astype(BF) for x in (dq, dk, dv)]
    dn = sum(nt(x, w) for x, w in zip(lows, weights))
    xhat, scale = norm_parts(rows.astype(F32))
    low = (xhat * vec[0] + vec[1]).astype(BF)
    d_regions = own(grads).astype(F32) + norm_back(dn, xhat, scale, vec[0])
    matrices = [dw[j] + tn(low, x) for j, x in enumerate(lows)] + [dw[3] + tn(mixed.astype(BF), band_grad)]
    vectors = [fold(x) for x in (dn * xhat, dn, dq, dv, band_grad.astype(F32))]
    return d_regions, jnp.stack(matrices).astype(BF), jnp.stack(vectors)


def per_device(patches, regions, image_ids, attn_w, mlp_in, mlp_out, vec_params, patch_cot, region_cot,
               attn_mom, mlp_in_mom, mlp_out_mom, adam_first, adam_second):
    dp_size = lax.axis_size("dp")
    dp_index = lax.axis_index("dp")
    opt_index = lax.axis_index("opt")
    _, grid_rows, cols, _, _ = patch_cot.shape
    grid_cols = patches.shape[2]
    tokens = grid_rows * grid_cols
    own_count = grid_rows * cols
    one_kernel = tokens <= 1024
    vec = vec_params
    order = opt_index ^ jnp.arange(OPT)
    move = lambda x: lax.all_to_all(x, "dp", 0, 0, tiled=True)

    attn_pieces = jnp.stack(pieces_of_owners(attn_w[0].astype(BF)))
    weights = [lax.dynamic_index_in_dim(attn_pieces, opt_index ^ j, 0, keepdims=False) for j in range(OPT)]
    canvas_blocks = share(regions[0])
    canvas = canvas_blocks.reshape(tokens, D)
    by_position = patch_cot[0].transpose(0, 2, 1, 3)
    split = 20
    last = jnp.concatenate([by_position[:, split:], region_cot[0][:, None]], axis=1)
    cots = [move(by_position[:, :split]), move(last)]
    first = pieces_of_owners(mlp_in.astype(BF))
    second = pieces_of_owners(mlp_out.astype(BF))
    bias_first = jnp.take(vec[8:], order, axis=0)

    band_of = lambda x: lax.dynamic_slice_in_dim(x, dp_index, 1, 1).reshape((grid_cols,) + x.shape[3:])
    own_of = lambda x: lax.dynamic_slice_in_dim(x, dp_index * own_count, own_count, 0)
    ids_blocks = image_ids[0].reshape(grid_rows, dp_size, cols).transpose(1, 0, 2)
    ids = ids_blocks.reshape(tokens)
    band_ids, own_ids = band_of(ids_blocks), own_of(ids)
    band = band_of(canvas_blocks)
    if one_kernel:
        repeat = lambda x: jnp.tile(x, 4)[None]
        region_rows, mixed, level, reg_q, reg_k, reg_v = in_vmem(
            regional_fwd_kernel,
            [((grid_cols, D), F32), ((grid_cols, D), F32), ((4, 4 * grid_cols), F32)] + [((tokens, D), BF)] * 3,
            "regional_attention_forward", canvas, band, ids[:, None], repeat(band_ids), *weights, vec)
        level = level.reshape(HEADS, grid_cols)
    else:
        region_rows, mixed, level, reg_q, reg_k, reg_v = regional_forward(
            canvas, band, band_ids[:, None] == ids[None, :], weights, vec)
    level = level.T
    level_high = level.astype(BF).astype(F32)
    level_mid = (level - level_high).astype(BF).astype(F32)
    level_parts = jnp.concatenate([level_high, level_mid, level - level_high - level_mid], axis=1)
    level_parts = jnp.pad(level_parts, ((0, 0), (2 * HEADS, GROUP - 5 * HEADS)))

    windows = patches[0, 0].transpose(1, 0, 2)
    x1, *saved = attn_fwd(windows, region_rows, weights, vec)
    outs = [mlp(x1, start, cot, first, second, vec, bias_first) for start, cot in zip((0, split), cots)]
    moved = [move(o[0]) for o in outs]
    out_patches = jnp.concatenate([moved[0], moved[1][:, : PATCH - split]], axis=1).transpose(0, 2, 1, 3)[None]
    out_regions = moved[1][None, :, PATCH - split]
    d_patches, d_region, d_attn, d_vec_attn = attn_bwd(windows, region_rows, [o[1] for o in outs], saved, weights, vec)
    d_patches = d_patches.transpose(1, 0, 2)[None, None]

    add = lambda n, j: (outs[0][n][j].astype(F32) + outs[1][n][j].astype(F32)).astype(BF)
    own_first = sum_at_owner([add(2, j) for j in range(OPT)])
    own_second = sum_at_owner([add(3, j) for j in range(OPT)])
    own_mlp = sum_over_dp(jnp.concatenate([own_first, own_second], axis=1).astype(BF))

    band_grad, extra = in_vmem(payload_kernel, [((grid_cols, D), BF), ((grid_cols, GROUP), BF)],
                               "regional_payload", d_region, mixed, level_parts, weights[3])
    payload = share(jnp.concatenate([band_grad, extra], axis=1)).reshape(grid_rows, dp_size, cols, D + GROUP)
    payload = payload.transpose(1, 0, 2, 3).reshape(tokens, D + GROUP)
    grads = payload[:, :D]
    extra = payload[:, D:].astype(F32)
    part = lambda n: extra[:, n * HEADS : (n + 1) * HEADS]
    delta = (part(0) + part(1)).T
    level = (part(2) + part(3) + part(4)).T
    if one_kernel:
        wide = lambda x: x.reshape(4, -1)
        own_columns = lambda x: wide(lax.dynamic_slice_in_dim(x, dp_index * own_count, own_count, 1))
        d_regions, grad_attn, d_vec_reg = in_vmem(
            partial(regional_bwd_kernel, own_count),
            [((own_count, D), F32), ((4, D, D), BF), ((5, 8, D), F32)],
            "regional_attention_backward", reg_q, reg_k, reg_v, grads, own_of(reg_q), own_of(reg_k), own_of(reg_v),
            own_of(canvas), ids[:, None], repeat(ids), own_ids[:, None], repeat(own_ids), wide(level), wide(delta),
            own_columns(level), own_columns(delta), own_of(grads), mixed, band_grad, d_attn, *weights, vec)
    else:
        d_regions, grad_attn, d_vec_reg = regional_backward(
            reg_q, reg_k, reg_v, grads, own_of, own_of(canvas), ids[:, None] == own_ids[None, :], level, delta,
            weights, vec, mixed, band_grad, d_attn)
    d_regions = d_regions.reshape(regions.shape)

    pieces = [lax.dynamic_index_in_dim(grad_attn, opt_index ^ j, 0, keepdims=False) for j in range(OPT)]
    own_attn = sum_over_dp(sum_at_owner(pieces).astype(BF))

    d_vec_attn = jnp.sum(d_vec_attn + d_vec_reg, axis=1)
    d_vec_mlp = jnp.sum(outs[0][4] + outs[1][4], axis=1)
    d_bias_first = jnp.take(jnp.sum(outs[0][5] + outs[1][5], axis=1), order, axis=0)
    grad_vec = jnp.concatenate([d_vec_attn[:2], d_vec_mlp[:2], d_vec_attn[2:], d_vec_mlp[2:], d_bias_first])
    grad_vec = grad_vec + pair(grad_vec, 1)
    grad_vec = grad_vec + pair(grad_vec, 2)
    grad_vec = jnp.sum(share(grad_vec), axis=0)

    squares = lambda x: jnp.sum(x.astype(F32) ** 2)
    total = jnp.full((8, 128), squares(own_attn) + squares(own_mlp))
    total = total + pair(total, 1)
    total = total + pair(total, 2)
    grad_norm = jnp.sqrt(total[0, 0] + squares(grad_vec))
    clip = jnp.minimum(1.0, CLIP_LIMIT / (grad_norm + 1e-06))
    clip_cell = clip.reshape(1, 1)
    first_mom, second_mom, gram_first, gram_second = whole_call(
        moments_kernel, [F32, F32, F32, F32], "mlp_moments", clip_cell,
        own_mlp[:, :D], own_mlp[:, D:], mlp_in_mom, mlp_out_mom)
    grams = jnp.stack([gram_first, gram_second])
    grams = grams + pair(grams, 1)
    grams = grams + pair(grams, 2)
    attn_mom_new, new_attn = whole_call(
        square_kernel, [F32, F32], "attention_update", clip_cell, own_attn, attn_mom[0], attn_w[0])
    new_first, new_second = whole_call(
        sharded_kernel, [F32, F32], "mlp_update", grams[0], grams[1], first_mom, second_mom, mlp_in, mlp_out)
    clipped = clip * grad_vec
    moment_one = BETA_FIRST * adam_first + (1.0 - BETA_FIRST) * clipped
    moment_two = BETA_SECOND * adam_second + (1.0 - BETA_SECOND) * clipped * clipped
    first_hat = moment_one / (1.0 - BETA_FIRST**OPT_STEP)
    second_hat = moment_two / (1.0 - BETA_SECOND**OPT_STEP)
    new_vec = vec_params - ADAM_RATE * first_hat / (jnp.sqrt(second_hat) + ADAM_EPS)
    return (out_patches, out_regions, d_patches, d_regions, new_attn[None], attn_mom_new[None], new_first, first_mom,
            new_second, second_mom, new_vec, moment_one, moment_two, grad_norm)


def solution(mesh):
    canvas = P("opt", None, "dp", None)
    wide = P("opt", None, "dp", None, None)
    bands = P("opt", "dp", None, None, None)
    square, right, down = P("opt", None, None), P(None, "opt"), P("opt", None)
    return jax.shard_map(
        per_device,
        mesh=mesh,
        in_specs=(bands, canvas, square, square, right, down, P(), wide, canvas, square, right, down, P(), P()),
        out_specs=(wide, canvas, bands, canvas, square, square, right, right, down, down, P(), P(), P(), P()),
        check_vma=False,
    )
```

```python
from functools import partial

import jax
import jax.numpy as jnp
from jax import lax
from jax.experimental import pallas as pl
from jax.experimental.pallas import tpu as pltpu
from jax.sharding import PartitionSpec as P

BF = jnp.bfloat16
F32 = jnp.float32

D = 512
HEADS = 16
HEAD_DIM = 32
FF = 2048
PATCH = 49
LIVE = 50
ROWS = 56
GROUP = 128
STACK = 4 * ROWS
OPT_STEP = 10
OPT = 4

SCALE = HEAD_DIM ** (-0.5)
NORM_EPS = 1e-05
MASKED = -1e30
NS_FIRST = 3.4445
NS_SECOND = -4.775
NS_THIRD = 2.0315
MUON_RATE = 0.5
MUON_MOMENTUM = 0.5
MUON_DECAY = 0.01
ADAM_RATE = 0.5
BETA_FIRST = 0.9
BETA_SECOND = 0.95
ADAM_EPS = 1e-08
CLIP_LIMIT = 1.0
DECAY_KEEP = 1.0 - MUON_RATE * MUON_DECAY
VMEM = 60 * 2**20
BRIEF = pl.CostEstimate(flops=10**6, bytes_accessed=10**5, transcendentals=0)

ERF_P = 0.3275911 * 0.5**0.5
ERF = tuple(0.5 * c for c in (0.254829592, -0.284496736, 1.421413741, -1.453152027, 1.061405429))
INV_SQRT_2PI = 0.3989422804014327
LOG2E = 1.4426950408889634


def nn(a, b):
    return lax.dot_general(a, b, (((1,), (0,)), ((), ())), preferred_element_type=F32)


def nt(a, b):
    return lax.dot_general(a, b, (((1,), (1,)), ((), ())), preferred_element_type=F32)


def tn(a, b):
    return lax.dot_general(a, b, (((0,), (0,)), ((), ())), preferred_element_type=F32)


def full(shape):
    return pl.BlockSpec(shape, lambda i: (0,) * len(shape))


def block(shape):
    return pl.BlockSpec(shape, lambda i: (i,) + (0,) * (len(shape) - 1))


def norm_parts(x):
    centre = x - jnp.mean(x, axis=-1, keepdims=True)
    scale = lax.rsqrt(jnp.mean(centre * centre, axis=-1, keepdims=True) + NORM_EPS)
    return centre * scale, scale


def norm_back(grad, xhat, scale, gain):
    inner = grad * gain
    first = jnp.mean(inner, axis=-1, keepdims=True)
    second = jnp.mean(inner * xhat, axis=-1, keepdims=True)
    return scale * (inner - first - xhat * second)


def head_masks():
    lane = lax.broadcasted_iota(jnp.int32, (1, GROUP), 1) // HEAD_DIM
    return [lane == h for h in range(4)]


def spread(rows, masks):
    return jnp.concatenate([jnp.where(m, rows, 0.0) for m in masks], axis=0).astype(BF)


def collect(stacked, masks, rows):
    out = stacked[:rows]
    for h in range(1, 4):
        out = jnp.where(masks[h], stacked[h * rows : (h + 1) * rows], out)
    return out


def lane_groups(x):
    return [x[:, GROUP * g : GROUP * (g + 1)] for g in range(4)]


def hold(ref, total, x):
    for g, part in enumerate(lane_groups(x)):
        ref[g, :total] = part


def held_rows(ref, total):
    return jnp.concatenate([ref[g, :total] for g in range(4)], axis=1)


def fold(x):
    return jnp.sum(x.reshape(x.shape[0] // 8, 8, x.shape[1]), axis=0)


def gelu_parts(a):
    bell = jnp.exp2(a * a * (-0.5 * LOG2E))
    t = 1.0 / (1.0 + ERF_P * jnp.abs(a))
    tail = ((((ERF[4] * t + ERF[3]) * t + ERF[2]) * t + ERF[1]) * t + ERF[0]) * t * bell
    share = jnp.where(a < 0, tail, 1.0 - tail)
    return a * share, share + a * bell * INV_SQRT_2PI


def attn_fwd_kernel(count, batch, p_ref, r_ref, wq_ref, wk_ref, wv_ref, wo_ref, vec_ref,
                    x1_ref, q_ref, k_ref, v_ref, o_ref, pt_ref, q_held, k_held, v_held, o_held):
    total = count * LIVE

    @pl.when(pl.program_id(0) == 0)
    def _():
        for ref in (q_held, k_held, v_held):
            ref[:, total:] = jnp.zeros((4, count * (ROWS - LIVE), GROUP), F32)

    x = jnp.concatenate([p_ref[...].astype(F32), r_ref[...][None]], axis=0).reshape(total, D)
    vec = vec_ref[...]
    xhat, _ = norm_parts(x)
    xn = (xhat * vec[0:1] + vec[1:2]).astype(BF)
    hold(q_held, total, nn(xn, wq_ref[...]) + vec[4:5])
    hold(k_held, total, nn(xn, wk_ref[...]))
    hold(v_held, total, nn(xn, wv_ref[...]) + vec[5:6])
    masks = head_masks()
    live = lax.broadcasted_iota(jnp.int32, (ROWS, 1), 0) < LIVE

    def body(step, carry):
        units = [(step * batch + w, g) for w in range(batch) for g in range(4)]
        scores, probs = [], []
        for w, g in units:
            lanes = slice(GROUP * g, GROUP * (g + 1))
            rows = pl.ds(w, ROWS, stride=count)
            q = q_held[g, rows, :]
            q_ref[w, :, lanes] = q.astype(BF)
            k = k_held[g, rows, :].astype(BF)
            k_ref[w, :, lanes] = k
            scores.append(nt(k, spread(q, masks)))
        for (w, g), s in zip(units, scores):
            s = jnp.where(live, s, MASKED)
            e = jnp.exp((s - jnp.max(s, axis=0, keepdims=True)) * SCALE)
            p = (e * (1.0 / jnp.sum(e, axis=0, keepdims=True))).astype(BF)
            pt_ref[w, g] = p
            probs.append(p)
        for (w, g), p in zip(units, probs):
            lanes = slice(GROUP * g, GROUP * (g + 1))
            rows = pl.ds(w, ROWS, stride=count)
            v = v_held[g, rows, :].astype(BF)
            v_ref[w, :, lanes] = v
            o_held[g, rows, :] = collect(tn(p, v), masks, ROWS)
        return carry

    lax.fori_loop(0, count // batch, body, 0)
    mixed = held_rows(o_held, total).astype(BF)
    o_ref[...] = mixed.reshape(LIVE, count, D)
    x1_ref[...] = (x + nn(mixed, wo_ref[...]) + vec[6:7]).reshape(LIVE, count, D)


def middle(rows, count):
    return pl.BlockSpec((rows, count, D), lambda i: (0, i, 0))


def attn_fwd(patches, region_rows, weights, vec, count=16, batch=4):
    windows = patches.shape[1]
    array = jax.ShapeDtypeStruct
    return pl.pallas_call(
        partial(attn_fwd_kernel, count, batch),
        grid=(windows // count,),
        in_specs=[middle(PATCH, count), block((count, D))] + [full((D, D))] * 4 + [full(vec.shape)],
        out_specs=[middle(LIVE, count)] + [block((count, ROWS, D))] * 3
        + [middle(LIVE, count), block((count, 4, ROWS, STACK))],
        out_shape=[array((LIVE, windows, D), F32)] + [array((windows, ROWS, D), BF)] * 3
        + [array((LIVE, windows, D), BF), array((windows, 4, ROWS, STACK), BF)],
        scratch_shapes=[pltpu.VMEM((4, count * ROWS, GROUP), F32)] * 4,
        compiler_params=pltpu.CompilerParams(vmem_limit_bytes=VMEM),
        cost_estimate=BRIEF,
        name="window_attention_forward",
    )(patches, region_rows, *weights, vec)


def mlp_kernel(many, sources, cols, steps, lanes, x1_ref, pc_ref, w1a, w1b, w1c, w1d, w2a, w2b, w2c, w2d,
               vec_ref, b1_ref, op_ref, dx1_ref, dw1_ref, dw2_ref, dv_ref, db1_ref, acc1, acc2):
    total = many * sources * cols
    step = pl.program_id(0)

    @pl.when(step == 0)
    def _():
        for ref in (acc1, acc2, dv_ref, db1_ref):
            ref[...] = jnp.zeros_like(ref)

    vec = vec_ref[...]
    gain = vec[2:3]
    x1 = x1_ref[...].reshape(total, D)
    xhat, scale = norm_parts(x1)
    h = (xhat * gain + vec[3:4]).astype(BF)
    for s in range(sources):
        dx1_ref[:, s * cols : (s + 1) * cols] = pc_ref[s].astype(F32)
    dy = dx1_ref[...].reshape(total, D)
    dm = dy.astype(BF)
    ht = h.T
    dmt = dm.T
    w1s, w2s = (w1a, w1b, w1c, w1d), (w2a, w2b, w2c, w2d)
    y = x1 + vec[7:8]
    dh = jnp.zeros((total, D), F32)
    parts = [(j, slice(c, c + lanes)) for j in range(4) for c in range(0, D, lanes)]

    def activate(j, s):
        u, slope = gelu_parts(nn(h, w1s[j][:, s]) + b1_ref[j : j + 1, s])
        da = slope * nt(dm, w2s[j][s, :])
        db1_ref[j, :, s] += fold(da)
        return u.astype(BF), da.astype(BF)

    def apply(j, s, u, da):
        acc1[j, :, s] += nn(ht, da)
        acc2[j, :, s] += nn(dmt, u)
        return nn(u, w2s[j][s, :]), nt(da, w1s[j][:, s])

    held_pair = activate(*parts[0])
    for n in range(1, len(parts) + 1):
        later = activate(*parts[n]) if n < len(parts) else None
        up, down = apply(*parts[n - 1], *held_pair)
        y, dh = y + up, dh + down
        held_pair = later
    y = y.reshape(many, sources * cols, D)
    for s in range(sources):
        op_ref[s] = y[:, s * cols : (s + 1) * cols].astype(BF)
    dy = dx1_ref[...].reshape(total, D)
    dx1_ref[...] = (dy + norm_back(dh, xhat, scale, gain)).reshape(dx1_ref.shape)
    dv_ref[0] += fold(dh * xhat)
    dv_ref[1] += fold(dh)
    dv_ref[2] += fold(dy)

    @pl.when(step == steps - 1)
    def _():
        dw1_ref[...] = acc1[...].astype(BF)
        dw2_ref[...] = acc2[...].astype(BF)


def mlp(x1, first_position, cot, first, second, vec, bias_first, many=10, lanes=256):
    sources, positions, cols, _ = cot.shape
    windows = x1.shape[1]
    steps = positions // many
    skip = first_position // many
    some = pl.BlockSpec((sources, many, cols, D), lambda i: (0, i, 0, 0))
    array = jax.ShapeDtypeStruct
    return pl.pallas_call(
        partial(mlp_kernel, many, sources, cols, steps, lanes),
        grid=(steps,),
        in_specs=[pl.BlockSpec((many, windows, D), lambda i: (i + skip, 0, 0)), some]
        + [full((D, D))] * 8 + [full(vec.shape), full((4, D))],
        out_specs=[some, block((many, windows, D)), full((4, D, D)), full((4, D, D)), full((3, 8, D)), full((4, 8, D))],
        out_shape=[array(cot.shape, BF), array((positions, windows, D), F32), array((4, D, D), BF),
                   array((4, D, D), BF), array((3, 8, D), F32), array((4, 8, D), F32)],
        scratch_shapes=[pltpu.VMEM((4, D, D), F32), pltpu.VMEM((4, D, D), F32)],
        compiler_params=pltpu.CompilerParams(vmem_limit_bytes=VMEM),
        cost_estimate=BRIEF,
        name="mlp_forward_backward",
    )(x1, cot, *first, *second, vec, bias_first)


def attn_bwd_kernel(count, batch, chunks, *refs):
    p_ref, r_ref, _ = refs[:3]
    dx1_refs = refs[3 : 3 + chunks]
    (q_ref, k_ref, v_ref, o_ref, pt_ref, wq_ref, wk_ref, wv_ref, wo_ref, vec_ref,
     dp_ref, dr_ref, dw_ref, dv_ref, dq_held, dk_held, dvv_held, do_held) = refs[3 + chunks :]
    total = count * LIVE

    @pl.when(pl.program_id(0) == 0)
    def _():
        dw_ref[...] = jnp.zeros_like(dw_ref)
        dv_ref[...] = jnp.zeros_like(dv_ref)
        do_held[:, total:] = jnp.zeros((4, count * (ROWS - LIVE), GROUP), F32)

    vec = vec_ref[...]
    gain = vec[0:1]
    dx1 = jnp.concatenate([ref[...] for ref in dx1_refs], axis=0).reshape(total, D)
    gb = dx1.astype(BF)
    hold(do_held, total, nt(gb, wo_ref[...]))
    masks = head_masks()

    def body(step, carry):
        units = [(step * batch + w, g) for w in range(batch) for g in range(4)]
        grads, scores = [], []
        for w, g in units:
            lanes = slice(GROUP * g, GROUP * (g + 1))
            rows = pl.ds(w, ROWS, stride=count)
            do_wide = spread(do_held[g, rows, :], masks)
            dvv_held[g, rows, :] = nn(pt_ref[w, g], do_wide)
            grads.append(nt(v_ref[w, :, lanes], do_wide))
        for (w, g), grad in zip(units, grads):
            p = pt_ref[w, g].astype(F32)
            both = p * grad
            scores.append((both - p * jnp.sum(both, axis=0, keepdims=True)).astype(BF))
        for (w, g), ds in zip(units, scores):
            lanes = slice(GROUP * g, GROUP * (g + 1))
            rows = pl.ds(w, ROWS, stride=count)
            dk_held[g, rows, :] = nn(ds, spread(q_ref[w, :, lanes].astype(F32), masks)) * SCALE
            dq_held[g, rows, :] = collect(tn(ds, k_ref[w, :, lanes]), masks, ROWS) * SCALE
        return carry

    lax.fori_loop(0, count // batch, body, 0)
    x = jnp.concatenate([p_ref[...].astype(F32), r_ref[...][None]], axis=0).reshape(total, D)
    xhat, scale = norm_parts(x)
    xn = (xhat * gain + vec[1:2]).astype(BF)
    dq_wide = held_rows(dq_held, total)
    dv_wide = held_rows(dvv_held, total)
    dq = dq_wide.astype(BF)
    dk = held_rows(dk_held, total).astype(BF)
    dv = dv_wide.astype(BF)
    dn = nt(dq, wq_ref[...]) + nt(dk, wk_ref[...]) + nt(dv, wv_ref[...])
    dx = (dx1 + norm_back(dn, xhat, scale, gain)).reshape(LIVE, count, D)
    dp_ref[...] = dx[:PATCH].astype(BF)
    dr_ref[...] = dx[PATCH]
    xt = xn.T
    dw_ref[0] += nn(xt, dq)
    dw_ref[1] += nn(xt, dk)
    dw_ref[2] += nn(xt, dv)
    dw_ref[3] += nn(o_ref[...].reshape(total, D).T, gb)
    dv_ref[0] += fold(dn * xhat)
    dv_ref[1] += fold(dn)
    dv_ref[2] += fold(dq_wide)
    dv_ref[3] += fold(dv_wide)
    dv_ref[4] += fold(dx1)


def attn_bwd(patches, region_rows, dx1_parts, saved, weights, vec, after, count=16, batch=4):
    windows = patches.shape[1]
    array = jax.ShapeDtypeStruct
    return pl.pallas_call(
        partial(attn_bwd_kernel, count, batch, len(dx1_parts)),
        grid=(windows // count,),
        in_specs=[middle(PATCH, count), block((count, D)), pl.BlockSpec(memory_space=pl.ANY)]
        + [middle(part.shape[0], count) for part in dx1_parts]
        + [block((count, ROWS, D))] * 3 + [middle(LIVE, count), block((count, 4, ROWS, STACK))]
        + [full((D, D))] * 4 + [full(vec.shape)],
        out_specs=[middle(PATCH, count), block((count, D)), full((4, D, D)), full((5, 8, D))],
        out_shape=[array((PATCH, windows, D), BF), array((windows, D), F32),
                   array((4, D, D), F32), array((5, 8, D), F32)],
        scratch_shapes=[pltpu.VMEM((4, count * ROWS, GROUP), F32)] * 4,
        compiler_params=pltpu.CompilerParams(vmem_limit_bytes=VMEM),
        cost_estimate=BRIEF,
        name="window_attention_backward",
    )(patches, region_rows, after, *dx1_parts, *saved, *weights, vec)


def regional_fwd_kernel(canvas_ref, band_ref, ids_ref, band_ids_ref, wq_ref, wk_ref, wv_ref, wo_ref, vec_ref,
                        r1_ref, mixed_ref, level_ref, q_ref, k_ref, v_ref):
    vec = vec_ref[...]
    xhat, _ = norm_parts(canvas_ref[...].astype(F32))
    low = (xhat * vec[0:1] + vec[1:2]).astype(BF)
    q_ref[...] = (nn(low, wq_ref[...]) + vec[4:5]).astype(BF)
    k_ref[...] = nn(low, wk_ref[...]).astype(BF)
    v_ref[...] = (nn(low, wv_ref[...]) + vec[5:6]).astype(BF)
    band = band_ref[...].astype(F32)
    rows = band.shape[0]
    xhat, _ = norm_parts(band)
    q = nn((xhat * vec[0:1] + vec[1:2]).astype(BF), wq_ref[...]) + vec[4:5]
    masks = head_masks()
    same = ids_ref[...] == band_ids_ref[...]
    scores, probs = [], []
    for g in range(4):
        lanes = slice(GROUP * g, GROUP * (g + 1))
        scores.append(nt(k_ref[:, lanes], spread(q[:, lanes], masks)))
    for g, s in enumerate(scores):
        s = jnp.where(same, s, MASKED)
        peak = jnp.max(s, axis=0, keepdims=True)
        e = jnp.exp((s - peak) * SCALE)
        sums = jnp.sum(e, axis=0, keepdims=True)
        level_ref[g : g + 1] = peak * SCALE + jnp.log(sums)
        probs.append((e * (1.0 / sums)).astype(BF))
    for g, p in enumerate(probs):
        lanes = slice(GROUP * g, GROUP * (g + 1))
        mixed_ref[:, lanes] = collect(tn(p, v_ref[:, lanes]), masks, rows)
    r1_ref[...] = band + nn(mixed_ref[...].astype(BF), wo_ref[...]) + vec[6:7]


def in_vmem(kernel, outs, name, *args, after=()):
    spaces = [pltpu.SMEM if arg.shape == (1, 1) else pltpu.VMEM for arg in args]
    count = len(args)
    return pl.pallas_call(
        lambda *refs: kernel(*refs[:count], *refs[count + len(after) :]),
        in_specs=[pl.BlockSpec(memory_space=space) for space in spaces]
        + [pl.BlockSpec(memory_space=pl.ANY) for _ in after],
        out_specs=[pl.BlockSpec(memory_space=pltpu.VMEM) for _ in outs],
        out_shape=[jax.ShapeDtypeStruct(*out) for out in outs],
        compiler_params=pltpu.CompilerParams(vmem_limit_bytes=VMEM),
        cost_estimate=BRIEF,
        name=name,
    )(*args, *after)


def payload_kernel(dr_ref, mixed_ref, level_ref, wo_ref, grad_ref, extra_ref):
    low = dr_ref[...].astype(BF)
    grad_ref[...] = low
    both = nt(low, wo_ref[...]).astype(BF).astype(F32) * mixed_ref[...]
    head = lax.broadcasted_iota(jnp.int32, (D, GROUP), 0) // HEAD_DIM
    lane = lax.broadcasted_iota(jnp.int32, (D, GROUP), 1)
    pick = ((head == lane) | (head + HEADS == lane)).astype(BF)
    high, low_part = halves(both)
    rest = (both - high.astype(F32) - low_part.astype(F32)).astype(BF)
    delta = nn(high, pick) + (nn(low_part, pick) + nn(rest, pick))
    top = delta.astype(BF).astype(F32)
    lane = lax.broadcasted_iota(jnp.int32, (1, GROUP), 1)
    level = level_ref[...]
    level_top = level.astype(BF).astype(F32)
    level_rest = level - level_top
    level_mid = level_rest.astype(BF).astype(F32)
    extra = level_rest - level_mid
    for place, term in ((4, level_mid), (3, level_top), (2, delta - top), (1, top)):
        extra = jnp.where(lane < place * HEADS, term, extra)
    extra_ref[...] = extra.astype(BF)


def regional_bwd_kernel(own_rows, q_ref, k_ref, v_ref, grads_ref, qo_ref, ko_ref, vo_ref, own_ref, ids_ref, ids_row_ref,
                        ids_own_ref, ids_own_row_ref, level_ref, delta_ref, level_own_ref, delta_own_ref,
                        grads_own_ref, mixed_ref, band_grad_ref, dw_ref, wq_ref, wk_ref, wv_ref, wo_ref, vec_ref,
                        dr_ref, gw_ref, gv_ref):
    vec = vec_ref[...]
    masks = head_masks()
    do = nt(grads_ref[...], wo_ref[...]).astype(BF).astype(F32)
    do_own = nt(grads_own_ref[...], wo_ref[...]).astype(BF).astype(F32)
    same_own = ids_ref[...] == ids_own_row_ref[...]
    same = ids_own_ref[...] == ids_row_ref[...]
    lanes = [slice(GROUP * g, GROUP * (g + 1)) for g in range(4)]
    first, second = [], []
    dqs, dks, dvs = [], [], []
    for g in range(4):
        q_wide = spread(qo_ref[:, lanes[g]].astype(F32), masks)
        do_wide = spread(do_own[:, lanes[g]], masks)
        first.append((nt(k_ref[:, lanes[g]], q_wide), nt(v_ref[:, lanes[g]], do_wide)))
        q_wide = spread(q_ref[:, lanes[g]].astype(F32), masks)
        do_wide = spread(do[:, lanes[g]], masks)
        second.append((nt(ko_ref[:, lanes[g]], q_wide), nt(vo_ref[:, lanes[g]], do_wide), q_wide, do_wide))
    for g in range(4):
        s, dp = first[g]
        p = jnp.where(same_own, jnp.exp(s * SCALE - level_own_ref[g : g + 1]), 0.0)
        ds = (p * (dp - delta_own_ref[g : g + 1])).astype(BF)
        dqs.append(collect(tn(ds, k_ref[:, lanes[g]]), masks, own_rows) * SCALE)
        s, dp, q_wide, do_wide = second[g]
        p = jnp.where(same, jnp.exp(s * SCALE - level_ref[g : g + 1]), 0.0)
        ds = (p * (dp - delta_ref[g : g + 1])).astype(BF)
        dvs.append(nn(p.astype(BF), do_wide))
        dks.append(nn(ds, q_wide) * SCALE)
    xhat, scale = norm_parts(own_ref[...].astype(F32))
    low = (xhat * vec[0:1] + vec[1:2]).astype(BF)
    dq_wide, dk_wide, dv_wide = (jnp.concatenate(x, axis=1) for x in (dqs, dks, dvs))
    dq, dk, dv = dq_wide.astype(BF), dk_wide.astype(BF), dv_wide.astype(BF)
    dn = nt(dq, wq_ref[...]) + nt(dk, wk_ref[...]) + nt(dv, wv_ref[...])
    dr_ref[...] = grads_own_ref[...].astype(F32) + norm_back(dn, xhat, scale, vec[0:1])
    gw_ref[0] = (dw_ref[0] + tn(low, dq)).astype(BF)
    gw_ref[1] = (dw_ref[1] + tn(low, dk)).astype(BF)
    gw_ref[2] = (dw_ref[2] + tn(low, dv)).astype(BF)
    gw_ref[3] = (dw_ref[3] + tn(mixed_ref[...].astype(BF), band_grad_ref[...])).astype(BF)
    gv_ref[0] = fold(dn * xhat)
    gv_ref[1] = fold(dn)
    gv_ref[2] = fold(dq_wide)
    gv_ref[3] = fold(dv_wide)
    gv_ref[4] = fold(band_grad_ref[...].astype(F32))


def halves(a):
    high = a.astype(BF)
    return high, (a - high.astype(F32)).astype(BF)


def terms(a, passes):
    return (a.astype(BF),) if passes == 1 else halves(a)


def product(a, b, dot=nn):
    if len(a) == 1:
        return dot(a[0], b[0])
    return dot(a[0], b[0]) + (dot(a[0], b[1]) + dot(a[1], b[0]))


def symmetric(a, b, dot=nn):
    half = D // 2
    right = (lambda x: x[half:]) if dot is nt else (lambda x: x[:, half:])
    top = product([x[:half] for x in a], b, dot)
    corner = product([x[half:] for x in a], [right(x) for x in b], dot)
    return jnp.concatenate([top, jnp.concatenate([top[:, half:].T, corner], axis=1)], axis=0)


DIRECT_STEPS = (1, 1, 1, -1, -1)
GRAM_STEPS = (1, 1, 3, 3, 3)
NEAR_ZERO = NS_FIRST + NS_SECOND + NS_THIRD
NEAR_ONE = NS_SECOND + 2.0 * NS_THIRD


def identity():
    rows = lax.broadcasted_iota(jnp.int32, (D, D), 0)
    return rows == lax.broadcasted_iota(jnp.int32, (D, D), 1)


def polynomial(gram, eye, step):
    if step > 0:
        parts = terms(gram, step)
        return NS_FIRST, NS_SECOND * gram + NS_THIRD * symmetric(parts, parts)
    rest = gram - jnp.where(eye, 1.0, 0.0)
    parts = terms(rest, -step)
    return NEAR_ZERO, NEAR_ONE * rest + NS_THIRD * symmetric(parts, parts)


def direct_steps(moment, eye):
    z = moment * (1.0 / (jnp.sqrt(jnp.sum(moment * moment)) + 1e-07))
    for step in DIRECT_STEPS:
        parts = terms(z, abs(step))
        gram = symmetric(parts, parts, nt)
        yield
        scale, poly = polynomial(gram, eye, step)
        yield
        z = scale * z + product(terms(poly, abs(step)), parts)
        yield
    return z


def gram_steps(gram, eye):
    factor = 1.0 / (jnp.sqrt(jnp.sum(jnp.where(eye, gram, 0.0))) + 1e-07)
    gram = gram * (factor * factor)
    steps = None
    for n, passes in enumerate(GRAM_STEPS):
        scale, poly = polynomial(gram, eye, passes)
        yield
        parts = terms(poly, passes)
        if steps is None:
            steps = jnp.where(eye, scale, 0.0) + poly
        else:
            steps = scale * steps + symmetric(parts, terms(steps, passes))
            yield
        if n < len(GRAM_STEPS) - 1:
            half = scale * gram + symmetric(parts, terms(gram, passes))
            yield
            gram = scale * half + symmetric(parts, terms(half, passes))
            yield
    return steps * factor


def in_turns(*chains):
    results = [None] * len(chains)
    running = list(enumerate(chains))
    while running:
        still = []
        for n, chain in running:
            try:
                next(chain)
                still.append((n, chain))
            except StopIteration as stop:
                results[n] = stop.value
        running = still
    return results


def grams_kernel(*refs):
    for n in range(2):
        old, mixed, new = (jnp.zeros((D, D), F32) for _ in range(3))
        cross = jnp.zeros((D, D), F32)
        for j in range(4):
            high, low = halves(refs[4 * n + j][...])
            if n == 1:
                high, low = high.T, low.T
            g = refs[8 + j][:, n * D : (n + 1) * D]
            old = old + nt(high, high)
            cross = cross + nt(high, low)
            mixed = mixed + (nt(high, g) + nt(low, g))
            new = new + nt(g, g)
        for k, x in enumerate((old + (cross + cross.T), mixed + mixed.T, new)):
            refs[12 + 3 * n + k][...] = x


def update_kernel(clip_ref, ga_ref, ma_ref, wa_ref, g_ref, m1_ref, m2_ref, w1_ref, w2_ref,
                  old1, mixed1, new1, old2, mixed2, new2, na_ref, newa_ref, n1_ref, new1_ref, n2_ref, new2_ref):
    clip = clip_ref[0, 0]
    eye = identity()
    na_ref[...] = MUON_MOMENTUM * ma_ref[...] + clip * ga_ref[...].astype(F32)
    n1_ref[...] = MUON_MOMENTUM * m1_ref[...] + clip * g_ref[:, :D].astype(F32)
    n2_ref[...] = MUON_MOMENTUM * m2_ref[...] + clip * g_ref[:, D:].astype(F32).T
    a, b, c = MUON_MOMENTUM * MUON_MOMENTUM, MUON_MOMENTUM * clip, clip * clip
    gram1 = a * old1[...] + b * mixed1[...] + c * new1[...]
    gram2 = a * old2[...] + b * mixed2[...] + c * new2[...]
    steps1, steps2, z = in_turns(gram_steps(gram1, eye), gram_steps(gram2, eye), direct_steps(na_ref[...], eye))
    newa_ref[...] = wa_ref[...] * DECAY_KEEP - MUON_RATE * z
    z = product(halves(steps1), halves(n1_ref[...]))
    new1_ref[...] = w1_ref[...] * DECAY_KEEP - MUON_RATE * z
    z = product(halves(n2_ref[...]), halves(steps2))
    new2_ref[...] = w2_ref[...] * DECAY_KEEP - (MUON_RATE * max(1.0, FF / D) ** 0.5) * z


def pair(values, bit):
    return lax.ppermute(values, "opt", [(i, i ^ bit) for i in range(OPT)])


def pieces_of_owners(own):
    mate = pair(own, 1)
    across = pair(own, 2)
    return [own, mate, across, pair(across, 1)]


def sum_at_owner(pieces):
    near = pair(jnp.stack([pieces[1], pieces[3]]), 1).astype(F32)
    far = (pieces[2].astype(F32) + near[1]).astype(BF)
    return pieces[0].astype(F32) + near[0] + pair(far, 2).astype(F32)


def share(x):
    copies = jnp.broadcast_to(x[None], (lax.axis_size("dp"),) + x.shape)
    return lax.all_to_all(copies, "dp", 0, 0, tiled=True)


def swap(x, bit):
    return lax.ppermute(x, "dp", [(i, i ^ bit) for i in range(lax.axis_size("dp"))])


def bits():
    return [1 << n for n in range(lax.axis_size("dp").bit_length() - 1)]


def sum_over_dp(x):
    index = lax.axis_index("dp")
    for bit in bits():
        half = x.shape[0] // 2
        side = (index // bit) % 2
        give = lax.dynamic_slice_in_dim(x, (1 - side) * half, half, 0)
        keep = lax.dynamic_slice_in_dim(x, side * half, half, 0)
        x = keep + swap(give.astype(BF), bit).astype(F32)
    x = x.astype(BF)
    for bit in reversed(bits()):
        other = swap(x, bit)
        side = (index // bit) % 2
        x = jnp.where(side == 0, jnp.concatenate([x, other]), jnp.concatenate([other, x]))
    return x


def sum_small_over_dp(x):
    for bit in bits():
        x = x + swap(x, bit)
    return x


def split_heads(x):
    return x.reshape(x.shape[0], HEADS, HEAD_DIM)


def regional_forward(canvas, band, same, weights, vec):
    low = lambda x: (norm_parts(x.astype(F32))[0] * vec[0] + vec[1]).astype(BF)
    normed = low(canvas)
    queries = (nn(normed, weights[0]) + vec[4]).astype(BF)
    keys = nn(normed, weights[1]).astype(BF)
    values = (nn(normed, weights[2]) + vec[5]).astype(BF)
    own = (nn(low(band), weights[0]) + vec[4]).astype(BF)
    scores = jnp.einsum("qhd,khd->hqk", split_heads(own), split_heads(keys), preferred_element_type=F32)
    scores = jnp.where(same[None], scores * SCALE, MASKED)
    peak = jnp.max(scores, axis=-1, keepdims=True)
    raised = jnp.exp(scores - peak)
    sums = jnp.sum(raised, axis=-1, keepdims=True)
    probs = (raised / sums).astype(BF)
    mixed = jnp.einsum("hqk,khd->qhd", probs, split_heads(values), preferred_element_type=F32).reshape(own.shape)
    region_rows = band.astype(F32) + nn(mixed.astype(BF), weights[3]) + vec[6]
    return region_rows, mixed, (peak + jnp.log(sums))[:, :, 0], queries, keys, values


def regional_terms(queries, keys, values, grad_mixed, same, level, delta):
    scores = jnp.einsum("qhd,khd->hqk", split_heads(queries), split_heads(keys), preferred_element_type=F32)
    probs = jnp.where(same[None], jnp.exp(scores * SCALE - level[:, :, None]), 0.0)
    grads = jnp.einsum("qhd,khd->hqk", split_heads(grad_mixed), split_heads(values), preferred_element_type=F32)
    return probs.astype(BF), (probs * (grads - delta[:, :, None])).astype(BF)


def regional_backward(queries, keys, values, grads, own, rows, same, level, delta, weights, vec, mixed, band_grad, dw):
    grad_mixed = nt(grads, weights[3]).astype(BF)
    level_own, delta_own = own(level.T).T, own(delta.T).T
    _, scores = regional_terms(own(queries), keys, values, own(grad_mixed), same.T, level_own, delta_own)
    dq = jnp.einsum("hqk,khd->qhd", scores, split_heads(keys), preferred_element_type=F32)
    probs, scores = regional_terms(queries, own(keys), own(values), grad_mixed, same, level, delta)
    dk = jnp.einsum("hqk,qhd->khd", scores, split_heads(queries), preferred_element_type=F32)
    dv = jnp.einsum("hqk,qhd->khd", probs, split_heads(grad_mixed), preferred_element_type=F32)
    flat = lambda x: x.reshape(-1, D)
    dq, dk, dv = flat(dq) * SCALE, flat(dk) * SCALE, flat(dv)
    lows = [x.astype(BF) for x in (dq, dk, dv)]
    dn = sum(nt(x, w) for x, w in zip(lows, weights))
    xhat, scale = norm_parts(rows.astype(F32))
    low = (xhat * vec[0] + vec[1]).astype(BF)
    d_regions = own(grads).astype(F32) + norm_back(dn, xhat, scale, vec[0])
    matrices = [dw[j] + tn(low, x) for j, x in enumerate(lows)] + [dw[3] + tn(mixed.astype(BF), band_grad)]
    vectors = [fold(x) for x in (dn * xhat, dn, dq, dv, band_grad.astype(F32))]
    return d_regions, jnp.stack(matrices).astype(BF), jnp.stack(vectors)


def per_device(patches, regions, image_ids, attn_w, mlp_in, mlp_out, vec_params, patch_cot, region_cot,
               attn_mom, mlp_in_mom, mlp_out_mom, adam_first, adam_second):
    dp_size = lax.axis_size("dp")
    dp_index = lax.axis_index("dp")
    opt_index = lax.axis_index("opt")
    _, grid_rows, cols, _, _ = patch_cot.shape
    grid_cols = patches.shape[2]
    tokens = grid_rows * grid_cols
    own_count = grid_rows * cols
    one_kernel = tokens <= 1024
    vec = vec_params
    order = opt_index ^ jnp.arange(OPT)
    move = lambda x: lax.all_to_all(x, "dp", 0, 0, tiled=True)

    attn_pieces = jnp.stack(pieces_of_owners(attn_w[0].astype(BF)))
    weights = [lax.dynamic_index_in_dim(attn_pieces, opt_index ^ j, 0, keepdims=False) for j in range(OPT)]
    canvas_blocks = share(regions[0])
    canvas = canvas_blocks.reshape(tokens, D)
    by_position = patch_cot[0].transpose(0, 2, 1, 3)
    split = 20
    last = jnp.concatenate([by_position[:, split:], region_cot[0][:, None]], axis=1)
    cots = [move(by_position[:, :split]), move(last)]
    first = pieces_of_owners(mlp_in.astype(BF))
    second = pieces_of_owners(mlp_out.astype(BF))
    bias_first = jnp.take(vec[8:], order, axis=0)

    band_of = lambda x: lax.dynamic_slice_in_dim(x, dp_index, 1, 1).reshape((grid_cols,) + x.shape[3:])
    own_of = lambda x: lax.dynamic_slice_in_dim(x, dp_index * own_count, own_count, 0)
    ids_blocks = image_ids[0].reshape(grid_rows, dp_size, cols).transpose(1, 0, 2)
    ids = ids_blocks.reshape(tokens)
    band_ids, own_ids = band_of(ids_blocks), own_of(ids)
    band = band_of(canvas_blocks)
    if one_kernel:
        repeat = lambda x: jnp.tile(x, 4)[None]
        region_rows, mixed, level, reg_q, reg_k, reg_v = in_vmem(
            regional_fwd_kernel,
            [((grid_cols, D), F32), ((grid_cols, D), F32), ((4, 4 * grid_cols), F32)] + [((tokens, D), BF)] * 3,
            "regional_attention_forward", canvas, band, ids[:, None], repeat(band_ids), *weights, vec)
        level = level.reshape(HEADS, grid_cols)
    else:
        region_rows, mixed, level, reg_q, reg_k, reg_v = regional_forward(
            canvas, band, band_ids[:, None] == ids[None, :], weights, vec)
    level_wide = jnp.tile(level.T, (1, GROUP // HEADS))

    windows = patches[0, 0].transpose(1, 0, 2)
    x1, *saved = attn_fwd(windows, region_rows, weights, vec)
    outs = [mlp(x1, start, cot, first, second, vec, bias_first) for start, cot in zip((0, split), cots)]
    moved = [move(o[0]) for o in outs]
    out_patches = jnp.concatenate([moved[0], moved[1][:, : PATCH - split]], axis=1).transpose(0, 2, 1, 3)[None]
    out_regions = moved[1][None, :, PATCH - split]
    d_patches, d_region, d_attn, d_vec_attn = attn_bwd(windows, region_rows, [o[1] for o in outs],
                                                     saved, weights, vec, moved[0])
    d_patches = d_patches.transpose(1, 0, 2)[None, None]

    add = lambda n, j: (outs[0][n][j].astype(F32) + outs[1][n][j].astype(F32)).astype(BF)
    own_first = sum_at_owner([add(2, j) for j in range(OPT)])
    own_second = sum_at_owner([add(3, j) for j in range(OPT)])
    own_mlp = sum_over_dp(jnp.concatenate([own_first, own_second], axis=1))
    grams = in_vmem(grams_kernel, [((D, D), F32)] * 6, "mlp_grams", *pieces_of_owners(mlp_in_mom),
                    *pieces_of_owners(mlp_out_mom), *pieces_of_owners(own_mlp))

    band_grad, extra = in_vmem(payload_kernel, [((grid_cols, D), BF), ((grid_cols, GROUP), BF)],
                               "regional_payload", d_region, mixed, level_wide, weights[3],
                               after=(own_first, own_second, moved[1]))
    payload = share(jnp.concatenate([band_grad, extra], axis=1)).reshape(grid_rows, dp_size, cols, D + GROUP)
    payload = payload.transpose(1, 0, 2, 3).reshape(tokens, D + GROUP)
    grads = payload[:, :D]
    extra = payload[:, D:].astype(F32)
    part = lambda n: extra[:, n * HEADS : (n + 1) * HEADS]
    delta = (part(0) + part(1)).T
    level = (part(2) + part(3) + part(4)).T
    if one_kernel:
        wide = lambda x: x.reshape(4, -1)
        own_columns = lambda x: wide(lax.dynamic_slice_in_dim(x, dp_index * own_count, own_count, 1))
        d_regions, grad_attn, d_vec_reg = in_vmem(
            partial(regional_bwd_kernel, own_count),
            [((own_count, D), F32), ((4, D, D), BF), ((5, 8, D), F32)],
            "regional_attention_backward", reg_q, reg_k, reg_v, grads, own_of(reg_q), own_of(reg_k), own_of(reg_v),
            own_of(canvas), ids[:, None], repeat(ids), own_ids[:, None], repeat(own_ids), wide(level), wide(delta),
            own_columns(level), own_columns(delta), own_of(grads), mixed, band_grad, d_attn, *weights, vec)
    else:
        d_regions, grad_attn, d_vec_reg = regional_backward(
            reg_q, reg_k, reg_v, grads, own_of, own_of(canvas), ids[:, None] == own_ids[None, :], level, delta,
            weights, vec, mixed, band_grad, d_attn)
    d_regions = d_regions.reshape(regions.shape)

    pieces = [lax.dynamic_index_in_dim(grad_attn, opt_index ^ j, 0, keepdims=False) for j in range(OPT)]
    own_attn = sum_over_dp(sum_at_owner(pieces))

    d_vec_attn = jnp.sum(d_vec_attn + d_vec_reg, axis=1)
    d_vec_mlp = jnp.sum(outs[0][4] + outs[1][4], axis=1)
    d_bias_first = jnp.take(jnp.sum(outs[0][5] + outs[1][5], axis=1), order, axis=0)
    grad_vec = jnp.concatenate([d_vec_attn[:2], d_vec_mlp[:2], d_vec_attn[2:], d_vec_mlp[2:], d_bias_first])
    grad_vec = grad_vec + pair(grad_vec, 1)
    grad_vec = grad_vec + pair(grad_vec, 2)
    grad_vec = sum_small_over_dp(grad_vec)

    squares = lambda x: jnp.sum(x.astype(F32) ** 2)
    total = jnp.full((8, 128), squares(own_attn) + squares(own_mlp))
    total = total + pair(total, 1)
    total = total + pair(total, 2)
    grad_norm = jnp.sqrt(total[0, 0] + squares(grad_vec))
    clip = jnp.minimum(1.0, CLIP_LIMIT / (grad_norm + 1e-06))
    attn_mom_new, new_attn, first_mom, new_first, second_mom, new_second = in_vmem(
        update_kernel, [((D, D), F32)] * 6, "matrix_updates", clip.reshape(1, 1), own_attn, attn_mom[0], attn_w[0],
        own_mlp, mlp_in_mom, mlp_out_mom, mlp_in, mlp_out, *grams)
    clipped = clip * grad_vec
    moment_one = BETA_FIRST * adam_first + (1.0 - BETA_FIRST) * clipped
    moment_two = BETA_SECOND * adam_second + (1.0 - BETA_SECOND) * clipped * clipped
    first_hat = moment_one / (1.0 - BETA_FIRST**OPT_STEP)
    second_hat = moment_two / (1.0 - BETA_SECOND**OPT_STEP)
    new_vec = vec_params - ADAM_RATE * first_hat / (jnp.sqrt(second_hat) + ADAM_EPS)
    return (out_patches, out_regions, d_patches, d_regions, new_attn[None], attn_mom_new[None], new_first, first_mom,
            new_second, second_mom, new_vec, moment_one, moment_two, grad_norm)


def solution(mesh):
    canvas = P("opt", None, "dp", None)
    wide = P("opt", None, "dp", None, None)
    bands = P("opt", "dp", None, None, None)
    square, right, down = P("opt", None, None), P(None, "opt"), P("opt", None)
    return jax.shard_map(
        per_device,
        mesh=mesh,
        in_specs=(bands, canvas, square, square, right, down, P(), wide, canvas, square, right, down, P(), P()),
        out_specs=(wide, canvas, bands, canvas, square, square, right, right, down, down, P(), P(), P(), P()),
        check_vma=False,
    )
```

```python
from functools import partial

import jax
import jax.numpy as jnp
from jax import lax
from jax.experimental import pallas as pl
from jax.experimental.pallas import tpu as pltpu
from jax.sharding import PartitionSpec as P

BF = jnp.bfloat16
F32 = jnp.float32

D = 512
HEADS = 16
HEAD_DIM = 32
FF = 2048
PATCH = 49
LIVE = 50
ROWS = 56
GROUP = 128
STACK = 4 * ROWS
OPT_STEP = 10
OPT = 4

SCALE = HEAD_DIM ** (-0.5)
NORM_EPS = 1e-05
MASKED = -1e30
NS_FIRST = 3.4445
NS_SECOND = -4.775
NS_THIRD = 2.0315
MUON_RATE = 0.5
MUON_MOMENTUM = 0.5
MUON_DECAY = 0.01
ADAM_RATE = 0.5
BETA_FIRST = 0.9
BETA_SECOND = 0.95
ADAM_EPS = 1e-08
CLIP_LIMIT = 1.0
DECAY_KEEP = 1.0 - MUON_RATE * MUON_DECAY
VMEM = 60 * 2**20
BRIEF = pl.CostEstimate(flops=10**6, bytes_accessed=10**5, transcendentals=0)

ERF_P = 0.3275911 * 0.5**0.5
ERF = tuple(0.5 * c for c in (0.254829592, -0.284496736, 1.421413741, -1.453152027, 1.061405429))
INV_SQRT_2PI = 0.3989422804014327
LOG2E = 1.4426950408889634


def nn(a, b):
    return lax.dot_general(a, b, (((1,), (0,)), ((), ())), preferred_element_type=F32)


def nt(a, b):
    return lax.dot_general(a, b, (((1,), (1,)), ((), ())), preferred_element_type=F32)


def tn(a, b):
    return lax.dot_general(a, b, (((0,), (0,)), ((), ())), preferred_element_type=F32)


def full(shape):
    return pl.BlockSpec(shape, lambda i: (0,) * len(shape))


def block(shape):
    return pl.BlockSpec(shape, lambda i: (i,) + (0,) * (len(shape) - 1))


def norm_parts(x):
    centre = x - jnp.mean(x, axis=-1, keepdims=True)
    scale = lax.rsqrt(jnp.mean(centre * centre, axis=-1, keepdims=True) + NORM_EPS)
    return centre * scale, scale


def norm_back(grad, xhat, scale, gain):
    inner = grad * gain
    first = jnp.mean(inner, axis=-1, keepdims=True)
    second = jnp.mean(inner * xhat, axis=-1, keepdims=True)
    return scale * (inner - first - xhat * second)


def head_masks():
    lane = lax.broadcasted_iota(jnp.int32, (1, GROUP), 1) // HEAD_DIM
    return [lane == h for h in range(4)]


def spread(rows, masks):
    return jnp.concatenate([jnp.where(m, rows, 0.0) for m in masks], axis=0).astype(BF)


def collect(stacked, masks, rows):
    out = stacked[:rows]
    for h in range(1, 4):
        out = jnp.where(masks[h], stacked[h * rows : (h + 1) * rows], out)
    return out


def lane_groups(x):
    return [x[:, GROUP * g : GROUP * (g + 1)] for g in range(4)]


def hold(ref, total, x):
    for g, part in enumerate(lane_groups(x)):
        ref[g, :total] = part


def held_rows(ref, total):
    return jnp.concatenate([ref[g, :total] for g in range(4)], axis=1)


def fold(x):
    return jnp.sum(x.reshape(x.shape[0] // 8, 8, x.shape[1]), axis=0)


def gelu_parts(a):
    bell = jnp.exp2(a * a * (-0.5 * LOG2E))
    t = 1.0 / (1.0 + ERF_P * jnp.abs(a))
    tail = ((((ERF[4] * t + ERF[3]) * t + ERF[2]) * t + ERF[1]) * t + ERF[0]) * t * bell
    share = jnp.where(a < 0, tail, 1.0 - tail)
    return a * share, share + a * bell * INV_SQRT_2PI


def attn_fwd_kernel(count, batch, p_ref, r_ref, wq_ref, wk_ref, wv_ref, wo_ref, vec_ref, _,
                    x1_ref, q_ref, k_ref, v_ref, o_ref, pt_ref, q_held, k_held, v_held, o_held):
    total = count * LIVE

    @pl.when(pl.program_id(0) == 0)
    def _():
        for ref in (q_held, k_held, v_held):
            ref[:, total:] = jnp.zeros((4, count * (ROWS - LIVE), GROUP), F32)

    x = jnp.concatenate([p_ref[...].astype(F32), r_ref[...][None]], axis=0).reshape(total, D)
    vec = vec_ref[...]
    xhat, _ = norm_parts(x)
    xn = (xhat * vec[0:1] + vec[1:2]).astype(BF)
    hold(q_held, total, nn(xn, wq_ref[...]) + vec[4:5])
    hold(k_held, total, nn(xn, wk_ref[...]))
    hold(v_held, total, nn(xn, wv_ref[...]) + vec[5:6])
    masks = head_masks()
    live = lax.broadcasted_iota(jnp.int32, (ROWS, 1), 0) < LIVE

    def body(step, carry):
        units = [(step * batch + w, g) for w in range(batch) for g in range(4)]
        scores, probs = [], []
        for w, g in units:
            lanes = slice(GROUP * g, GROUP * (g + 1))
            rows = pl.ds(w, ROWS, stride=count)
            q = q_held[g, rows, :]
            q_ref[w, :, lanes] = q.astype(BF)
            k = k_held[g, rows, :].astype(BF)
            k_ref[w, :, lanes] = k
            scores.append(nt(k, spread(q, masks)))
        for (w, g), s in zip(units, scores):
            s = jnp.where(live, s, MASKED)
            e = jnp.exp((s - jnp.max(s, axis=0, keepdims=True)) * SCALE)
            p = (e * (1.0 / jnp.sum(e, axis=0, keepdims=True))).astype(BF)
            pt_ref[w, g] = p
            probs.append(p)
        for (w, g), p in zip(units, probs):
            lanes = slice(GROUP * g, GROUP * (g + 1))
            rows = pl.ds(w, ROWS, stride=count)
            v = v_held[g, rows, :].astype(BF)
            v_ref[w, :, lanes] = v
            o_held[g, rows, :] = collect(tn(p, v), masks, ROWS)
        return carry

    lax.fori_loop(0, count // batch, body, 0)
    mixed = held_rows(o_held, total).astype(BF)
    o_ref[...] = mixed.reshape(LIVE, count, D)
    x1_ref[...] = (x + nn(mixed, wo_ref[...]) + vec[6:7]).reshape(LIVE, count, D)


def middle(rows, count, skip=0):
    return pl.BlockSpec((rows, count, D), lambda i: (0, i + skip, 0))


def attn_fwd(patches, region_rows, weights, vec, start, windows, after, count=16, batch=4):
    skip = start // count
    array = jax.ShapeDtypeStruct
    return pl.pallas_call(
        partial(attn_fwd_kernel, count, batch),
        grid=(windows // count,),
        in_specs=[middle(PATCH, count, skip), pl.BlockSpec((count, D), lambda i: (i + skip, 0))]
        + [full((D, D))] * 4 + [full(vec.shape), pl.BlockSpec(memory_space=pl.ANY)],
        out_specs=[middle(LIVE, count)] + [block((count, ROWS, D))] * 3
        + [middle(LIVE, count), block((count, 4, ROWS, STACK))],
        out_shape=[array((LIVE, windows, D), F32)] + [array((windows, ROWS, D), BF)] * 3
        + [array((LIVE, windows, D), BF), array((windows, 4, ROWS, STACK), BF)],
        scratch_shapes=[pltpu.VMEM((4, count * ROWS, GROUP), F32)] * 4,
        compiler_params=pltpu.CompilerParams(vmem_limit_bytes=VMEM),
        cost_estimate=BRIEF,
        name="window_attention_forward",
    )(patches, region_rows, *weights, vec, after)


def mlp_kernel(many, sources, cols, steps, lanes, last, *refs):
    x1a_ref, x1b_ref, pc_ref, *w_refs, vec_ref, b1_ref = refs[:9]
    prev_refs = refs[9 : 11 if last else 9]
    op_ref, dx1_ref, dwa_ref, dwb_ref, dv_ref, db1_ref, acc1, acc2 = refs[9 + len(prev_refs) :]
    total = many * sources * cols
    step = pl.program_id(0)

    @pl.when(step == 0)
    def _():
        for ref in (acc1, acc2, dv_ref, db1_ref):
            ref[...] = jnp.zeros_like(ref)

    vec = vec_ref[...]
    gain = vec[2:3]
    x1 = jnp.concatenate([x1a_ref[...], x1b_ref[...]], axis=1).reshape(total, D)
    xhat, scale = norm_parts(x1)
    h = (xhat * gain + vec[3:4]).astype(BF)
    for s in range(sources):
        dx1_ref[:, s * cols : (s + 1) * cols] = pc_ref[s].astype(F32)
    dy = dx1_ref[...].reshape(total, D)
    dm = dy.astype(BF)
    ht = h.T
    dmt = dm.T
    y = x1 + vec[7:8]
    dh = jnp.zeros((total, D), F32)
    parts = [(j, slice(c, c + lanes)) for j in range(4) for c in range(0, D, lanes)]

    def activate(j, s):
        u, slope = gelu_parts(nn(h, w_refs[j][0, :, s]) + b1_ref[j : j + 1, s])
        da = slope * nt(dm, w_refs[j][1, s, :])
        db1_ref[j, :, s] += fold(da)
        return u.astype(BF), da.astype(BF)

    def apply(j, s, u, da):
        acc1[j, :, s] += nn(ht, da)
        acc2[j, :, s] += nn(dmt, u)
        return nn(u, w_refs[j][1, s, :]), nt(da, w_refs[j][0, :, s])

    held_pair = activate(*parts[0])
    for n in range(1, len(parts) + 1):
        later = activate(*parts[n]) if n < len(parts) else None
        up, down = apply(*parts[n - 1], *held_pair)
        y, dh = y + up, dh + down
        held_pair = later
    y = y.reshape(many, sources * cols, D)
    for s in range(sources):
        op_ref[s] = y[:, s * cols : (s + 1) * cols].astype(BF)
    dy = dx1_ref[...].reshape(total, D)
    dx1_ref[...] = (dy + norm_back(dh, xhat, scale, gain)).reshape(dx1_ref.shape)
    dv_ref[0] += fold(dh * xhat)
    dv_ref[1] += fold(dh)
    dv_ref[2] += fold(dy)

    @pl.when(step == steps - 1)
    def _():
        for refs_out, first in ((dwa_ref, 0), (dwb_ref, 1)):
            for n, acc in enumerate((acc1, acc2)):
                for m in range(2):
                    piece = acc[first + 2 * m]
                    for prev in prev_refs[first : first + 1]:
                        piece = piece + prev[2 * n + m].astype(F32)
                    refs_out[2 * n + m] = piece.astype(BF)


def mlp(x1_parts, first_position, cot, weights, vec, bias_first, prev=(), many=10, lanes=256):
    sources, positions, cols, _ = cot.shape
    windows = sources * cols
    steps = positions // many
    skip = first_position // many
    some = pl.BlockSpec((sources, many, cols, D), lambda i: (0, i, 0, 0))
    array = jax.ShapeDtypeStruct
    matrices = full((4, D, D))
    return pl.pallas_call(
        partial(mlp_kernel, many, sources, cols, steps, lanes, len(prev) > 0),
        grid=(steps,),
        in_specs=[pl.BlockSpec((many, part.shape[1], D), lambda i: (i + skip, 0, 0)) for part in x1_parts] + [some]
        + [full((2, D, D))] * 4 + [full(vec.shape), full((4, D))] + [matrices] * len(prev),
        out_specs=[some, block((many, windows, D)), matrices, matrices, full((3, 8, D)), full((4, 8, D))],
        out_shape=[array(cot.shape, BF), array((positions, windows, D), F32), array((4, D, D), BF),
                   array((4, D, D), BF), array((3, 8, D), F32), array((4, 8, D), F32)],
        scratch_shapes=[pltpu.VMEM((4, D, D), F32), pltpu.VMEM((4, D, D), F32)],
        compiler_params=pltpu.CompilerParams(vmem_limit_bytes=VMEM),
        cost_estimate=BRIEF,
        name="mlp_forward_backward",
    )(*x1_parts, cot, *weights, vec, bias_first, *prev)


def attn_bwd_kernel(count, batch, chunks, more, *refs):
    p_ref, r_ref, _ = refs[:3]
    dx1_refs = refs[3 : 3 + chunks]
    q_ref, k_ref, v_ref, o_ref, pt_ref, wq_ref, wk_ref, wv_ref, wo_ref, vec_ref = refs[3 + chunks : 13 + chunks]
    prev_refs = refs[13 + chunks : 17 + chunks] if more else ()
    dp_ref, dr_ref, dw_ref, dv_ref, dq_held, dk_held, dvv_held, do_held = refs[13 + chunks + len(prev_refs) :]
    total = count * LIVE

    @pl.when(pl.program_id(0) == 0)
    def _():
        dw_ref[...] = prev_refs[2][...] if more else jnp.zeros_like(dw_ref)
        dv_ref[...] = prev_refs[3][...] if more else jnp.zeros_like(dv_ref)
        do_held[:, total:] = jnp.zeros((4, count * (ROWS - LIVE), GROUP), F32)

    vec = vec_ref[...]
    gain = vec[0:1]
    dx1 = jnp.concatenate([ref[...] for ref in dx1_refs], axis=0).reshape(total, D)
    gb = dx1.astype(BF)
    hold(do_held, total, nt(gb, wo_ref[...]))
    masks = head_masks()

    def body(step, carry):
        units = [(step * batch + w, g) for w in range(batch) for g in range(4)]
        grads, scores = [], []
        for w, g in units:
            lanes = slice(GROUP * g, GROUP * (g + 1))
            rows = pl.ds(w, ROWS, stride=count)
            do_wide = spread(do_held[g, rows, :], masks)
            dvv_held[g, rows, :] = nn(pt_ref[w, g], do_wide)
            grads.append(nt(v_ref[w, :, lanes], do_wide))
        for (w, g), grad in zip(units, grads):
            p = pt_ref[w, g].astype(F32)
            both = p * grad
            scores.append((both - p * jnp.sum(both, axis=0, keepdims=True)).astype(BF))
        for (w, g), ds in zip(units, scores):
            lanes = slice(GROUP * g, GROUP * (g + 1))
            rows = pl.ds(w, ROWS, stride=count)
            dk_held[g, rows, :] = nn(ds, spread(q_ref[w, :, lanes].astype(F32), masks)) * SCALE
            dq_held[g, rows, :] = collect(tn(ds, k_ref[w, :, lanes]), masks, ROWS) * SCALE
        return carry

    lax.fori_loop(0, count // batch, body, 0)
    x = jnp.concatenate([p_ref[...].astype(F32), r_ref[...][None]], axis=0).reshape(total, D)
    xhat, scale = norm_parts(x)
    xn = (xhat * gain + vec[1:2]).astype(BF)
    dq_wide = held_rows(dq_held, total)
    dv_wide = held_rows(dvv_held, total)
    dq = dq_wide.astype(BF)
    dk = held_rows(dk_held, total).astype(BF)
    dv = dv_wide.astype(BF)
    dn = nt(dq, wq_ref[...]) + nt(dk, wk_ref[...]) + nt(dv, wv_ref[...])
    dx = (dx1 + norm_back(dn, xhat, scale, gain)).reshape(LIVE, count, D)
    dp_ref[...] = dx[:PATCH].astype(BF)
    dr_ref[...] = dx[PATCH]
    xt = xn.T
    dw_ref[0] += nn(xt, dq)
    dw_ref[1] += nn(xt, dk)
    dw_ref[2] += nn(xt, dv)
    dw_ref[3] += nn(o_ref[...].reshape(total, D).T, gb)
    dv_ref[0] += fold(dn * xhat)
    dv_ref[1] += fold(dn)
    dv_ref[2] += fold(dq_wide)
    dv_ref[3] += fold(dv_wide)
    dv_ref[4] += fold(dx1)


def attn_bwd(patches, region_rows, dx1_parts, saved, weights, vec, start, windows, after, prev=(), count=16, batch=4):
    skip = start // count
    array = jax.ShapeDtypeStruct
    sums = [full((4, D, D)), full((5, 8, D))]
    anywhere = pl.BlockSpec(memory_space=pl.ANY)
    rows = pl.BlockSpec((count, D), lambda i: (i + skip, 0))
    before = 13 + len(dx1_parts)
    return pl.pallas_call(
        partial(attn_bwd_kernel, count, batch, len(dx1_parts), len(prev) > 0),
        grid=(windows // count,),
        in_specs=[middle(PATCH, count, skip), rows, anywhere]
        + [middle(part.shape[0], count, skip) for part in dx1_parts]
        + [block((count, ROWS, D))] * 3 + [middle(LIVE, count), block((count, 4, ROWS, STACK))]
        + [full((D, D))] * 4 + [full(vec.shape)] + ([anywhere] * 2 + sums)[: len(prev)],
        out_specs=[middle(PATCH, count, skip), rows] + sums,
        out_shape=[array(patches.shape, BF), array(region_rows.shape, F32),
                   array((4, D, D), F32), array((5, 8, D), F32)],
        scratch_shapes=[pltpu.VMEM((4, count * ROWS, GROUP), F32)] * 4,
        input_output_aliases={before: 0, before + 1: 1} if prev else {},
        compiler_params=pltpu.CompilerParams(vmem_limit_bytes=VMEM),
        cost_estimate=BRIEF,
        name="window_attention_backward",
    )(patches, region_rows, after, *dx1_parts, *saved, *weights, vec, *prev)


def regional_fwd_kernel(canvas_ref, band_ref, ids_ref, band_ids_ref, wq_ref, wk_ref, wv_ref, wo_ref, vec_ref,
                        r1_ref, mixed_ref, level_ref, q_ref, k_ref, v_ref):
    vec = vec_ref[...]
    xhat, _ = norm_parts(canvas_ref[...].astype(F32))
    low = (xhat * vec[0:1] + vec[1:2]).astype(BF)
    q_ref[...] = (nn(low, wq_ref[...]) + vec[4:5]).astype(BF)
    k_ref[...] = nn(low, wk_ref[...]).astype(BF)
    v_ref[...] = (nn(low, wv_ref[...]) + vec[5:6]).astype(BF)
    band = band_ref[...].astype(F32)
    rows = band.shape[0]
    xhat, _ = norm_parts(band)
    q = nn((xhat * vec[0:1] + vec[1:2]).astype(BF), wq_ref[...]) + vec[4:5]
    masks = head_masks()
    same = ids_ref[...] == band_ids_ref[...]
    scores, probs = [], []
    for g in range(4):
        lanes = slice(GROUP * g, GROUP * (g + 1))
        scores.append(nt(k_ref[:, lanes], spread(q[:, lanes], masks)))
    for g, s in enumerate(scores):
        s = jnp.where(same, s, MASKED)
        peak = jnp.max(s, axis=0, keepdims=True)
        e = jnp.exp((s - peak) * SCALE)
        sums = jnp.sum(e, axis=0, keepdims=True)
        level_ref[g : g + 1] = peak * SCALE + jnp.log(sums)
        probs.append((e * (1.0 / sums)).astype(BF))
    for g, p in enumerate(probs):
        lanes = slice(GROUP * g, GROUP * (g + 1))
        mixed_ref[:, lanes] = collect(tn(p, v_ref[:, lanes]), masks, rows)
    r1_ref[...] = band + nn(mixed_ref[...].astype(BF), wo_ref[...]) + vec[6:7]


def in_vmem(kernel, outs, name, *args, after=(), scratch=()):
    spaces = [pltpu.SMEM if arg.shape == (1, 1) else pltpu.VMEM for arg in args]
    count = len(args)
    return pl.pallas_call(
        lambda *refs: kernel(*refs[:count], *refs[count + len(after) :]),
        in_specs=[pl.BlockSpec(memory_space=space) for space in spaces]
        + [pl.BlockSpec(memory_space=pl.ANY) for _ in after],
        out_specs=[pl.BlockSpec(memory_space=pltpu.VMEM) for _ in outs],
        out_shape=[jax.ShapeDtypeStruct(*out) for out in outs],
        scratch_shapes=list(scratch),
        compiler_params=pltpu.CompilerParams(vmem_limit_bytes=VMEM),
        cost_estimate=BRIEF,
        name=name,
    )(*args, *after)


def payload_kernel(dr_ref, mixed_ref, level_ref, wo_ref, grad_ref, extra_ref):
    low = dr_ref[...].astype(BF)
    grad_ref[...] = low
    both = nt(low, wo_ref[...]).astype(BF).astype(F32) * mixed_ref[...]
    head = lax.broadcasted_iota(jnp.int32, (D, GROUP), 0) // HEAD_DIM
    lane = lax.broadcasted_iota(jnp.int32, (D, GROUP), 1)
    pick = ((head == lane) | (head + HEADS == lane)).astype(BF)
    high, low_part = halves(both)
    rest = (both - high.astype(F32) - low_part.astype(F32)).astype(BF)
    delta = nn(high, pick) + (nn(low_part, pick) + nn(rest, pick))
    top = delta.astype(BF).astype(F32)
    lane = lax.broadcasted_iota(jnp.int32, (1, GROUP), 1)
    level = level_ref[...]
    level_top = level.astype(BF).astype(F32)
    level_rest = level - level_top
    level_mid = level_rest.astype(BF).astype(F32)
    extra = level_rest - level_mid
    for place, term in ((4, level_mid), (3, level_top), (2, delta - top), (1, top)):
        extra = jnp.where(lane < place * HEADS, term, extra)
    extra_ref[...] = extra.astype(BF)


def regional_bwd_kernel(own_rows, owner_ref, q_ref, k_ref, v_ref, grads_ref, qo_ref, ko_ref, vo_ref, own_ref, ids_ref, ids_row_ref,
                        ids_own_ref, ids_own_row_ref, level_ref, delta_ref, level_own_ref, delta_own_ref,
                        grads_own_ref, mixed_ref, band_grad_ref, dw_ref, wq_ref, wk_ref, wv_ref, wo_ref, vec_ref,
                        dr_ref, keep_ref, give_ref, gv_ref, sum_held):
    vec = vec_ref[...]
    masks = head_masks()
    do = nt(grads_ref[...], wo_ref[...]).astype(BF).astype(F32)
    do_own = nt(grads_own_ref[...], wo_ref[...]).astype(BF).astype(F32)
    same_own = ids_ref[...] == ids_own_row_ref[...]
    same = ids_own_ref[...] == ids_row_ref[...]
    lanes = [slice(GROUP * g, GROUP * (g + 1)) for g in range(4)]
    first, second = [], []
    dqs, dks, dvs = [], [], []
    for g in range(4):
        q_wide = spread(qo_ref[:, lanes[g]].astype(F32), masks)
        do_wide = spread(do_own[:, lanes[g]], masks)
        first.append((nt(k_ref[:, lanes[g]], q_wide), nt(v_ref[:, lanes[g]], do_wide)))
        q_wide = spread(q_ref[:, lanes[g]].astype(F32), masks)
        do_wide = spread(do[:, lanes[g]], masks)
        second.append((nt(ko_ref[:, lanes[g]], q_wide), nt(vo_ref[:, lanes[g]], do_wide), q_wide, do_wide))
    for g in range(4):
        s, dp = first[g]
        p = jnp.where(same_own, jnp.exp(s * SCALE - level_own_ref[g : g + 1]), 0.0)
        ds = (p * (dp - delta_own_ref[g : g + 1])).astype(BF)
        dqs.append(collect(tn(ds, k_ref[:, lanes[g]]), masks, own_rows) * SCALE)
        s, dp, q_wide, do_wide = second[g]
        p = jnp.where(same, jnp.exp(s * SCALE - level_ref[g : g + 1]), 0.0)
        ds = (p * (dp - delta_ref[g : g + 1])).astype(BF)
        dvs.append(nn(p.astype(BF), do_wide))
        dks.append(nn(ds, q_wide) * SCALE)
    xhat, scale = norm_parts(own_ref[...].astype(F32))
    low = (xhat * vec[0:1] + vec[1:2]).astype(BF)
    dq_wide, dk_wide, dv_wide = (jnp.concatenate(x, axis=1) for x in (dqs, dks, dvs))
    dq, dk, dv = dq_wide.astype(BF), dk_wide.astype(BF), dv_wide.astype(BF)
    dn = nt(dq, wq_ref[...]) + nt(dk, wk_ref[...]) + nt(dv, wv_ref[...])
    dr_ref[...] = grads_own_ref[...].astype(F32) + norm_back(dn, xhat, scale, vec[0:1])
    sum_held[0] = dw_ref[0] + tn(low, dq)
    sum_held[1] = dw_ref[1] + tn(low, dk)
    sum_held[2] = dw_ref[2] + tn(low, dv)
    sum_held[3] = dw_ref[3] + tn(mixed_ref[...].astype(BF), band_grad_ref[...])
    owner = owner_ref[0, 0]
    for n in range(2):
        keep_ref[n] = sum_held[owner ^ (2 * n)].astype(BF)
        give_ref[n] = sum_held[owner ^ (2 * n + 1)].astype(BF)
    gv_ref[0] = fold(dn * xhat)
    gv_ref[1] = fold(dn)
    gv_ref[2] = fold(dq_wide)
    gv_ref[3] = fold(dv_wide)
    gv_ref[4] = fold(band_grad_ref[...].astype(F32))


def halves(a):
    high = a.astype(BF)
    return high, (a - high.astype(F32)).astype(BF)


def terms(a, passes):
    return (a.astype(BF),) if passes == 1 else halves(a)


def product(a, b, dot=nn):
    if len(a) == 1:
        return dot(a[0], b[0])
    return dot(a[0], b[0]) + (dot(a[0], b[1]) + dot(a[1], b[0]))


def symmetric(a, b, dot=nn):
    half = D // 2
    right = (lambda x: x[half:]) if dot is nt else (lambda x: x[:, half:])
    top = product([x[:half] for x in a], b, dot)
    corner = product([x[half:] for x in a], [right(x) for x in b], dot)
    return jnp.concatenate([top, jnp.concatenate([top[:, half:].T, corner], axis=1)], axis=0)


DIRECT_STEPS = (1, 1, 1, -1, -1)
GRAM_STEPS = (1, 1, 3, 3, 3)
NEAR_ZERO = NS_FIRST + NS_SECOND + NS_THIRD
NEAR_ONE = NS_SECOND + 2.0 * NS_THIRD


def identity():
    rows = lax.broadcasted_iota(jnp.int32, (D, D), 0)
    return rows == lax.broadcasted_iota(jnp.int32, (D, D), 1)


def polynomial(gram, eye, step):
    if step > 0:
        parts = terms(gram, step)
        return NS_FIRST, NS_SECOND * gram + NS_THIRD * symmetric(parts, parts)
    rest = gram - jnp.where(eye, 1.0, 0.0)
    parts = terms(rest, -step)
    return NEAR_ZERO, NEAR_ONE * rest + NS_THIRD * symmetric(parts, parts)


def direct_steps(moment, eye):
    z = moment * (1.0 / (jnp.sqrt(jnp.sum(moment * moment)) + 1e-07))
    for step in DIRECT_STEPS:
        parts = terms(z, abs(step))
        gram = symmetric(parts, parts, nt)
        yield
        scale, poly = polynomial(gram, eye, step)
        yield
        z = scale * z + product(terms(poly, abs(step)), parts)
        yield
    return z


def gram_steps(gram, eye):
    factor = 1.0 / (jnp.sqrt(jnp.sum(jnp.where(eye, gram, 0.0))) + 1e-07)
    gram = gram * (factor * factor)
    steps = None
    for n, passes in enumerate(GRAM_STEPS):
        scale, poly = polynomial(gram, eye, passes)
        yield
        parts = terms(poly, passes)
        if steps is None:
            steps = jnp.where(eye, scale, 0.0) + poly
        else:
            steps = scale * steps + symmetric(parts, terms(steps, passes))
            yield
        if n < len(GRAM_STEPS) - 1:
            half = scale * gram + symmetric(parts, terms(gram, passes))
            yield
            gram = scale * half + symmetric(parts, terms(half, passes))
            yield
    return steps * factor


def in_turns(*chains):
    results = [None] * len(chains)
    running = list(enumerate(chains))
    while running:
        still = []
        for n, chain in running:
            try:
                next(chain)
                still.append((n, chain))
            except StopIteration as stop:
                results[n] = stop.value
        running = still
    return results


def grams_kernel(*refs):
    for n in range(2):
        old, mixed, new = (jnp.zeros((D, D), F32) for _ in range(3))
        cross = jnp.zeros((D, D), F32)
        for j in range(4):
            high, low = halves(refs[j][n])
            if n == 1:
                high, low = high.T, low.T
            g = refs[4 + j][:, n * D : (n + 1) * D]
            old = old + nt(high, high)
            cross = cross + nt(high, low)
            mixed = mixed + (nt(high, g) + nt(low, g))
            new = new + nt(g, g)
        for k, x in enumerate((old + (cross + cross.T), mixed + mixed.T, new)):
            refs[8 + 3 * n + k][...] = x


def update_kernel(clip_ref, ga_ref, ma_ref, wa_ref, g_ref, m1_ref, m2_ref, w1_ref, w2_ref,
                  old1, mixed1, new1, old2, mixed2, new2, na_ref, newa_ref, n1_ref, new1_ref, n2_ref, new2_ref):
    clip = clip_ref[0, 0]
    eye = identity()
    na_ref[...] = MUON_MOMENTUM * ma_ref[...] + clip * ga_ref[...].astype(F32)
    n1_ref[...] = MUON_MOMENTUM * m1_ref[...] + clip * g_ref[:, :D].astype(F32)
    n2_ref[...] = MUON_MOMENTUM * m2_ref[...] + clip * g_ref[:, D:].astype(F32).T
    a, b, c = MUON_MOMENTUM * MUON_MOMENTUM, MUON_MOMENTUM * clip, clip * clip
    gram1 = a * old1[...] + b * mixed1[...] + c * new1[...]
    gram2 = a * old2[...] + b * mixed2[...] + c * new2[...]
    steps1, steps2, z = in_turns(gram_steps(gram1, eye), gram_steps(gram2, eye), direct_steps(na_ref[...], eye))
    newa_ref[...] = wa_ref[...] * DECAY_KEEP - MUON_RATE * z
    z = product(halves(steps1), halves(n1_ref[...]))
    new1_ref[...] = w1_ref[...] * DECAY_KEEP - MUON_RATE * z
    z = product(halves(n2_ref[...]), halves(steps2))
    new2_ref[...] = w2_ref[...] * DECAY_KEEP - (MUON_RATE * max(1.0, FF / D) ** 0.5) * z


def pair(values, bit):
    return lax.ppermute(values, "opt", [(i, i ^ bit) for i in range(OPT)])


def fence(x, *first):
    here = pl.BlockSpec(memory_space=pl.ANY)
    return pl.pallas_call(
        lambda *refs: None,
        in_specs=[here] * (1 + len(first)),
        out_specs=here,
        out_shape=jax.ShapeDtypeStruct(x.shape, x.dtype),
        input_output_aliases={0: 0},
        cost_estimate=BRIEF,
        name="fence",
    )(x, *first)


def pieces_of_owners(own, before_relay=()):
    mate = pair(own, 1)
    across = pair(own, 2)
    relay = fence(across, *before_relay) if before_relay else across
    return [own, mate, relay, pair(relay, 1)]


def share(x):
    copies = jnp.broadcast_to(x[None], (lax.axis_size("dp"),) + x.shape)
    return lax.all_to_all(copies, "dp", 0, 0, tiled=True)


def swap(x, bit):
    return lax.ppermute(x, "dp", [(i, i ^ bit) for i in range(lax.axis_size("dp"))])


def bits():
    return [1 << n for n in range(lax.axis_size("dp").bit_length() - 1)]


def halving_step(x, bit):
    half = x.shape[0] // 2
    side = (lax.axis_index("dp") // bit) % 2
    give = lax.dynamic_slice_in_dim(x, (1 - side) * half, half, 0).astype(BF)
    return lax.dynamic_slice_in_dim(x, side * half, half, 0), give


def doubling_step(x, bit):
    other = swap(x, bit)
    side = (lax.axis_index("dp") // bit) % 2
    return jnp.where(side == 0, jnp.concatenate([x, other]), jnp.concatenate([other, x]))


def sum_small_over_dp(x):
    for bit in bits():
        x = x + swap(x, bit)
    return x


def split_heads(x):
    return x.reshape(x.shape[0], HEADS, HEAD_DIM)


def regional_forward(canvas, band, same, weights, vec):
    low = lambda x: (norm_parts(x.astype(F32))[0] * vec[0] + vec[1]).astype(BF)
    normed = low(canvas)
    queries = (nn(normed, weights[0]) + vec[4]).astype(BF)
    keys = nn(normed, weights[1]).astype(BF)
    values = (nn(normed, weights[2]) + vec[5]).astype(BF)
    own = (nn(low(band), weights[0]) + vec[4]).astype(BF)
    scores = jnp.einsum("qhd,khd->hqk", split_heads(own), split_heads(keys), preferred_element_type=F32)
    scores = jnp.where(same[None], scores * SCALE, MASKED)
    peak = jnp.max(scores, axis=-1, keepdims=True)
    raised = jnp.exp(scores - peak)
    sums = jnp.sum(raised, axis=-1, keepdims=True)
    probs = (raised / sums).astype(BF)
    mixed = jnp.einsum("hqk,khd->qhd", probs, split_heads(values), preferred_element_type=F32).reshape(own.shape)
    region_rows = band.astype(F32) + nn(mixed.astype(BF), weights[3]) + vec[6]
    return region_rows, mixed, (peak + jnp.log(sums))[:, :, 0], queries, keys, values


def regional_terms(queries, keys, values, grad_mixed, same, level, delta):
    scores = jnp.einsum("qhd,khd->hqk", split_heads(queries), split_heads(keys), preferred_element_type=F32)
    probs = jnp.where(same[None], jnp.exp(scores * SCALE - level[:, :, None]), 0.0)
    grads = jnp.einsum("qhd,khd->hqk", split_heads(grad_mixed), split_heads(values), preferred_element_type=F32)
    return probs.astype(BF), (probs * (grads - delta[:, :, None])).astype(BF)


def regional_backward(queries, keys, values, grads, own, rows, same, level, delta, weights, vec, mixed, band_grad, dw):
    grad_mixed = nt(grads, weights[3]).astype(BF)
    level_own, delta_own = own(level.T).T, own(delta.T).T
    _, scores = regional_terms(own(queries), keys, values, own(grad_mixed), same.T, level_own, delta_own)
    dq = jnp.einsum("hqk,khd->qhd", scores, split_heads(keys), preferred_element_type=F32)
    probs, scores = regional_terms(queries, own(keys), own(values), grad_mixed, same, level, delta)
    dk = jnp.einsum("hqk,qhd->khd", scores, split_heads(queries), preferred_element_type=F32)
    dv = jnp.einsum("hqk,qhd->khd", probs, split_heads(grad_mixed), preferred_element_type=F32)
    flat = lambda x: x.reshape(-1, D)
    dq, dk, dv = flat(dq) * SCALE, flat(dk) * SCALE, flat(dv)
    lows = [x.astype(BF) for x in (dq, dk, dv)]
    dn = sum(nt(x, w) for x, w in zip(lows, weights))
    xhat, scale = norm_parts(rows.astype(F32))
    low = (xhat * vec[0] + vec[1]).astype(BF)
    d_regions = own(grads).astype(F32) + norm_back(dn, xhat, scale, vec[0])
    matrices = [dw[j] + tn(low, x) for j, x in enumerate(lows)] + [dw[3] + tn(mixed.astype(BF), band_grad)]
    vectors = [fold(x) for x in (dn * xhat, dn, dq, dv, band_grad.astype(F32))]
    return d_regions, jnp.stack(matrices).astype(BF), jnp.stack(vectors)


def per_device(patches, regions, image_ids, attn_w, mlp_in, mlp_out, vec_params, patch_cot, region_cot,
               attn_mom, mlp_in_mom, mlp_out_mom, adam_first, adam_second):
    dp_size = lax.axis_size("dp")
    dp_index = lax.axis_index("dp")
    opt_index = lax.axis_index("opt")
    _, grid_rows, cols, _, _ = patch_cot.shape
    grid_cols = patches.shape[2]
    tokens = grid_rows * grid_cols
    own_count = grid_rows * cols
    one_kernel = tokens <= 1024
    vec = vec_params
    order = opt_index ^ jnp.arange(OPT)
    move = lambda x: lax.all_to_all(x, "dp", 0, 0, tiled=True)

    attn_pieces = pieces_of_owners(attn_w[0].astype(BF))
    across = attn_pieces[2]
    attn_pieces = jnp.stack(attn_pieces)
    weights = [lax.dynamic_index_in_dim(attn_pieces, opt_index ^ j, 0, keepdims=False) for j in range(OPT)]
    canvas_blocks = share(regions[0])
    canvas = canvas_blocks.reshape(tokens, D)
    by_position = patch_cot[0].transpose(0, 2, 1, 3)
    split = 20
    last = jnp.concatenate([by_position[:, split:], region_cot[0][:, None]], axis=1)
    first_cot = move(fence(by_position[:, :split], canvas))
    bias_first = jnp.take(vec[8:], order, axis=0)

    band_of = lambda x: lax.dynamic_slice_in_dim(x, dp_index, 1, 1).reshape((grid_cols,) + x.shape[3:])
    own_of = lambda x: lax.dynamic_slice_in_dim(x, dp_index * own_count, own_count, 0)
    ids_blocks = image_ids[0].reshape(grid_rows, dp_size, cols).transpose(1, 0, 2)
    ids = ids_blocks.reshape(tokens)
    band_ids, own_ids = band_of(ids_blocks), own_of(ids)
    band = band_of(canvas_blocks)
    if one_kernel:
        repeat = lambda x: jnp.tile(x, 4)[None]
        region_rows, mixed, level, reg_q, reg_k, reg_v = in_vmem(
            regional_fwd_kernel,
            [((grid_cols, D), F32), ((grid_cols, D), F32), ((4, 4 * grid_cols), F32)] + [((tokens, D), BF)] * 3,
            "regional_attention_forward", canvas, band, ids[:, None], repeat(band_ids), *weights, vec)
        level = level.reshape(HEADS, grid_cols)
    else:
        region_rows, mixed, level, reg_q, reg_k, reg_v = regional_forward(
            canvas, band, band_ids[:, None] == ids[None, :], weights, vec)
    level_wide = jnp.tile(level.T, (1, GROUP // HEADS))

    windows = patches[0, 0].transpose(1, 0, 2)
    some = grid_cols // 2
    x1a, *saved_a = attn_fwd(windows, region_rows, weights, vec, 0, some, across)
    own_mlp_w = fence(jnp.stack([mlp_in, mlp_out]).astype(BF), across)
    mlp_w = pieces_of_owners(own_mlp_w, before_relay=(x1a,))
    last_cot = move(fence(last, x1a))
    x1b, *saved_b = attn_fwd(windows, region_rows, weights, vec, some, some, first_cot)
    x1 = (x1a, x1b)
    out_a = mlp(x1, 0, first_cot, mlp_w, vec, bias_first)
    moms = pieces_of_owners(fence(jnp.stack([mlp_in_mom, mlp_out_mom]), x1b), before_relay=(out_a[1],))
    moved_a = move(out_a[0])
    out_b = mlp(x1, split, last_cot, mlp_w, vec, bias_first, prev=out_a[2:4])
    moved_b = move(out_b[0])
    out_patches = jnp.concatenate([moved_a, moved_b[:, : PATCH - split]], axis=1).transpose(0, 2, 1, 3)[None]
    out_regions = moved_b[None, :, PATCH - split]

    near = pair(out_b[3], 1).astype(F32) + out_b[2].astype(F32)
    far = jnp.stack([near[1], near[3]]).astype(BF)
    dx1 = (out_a[1], out_b[1])
    early = attn_bwd(windows, region_rows, dx1, saved_a, weights, vec, 0, some, far)
    far = pair(far, 2).astype(F32)
    own_mlp = jnp.concatenate([near[0] + far[0], near[2] + far[1]], axis=1)
    keep, give = halving_step(own_mlp, 1)
    d_patches, d_region, d_attn, d_vec_attn = attn_bwd(
        windows, region_rows, dx1, saved_b, weights, vec, some, some, give, prev=early)
    d_patches = d_patches.transpose(1, 0, 2)[None, None]
    gives = []
    for bit in bits()[1:]:
        keep, give = halving_step(keep + swap(give, bit // 2).astype(F32), bit)
        gives.append(give)
    piece_mlp = (keep + swap(give, bits()[-1]).astype(F32)).astype(BF)

    band_grad, extra = in_vmem(payload_kernel, [((grid_cols, D), BF), ((grid_cols, GROUP), BF)],
                               "regional_payload", d_region, mixed, level_wide, weights[3],
                               after=(gives[0], moved_b))
    payload = share(jnp.concatenate([band_grad, extra], axis=1)).reshape(grid_rows, dp_size, cols, D + GROUP)
    payload = payload.transpose(1, 0, 2, 3).reshape(tokens, D + GROUP)
    grads = payload[:, :D]
    extra = payload[:, D:].astype(F32)
    part = lambda n: extra[:, n * HEADS : (n + 1) * HEADS]
    delta = (part(0) + part(1)).T
    level = (part(2) + part(3) + part(4)).T
    if one_kernel:
        wide = lambda x: x.reshape(4, -1)
        own_columns = lambda x: wide(lax.dynamic_slice_in_dim(x, dp_index * own_count, own_count, 1))
        matrices = ((2, D, D), BF)
        d_regions, keep_attn, give_attn, d_vec_reg = in_vmem(
            partial(regional_bwd_kernel, own_count),
            [((own_count, D), F32), matrices, matrices, ((5, 8, D), F32)],
            "regional_attention_backward", opt_index.reshape(1, 1),
            reg_q, reg_k, reg_v, grads, own_of(reg_q), own_of(reg_k), own_of(reg_v),
            own_of(canvas), ids[:, None], repeat(ids), own_ids[:, None], repeat(own_ids), wide(level), wide(delta),
            own_columns(level), own_columns(delta), own_of(grads), mixed, band_grad, d_attn, *weights, vec,
            after=tuple(gives[1:2]), scratch=[pltpu.VMEM((4, D, D), F32)])
    else:
        d_regions, grad_attn, d_vec_reg = regional_backward(
            reg_q, reg_k, reg_v, grads, own_of, own_of(canvas), ids[:, None] == own_ids[None, :], level, delta,
            weights, vec, mixed, band_grad, d_attn)
        pick = lambda j: lax.dynamic_index_in_dim(grad_attn, opt_index ^ j, 0, keepdims=False)
        keep_attn, give_attn = jnp.stack([pick(0), pick(2)]), jnp.stack([pick(1), pick(3)])
    d_regions = d_regions.reshape(regions.shape)

    near = pair(give_attn, 1).astype(F32) + keep_attn.astype(F32)
    piece_attn = near[0] + pair(near[1].astype(BF), 2).astype(F32)
    piece_attn = move(piece_attn.astype(BF).reshape(dp_size, D // dp_size, D))
    piece_attn = jnp.sum(piece_attn.astype(F32), axis=0).astype(BF)
    own_attn = share(piece_attn).reshape(D, D)
    own_mlp = piece_mlp
    for bit in reversed(bits()):
        own_mlp = doubling_step(own_mlp, bit)
    grams = in_vmem(grams_kernel, [((D, D), F32)] * 6, "mlp_grams", *moms, *pieces_of_owners(own_mlp))

    d_vec_attn = jnp.sum(d_vec_attn + d_vec_reg, axis=1)
    d_vec_mlp = jnp.sum(out_a[4] + out_b[4], axis=1)
    d_bias_first = jnp.take(jnp.sum(out_a[5] + out_b[5], axis=1), order, axis=0)
    grad_vec = jnp.concatenate([d_vec_attn[:2], d_vec_mlp[:2], d_vec_attn[2:], d_vec_mlp[2:], d_bias_first])
    grad_vec = grad_vec + pair(grad_vec, 1)
    grad_vec = grad_vec + pair(grad_vec, 2)
    grad_vec = sum_small_over_dp(grad_vec)

    squares = lambda x: jnp.sum(x.astype(F32) ** 2)
    total = jnp.full((8, 128), squares(piece_attn) + squares(piece_mlp))
    total = total + pair(total, 1)
    total = total + pair(total, 2)
    total = sum_small_over_dp(total)
    grad_norm = jnp.sqrt(total[0, 0] + squares(grad_vec))
    clip = jnp.minimum(1.0, CLIP_LIMIT / (grad_norm + 1e-06))
    attn_mom_new, new_attn, first_mom, new_first, second_mom, new_second = in_vmem(
        update_kernel, [((D, D), F32)] * 6, "matrix_updates", clip.reshape(1, 1), own_attn, attn_mom[0], attn_w[0],
        own_mlp, mlp_in_mom, mlp_out_mom, mlp_in, mlp_out, *grams)
    clipped = clip * grad_vec
    moment_one = BETA_FIRST * adam_first + (1.0 - BETA_FIRST) * clipped
    moment_two = BETA_SECOND * adam_second + (1.0 - BETA_SECOND) * clipped * clipped
    first_hat = moment_one / (1.0 - BETA_FIRST**OPT_STEP)
    second_hat = moment_two / (1.0 - BETA_SECOND**OPT_STEP)
    new_vec = vec_params - ADAM_RATE * first_hat / (jnp.sqrt(second_hat) + ADAM_EPS)
    return (out_patches, out_regions, d_patches, d_regions, new_attn[None], attn_mom_new[None], new_first, first_mom,
            new_second, second_mom, new_vec, moment_one, moment_two, grad_norm)


def solution(mesh):
    canvas = P("opt", None, "dp", None)
    wide = P("opt", None, "dp", None, None)
    bands = P("opt", "dp", None, None, None)
    square, right, down = P("opt", None, None), P(None, "opt"), P("opt", None)
    return jax.shard_map(
        per_device,
        mesh=mesh,
        in_specs=(bands, canvas, square, square, right, down, P(), wide, canvas, square, right, down, P(), P()),
        out_specs=(wide, canvas, bands, canvas, square, square, right, right, down, down, P(), P(), P(), P()),
        check_vma=False,
    )
```

```python
from functools import partial

import jax
import jax.numpy as jnp
from jax import lax
from jax.experimental import pallas as pl
from jax.experimental.pallas import tpu as pltpu
from jax.sharding import PartitionSpec as P

BF = jnp.bfloat16
F32 = jnp.float32

D = 512
HEADS = 16
HEAD_DIM = 32
FF = 2048
PATCH = 49
LIVE = 50
ROWS = 56
GROUP = 128
STACK = 4 * ROWS
OPT_STEP = 10
OPT = 4

SCALE = HEAD_DIM ** (-0.5)
NORM_EPS = 1e-05
MASKED = -1e30
NS_FIRST = 3.4445
NS_SECOND = -4.775
NS_THIRD = 2.0315
MUON_RATE = 0.5
MUON_MOMENTUM = 0.5
MUON_DECAY = 0.01
ADAM_RATE = 0.5
BETA_FIRST = 0.9
BETA_SECOND = 0.95
ADAM_EPS = 1e-08
CLIP_LIMIT = 1.0
DECAY_KEEP = 1.0 - MUON_RATE * MUON_DECAY
VMEM = 60 * 2**20


def cost(flops):
    return pl.CostEstimate(flops=int(flops), bytes_accessed=10**5, transcendentals=0)

ERF_P = 0.3275911 * 0.5**0.5
ERF = tuple(0.5 * c for c in (0.254829592, -0.284496736, 1.421413741, -1.453152027, 1.061405429))
INV_SQRT_2PI = 0.3989422804014327
LOG2E = 1.4426950408889634


def nn(a, b):
    return lax.dot_general(a, b, (((1,), (0,)), ((), ())), preferred_element_type=F32)


def nt(a, b):
    return lax.dot_general(a, b, (((1,), (1,)), ((), ())), preferred_element_type=F32)


def tn(a, b):
    return lax.dot_general(a, b, (((0,), (0,)), ((), ())), preferred_element_type=F32)


def full(shape):
    return pl.BlockSpec(shape, lambda i: (0,) * len(shape))


def block(shape):
    return pl.BlockSpec(shape, lambda i: (i,) + (0,) * (len(shape) - 1))


def norm_parts(x):
    centre = x - jnp.mean(x, axis=-1, keepdims=True)
    scale = lax.rsqrt(jnp.mean(centre * centre, axis=-1, keepdims=True) + NORM_EPS)
    return centre * scale, scale


def norm_back(grad, xhat, scale, gain):
    inner = grad * gain
    first = jnp.mean(inner, axis=-1, keepdims=True)
    second = jnp.mean(inner * xhat, axis=-1, keepdims=True)
    return scale * (inner - first - xhat * second)


def head_masks():
    lane = lax.broadcasted_iota(jnp.int32, (1, GROUP), 1) // HEAD_DIM
    return [lane == h for h in range(4)]


def spread(rows, masks):
    return jnp.concatenate([jnp.where(m, rows, 0.0) for m in masks], axis=0).astype(BF)


def collect(stacked, masks, rows):
    out = stacked[:rows]
    for h in range(1, 4):
        out = jnp.where(masks[h], stacked[h * rows : (h + 1) * rows], out)
    return out


def lane_groups(x):
    return [x[:, GROUP * g : GROUP * (g + 1)] for g in range(4)]


def hold(ref, total, x):
    for g, part in enumerate(lane_groups(x)):
        ref[g, :total] = part


def held_rows(ref, total):
    return jnp.concatenate([ref[g, :total] for g in range(4)], axis=1)


def fold(x):
    return jnp.sum(x.reshape(x.shape[0] // 8, 8, x.shape[1]), axis=0)


def gelu_parts(a):
    bell = jnp.exp2(a * a * (-0.5 * LOG2E))
    t = 1.0 / (1.0 + ERF_P * jnp.abs(a))
    tail = ((((ERF[4] * t + ERF[3]) * t + ERF[2]) * t + ERF[1]) * t + ERF[0]) * t * bell
    share = jnp.where(a < 0, tail, 1.0 - tail)
    return a * share, share + a * bell * INV_SQRT_2PI


def attn_fwd_kernel(count, batch, p_ref, r_ref, wq_ref, wk_ref, wv_ref, wo_ref, vec_ref,
                    x1_ref, q_ref, k_ref, v_ref, o_ref, pt_ref, q_held, k_held, v_held, o_held):
    total = count * LIVE

    @pl.when(pl.program_id(0) == 0)
    def _():
        for ref in (q_held, k_held, v_held):
            ref[:, total:] = jnp.zeros((4, count * (ROWS - LIVE), GROUP), F32)

    x = jnp.concatenate([p_ref[...].astype(F32), r_ref[...][None]], axis=0).reshape(total, D)
    vec = vec_ref[...]
    xhat, _ = norm_parts(x)
    xn = (xhat * vec[0:1] + vec[1:2]).astype(BF)
    hold(q_held, total, nn(xn, wq_ref[...]) + vec[4:5])
    hold(k_held, total, nn(xn, wk_ref[...]))
    hold(v_held, total, nn(xn, wv_ref[...]) + vec[5:6])
    masks = head_masks()
    live = lax.broadcasted_iota(jnp.int32, (ROWS, 1), 0) < LIVE

    def body(step, carry):
        units = [(step * batch + w, g) for w in range(batch) for g in range(4)]
        scores, probs = [], []
        for w, g in units:
            lanes = slice(GROUP * g, GROUP * (g + 1))
            rows = pl.ds(w, ROWS, stride=count)
            q = q_held[g, rows, :]
            q_ref[w, :, lanes] = q.astype(BF)
            k = k_held[g, rows, :].astype(BF)
            k_ref[w, :, lanes] = k
            scores.append(nt(k, spread(q, masks)))
        for (w, g), s in zip(units, scores):
            s = jnp.where(live, s, MASKED)
            e = jnp.exp((s - jnp.max(s, axis=0, keepdims=True)) * SCALE)
            p = (e * (1.0 / jnp.sum(e, axis=0, keepdims=True))).astype(BF)
            pt_ref[w, g] = p
            probs.append(p)
        for (w, g), p in zip(units, probs):
            lanes = slice(GROUP * g, GROUP * (g + 1))
            rows = pl.ds(w, ROWS, stride=count)
            v = v_held[g, rows, :].astype(BF)
            v_ref[w, :, lanes] = v
            o_held[g, rows, :] = collect(tn(p, v), masks, ROWS)
        return carry

    lax.fori_loop(0, count // batch, body, 0)
    mixed = held_rows(o_held, total).astype(BF)
    o_ref[...] = mixed.reshape(LIVE, count, D)
    x1_ref[...] = (x + nn(mixed, wo_ref[...]) + vec[6:7]).reshape(LIVE, count, D)


def middle(rows, count, skip=0):
    return pl.BlockSpec((rows, count, D), lambda i: (0, i + skip, 0))


def attn_fwd(patches, region_rows, weights, vec, count=16, batch=4):
    windows = patches.shape[1]
    array = jax.ShapeDtypeStruct
    return pl.pallas_call(
        partial(attn_fwd_kernel, count, batch),
        grid=(windows // count,),
        in_specs=[middle(PATCH, count), block((count, D))] + [full((D, D))] * 4 + [full(vec.shape)],
        out_specs=[middle(LIVE, count)] + [block((count, ROWS, D))] * 3
        + [middle(LIVE, count), block((count, 4, ROWS, STACK))],
        out_shape=[array((LIVE, windows, D), F32)] + [array((windows, ROWS, D), BF)] * 3
        + [array((LIVE, windows, D), BF), array((windows, 4, ROWS, STACK), BF)],
        scratch_shapes=[pltpu.VMEM((4, count * ROWS, GROUP), F32)] * 4,
        compiler_params=pltpu.CompilerParams(vmem_limit_bytes=VMEM),
        cost_estimate=cost(16e9),
        name="window_attention_forward",
    )(patches, region_rows, *weights, vec)


def mlp_kernel(many, sources, cols, steps, lanes, last, *refs):
    x1_ref, pc_ref, *w_refs, vec_ref, b1_ref = refs[:8]
    if last:
        prev_refs = refs[9:11]
        op_ref, dx1_ref, dwa_ref, dwb_ref, dv_ref, db1_ref, acc1, acc2 = refs[11:]
    else:
        prev_refs = ()
        early_ref, op_ref, dx1_ref, dwa_ref, dwb_ref, dv_ref, db1_ref, acc1, acc2 = refs[8:]
    total = many * sources * cols
    step = pl.program_id(0)

    @pl.when(step == 0)
    def _():
        for ref in (acc1, acc2, dv_ref, db1_ref):
            ref[...] = jnp.zeros_like(ref)

    vec = vec_ref[...]
    gain = vec[2:3]
    x1 = x1_ref[...].reshape(total, D)
    xhat, scale = norm_parts(x1)
    h = (xhat * gain + vec[3:4]).astype(BF)
    for s in range(sources):
        dx1_ref[:, s * cols : (s + 1) * cols] = pc_ref[s].astype(F32)
    dy = dx1_ref[...].reshape(total, D)
    dm = dy.astype(BF)
    ht = h.T
    dmt = dm.T
    y = x1 + vec[7:8]
    dh = jnp.zeros((total, D), F32)
    parts = [(j, slice(c, c + lanes)) for j in range(4) for c in range(0, D, lanes)]

    def activate(j, s):
        u, slope = gelu_parts(nn(h, w_refs[j][0, :, s]) + b1_ref[j : j + 1, s])
        da = slope * nt(dm, w_refs[j][1, s, :])
        db1_ref[j, :, s] += fold(da)
        return u.astype(BF), da.astype(BF)

    def apply(j, s, u, da):
        acc1[j, :, s] += nn(ht, da)
        acc2[j, :, s] += nn(dmt, u)
        return nn(u, w_refs[j][1, s, :]), nt(da, w_refs[j][0, :, s])

    held_pair = activate(*parts[0])
    for n in range(1, len(parts) + 1):
        later = activate(*parts[n]) if n < len(parts) else None
        up, down = apply(*parts[n - 1], *held_pair)
        y, dh = y + up, dh + down
        held_pair = later
    y = y.reshape(many, sources * cols, D)

    def put(ref):
        for s in range(sources):
            ref[s] = y[:, s * cols : (s + 1) * cols].astype(BF)

    if last:
        put(op_ref)
    else:
        pl.when(step < steps - 1)(lambda: put(early_ref))
        pl.when(step == steps - 1)(lambda: put(op_ref))
    dy = dx1_ref[...].reshape(total, D)
    dx1_ref[...] = (dy + norm_back(dh, xhat, scale, gain)).reshape(dx1_ref.shape)
    dv_ref[0] += fold(dh * xhat)
    dv_ref[1] += fold(dh)
    dv_ref[2] += fold(dy)

    @pl.when(step == steps - 1)
    def _():
        for refs_out, first in ((dwa_ref, 0), (dwb_ref, 1)):
            for n, acc in enumerate((acc1, acc2)):
                for m in range(2):
                    piece = acc[first + 2 * m]
                    for prev in prev_refs[first : first + 1]:
                        piece = piece + prev[2 * m + n].astype(F32)
                    refs_out[2 * m + n] = piece.astype(BF)


def mlp(x1, first_position, cot, weights, vec, bias_first, prev=(), many=10, lanes=256):
    sources, positions, cols, _ = cot.shape
    windows = sources * cols
    steps = positions // many
    skip = first_position // many
    some = lambda place: pl.BlockSpec((sources, many, cols, D), lambda i: (0, place(i), 0, 0))
    array = jax.ShapeDtypeStruct
    matrices = full((4, D, D))
    rows = lambda count: array((sources, count, cols, D), BF)
    late = (LIVE - positions if not prev else positions) + many
    outs = [some(lambda i: i + 1)] if prev else [some(lambda i: jnp.minimum(i, steps - 2)), some(lambda i: 0)]
    shapes = [rows(late)] if prev else [rows(positions - many), rows(late)]
    return pl.pallas_call(
        partial(mlp_kernel, many, sources, cols, steps, lanes, len(prev) > 0),
        grid=(steps,),
        in_specs=[pl.BlockSpec((many, windows, D), lambda i: (i + skip, 0, 0)), some(lambda i: i)]
        + [full((2, D, D))] * 4 + [full(vec.shape), full((4, D))]
        + ([pl.BlockSpec(memory_space=pl.ANY)] + [matrices] * 2 if prev else []),
        out_specs=outs + [block((many, windows, D)), matrices, matrices, full((3, 8, D)), full((4, 8, D))],
        out_shape=shapes + [array((positions, windows, D), F32), array((4, D, D), BF),
                            array((4, D, D), BF), array((3, 8, D), F32), array((4, 8, D), F32)],
        scratch_shapes=[pltpu.VMEM((4, D, D), F32), pltpu.VMEM((4, D, D), F32)],
        input_output_aliases={8: 0} if prev else {},
        compiler_params=pltpu.CompilerParams(vmem_limit_bytes=VMEM),
        cost_estimate=cost(4e9 * steps),
        name="mlp_forward_backward",
    )(x1, cot, *weights, vec, bias_first, *prev)


def attn_bwd_kernel(count, batch, chunks, more, *refs):
    p_ref, r_ref = refs[:2]
    refs = refs[:3] + refs[4:]
    dx1_refs = refs[3 : 3 + chunks]
    q_ref, k_ref, v_ref, o_ref, pt_ref, wq_ref, wk_ref, wv_ref, wo_ref, vec_ref = refs[3 + chunks : 13 + chunks]
    prev_refs = refs[13 + chunks : 17 + chunks] if more else ()
    dp_ref, dr_ref, dw_ref, dv_ref, dq_held, dk_held, dvv_held, do_held = refs[13 + chunks + len(prev_refs) :]
    total = count * LIVE

    @pl.when(pl.program_id(0) == 0)
    def _():
        dw_ref[...] = prev_refs[2][...] if more else jnp.zeros_like(dw_ref)
        dv_ref[...] = prev_refs[3][...] if more else jnp.zeros_like(dv_ref)
        do_held[:, total:] = jnp.zeros((4, count * (ROWS - LIVE), GROUP), F32)

    vec = vec_ref[...]
    gain = vec[0:1]
    dx1 = jnp.concatenate([ref[...] for ref in dx1_refs], axis=0).reshape(total, D)
    gb = dx1.astype(BF)
    hold(do_held, total, nt(gb, wo_ref[...]))
    masks = head_masks()

    def body(step, carry):
        units = [(step * batch + w, g) for w in range(batch) for g in range(4)]
        grads, scores = [], []
        for w, g in units:
            lanes = slice(GROUP * g, GROUP * (g + 1))
            rows = pl.ds(w, ROWS, stride=count)
            do_wide = spread(do_held[g, rows, :], masks)
            dvv_held[g, rows, :] = nn(pt_ref[w, g], do_wide)
            grads.append(nt(v_ref[w, :, lanes], do_wide))
        for (w, g), grad in zip(units, grads):
            p = pt_ref[w, g].astype(F32)
            both = p * grad
            scores.append((both - p * jnp.sum(both, axis=0, keepdims=True)).astype(BF))
        for (w, g), ds in zip(units, scores):
            lanes = slice(GROUP * g, GROUP * (g + 1))
            rows = pl.ds(w, ROWS, stride=count)
            dk_held[g, rows, :] = nn(ds, spread(q_ref[w, :, lanes].astype(F32), masks)) * SCALE
            dq_held[g, rows, :] = collect(tn(ds, k_ref[w, :, lanes]), masks, ROWS) * SCALE
        return carry

    lax.fori_loop(0, count // batch, body, 0)
    x = jnp.concatenate([p_ref[...].astype(F32), r_ref[...][None]], axis=0).reshape(total, D)
    xhat, scale = norm_parts(x)
    xn = (xhat * gain + vec[1:2]).astype(BF)
    dq_wide = held_rows(dq_held, total)
    dv_wide = held_rows(dvv_held, total)
    dq = dq_wide.astype(BF)
    dk = held_rows(dk_held, total).astype(BF)
    dv = dv_wide.astype(BF)
    dn = nt(dq, wq_ref[...]) + nt(dk, wk_ref[...]) + nt(dv, wv_ref[...])
    dx = (dx1 + norm_back(dn, xhat, scale, gain)).reshape(LIVE, count, D)
    dp_ref[...] = dx[:PATCH].astype(BF)
    dr_ref[...] = dx[PATCH]
    xt = xn.T
    dw_ref[0] += nn(xt, dq)
    dw_ref[1] += nn(xt, dk)
    dw_ref[2] += nn(xt, dv)
    dw_ref[3] += nn(o_ref[...].reshape(total, D).T, gb)
    dv_ref[0] += fold(dn * xhat)
    dv_ref[1] += fold(dn)
    dv_ref[2] += fold(dq_wide)
    dv_ref[3] += fold(dv_wide)
    dv_ref[4] += fold(dx1)


def attn_bwd(patches, region_rows, dx1_parts, saved, weights, vec, start, windows, after, prev=(), count=16, batch=4):
    skip = start // count
    array = jax.ShapeDtypeStruct
    sums = [full((4, D, D)), full((5, 8, D))]
    anywhere = pl.BlockSpec(memory_space=pl.ANY)
    rows = pl.BlockSpec((count, D), lambda i: (i + skip, 0))
    before = 14 + len(dx1_parts)
    return pl.pallas_call(
        partial(attn_bwd_kernel, count, batch, len(dx1_parts), len(prev) > 0),
        grid=(windows // count,),
        in_specs=[middle(PATCH, count, skip), rows, anywhere, anywhere]
        + [middle(part.shape[0], count, skip) for part in dx1_parts]
        + [pl.BlockSpec((count, ROWS, D), lambda i: (i + skip, 0, 0))] * 3
        + [middle(LIVE, count, skip), pl.BlockSpec((count, 4, ROWS, STACK), lambda i: (i + skip, 0, 0, 0))]
        + [full((D, D))] * 4 + [full(vec.shape)] + ([anywhere] * 2 + sums)[: len(prev)],
        out_specs=[middle(PATCH, count, skip), rows] + sums,
        out_shape=[array(patches.shape, BF), array(region_rows.shape, F32),
                   array((4, D, D), F32), array((5, 8, D), F32)],
        scratch_shapes=[pltpu.VMEM((4, count * ROWS, GROUP), F32)] * 4,
        input_output_aliases={before: 0, before + 1: 1} if prev else {},
        compiler_params=pltpu.CompilerParams(vmem_limit_bytes=VMEM),
        cost_estimate=cost(12e9),
        name="window_attention_backward",
    )(patches, region_rows, *after, *dx1_parts, *saved, *weights, vec, *prev)


def regional_fwd_kernel(canvas_ref, band_ref, ids_ref, band_ids_ref, wq_ref, wk_ref, wv_ref, wo_ref, vec_ref,
                        r1_ref, mixed_ref, level_ref, q_ref, k_ref, v_ref):
    vec = vec_ref[...]
    xhat, _ = norm_parts(canvas_ref[...].astype(F32))
    low = (xhat * vec[0:1] + vec[1:2]).astype(BF)
    q_ref[...] = (nn(low, wq_ref[...]) + vec[4:5]).astype(BF)
    k_ref[...] = nn(low, wk_ref[...]).astype(BF)
    v_ref[...] = (nn(low, wv_ref[...]) + vec[5:6]).astype(BF)
    band = band_ref[...].astype(F32)
    rows = band.shape[0]
    xhat, _ = norm_parts(band)
    q = nn((xhat * vec[0:1] + vec[1:2]).astype(BF), wq_ref[...]) + vec[4:5]
    masks = head_masks()
    same = ids_ref[...] == band_ids_ref[...]
    scores, probs = [], []
    for g in range(4):
        lanes = slice(GROUP * g, GROUP * (g + 1))
        scores.append(nt(k_ref[:, lanes], spread(q[:, lanes], masks)))
    for g, s in enumerate(scores):
        s = jnp.where(same, s, MASKED)
        peak = jnp.max(s, axis=0, keepdims=True)
        e = jnp.exp((s - peak) * SCALE)
        sums = jnp.sum(e, axis=0, keepdims=True)
        level_ref[g : g + 1] = peak * SCALE + jnp.log(sums)
        probs.append((e * (1.0 / sums)).astype(BF))
    for g, p in enumerate(probs):
        lanes = slice(GROUP * g, GROUP * (g + 1))
        mixed_ref[:, lanes] = collect(tn(p, v_ref[:, lanes]), masks, rows)
    r1_ref[...] = band + nn(mixed_ref[...].astype(BF), wo_ref[...]) + vec[6:7]


def in_vmem(kernel, outs, name, *args, after=(), scratch=(), flops=2e9):
    spaces = [pltpu.SMEM if arg.shape == (1, 1) else pltpu.VMEM for arg in args]
    count = len(args)
    return pl.pallas_call(
        lambda *refs: kernel(*refs[:count], *refs[count + len(after) :]),
        in_specs=[pl.BlockSpec(memory_space=space) for space in spaces]
        + [pl.BlockSpec(memory_space=pl.ANY) for _ in after],
        out_specs=[pl.BlockSpec(memory_space=pltpu.VMEM) for _ in outs],
        out_shape=[jax.ShapeDtypeStruct(*out) for out in outs],
        scratch_shapes=list(scratch),
        compiler_params=pltpu.CompilerParams(vmem_limit_bytes=VMEM),
        cost_estimate=cost(flops),
        name=name,
    )(*args, *after)


def payload_kernel(dr_ref, mixed_ref, level_ref, wo_ref, grad_ref, extra_ref):
    low = dr_ref[...].astype(BF)
    grad_ref[...] = low
    both = nt(low, wo_ref[...]).astype(BF).astype(F32) * mixed_ref[...]
    head = lax.broadcasted_iota(jnp.int32, (D, GROUP), 0) // HEAD_DIM
    lane = lax.broadcasted_iota(jnp.int32, (D, GROUP), 1)
    pick = ((head == lane) | (head + HEADS == lane)).astype(BF)
    high, low_part = halves(both)
    rest = (both - high.astype(F32) - low_part.astype(F32)).astype(BF)
    delta = nn(high, pick) + (nn(low_part, pick) + nn(rest, pick))
    top = delta.astype(BF).astype(F32)
    lane = lax.broadcasted_iota(jnp.int32, (1, GROUP), 1)
    level = level_ref[...]
    level_top = level.astype(BF).astype(F32)
    level_rest = level - level_top
    level_mid = level_rest.astype(BF).astype(F32)
    extra = level_rest - level_mid
    for place, term in ((4, level_mid), (3, level_top), (2, delta - top), (1, top)):
        extra = jnp.where(lane < place * HEADS, term, extra)
    extra_ref[...] = extra.astype(BF)


def regional_bwd_kernel(own_rows, owner_ref, q_ref, k_ref, v_ref, grads_ref, qo_ref, ko_ref, vo_ref, own_ref, ids_ref, ids_row_ref,
                        ids_own_ref, ids_own_row_ref, level_ref, delta_ref, level_own_ref, delta_own_ref,
                        grads_own_ref, mixed_ref, band_grad_ref, dw_ref, wq_ref, wk_ref, wv_ref, wo_ref, vec_ref,
                        dr_ref, keep_ref, give_ref, gv_ref, sum_held):
    vec = vec_ref[...]
    masks = head_masks()
    do = nt(grads_ref[...], wo_ref[...]).astype(BF).astype(F32)
    do_own = nt(grads_own_ref[...], wo_ref[...]).astype(BF).astype(F32)
    same_own = ids_ref[...] == ids_own_row_ref[...]
    same = ids_own_ref[...] == ids_row_ref[...]
    lanes = [slice(GROUP * g, GROUP * (g + 1)) for g in range(4)]
    first, second = [], []
    dqs, dks, dvs = [], [], []
    for g in range(4):
        q_wide = spread(qo_ref[:, lanes[g]].astype(F32), masks)
        do_wide = spread(do_own[:, lanes[g]], masks)
        first.append((nt(k_ref[:, lanes[g]], q_wide), nt(v_ref[:, lanes[g]], do_wide)))
        q_wide = spread(q_ref[:, lanes[g]].astype(F32), masks)
        do_wide = spread(do[:, lanes[g]], masks)
        second.append((nt(ko_ref[:, lanes[g]], q_wide), nt(vo_ref[:, lanes[g]], do_wide), q_wide, do_wide))
    for g in range(4):
        s, dp = first[g]
        p = jnp.where(same_own, jnp.exp(s * SCALE - level_own_ref[g : g + 1]), 0.0)
        ds = (p * (dp - delta_own_ref[g : g + 1])).astype(BF)
        dqs.append(collect(tn(ds, k_ref[:, lanes[g]]), masks, own_rows) * SCALE)
        s, dp, q_wide, do_wide = second[g]
        p = jnp.where(same, jnp.exp(s * SCALE - level_ref[g : g + 1]), 0.0)
        ds = (p * (dp - delta_ref[g : g + 1])).astype(BF)
        dvs.append(nn(p.astype(BF), do_wide))
        dks.append(nn(ds, q_wide) * SCALE)
    xhat, scale = norm_parts(own_ref[...].astype(F32))
    low = (xhat * vec[0:1] + vec[1:2]).astype(BF)
    dq_wide, dk_wide, dv_wide = (jnp.concatenate(x, axis=1) for x in (dqs, dks, dvs))
    dq, dk, dv = dq_wide.astype(BF), dk_wide.astype(BF), dv_wide.astype(BF)
    dn = nt(dq, wq_ref[...]) + nt(dk, wk_ref[...]) + nt(dv, wv_ref[...])
    dr_ref[...] = grads_own_ref[...].astype(F32) + norm_back(dn, xhat, scale, vec[0:1])
    sum_held[0] = dw_ref[0] + tn(low, dq)
    sum_held[1] = dw_ref[1] + tn(low, dk)
    sum_held[2] = dw_ref[2] + tn(low, dv)
    sum_held[3] = dw_ref[3] + tn(mixed_ref[...].astype(BF), band_grad_ref[...])
    owner = owner_ref[0, 0]
    for n in range(2):
        keep_ref[n] = sum_held[owner ^ (2 * n)].astype(BF)
        give_ref[n] = sum_held[owner ^ (2 * n + 1)].astype(BF)
    gv_ref[0] = fold(dn * xhat)
    gv_ref[1] = fold(dn)
    gv_ref[2] = fold(dq_wide)
    gv_ref[3] = fold(dv_wide)
    gv_ref[4] = fold(band_grad_ref[...].astype(F32))


def halves(a):
    high = a.astype(BF)
    return high, (a - high.astype(F32)).astype(BF)


def terms(a, passes):
    return (a.astype(BF),) if passes == 1 else halves(a)


def product(a, b, dot=nn):
    if len(a) == 1:
        return dot(a[0], b[0])
    return dot(a[0], b[0]) + (dot(a[0], b[1]) + dot(a[1], b[0]))


def symmetric(a, b, dot=nn):
    half = D // 2
    right = (lambda x: x[half:]) if dot is nt else (lambda x: x[:, half:])
    top = product([x[:half] for x in a], b, dot)
    corner = product([x[half:] for x in a], [right(x) for x in b], dot)
    return jnp.concatenate([top, jnp.concatenate([top[:, half:].T, corner], axis=1)], axis=0)


DIRECT_STEPS = (1, 1, 1, -1, -1)
GRAM_STEPS = (1, 1, 3, 3, 3)
NEAR_ZERO = NS_FIRST + NS_SECOND + NS_THIRD
NEAR_ONE = NS_SECOND + 2.0 * NS_THIRD


def identity():
    rows = lax.broadcasted_iota(jnp.int32, (D, D), 0)
    return rows == lax.broadcasted_iota(jnp.int32, (D, D), 1)


def polynomial(gram, eye, step):
    if step > 0:
        parts = terms(gram, step)
        return NS_FIRST, NS_SECOND * gram + NS_THIRD * symmetric(parts, parts)
    rest = gram - jnp.where(eye, 1.0, 0.0)
    parts = terms(rest, -step)
    return NEAR_ZERO, NEAR_ONE * rest + NS_THIRD * symmetric(parts, parts)


def direct_steps(moment, eye):
    z = moment * (1.0 / (jnp.sqrt(jnp.sum(moment * moment)) + 1e-07))
    for step in DIRECT_STEPS:
        parts = terms(z, abs(step))
        gram = symmetric(parts, parts, nt)
        yield
        scale, poly = polynomial(gram, eye, step)
        yield
        z = scale * z + product(terms(poly, abs(step)), parts)
        yield
    return z


def gram_steps(gram, eye):
    factor = 1.0 / (jnp.sqrt(jnp.sum(jnp.where(eye, gram, 0.0))) + 1e-07)
    gram = gram * (factor * factor)
    steps = None
    for n, passes in enumerate(GRAM_STEPS):
        scale, poly = polynomial(gram, eye, passes)
        yield
        parts = terms(poly, passes)
        if steps is None:
            steps = jnp.where(eye, scale, 0.0) + poly
        else:
            steps = scale * steps + symmetric(parts, terms(steps, passes))
            yield
        if n < len(GRAM_STEPS) - 1:
            half = scale * gram + symmetric(parts, terms(gram, passes))
            yield
            gram = scale * half + symmetric(parts, terms(half, passes))
            yield
    return steps * factor


def in_turns(*chains):
    results = [None] * len(chains)
    running = list(enumerate(chains))
    while running:
        still = []
        for n, chain in running:
            try:
                next(chain)
                still.append((n, chain))
            except StopIteration as stop:
                results[n] = stop.value
        running = still
    return results


def old_grams_kernel(moms_ref, *out_refs):
    for n, out_ref in enumerate(out_refs):
        square, cross = jnp.zeros((D, D), F32), jnp.zeros((D, D), F32)
        for j in range(OPT):
            high, low = halves(moms_ref[j, n])
            if n == 1:
                high, low = high.T, low.T
            square = square + nt(high, high)
            cross = cross + nt(high, low)
        out_ref[...] = square + (cross + cross.T)


def grams_kernel(places, owner_ref, moms_ref, all_ref, mixed1_ref, new1_ref, mixed2_ref, new2_ref, own_ref):
    half = len(places) // 2
    for n, (mixed_ref, new_ref) in enumerate(((mixed1_ref, new1_ref), (mixed2_ref, new2_ref))):
        mixed, new = jnp.zeros((D, D), F32), jnp.zeros((D, D), F32)
        mine = places[n * half : (n + 1) * half]
        for j in range(OPT):
            high, low = halves(moms_ref[j, n])
            if n == 1:
                high, low = high.T, low.T
            g = jnp.concatenate([all_ref[d, j] for d in mine], axis=0)
            mixed = mixed + (nt(high, g) + nt(low, g))
            new = new + nt(g, g)
        mixed_ref[...] = mixed + mixed.T
        new_ref[...] = new
        own_ref[n] = jnp.concatenate([all_ref[d, owner_ref[0, 0]] for d in mine], axis=0)


def update_kernel(clip_ref, ga_ref, ma_ref, wa_ref, g_ref, m1_ref, m2_ref, w1_ref, w2_ref,
                  old1, mixed1, new1, old2, mixed2, new2, na_ref, newa_ref, n1_ref, new1_ref, n2_ref, new2_ref):
    clip = clip_ref[0, 0]
    eye = identity()
    na_ref[...] = MUON_MOMENTUM * ma_ref[...] + clip * ga_ref[...].astype(F32)
    n1_ref[...] = MUON_MOMENTUM * m1_ref[...] + clip * g_ref[0].astype(F32)
    n2_ref[...] = MUON_MOMENTUM * m2_ref[...] + clip * g_ref[1].astype(F32).T
    a, b, c = MUON_MOMENTUM * MUON_MOMENTUM, MUON_MOMENTUM * clip, clip * clip
    gram1 = a * old1[...] + b * mixed1[...] + c * new1[...]
    gram2 = a * old2[...] + b * mixed2[...] + c * new2[...]
    steps1, steps2, z = in_turns(gram_steps(gram1, eye), gram_steps(gram2, eye), direct_steps(na_ref[...], eye))
    newa_ref[...] = wa_ref[...] * DECAY_KEEP - MUON_RATE * z
    z = product(halves(steps1), halves(n1_ref[...]))
    new1_ref[...] = w1_ref[...] * DECAY_KEEP - MUON_RATE * z
    z = product(halves(n2_ref[...]), halves(steps2))
    new2_ref[...] = w2_ref[...] * DECAY_KEEP - (MUON_RATE * max(1.0, FF / D) ** 0.5) * z


def pair(values, bit):
    return lax.ppermute(values, "opt", [(i, i ^ bit) for i in range(OPT)])


def fence(x, *first):
    here = pl.BlockSpec(memory_space=pl.ANY)
    return pl.pallas_call(
        lambda *refs: None,
        in_specs=[here] * (1 + len(first)),
        out_specs=here,
        out_shape=jax.ShapeDtypeStruct(x.shape, x.dtype),
        input_output_aliases={0: 0},
        cost_estimate=cost(1e3),
        name="fence",
    )(x, *first)


def pieces_of_owners(own):
    mate = pair(own, 1)
    across = pair(own, 2)
    return [own, mate, across, pair(across, 1)]


def share(x):
    copies = jnp.broadcast_to(x[None], (lax.axis_size("dp"),) + x.shape)
    return lax.all_to_all(copies, "dp", 0, 0, tiled=True)


def swap(x, bit):
    return lax.ppermute(x, "dp", [(i, i ^ bit) for i in range(lax.axis_size("dp"))])


def bits():
    return [1 << n for n in range(lax.axis_size("dp").bit_length() - 1)]


def halving_step(x, bit):
    half = x.shape[0] // 2
    side = (lax.axis_index("dp") // bit) % 2
    give = lax.dynamic_slice_in_dim(x, (1 - side) * half, half, 0).astype(BF)
    return lax.dynamic_slice_in_dim(x, side * half, half, 0), give


def order_of_halves(count):
    width = count.bit_length() - 1
    return [int(format(n, "b").zfill(width)[::-1], 2) if width else 0 for n in range(count)]


def sum_small_over_dp(x):
    for bit in bits():
        x = x + swap(x, bit)
    return x


def split_heads(x):
    return x.reshape(x.shape[0], HEADS, HEAD_DIM)


def regional_forward(canvas, band, same, weights, vec):
    low = lambda x: (norm_parts(x.astype(F32))[0] * vec[0] + vec[1]).astype(BF)
    normed = low(canvas)
    queries = (nn(normed, weights[0]) + vec[4]).astype(BF)
    keys = nn(normed, weights[1]).astype(BF)
    values = (nn(normed, weights[2]) + vec[5]).astype(BF)
    own = (nn(low(band), weights[0]) + vec[4]).astype(BF)
    scores = jnp.einsum("qhd,khd->hqk", split_heads(own), split_heads(keys), preferred_element_type=F32)
    scores = jnp.where(same[None], scores * SCALE, MASKED)
    peak = jnp.max(scores, axis=-1, keepdims=True)
    raised = jnp.exp(scores - peak)
    sums = jnp.sum(raised, axis=-1, keepdims=True)
    probs = (raised / sums).astype(BF)
    mixed = jnp.einsum("hqk,khd->qhd", probs, split_heads(values), preferred_element_type=F32).reshape(own.shape)
    region_rows = band.astype(F32) + nn(mixed.astype(BF), weights[3]) + vec[6]
    return region_rows, mixed, (peak + jnp.log(sums))[:, :, 0], queries, keys, values


def regional_terms(queries, keys, values, grad_mixed, same, level, delta):
    scores = jnp.einsum("qhd,khd->hqk", split_heads(queries), split_heads(keys), preferred_element_type=F32)
    probs = jnp.where(same[None], jnp.exp(scores * SCALE - level[:, :, None]), 0.0)
    grads = jnp.einsum("qhd,khd->hqk", split_heads(grad_mixed), split_heads(values), preferred_element_type=F32)
    return probs.astype(BF), (probs * (grads - delta[:, :, None])).astype(BF)


def regional_backward(queries, keys, values, grads, own, rows, same, level, delta, weights, vec, mixed, band_grad, dw):
    grad_mixed = nt(grads, weights[3]).astype(BF)
    level_own, delta_own = own(level.T).T, own(delta.T).T
    _, scores = regional_terms(own(queries), keys, values, own(grad_mixed), same.T, level_own, delta_own)
    dq = jnp.einsum("hqk,khd->qhd", scores, split_heads(keys), preferred_element_type=F32)
    probs, scores = regional_terms(queries, own(keys), own(values), grad_mixed, same, level, delta)
    dk = jnp.einsum("hqk,qhd->khd", scores, split_heads(queries), preferred_element_type=F32)
    dv = jnp.einsum("hqk,qhd->khd", probs, split_heads(grad_mixed), preferred_element_type=F32)
    flat = lambda x: x.reshape(-1, D)
    dq, dk, dv = flat(dq) * SCALE, flat(dk) * SCALE, flat(dv)
    lows = [x.astype(BF) for x in (dq, dk, dv)]
    dn = sum(nt(x, w) for x, w in zip(lows, weights))
    xhat, scale = norm_parts(rows.astype(F32))
    low = (xhat * vec[0] + vec[1]).astype(BF)
    d_regions = own(grads).astype(F32) + norm_back(dn, xhat, scale, vec[0])
    matrices = [dw[j] + tn(low, x) for j, x in enumerate(lows)] + [dw[3] + tn(mixed.astype(BF), band_grad)]
    vectors = [fold(x) for x in (dn * xhat, dn, dq, dv, band_grad.astype(F32))]
    return d_regions, jnp.stack(matrices).astype(BF), jnp.stack(vectors)


def per_device(patches, regions, image_ids, attn_w, mlp_in, mlp_out, vec_params, patch_cot, region_cot,
               attn_mom, mlp_in_mom, mlp_out_mom, adam_first, adam_second):
    dp_size = lax.axis_size("dp")
    dp_index = lax.axis_index("dp")
    opt_index = lax.axis_index("opt")
    _, grid_rows, cols, _, _ = patch_cot.shape
    grid_cols = patches.shape[2]
    tokens = grid_rows * grid_cols
    own_count = grid_rows * cols
    one_kernel = tokens <= 1024
    vec = vec_params
    order = opt_index ^ jnp.arange(OPT)
    move = lambda x: lax.all_to_all(x, "dp", 0, 0, tiled=True)

    attn_pieces = jnp.stack(pieces_of_owners(attn_w[0].astype(BF)))
    mlp_w = pieces_of_owners(jnp.stack([mlp_in, mlp_out]).astype(BF))
    weights = [lax.dynamic_index_in_dim(attn_pieces, opt_index ^ j, 0, keepdims=False) for j in range(OPT)]
    canvas_blocks = share(regions[0])
    canvas = canvas_blocks.reshape(tokens, D)
    by_position = patch_cot[0].transpose(0, 2, 1, 3)
    split = 30
    last = jnp.concatenate([by_position[:, split:], region_cot[0][:, None]], axis=1)
    first_cot = move(fence(by_position[:, :split], canvas))
    bias_first = jnp.take(vec[8:], order, axis=0)

    band_of = lambda x: lax.dynamic_slice_in_dim(x, dp_index, 1, 1).reshape((grid_cols,) + x.shape[3:])
    own_of = lambda x: lax.dynamic_slice_in_dim(x, dp_index * own_count, own_count, 0)
    ids_blocks = image_ids[0].reshape(grid_rows, dp_size, cols).transpose(1, 0, 2)
    ids = ids_blocks.reshape(tokens)
    band_ids, own_ids = band_of(ids_blocks), own_of(ids)
    band = band_of(canvas_blocks)
    if one_kernel:
        repeat = lambda x: jnp.tile(x, 4)[None]
        region_rows, mixed, level, reg_q, reg_k, reg_v = in_vmem(
            regional_fwd_kernel,
            [((grid_cols, D), F32), ((grid_cols, D), F32), ((4, 4 * grid_cols), F32)] + [((tokens, D), BF)] * 3,
            "regional_attention_forward", canvas, band, ids[:, None], repeat(band_ids), *weights, vec,
            after=(mlp_w[2],))
        level = level.reshape(HEADS, grid_cols)
    else:
        region_rows, mixed, level, reg_q, reg_k, reg_v = regional_forward(
            canvas, band, band_ids[:, None] == ids[None, :], weights, vec)
    level_wide = jnp.tile(level.T, (1, GROUP // HEADS))

    windows = patches[0, 0].transpose(1, 0, 2)
    some = grid_cols // 2
    x1, *saved = attn_fwd(windows, region_rows, weights, vec)
    last_cot = move(fence(last, x1))
    early_out, late_out, dx1_a, *grads_a = mlp(x1, 0, first_cot, mlp_w, vec, bias_first)
    moved_a = move(early_out)
    moms = lax.all_gather(fence(jnp.stack([mlp_in_mom, mlp_out_mom]), x1), "opt", axis=0)
    late_out, dx1_b, *grads_b = mlp(x1, split, last_cot, mlp_w, vec, bias_first, prev=(late_out, *grads_a[:2]))
    near = pair(fence(grads_b[1], moved_a), 1)
    far = (near[2:].astype(F32) + grads_b[0][2:].astype(F32)).astype(BF)
    moved_b = move(fence(late_out, far))
    out_patches = jnp.concatenate([moved_a, moved_b[:, :-1]], axis=1).transpose(0, 2, 1, 3)[None]
    out_regions = moved_b[None, :, -1]

    dx1 = (dx1_a, dx1_b)
    early = attn_bwd(windows, region_rows, dx1, saved, weights, vec, 0, some, (far, far))
    own_mlp = near[:2].astype(F32) + grads_b[0][:2].astype(F32) + fence(pair(far, 2), early[3]).astype(F32)
    keep, give = halving_step(own_mlp.reshape(2 * D, D), 1)
    d_patches, d_region, d_attn, d_vec_attn = attn_bwd(
        windows, region_rows, dx1, saved, weights, vec, some, some, (give, moms), prev=early)
    d_patches = d_patches.transpose(1, 0, 2)[None, None]
    gives, owner = [], opt_index.reshape(1, 1)
    old_grams = in_vmem(old_grams_kernel, [((D, D), F32)] * 2, "momentum_grams", moms, after=(d_vec_attn,),
                         flops=4e9)

    band_grad, extra = in_vmem(payload_kernel, [((grid_cols, D), BF), ((grid_cols, GROUP), BF)],
                               "regional_payload", d_region, mixed, level_wide, weights[3],
                               after=(give, moved_b))
    taken = fence(swap(give, 1), band_grad)
    for bit in bits()[1:]:
        keep, give = halving_step(keep + taken.astype(F32), bit)
        gives.append(give)
        taken = swap(give, bit)
    payload = share(jnp.concatenate([band_grad, extra], axis=1)).reshape(grid_rows, dp_size, cols, D + GROUP)
    payload = payload.transpose(1, 0, 2, 3).reshape(tokens, D + GROUP)
    grads = payload[:, :D]
    extra = payload[:, D:].astype(F32)
    part = lambda n: extra[:, n * HEADS : (n + 1) * HEADS]
    delta = (part(0) + part(1)).T
    level = (part(2) + part(3) + part(4)).T
    if one_kernel:
        wide = lambda x: x.reshape(4, -1)
        own_columns = lambda x: wide(lax.dynamic_slice_in_dim(x, dp_index * own_count, own_count, 1))
        matrices = ((2, D, D), BF)
        d_regions, keep_attn, give_attn, d_vec_reg = in_vmem(
            partial(regional_bwd_kernel, own_count),
            [((own_count, D), F32), matrices, matrices, ((5, 8, D), F32)],
            "regional_attention_backward", owner,
            reg_q, reg_k, reg_v, grads, own_of(reg_q), own_of(reg_k), own_of(reg_v),
            own_of(canvas), ids[:, None], repeat(ids), own_ids[:, None], repeat(own_ids), wide(level), wide(delta),
            own_columns(level), own_columns(delta), own_of(grads), mixed, band_grad, d_attn, *weights, vec,
            after=tuple(gives[-1:]) + tuple(old_grams), scratch=[pltpu.VMEM((4, D, D), F32)], flops=4e9)
    else:
        d_regions, grad_attn, d_vec_reg = regional_backward(
            reg_q, reg_k, reg_v, grads, own_of, own_of(canvas), ids[:, None] == own_ids[None, :], level, delta,
            weights, vec, mixed, band_grad, d_attn)
        pick = lambda j: lax.dynamic_index_in_dim(grad_attn, opt_index ^ j, 0, keepdims=False)
        keep_attn, give_attn = jnp.stack([pick(0), pick(2)]), jnp.stack([pick(1), pick(3)])
    d_regions = d_regions.reshape(regions.shape)

    piece_mlp = (keep + fence(taken, give_attn).astype(F32)).astype(BF)

    near = pair(give_attn, 1)
    far = (near[1].astype(F32) + keep_attn[1].astype(F32)).astype(BF)
    piece_attn = near[0].astype(F32) + keep_attn[0].astype(F32) + pair(far, 2).astype(F32)
    piece_attn = move(piece_attn.astype(BF).reshape(dp_size, D // dp_size, D))
    piece_attn = jnp.sum(piece_attn.astype(F32), axis=0).astype(BF)
    own_attn = share(piece_attn).reshape(D, D)
    all_mlp = lax.all_gather(piece_mlp, ("dp", "opt"), axis=0).reshape(dp_size, OPT, -1, D)
    *grams, own_mlp = in_vmem(partial(grams_kernel, order_of_halves(dp_size)),
                              [((D, D), F32)] * 4 + [((2, D, D), BF)], "mlp_grams", owner, moms, all_mlp, flops=4e9)
    grams = [old_grams[0], *grams[:2], old_grams[1], *grams[2:]]

    d_vec_attn = jnp.sum(d_vec_attn + d_vec_reg, axis=1)
    d_vec_mlp = jnp.sum(grads_a[2] + grads_b[2], axis=1)
    d_bias_first = jnp.take(jnp.sum(grads_a[3] + grads_b[3], axis=1), order, axis=0)
    grad_vec = jnp.concatenate([d_vec_attn[:2], d_vec_mlp[:2], d_vec_attn[2:], d_vec_mlp[2:], d_bias_first])
    grad_vec = grad_vec + pair(grad_vec, 1)
    grad_vec = grad_vec + pair(grad_vec, 2)
    grad_vec = sum_small_over_dp(grad_vec)

    squares = lambda x: jnp.sum(x.astype(F32) ** 2)
    total = jnp.full((8, 128), squares(piece_attn) + squares(piece_mlp))
    total = total + pair(total, 1)
    total = total + pair(total, 2)
    total = sum_small_over_dp(total)
    grad_norm = jnp.sqrt(total[0, 0] + squares(grad_vec))
    clip = jnp.minimum(1.0, CLIP_LIMIT / (grad_norm + 1e-06))
    attn_mom_new, new_attn, first_mom, new_first, second_mom, new_second = in_vmem(
        update_kernel, [((D, D), F32)] * 6, "matrix_updates", clip.reshape(1, 1), own_attn, attn_mom[0], attn_w[0],
        own_mlp, mlp_in_mom, mlp_out_mom, mlp_in, mlp_out, *grams, flops=12e9)
    clipped = clip * grad_vec
    moment_one = BETA_FIRST * adam_first + (1.0 - BETA_FIRST) * clipped
    moment_two = BETA_SECOND * adam_second + (1.0 - BETA_SECOND) * clipped * clipped
    first_hat = moment_one / (1.0 - BETA_FIRST**OPT_STEP)
    second_hat = moment_two / (1.0 - BETA_SECOND**OPT_STEP)
    new_vec = vec_params - ADAM_RATE * first_hat / (jnp.sqrt(second_hat) + ADAM_EPS)
    return (out_patches, out_regions, d_patches, d_regions, new_attn[None], attn_mom_new[None], new_first, first_mom,
            new_second, second_mom, new_vec, moment_one, moment_two, grad_norm)


def solution(mesh):
    canvas = P("opt", None, "dp", None)
    wide = P("opt", None, "dp", None, None)
    bands = P("opt", "dp", None, None, None)
    square, right, down = P("opt", None, None), P(None, "opt"), P("opt", None)
    return jax.shard_map(
        per_device,
        mesh=mesh,
        in_specs=(bands, canvas, square, square, right, down, P(), wide, canvas, square, right, down, P(), P()),
        out_specs=(wide, canvas, bands, canvas, square, square, right, right, down, down, P(), P(), P(), P()),
        check_vma=False,
    )
```

```python
from functools import partial

import jax
import jax.numpy as jnp
from jax import lax
from jax.experimental import pallas as pl
from jax.experimental.pallas import tpu as pltpu
from jax.sharding import PartitionSpec as P

BF = jnp.bfloat16
F32 = jnp.float32

D = 512
HEADS = 16
HEAD_DIM = 32
FF = 2048
PATCH = 49
LIVE = 50
ROWS = 56
GROUP = 128
STACK = 4 * ROWS
OPT_STEP = 10
OPT = 4

SCALE = HEAD_DIM ** (-0.5)
NORM_EPS = 1e-05
MASKED = -1e30
NS_FIRST = 3.4445
NS_SECOND = -4.775
NS_THIRD = 2.0315
MUON_RATE = 0.5
MUON_MOMENTUM = 0.5
MUON_DECAY = 0.01
ADAM_RATE = 0.5
BETA_FIRST = 0.9
BETA_SECOND = 0.95
ADAM_EPS = 1e-08
CLIP_LIMIT = 1.0
DECAY_KEEP = 1.0 - MUON_RATE * MUON_DECAY
VMEM = 60 * 2**20


def cost(flops):
    return pl.CostEstimate(flops=int(flops), bytes_accessed=10**5, transcendentals=0)

ERF_P = 0.3275911 * 0.5**0.5
ERF = tuple(0.5 * c for c in (0.254829592, -0.284496736, 1.421413741, -1.453152027, 1.061405429))
INV_SQRT_2PI = 0.3989422804014327
LOG2E = 1.4426950408889634


def nn(a, b):
    return lax.dot_general(a, b, (((1,), (0,)), ((), ())), preferred_element_type=F32)


def nt(a, b):
    return lax.dot_general(a, b, (((1,), (1,)), ((), ())), preferred_element_type=F32)


def tn(a, b):
    return lax.dot_general(a, b, (((0,), (0,)), ((), ())), preferred_element_type=F32)


def full(shape):
    return pl.BlockSpec(shape, lambda i: (0,) * len(shape))


def block(shape):
    return pl.BlockSpec(shape, lambda i: (i,) + (0,) * (len(shape) - 1))


def norm_parts(x):
    centre = x - jnp.mean(x, axis=-1, keepdims=True)
    scale = lax.rsqrt(jnp.mean(centre * centre, axis=-1, keepdims=True) + NORM_EPS)
    return centre * scale, scale


def norm_back(grad, xhat, scale, gain):
    inner = grad * gain
    first = jnp.mean(inner, axis=-1, keepdims=True)
    second = jnp.mean(inner * xhat, axis=-1, keepdims=True)
    return scale * (inner - first - xhat * second)


def head_masks():
    lane = lax.broadcasted_iota(jnp.int32, (1, GROUP), 1) // HEAD_DIM
    return [lane == h for h in range(4)]


def spread(rows, masks):
    return jnp.concatenate([jnp.where(m, rows, 0.0) for m in masks], axis=0).astype(BF)


def collect(stacked, masks, rows):
    out = stacked[:rows]
    for h in range(1, 4):
        out = jnp.where(masks[h], stacked[h * rows : (h + 1) * rows], out)
    return out


def lane_groups(x):
    return [x[:, GROUP * g : GROUP * (g + 1)] for g in range(4)]


def hold(ref, total, x):
    for g, part in enumerate(lane_groups(x)):
        ref[g, :total] = part


def held_rows(ref, total):
    return jnp.concatenate([ref[g, :total] for g in range(4)], axis=1)


def fold(x):
    return jnp.sum(x.reshape(x.shape[0] // 8, 8, x.shape[1]), axis=0)


def gelu_parts(a):
    bell = jnp.exp2(a * a * (-0.5 * LOG2E))
    t = 1.0 / (1.0 + ERF_P * jnp.abs(a))
    tail = ((((ERF[4] * t + ERF[3]) * t + ERF[2]) * t + ERF[1]) * t + ERF[0]) * t * bell
    share = jnp.where(a < 0, tail, 1.0 - tail)
    return a * share, share + a * bell * INV_SQRT_2PI


def attn_fwd_kernel(count, batch, owner_ref, p_ref, r_ref, w_ref, vec_ref, _,
                    x1_ref, q_ref, k_ref, v_ref, o_ref, pt_ref, q_held, k_held, v_held, o_held):
    total = count * LIVE
    owner = owner_ref[0, 0]

    @pl.when(pl.program_id(0) == 0)
    def _():
        for ref in (q_held, k_held, v_held):
            ref[:, total:] = jnp.zeros((4, count * (ROWS - LIVE), GROUP), F32)

    x = jnp.concatenate([p_ref[...].astype(F32), r_ref[...][None]], axis=0).reshape(total, D)
    vec = vec_ref[...]
    xhat, _ = norm_parts(x)
    xn = (xhat * vec[0:1] + vec[1:2]).astype(BF)
    hold(q_held, total, nn(xn, w_ref[owner ^ 0]) + vec[4:5])
    hold(k_held, total, nn(xn, w_ref[owner ^ 1]))
    hold(v_held, total, nn(xn, w_ref[owner ^ 2]) + vec[5:6])
    masks = head_masks()
    live = lax.broadcasted_iota(jnp.int32, (ROWS, 1), 0) < LIVE

    def body(step, carry):
        units = [(step * batch + w, g) for w in range(batch) for g in range(4)]
        scores, probs = [], []
        for w, g in units:
            lanes = slice(GROUP * g, GROUP * (g + 1))
            rows = pl.ds(w, ROWS, stride=count)
            q = q_held[g, rows, :]
            q_ref[w, :, lanes] = q.astype(BF)
            k = k_held[g, rows, :].astype(BF)
            k_ref[w, :, lanes] = k
            scores.append(nt(k, spread(q, masks)))
        for (w, g), s in zip(units, scores):
            s = jnp.where(live, s, MASKED)
            e = jnp.exp((s - jnp.max(s, axis=0, keepdims=True)) * SCALE)
            p = (e * (1.0 / jnp.sum(e, axis=0, keepdims=True))).astype(BF)
            pt_ref[w, g] = p
            probs.append(p)
        for (w, g), p in zip(units, probs):
            lanes = slice(GROUP * g, GROUP * (g + 1))
            rows = pl.ds(w, ROWS, stride=count)
            v = v_held[g, rows, :].astype(BF)
            v_ref[w, :, lanes] = v
            o_held[g, rows, :] = collect(tn(p, v), masks, ROWS)
        return carry

    lax.fori_loop(0, count // batch, body, 0)
    mixed = held_rows(o_held, total).astype(BF)
    o_ref[...] = mixed.reshape(LIVE, count, D)
    x1_ref[...] = (x + nn(mixed, w_ref[owner ^ 3]) + vec[6:7]).reshape(LIVE, count, D)


def middle(rows, count, skip=0):
    return pl.BlockSpec((rows, count, D), lambda i: (0, i + skip, 0))


def attn_fwd(owner, patches, region_rows, weights, vec, after, count=16, batch=8):
    windows = patches.shape[1]
    array = jax.ShapeDtypeStruct
    return pl.pallas_call(
        partial(attn_fwd_kernel, count, batch),
        grid=(windows // count,),
        in_specs=[pl.BlockSpec(memory_space=pltpu.SMEM), middle(PATCH, count), block((count, D)), full((4, D, D)),
                  full(vec.shape), pl.BlockSpec(memory_space=pl.ANY)],
        out_specs=[middle(LIVE, count)] + [block((count, ROWS, D))] * 3
        + [middle(LIVE, count), block((count, 4, ROWS, STACK))],
        out_shape=[array((LIVE, windows, D), F32)] + [array((windows, ROWS, D), BF)] * 3
        + [array((LIVE, windows, D), BF), array((windows, 4, ROWS, STACK), BF)],
        scratch_shapes=[pltpu.VMEM((4, count * ROWS, GROUP), F32)] * 4,
        compiler_params=pltpu.CompilerParams(vmem_limit_bytes=VMEM),
        cost_estimate=cost(16e9),
        name="window_attention_forward",
    )(owner, patches, region_rows, weights, vec, after)


def mlp_kernel(many, sources, cols, steps, lanes, last, *refs):
    x1_ref, pc_ref, *w_refs, vec_ref, b1_ref = refs[:8]
    if last:
        prev_refs = refs[9:11]
        op_ref, dx1_ref, dwa_ref, dwb_ref, dv_ref, db1_ref, acc1, acc2 = refs[11:]
    else:
        prev_refs = ()
        early_ref, op_ref, dx1_ref, dwa_ref, dwb_ref, dv_ref, db1_ref, acc1, acc2 = refs[8:]
    total = many * sources * cols
    step = pl.program_id(0)

    @pl.when(step == 0)
    def _():
        for ref in (acc1, acc2, dv_ref, db1_ref):
            ref[...] = jnp.zeros_like(ref)

    vec = vec_ref[...]
    gain = vec[2:3]
    x1 = x1_ref[...].reshape(total, D)
    xhat, scale = norm_parts(x1)
    h = (xhat * gain + vec[3:4]).astype(BF)
    for s in range(sources):
        dx1_ref[:, s * cols : (s + 1) * cols] = pc_ref[s].astype(F32)
    dy = dx1_ref[...].reshape(total, D)
    dm = dy.astype(BF)
    ht = h.T
    dmt = dm.T
    y = x1 + vec[7:8]
    dh = jnp.zeros((total, D), F32)
    parts = [(j, slice(c, c + lanes)) for j in range(4) for c in range(0, D, lanes)]

    def activate(j, s):
        u, slope = gelu_parts(nn(h, w_refs[j][0, :, s]) + b1_ref[j : j + 1, s])
        da = slope * nt(dm, w_refs[j][1, s, :])
        db1_ref[j, :, s] += fold(da)
        return u.astype(BF), da.astype(BF)

    def apply(j, s, u, da):
        acc1[j, :, s] += nn(ht, da)
        acc2[j, :, s] += nn(dmt, u)
        return nn(u, w_refs[j][1, s, :]), nt(da, w_refs[j][0, :, s])

    held_pair = activate(*parts[0])
    for n in range(1, len(parts) + 1):
        later = activate(*parts[n]) if n < len(parts) else None
        up, down = apply(*parts[n - 1], *held_pair)
        y, dh = y + up, dh + down
        held_pair = later
    y = y.reshape(many, sources * cols, D)

    def put(ref):
        for s in range(sources):
            ref[s] = y[:, s * cols : (s + 1) * cols].astype(BF)

    if last:
        put(op_ref)
    else:
        pl.when(step < steps - 1)(lambda: put(early_ref))
        pl.when(step == steps - 1)(lambda: put(op_ref))
    dy = dx1_ref[...].reshape(total, D)
    dx1_ref[...] = (dy + norm_back(dh, xhat, scale, gain)).reshape(dx1_ref.shape)
    dv_ref[0] += fold(dh * xhat)
    dv_ref[1] += fold(dh)
    dv_ref[2] += fold(dy)

    @pl.when(step == steps - 1)
    def _():
        for refs_out, first in ((dwa_ref, 0), (dwb_ref, 1)):
            for n, acc in enumerate((acc1, acc2)):
                for m in range(2):
                    piece = acc[first + 2 * m]
                    for prev in prev_refs[first : first + 1]:
                        piece = piece + prev[2 * m + n].astype(F32)
                    refs_out[2 * m + n] = piece.astype(BF)


def mlp(x1, first_position, cot, weights, vec, bias_first, prev=(), many=10, lanes=256):
    sources, positions, cols, _ = cot.shape
    windows = sources * cols
    steps = positions // many
    skip = first_position // many
    some = lambda place: pl.BlockSpec((sources, many, cols, D), lambda i: (0, place(i), 0, 0))
    array = jax.ShapeDtypeStruct
    matrices = full((4, D, D))
    rows = lambda count: array((sources, count, cols, D), BF)
    late = (LIVE - positions if not prev else positions) + many
    outs = [some(lambda i: i + 1)] if prev else [some(lambda i: jnp.minimum(i, steps - 2)), some(lambda i: 0)]
    shapes = [rows(late)] if prev else [rows(positions - many), rows(late)]
    return pl.pallas_call(
        partial(mlp_kernel, many, sources, cols, steps, lanes, len(prev) > 0),
        grid=(steps,),
        in_specs=[pl.BlockSpec((many, windows, D), lambda i: (i + skip, 0, 0)), some(lambda i: i)]
        + [full((2, D, D))] * 4 + [full(vec.shape), full((4, D))]
        + ([pl.BlockSpec(memory_space=pl.ANY)] + [matrices] * 2 if prev else []),
        out_specs=outs + [block((many, windows, D)), matrices, matrices, full((3, 8, D)), full((4, 8, D))],
        out_shape=shapes + [array((positions, windows, D), F32), array((4, D, D), BF),
                            array((4, D, D), BF), array((3, 8, D), F32), array((4, 8, D), F32)],
        scratch_shapes=[pltpu.VMEM((4, D, D), F32), pltpu.VMEM((4, D, D), F32)],
        input_output_aliases={8: 0} if prev else {},
        compiler_params=pltpu.CompilerParams(vmem_limit_bytes=VMEM),
        cost_estimate=cost(4e9 * steps),
        name="mlp_forward_backward",
    )(x1, cot, *weights, vec, bias_first, *prev)


def attn_bwd_kernel(count, batch, chunks, more, owner_ref, *refs):
    p_ref, r_ref = refs[:2]
    refs = refs[:3] + refs[4:]
    dx1_refs = refs[3 : 3 + chunks]
    q_ref, k_ref, v_ref, o_ref, pt_ref, w_ref, vec_ref = refs[3 + chunks : 10 + chunks]
    owner = owner_ref[0, 0]
    prev_refs = refs[10 + chunks : 14 + chunks] if more else ()
    dp_ref, dr_ref, dw_ref, dv_ref, dq_held, dk_held, dvv_held, do_held = refs[10 + chunks + len(prev_refs) :]
    total = count * LIVE

    @pl.when(pl.program_id(0) == 0)
    def _():
        dw_ref[...] = prev_refs[2][...] if more else jnp.zeros_like(dw_ref)
        dv_ref[...] = prev_refs[3][...] if more else jnp.zeros_like(dv_ref)
        do_held[:, total:] = jnp.zeros((4, count * (ROWS - LIVE), GROUP), F32)

    vec = vec_ref[...]
    gain = vec[0:1]
    dx1 = jnp.concatenate([ref[...] for ref in dx1_refs], axis=0).reshape(total, D)
    gb = dx1.astype(BF)
    hold(do_held, total, nt(gb, w_ref[owner ^ 3]))
    masks = head_masks()

    def body(step, carry):
        units = [(step * batch + w, g) for w in range(batch) for g in range(4)]
        grads, scores = [], []
        for w, g in units:
            lanes = slice(GROUP * g, GROUP * (g + 1))
            rows = pl.ds(w, ROWS, stride=count)
            do_wide = spread(do_held[g, rows, :], masks)
            dvv_held[g, rows, :] = nn(pt_ref[w, g], do_wide)
            grads.append(nt(v_ref[w, :, lanes], do_wide))
        for (w, g), grad in zip(units, grads):
            p = pt_ref[w, g].astype(F32)
            both = p * grad
            scores.append((both - p * jnp.sum(both, axis=0, keepdims=True)).astype(BF))
        for (w, g), ds in zip(units, scores):
            lanes = slice(GROUP * g, GROUP * (g + 1))
            rows = pl.ds(w, ROWS, stride=count)
            dk_held[g, rows, :] = nn(ds, spread(q_ref[w, :, lanes].astype(F32), masks)) * SCALE
            dq_held[g, rows, :] = collect(tn(ds, k_ref[w, :, lanes]), masks, ROWS) * SCALE
        return carry

    lax.fori_loop(0, count // batch, body, 0)
    x = jnp.concatenate([p_ref[...].astype(F32), r_ref[...][None]], axis=0).reshape(total, D)
    xhat, scale = norm_parts(x)
    xn = (xhat * gain + vec[1:2]).astype(BF)
    dq_wide = held_rows(dq_held, total)
    dv_wide = held_rows(dvv_held, total)
    dq = dq_wide.astype(BF)
    dk = held_rows(dk_held, total).astype(BF)
    dv = dv_wide.astype(BF)
    dn = nt(dq, w_ref[owner ^ 0]) + nt(dk, w_ref[owner ^ 1]) + nt(dv, w_ref[owner ^ 2])
    dx = (dx1 + norm_back(dn, xhat, scale, gain)).reshape(LIVE, count, D)
    dp_ref[...] = dx[:PATCH].astype(BF)
    dr_ref[...] = dx[PATCH]
    xt = xn.T
    dw_ref[0] += nn(xt, dq)
    dw_ref[1] += nn(xt, dk)
    dw_ref[2] += nn(xt, dv)
    dw_ref[3] += nn(o_ref[...].reshape(total, D).T, gb)
    dv_ref[0] += fold(dn * xhat)
    dv_ref[1] += fold(dn)
    dv_ref[2] += fold(dq_wide)
    dv_ref[3] += fold(dv_wide)
    dv_ref[4] += fold(dx1)


def attn_bwd(owner, patches, region_rows, dx1_parts, saved, weights, vec, start, windows, after, prev=(), count=16, batch=4):
    skip = start // count
    array = jax.ShapeDtypeStruct
    sums = [full((4, D, D)), full((5, 8, D))]
    anywhere = pl.BlockSpec(memory_space=pl.ANY)
    rows = pl.BlockSpec((count, D), lambda i: (i + skip, 0))
    before = 12 + len(dx1_parts)
    return pl.pallas_call(
        partial(attn_bwd_kernel, count, batch, len(dx1_parts), len(prev) > 0),
        grid=(windows // count,),
        in_specs=[pl.BlockSpec(memory_space=pltpu.SMEM), middle(PATCH, count, skip), rows, anywhere, anywhere]
        + [middle(part.shape[0], count, skip) for part in dx1_parts]
        + [pl.BlockSpec((count, ROWS, D), lambda i: (i + skip, 0, 0))] * 3
        + [middle(LIVE, count, skip), pl.BlockSpec((count, 4, ROWS, STACK), lambda i: (i + skip, 0, 0, 0))]
        + [full((4, D, D)), full(vec.shape)] + ([anywhere] * 2 + sums)[: len(prev)],
        out_specs=[middle(PATCH, count, skip), rows] + sums,
        out_shape=[array(patches.shape, BF), array(region_rows.shape, F32),
                   array((4, D, D), F32), array((5, 8, D), F32)],
        scratch_shapes=[pltpu.VMEM((4, count * ROWS, GROUP), F32)] * 4,
        input_output_aliases={before: 0, before + 1: 1} if prev else {},
        compiler_params=pltpu.CompilerParams(vmem_limit_bytes=VMEM),
        cost_estimate=cost(12e9),
        name="window_attention_backward",
    )(owner, patches, region_rows, *after, *dx1_parts, *saved, weights, vec, *prev)


def regional_fwd_kernel(owner_ref, canvas_ref, band_ref, ids_ref, band_ids_ref, w_ref, vec_ref,
                        r1_ref, mixed_ref, level_ref, q_ref, k_ref, v_ref):
    vec = vec_ref[...]
    owner = owner_ref[0, 0]
    xhat, _ = norm_parts(canvas_ref[...].astype(F32))
    low = (xhat * vec[0:1] + vec[1:2]).astype(BF)
    q_ref[...] = (nn(low, w_ref[owner ^ 0]) + vec[4:5]).astype(BF)
    k_ref[...] = nn(low, w_ref[owner ^ 1]).astype(BF)
    v_ref[...] = (nn(low, w_ref[owner ^ 2]) + vec[5:6]).astype(BF)
    band = band_ref[...].astype(F32)
    rows = band.shape[0]
    xhat, _ = norm_parts(band)
    q = nn((xhat * vec[0:1] + vec[1:2]).astype(BF), w_ref[owner ^ 0]) + vec[4:5]
    masks = head_masks()
    same = ids_ref[...] == band_ids_ref[...]
    scores, probs = [], []
    for g in range(4):
        lanes = slice(GROUP * g, GROUP * (g + 1))
        scores.append(nt(k_ref[:, lanes], spread(q[:, lanes], masks)))
    for g, s in enumerate(scores):
        s = jnp.where(same, s, MASKED)
        peak = jnp.max(s, axis=0, keepdims=True)
        e = jnp.exp((s - peak) * SCALE)
        sums = jnp.sum(e, axis=0, keepdims=True)
        level_ref[g : g + 1] = peak * SCALE + jnp.log(sums)
        probs.append((e * (1.0 / sums)).astype(BF))
    for g, p in enumerate(probs):
        lanes = slice(GROUP * g, GROUP * (g + 1))
        mixed_ref[:, lanes] = collect(tn(p, v_ref[:, lanes]), masks, rows)
    r1_ref[...] = band + nn(mixed_ref[...].astype(BF), w_ref[owner ^ 3]) + vec[6:7]


def in_vmem(kernel, outs, name, *args, after=(), scratch=(), flops=2e9):
    spaces = [pltpu.SMEM if arg.shape == (1, 1) else pltpu.VMEM for arg in args]
    count = len(args)
    return pl.pallas_call(
        lambda *refs: kernel(*refs[:count], *refs[count + len(after) :]),
        in_specs=[pl.BlockSpec(memory_space=space) for space in spaces]
        + [pl.BlockSpec(memory_space=pl.ANY) for _ in after],
        out_specs=[pl.BlockSpec(memory_space=pltpu.VMEM) for _ in outs],
        out_shape=[jax.ShapeDtypeStruct(*out) for out in outs],
        scratch_shapes=list(scratch),
        compiler_params=pltpu.CompilerParams(vmem_limit_bytes=VMEM),
        cost_estimate=cost(flops),
        name=name,
    )(*args, *after)


def payload_kernel(owner_ref, dr_ref, mixed_ref, level_ref, w_ref, grad_ref, extra_ref):
    low = dr_ref[...].astype(BF)
    grad_ref[...] = low
    both = nt(low, w_ref[owner_ref[0, 0] ^ 3]).astype(BF).astype(F32) * mixed_ref[...]
    head = lax.broadcasted_iota(jnp.int32, (D, GROUP), 0) // HEAD_DIM
    lane = lax.broadcasted_iota(jnp.int32, (D, GROUP), 1)
    pick = ((head == lane) | (head + HEADS == lane)).astype(BF)
    high, low_part = halves(both)
    rest = (both - high.astype(F32) - low_part.astype(F32)).astype(BF)
    delta = nn(high, pick) + (nn(low_part, pick) + nn(rest, pick))
    top = delta.astype(BF).astype(F32)
    lane = lax.broadcasted_iota(jnp.int32, (1, GROUP), 1)
    level = level_ref[...]
    level_top = level.astype(BF).astype(F32)
    level_rest = level - level_top
    level_mid = level_rest.astype(BF).astype(F32)
    extra = level_rest - level_mid
    for place, term in ((4, level_mid), (3, level_top), (2, delta - top), (1, top)):
        extra = jnp.where(lane < place * HEADS, term, extra)
    extra_ref[...] = extra.astype(BF)


def regional_bwd_kernel(own_rows, owner_ref, place_ref, q_ref, k_ref, v_ref, canvas_ref, grads_ref, extra_ref, ids_ref,
                        ids_row_ref, ids_own_ref, ids_own_row_ref, mixed_ref, band_grad_ref, dw_ref, w_ref, vec_ref,
                        dr_ref, keep_ref, give_ref, gv_ref, sum_held):
    vec = vec_ref[...]
    owner = owner_ref[0, 0]
    mine = pl.ds(pl.multiple_of(place_ref[0, 0] * own_rows, own_rows), own_rows)
    masks = head_masks()
    grads_own = grads_ref[mine]
    do = nt(grads_ref[...], w_ref[owner ^ 3]).astype(BF).astype(F32)
    do_own = nt(grads_own, w_ref[owner ^ 3]).astype(BF).astype(F32)
    same_own = ids_ref[...] == ids_own_row_ref[...]
    same = ids_own_ref[...] == ids_row_ref[...]
    lanes = [slice(GROUP * g, GROUP * (g + 1)) for g in range(4)]

    def columns(rows):
        term = rows.astype(F32).T
        part = lambda n: term[n * HEADS : (n + 1) * HEADS]
        wide = lambda x: [jnp.concatenate([x[h : h + 1] for h in range(4 * g, 4 * g + 4)], axis=1) for g in range(4)]
        return wide(part(0) + part(1)), wide(part(2) + part(3) + part(4))

    delta, level = columns(extra_ref[...])
    delta_own, level_own = columns(extra_ref[mine])
    first, second = [], []
    dqs, dks, dvs = [], [], []
    for g in range(4):
        q_wide = spread(q_ref[mine, lanes[g]].astype(F32), masks)
        do_wide = spread(do_own[:, lanes[g]], masks)
        first.append((nt(k_ref[:, lanes[g]], q_wide), nt(v_ref[:, lanes[g]], do_wide)))
        q_wide = spread(q_ref[:, lanes[g]].astype(F32), masks)
        do_wide = spread(do[:, lanes[g]], masks)
        second.append((nt(k_ref[mine, lanes[g]], q_wide), nt(v_ref[mine, lanes[g]], do_wide), q_wide, do_wide))
    for g in range(4):
        s, dp = first[g]
        p = jnp.where(same_own, jnp.exp(s * SCALE - level_own[g]), 0.0)
        ds = (p * (dp - delta_own[g])).astype(BF)
        dqs.append(collect(tn(ds, k_ref[:, lanes[g]]), masks, own_rows) * SCALE)
        s, dp, q_wide, do_wide = second[g]
        p = jnp.where(same, jnp.exp(s * SCALE - level[g]), 0.0)
        ds = (p * (dp - delta[g])).astype(BF)
        dvs.append(nn(p.astype(BF), do_wide))
        dks.append(nn(ds, q_wide) * SCALE)
    xhat, scale = norm_parts(canvas_ref[mine].astype(F32))
    low = (xhat * vec[0:1] + vec[1:2]).astype(BF)
    dq_wide, dk_wide, dv_wide = (jnp.concatenate(x, axis=1) for x in (dqs, dks, dvs))
    dq, dk, dv = dq_wide.astype(BF), dk_wide.astype(BF), dv_wide.astype(BF)
    dn = nt(dq, w_ref[owner ^ 0]) + nt(dk, w_ref[owner ^ 1]) + nt(dv, w_ref[owner ^ 2])
    dr_ref[...] = grads_own.astype(F32) + norm_back(dn, xhat, scale, vec[0:1])
    sum_held[0] = dw_ref[0] + tn(low, dq)
    sum_held[1] = dw_ref[1] + tn(low, dk)
    sum_held[2] = dw_ref[2] + tn(low, dv)
    sum_held[3] = dw_ref[3] + tn(mixed_ref[...].astype(BF), band_grad_ref[...])
    for n in range(2):
        keep_ref[n] = sum_held[owner ^ (2 * n)].astype(BF)
        give_ref[n] = sum_held[owner ^ (2 * n + 1)].astype(BF)
    gv_ref[0] = fold(dn * xhat)
    gv_ref[1] = fold(dn)
    gv_ref[2] = fold(dq_wide)
    gv_ref[3] = fold(dv_wide)
    gv_ref[4] = fold(band_grad_ref[...].astype(F32))


def halves(a):
    high = a.astype(BF)
    return high, (a - high.astype(F32)).astype(BF)


def terms(a, passes):
    return (a.astype(BF),) if passes == 1 else halves(a)


def product(a, b, dot=nn):
    if len(a) == 1:
        return dot(a[0], b[0])
    return dot(a[0], b[0]) + (dot(a[0], b[1]) + dot(a[1], b[0]))


def symmetric(a, b, dot=nn):
    half = D // 2
    right = (lambda x: x[half:]) if dot is nt else (lambda x: x[:, half:])
    top = product([x[:half] for x in a], b, dot)
    corner = product([x[half:] for x in a], [right(x) for x in b], dot)
    return jnp.concatenate([top, jnp.concatenate([top[:, half:].T, corner], axis=1)], axis=0)


DIRECT_STEPS = (1, 1, 1, -1, -1)
GRAM_STEPS = (1, 1, 3, 3, 3)
NEAR_ZERO = NS_FIRST + NS_SECOND + NS_THIRD
NEAR_ONE = NS_SECOND + 2.0 * NS_THIRD


def identity():
    rows = lax.broadcasted_iota(jnp.int32, (D, D), 0)
    return rows == lax.broadcasted_iota(jnp.int32, (D, D), 1)


def polynomial(gram, eye, step):
    if step > 0:
        parts = terms(gram, step)
        return NS_FIRST, NS_SECOND * gram + NS_THIRD * symmetric(parts, parts)
    rest = gram - jnp.where(eye, 1.0, 0.0)
    parts = terms(rest, -step)
    return NEAR_ZERO, NEAR_ONE * rest + NS_THIRD * symmetric(parts, parts)


def direct_steps(moment, eye):
    z = moment * (1.0 / (jnp.sqrt(jnp.sum(moment * moment)) + 1e-07))
    for step in DIRECT_STEPS:
        parts = terms(z, abs(step))
        gram = symmetric(parts, parts, nt)
        yield
        scale, poly = polynomial(gram, eye, step)
        yield
        z = scale * z + product(terms(poly, abs(step)), parts)
        yield
    return z


def gram_steps(gram, eye):
    factor = 1.0 / (jnp.sqrt(jnp.sum(jnp.where(eye, gram, 0.0))) + 1e-07)
    gram = gram * (factor * factor)
    steps = None
    for n, passes in enumerate(GRAM_STEPS):
        scale, poly = polynomial(gram, eye, passes)
        yield
        parts = terms(poly, passes)
        if steps is None:
            steps = jnp.where(eye, scale, 0.0) + poly
        else:
            steps = scale * steps + symmetric(parts, terms(steps, passes))
            yield
        if n < len(GRAM_STEPS) - 1:
            half = scale * gram + symmetric(parts, terms(gram, passes))
            yield
            gram = scale * half + symmetric(parts, terms(half, passes))
            yield
    return steps * factor


def in_turns(*chains):
    results = [None] * len(chains)
    running = list(enumerate(chains))
    while running:
        still = []
        for n, chain in running:
            try:
                next(chain)
                still.append((n, chain))
            except StopIteration as stop:
                results[n] = stop.value
        running = still
    return results


def old_grams_kernel(moms_ref, *out_refs):
    for n, out_ref in enumerate(out_refs):
        square, cross = jnp.zeros((D, D), F32), jnp.zeros((D, D), F32)
        for j in range(OPT):
            high, low = halves(moms_ref[j, n])
            if n == 1:
                high, low = high.T, low.T
            square = square + nt(high, high)
            cross = cross + nt(high, low)
        out_ref[...] = square + (cross + cross.T)


def grams_kernel(places, owner_ref, moms_ref, all_ref, mixed1_ref, new1_ref, mixed2_ref, new2_ref, own_ref):
    half = len(places) // 2
    for n, (mixed_ref, new_ref) in enumerate(((mixed1_ref, new1_ref), (mixed2_ref, new2_ref))):
        mixed, new = jnp.zeros((D, D), F32), jnp.zeros((D, D), F32)
        mine = places[n * half : (n + 1) * half]
        for j in range(OPT):
            high, low = halves(moms_ref[j, n])
            if n == 1:
                high, low = high.T, low.T
            g = jnp.concatenate([all_ref[d, j] for d in mine], axis=0)
            mixed = mixed + (nt(high, g) + nt(low, g))
            new = new + nt(g, g)
        mixed_ref[...] = mixed + mixed.T
        new_ref[...] = new
        own_ref[n] = jnp.concatenate([all_ref[d, owner_ref[0, 0]] for d in mine], axis=0)


def update_kernel(clip_ref, ga_ref, ma_ref, wa_ref, g_ref, m1_ref, m2_ref, w1_ref, w2_ref,
                  old1, mixed1, new1, old2, mixed2, new2, na_ref, newa_ref, n1_ref, new1_ref, n2_ref, new2_ref):
    clip = clip_ref[0, 0]
    eye = identity()
    na_ref[...] = MUON_MOMENTUM * ma_ref[...] + clip * ga_ref[...].astype(F32)
    n1_ref[...] = MUON_MOMENTUM * m1_ref[...] + clip * g_ref[0].astype(F32)
    n2_ref[...] = MUON_MOMENTUM * m2_ref[...] + clip * g_ref[1].astype(F32).T
    a, b, c = MUON_MOMENTUM * MUON_MOMENTUM, MUON_MOMENTUM * clip, clip * clip
    gram1 = a * old1[...] + b * mixed1[...] + c * new1[...]
    gram2 = a * old2[...] + b * mixed2[...] + c * new2[...]
    steps1, steps2, z = in_turns(gram_steps(gram1, eye), gram_steps(gram2, eye), direct_steps(na_ref[...], eye))
    newa_ref[...] = wa_ref[...] * DECAY_KEEP - MUON_RATE * z
    z = product(halves(steps1), halves(n1_ref[...]))
    new1_ref[...] = w1_ref[...] * DECAY_KEEP - MUON_RATE * z
    z = product(halves(n2_ref[...]), halves(steps2))
    new2_ref[...] = w2_ref[...] * DECAY_KEEP - (MUON_RATE * max(1.0, FF / D) ** 0.5) * z


def pair(values, bit):
    return lax.ppermute(values, "opt", [(i, i ^ bit) for i in range(OPT)])


def fence(x, *first):
    here = pl.BlockSpec(memory_space=pl.ANY)
    return pl.pallas_call(
        lambda *refs: None,
        in_specs=[here] * (1 + len(first)),
        out_specs=here,
        out_shape=jax.ShapeDtypeStruct(x.shape, x.dtype),
        input_output_aliases={0: 0},
        cost_estimate=cost(1e3),
        name="fence",
    )(x, *first)


def pieces_of_owners(own):
    mate = pair(own, 1)
    across = pair(own, 2)
    return [own, mate, across, pair(across, 1)]


def share(x):
    copies = jnp.broadcast_to(x[None], (lax.axis_size("dp"),) + x.shape)
    return lax.all_to_all(copies, "dp", 0, 0, tiled=True)


def swap(x, bit):
    return lax.ppermute(x, "dp", [(i, i ^ bit) for i in range(lax.axis_size("dp"))])


def bits():
    return [1 << n for n in range(lax.axis_size("dp").bit_length() - 1)]


def halving_step(x, bit):
    half = x.shape[0] // 2
    side = (lax.axis_index("dp") // bit) % 2
    give = lax.dynamic_slice_in_dim(x, (1 - side) * half, half, 0).astype(BF)
    return lax.dynamic_slice_in_dim(x, side * half, half, 0), give


def order_of_halves(count):
    width = count.bit_length() - 1
    return [int(format(n, "b").zfill(width)[::-1], 2) if width else 0 for n in range(count)]


def sum_small_over_dp(x):
    for bit in bits():
        x = x + swap(x, bit)
    return x


def split_heads(x):
    return x.reshape(x.shape[0], HEADS, HEAD_DIM)


def regional_forward(canvas, band, same, weights, vec):
    low = lambda x: (norm_parts(x.astype(F32))[0] * vec[0] + vec[1]).astype(BF)
    normed = low(canvas)
    queries = (nn(normed, weights[0]) + vec[4]).astype(BF)
    keys = nn(normed, weights[1]).astype(BF)
    values = (nn(normed, weights[2]) + vec[5]).astype(BF)
    own = (nn(low(band), weights[0]) + vec[4]).astype(BF)
    scores = jnp.einsum("qhd,khd->hqk", split_heads(own), split_heads(keys), preferred_element_type=F32)
    scores = jnp.where(same[None], scores * SCALE, MASKED)
    peak = jnp.max(scores, axis=-1, keepdims=True)
    raised = jnp.exp(scores - peak)
    sums = jnp.sum(raised, axis=-1, keepdims=True)
    probs = (raised / sums).astype(BF)
    mixed = jnp.einsum("hqk,khd->qhd", probs, split_heads(values), preferred_element_type=F32).reshape(own.shape)
    region_rows = band.astype(F32) + nn(mixed.astype(BF), weights[3]) + vec[6]
    return region_rows, mixed, (peak + jnp.log(sums))[:, :, 0], queries, keys, values


def regional_terms(queries, keys, values, grad_mixed, same, level, delta):
    scores = jnp.einsum("qhd,khd->hqk", split_heads(queries), split_heads(keys), preferred_element_type=F32)
    probs = jnp.where(same[None], jnp.exp(scores * SCALE - level[:, :, None]), 0.0)
    grads = jnp.einsum("qhd,khd->hqk", split_heads(grad_mixed), split_heads(values), preferred_element_type=F32)
    return probs.astype(BF), (probs * (grads - delta[:, :, None])).astype(BF)


def regional_backward(queries, keys, values, grads, own, rows, same, level, delta, weights, vec, mixed, band_grad, dw):
    grad_mixed = nt(grads, weights[3]).astype(BF)
    level_own, delta_own = own(level.T).T, own(delta.T).T
    _, scores = regional_terms(own(queries), keys, values, own(grad_mixed), same.T, level_own, delta_own)
    dq = jnp.einsum("hqk,khd->qhd", scores, split_heads(keys), preferred_element_type=F32)
    probs, scores = regional_terms(queries, own(keys), own(values), grad_mixed, same, level, delta)
    dk = jnp.einsum("hqk,qhd->khd", scores, split_heads(queries), preferred_element_type=F32)
    dv = jnp.einsum("hqk,qhd->khd", probs, split_heads(grad_mixed), preferred_element_type=F32)
    flat = lambda x: x.reshape(-1, D)
    dq, dk, dv = flat(dq) * SCALE, flat(dk) * SCALE, flat(dv)
    lows = [x.astype(BF) for x in (dq, dk, dv)]
    dn = sum(nt(x, w) for x, w in zip(lows, weights))
    xhat, scale = norm_parts(rows.astype(F32))
    low = (xhat * vec[0] + vec[1]).astype(BF)
    d_regions = own(grads).astype(F32) + norm_back(dn, xhat, scale, vec[0])
    matrices = [dw[j] + tn(low, x) for j, x in enumerate(lows)] + [dw[3] + tn(mixed.astype(BF), band_grad)]
    vectors = [fold(x) for x in (dn * xhat, dn, dq, dv, band_grad.astype(F32))]
    return d_regions, jnp.stack(matrices).astype(BF), jnp.stack(vectors)


def per_device(patches, regions, image_ids, attn_w, mlp_in, mlp_out, vec_params, patch_cot, region_cot,
               attn_mom, mlp_in_mom, mlp_out_mom, adam_first, adam_second):
    dp_size = lax.axis_size("dp")
    dp_index = lax.axis_index("dp")
    opt_index = lax.axis_index("opt")
    _, grid_rows, cols, _, _ = patch_cot.shape
    grid_cols = patches.shape[2]
    tokens = grid_rows * grid_cols
    own_count = grid_rows * cols
    one_kernel = tokens <= 1024
    vec = vec_params
    order = opt_index ^ jnp.arange(OPT)
    move = lambda x: lax.all_to_all(x, "dp", 0, 0, tiled=True)

    attn_pieces = jnp.stack(pieces_of_owners(attn_w[0].astype(BF)))
    mlp_w = pieces_of_owners(jnp.stack([mlp_in, mlp_out]).astype(BF))
    owner = opt_index.reshape(1, 1)
    if not one_kernel:
        weights = [lax.dynamic_index_in_dim(attn_pieces, opt_index ^ j, 0, keepdims=False) for j in range(OPT)]
    canvas_blocks = share(regions[0])
    canvas = canvas_blocks.reshape(tokens, D)
    by_position = patch_cot[0].transpose(0, 2, 1, 3)
    split = 30
    last = jnp.concatenate([by_position[:, split:], region_cot[0][:, None]], axis=1)
    first_cot = move(fence(by_position[:, :split], canvas))
    bias_first = jnp.take(vec[8:], order, axis=0)

    band_of = lambda x: lax.dynamic_slice_in_dim(x, dp_index, 1, 1).reshape((grid_cols,) + x.shape[3:])
    own_of = lambda x: lax.dynamic_slice_in_dim(x, dp_index * own_count, own_count, 0)
    ids_blocks = image_ids[0].reshape(grid_rows, dp_size, cols).transpose(1, 0, 2)
    ids = ids_blocks.reshape(tokens)
    band_ids, own_ids = band_of(ids_blocks), own_of(ids)
    band = band_of(canvas_blocks)
    if one_kernel:
        repeat = lambda x: jnp.tile(x, 4)[None]
        region_rows, mixed, level, reg_q, reg_k, reg_v = in_vmem(
            regional_fwd_kernel,
            [((grid_cols, D), F32), ((grid_cols, D), F32), ((4, 4 * grid_cols), F32)] + [((tokens, D), BF)] * 3,
            "regional_attention_forward", owner, canvas, band, ids[:, None], repeat(band_ids), attn_pieces, vec)
        level = level.reshape(HEADS, grid_cols)
    else:
        region_rows, mixed, level, reg_q, reg_k, reg_v = regional_forward(
            canvas, band, band_ids[:, None] == ids[None, :], weights, vec)
    level_wide = jnp.tile(level.T, (1, GROUP // HEADS))

    windows = patches[0, 0].transpose(1, 0, 2)
    some = grid_cols // 2
    x1, *saved = attn_fwd(owner, windows, region_rows, attn_pieces, vec, mlp_w[2])
    last_cot = move(fence(last, x1))
    early_out, late_out, dx1_a, *grads_a = mlp(x1, 0, first_cot, mlp_w, vec, bias_first)
    moved_a = move(early_out)
    moms = lax.all_gather(fence(jnp.stack([mlp_in_mom, mlp_out_mom]), x1), "opt", axis=0)
    late_out, dx1_b, *grads_b = mlp(x1, split, last_cot, mlp_w, vec, bias_first, prev=(late_out, *grads_a[:2]))
    near = pair(fence(grads_b[1], moved_a), 1)
    far = (near[2:].astype(F32) + grads_b[0][2:].astype(F32)).astype(BF)
    moved_b = move(fence(late_out, far))
    out_patches = jnp.concatenate([moved_a, moved_b[:, :-1]], axis=1).transpose(0, 2, 1, 3)[None]
    out_regions = moved_b[None, :, -1]

    dx1 = (dx1_a, dx1_b)
    early = attn_bwd(owner, windows, region_rows, dx1, saved, attn_pieces, vec, 0, some, (far, far))
    own_mlp = near[:2].astype(F32) + grads_b[0][:2].astype(F32) + fence(pair(far, 2), early[3]).astype(F32)
    keep, give = halving_step(own_mlp.reshape(2 * D, D), 1)
    d_patches, d_region, d_attn, d_vec_attn = attn_bwd(
        owner, windows, region_rows, dx1, saved, attn_pieces, vec, some, some, (give, moms), prev=early)
    d_patches = d_patches.transpose(1, 0, 2)[None, None]
    gives = []
    old_grams = in_vmem(old_grams_kernel, [((D, D), F32)] * 2, "momentum_grams", moms, after=(d_vec_attn,),
                         flops=4e9)

    band_grad, extra = in_vmem(payload_kernel, [((grid_cols, D), BF), ((grid_cols, GROUP), BF)],
                               "regional_payload", owner, d_region, mixed, level_wide, attn_pieces,
                               after=(give, moved_b))
    taken = fence(swap(give, 1), band_grad)
    for bit in bits()[1:]:
        keep, give = halving_step(keep + taken.astype(F32), bit)
        gives.append(give)
        taken = swap(give, bit)
    payload = share(jnp.concatenate([band_grad, extra], axis=1)).reshape(grid_rows, dp_size, cols, D + GROUP)
    payload = payload.transpose(1, 0, 2, 3).reshape(tokens, D + GROUP)
    grads = payload[:, :D]
    extra = payload[:, D:]
    if one_kernel:
        matrices = ((2, D, D), BF)
        d_regions, keep_attn, give_attn, d_vec_reg = in_vmem(
            partial(regional_bwd_kernel, own_count),
            [((own_count, D), F32), matrices, matrices, ((5, 8, D), F32)],
            "regional_attention_backward", owner, dp_index.reshape(1, 1), reg_q, reg_k, reg_v, canvas, grads, extra,
            ids[:, None], repeat(ids), own_ids[:, None], repeat(own_ids), mixed, band_grad, d_attn, attn_pieces, vec,
            after=tuple(gives[-1:]) + tuple(old_grams), scratch=[pltpu.VMEM((4, D, D), F32)], flops=4e9)
    else:
        part = lambda n: extra[:, n * HEADS : (n + 1) * HEADS].astype(F32)
        delta, level = (part(0) + part(1)).T, (part(2) + part(3) + part(4)).T
        d_regions, grad_attn, d_vec_reg = regional_backward(
            reg_q, reg_k, reg_v, grads, own_of, own_of(canvas), ids[:, None] == own_ids[None, :], level, delta,
            weights, vec, mixed, band_grad, d_attn)
        pick = lambda j: lax.dynamic_index_in_dim(grad_attn, opt_index ^ j, 0, keepdims=False)
        keep_attn, give_attn = jnp.stack([pick(0), pick(2)]), jnp.stack([pick(1), pick(3)])
    d_regions = d_regions.reshape(regions.shape)

    piece_mlp = (keep + fence(taken, give_attn).astype(F32)).astype(BF)

    near = pair(give_attn, 1)
    far = (near[1].astype(F32) + keep_attn[1].astype(F32)).astype(BF)
    piece_attn = near[0].astype(F32) + keep_attn[0].astype(F32) + pair(far, 2).astype(F32)
    piece_attn = move(piece_attn.astype(BF).reshape(dp_size, D // dp_size, D))
    piece_attn = jnp.sum(piece_attn.astype(F32), axis=0).astype(BF)
    shared_attn = share(piece_attn)
    all_mlp = lax.all_gather(piece_mlp, ("dp", "opt"), axis=0).reshape(dp_size, OPT, -1, D)
    *grams, own_mlp = in_vmem(partial(grams_kernel, order_of_halves(dp_size)),
                              [((D, D), F32)] * 4 + [((2, D, D), BF)], "mlp_grams", owner, moms, all_mlp, flops=4e9)
    grams = [old_grams[0], *grams[:2], old_grams[1], *grams[2:]]
    own_attn = fence(shared_attn, own_mlp).reshape(D, D)

    d_vec_attn = jnp.sum(d_vec_attn + d_vec_reg, axis=1)
    d_vec_mlp = jnp.sum(grads_a[2] + grads_b[2], axis=1)
    d_bias_first = jnp.take(jnp.sum(grads_a[3] + grads_b[3], axis=1), order, axis=0)
    grad_vec = jnp.concatenate([d_vec_attn[:2], d_vec_mlp[:2], d_vec_attn[2:], d_vec_mlp[2:], d_bias_first])

    squares = lambda x: jnp.sum(x.astype(F32) ** 2)
    part = jnp.full((1, D), squares(piece_attn) + squares(piece_mlp))
    sums = jnp.concatenate([grad_vec, part])
    sums = sums + pair(sums, 1)
    sums = sums + pair(sums, 2)
    sums = sum_small_over_dp(sums)
    grad_vec, total = sums[:-1], sums[-1]

    grad_norm = jnp.sqrt(total[0] + squares(grad_vec))
    clip = jnp.minimum(1.0, CLIP_LIMIT / (grad_norm + 1e-06))
    attn_mom_new, new_attn, first_mom, new_first, second_mom, new_second = in_vmem(
        update_kernel, [((D, D), F32)] * 6, "matrix_updates", clip.reshape(1, 1), own_attn, attn_mom[0], attn_w[0],
        own_mlp, mlp_in_mom, mlp_out_mom, mlp_in, mlp_out, *grams, flops=12e9)
    clipped = clip * grad_vec
    moment_one = BETA_FIRST * adam_first + (1.0 - BETA_FIRST) * clipped
    moment_two = BETA_SECOND * adam_second + (1.0 - BETA_SECOND) * clipped * clipped
    first_hat = moment_one / (1.0 - BETA_FIRST**OPT_STEP)
    second_hat = moment_two / (1.0 - BETA_SECOND**OPT_STEP)
    new_vec = vec_params - ADAM_RATE * first_hat / (jnp.sqrt(second_hat) + ADAM_EPS)
    return (out_patches, out_regions, d_patches, d_regions, new_attn[None], attn_mom_new[None], new_first, first_mom,
            new_second, second_mom, new_vec, moment_one, moment_two, grad_norm)


def solution(mesh):
    canvas = P("opt", None, "dp", None)
    wide = P("opt", None, "dp", None, None)
    bands = P("opt", "dp", None, None, None)
    square, right, down = P("opt", None, None), P(None, "opt"), P("opt", None)
    return jax.shard_map(
        per_device,
        mesh=mesh,
        in_specs=(bands, canvas, square, square, right, down, P(), wide, canvas, square, right, down, P(), P()),
        out_specs=(wide, canvas, bands, canvas, square, square, right, right, down, down, P(), P(), P(), P()),
        check_vma=False,
    )
```

```python
from functools import partial

import jax
import jax.numpy as jnp
from jax import lax
from jax.experimental import pallas as pl
from jax.experimental.pallas import tpu as pltpu
from jax.sharding import PartitionSpec as P

BF = jnp.bfloat16
F32 = jnp.float32

D = 512
HEADS = 16
HEAD_DIM = 32
FF = 2048
PATCH = 49
LIVE = 50
ROWS = 56
GROUP = 128
QUERIES = 64
STACK = 4 * QUERIES
OPT_STEP = 10
OPT = 4

SCALE = HEAD_DIM ** (-0.5)
NORM_EPS = 1e-05
MASKED = -1e30
NS_FIRST = 3.4445
NS_SECOND = -4.775
NS_THIRD = 2.0315
MUON_RATE = 0.5
MUON_MOMENTUM = 0.5
MUON_DECAY = 0.01
ADAM_RATE = 0.5
BETA_FIRST = 0.9
BETA_SECOND = 0.95
ADAM_EPS = 1e-08
CLIP_LIMIT = 1.0
DECAY_KEEP = 1.0 - MUON_RATE * MUON_DECAY
VMEM = 60 * 2**20


def cost(flops):
    return pl.CostEstimate(flops=int(flops), bytes_accessed=10**5, transcendentals=0)

ERF_P = 0.3275911 * 0.5**0.5
ERF = tuple(0.5 * c for c in (0.254829592, -0.284496736, 1.421413741, -1.453152027, 1.061405429))
INV_SQRT_2PI = 0.3989422804014327
LOG2E = 1.4426950408889634


def nn(a, b):
    return lax.dot_general(a, b, (((1,), (0,)), ((), ())), preferred_element_type=F32)


def nt(a, b):
    return lax.dot_general(a, b, (((1,), (1,)), ((), ())), preferred_element_type=F32)


def tn(a, b):
    return lax.dot_general(a, b, (((0,), (0,)), ((), ())), preferred_element_type=F32)


def full(shape):
    return pl.BlockSpec(shape, lambda i: (0,) * len(shape))


def block(shape):
    return pl.BlockSpec(shape, lambda i: (i,) + (0,) * (len(shape) - 1))


def norm_parts(x):
    centre = x - jnp.mean(x, axis=-1, keepdims=True)
    scale = lax.rsqrt(jnp.mean(centre * centre, axis=-1, keepdims=True) + NORM_EPS)
    return centre * scale, scale


def norm_back(grad, xhat, scale, gain):
    inner = grad * gain
    first = jnp.mean(inner, axis=-1, keepdims=True)
    second = jnp.mean(inner * xhat, axis=-1, keepdims=True)
    return scale * (inner - first - xhat * second)


def head_masks():
    lane = lax.broadcasted_iota(jnp.int32, (1, GROUP), 1) // HEAD_DIM
    return [lane == h for h in range(4)]


def spread(rows, masks):
    return jnp.concatenate([jnp.where(m, rows, 0.0) for m in masks], axis=0).astype(BF)


def spread_low(rows):
    lane = lax.broadcasted_iota(jnp.int32, (1, GROUP), 1) // HEAD_DIM
    return jnp.concatenate([rows * (lane == h).astype(F32).astype(BF) for h in range(4)], axis=0)


def collect(stacked, masks, rows, step=None):
    step = step or rows
    out = stacked[:rows]
    for h in range(1, 4):
        out = jnp.where(masks[h], stacked[h * step : h * step + rows], out)
    return out


def staggered(windows, batch, first, second, third):
    steps = [[(w, g) for w in range(n, n + batch) for g in range(4)] for n in range(0, windows, batch)]
    one, two = {}, {}
    for n in range(len(steps) + 2):
        if n < len(steps):
            one.update({unit: first(*unit) for unit in steps[n]})
        if 0 <= n - 1 < len(steps):
            two.update({unit: second(*unit, one.pop(unit)) for unit in steps[n - 1]})
        if 0 <= n - 2:
            for unit in steps[n - 2]:
                third(*unit, two.pop(unit))


def lane_groups(x):
    return [x[:, GROUP * g : GROUP * (g + 1)] for g in range(4)]


def hold(ref, total, x):
    for g, part in enumerate(lane_groups(x)):
        ref[g, :total] = part


def held_rows(ref, total):
    return jnp.concatenate([ref[g, :total] for g in range(4)], axis=1)


def fold(x):
    return jnp.sum(x.reshape(x.shape[0] // 8, 8, x.shape[1]), axis=0)


def gelu_parts(a):
    bell = jnp.exp2(a * a * (-0.5 * LOG2E))
    t = 1.0 / (1.0 + ERF_P * jnp.abs(a))
    tail = ((((ERF[4] * t + ERF[3]) * t + ERF[2]) * t + ERF[1]) * t + ERF[0]) * t * bell
    share = jnp.where(a < 0, tail, 1.0 - tail)
    return a * share, share + a * bell * INV_SQRT_2PI


def attn_fwd_kernel(count, batch, owner_ref, p_ref, r_ref, w_ref, vec_ref, _,
                    x1_ref, q_ref, k_ref, v_ref, o_ref, pt_ref, q_held, k_held, v_held, o_held):
    total = count * LIVE
    owner = owner_ref[0, 0]

    @pl.when(pl.program_id(0) == 0)
    def _():
        for ref in (q_held, k_held, v_held):
            ref[:, total:] = jnp.zeros((4, ref.shape[1] - total, GROUP), F32)

    x = jnp.concatenate([p_ref[...].astype(F32), r_ref[...][None]], axis=0).reshape(total, D)
    vec = vec_ref[...]
    xhat, _ = norm_parts(x)
    xn = (xhat * vec[0:1] + vec[1:2]).astype(BF)
    hold(q_held, total, nn(xn, w_ref[owner ^ 0]) + vec[4:5])
    hold(k_held, total, nn(xn, w_ref[owner ^ 1]))
    hold(v_held, total, nn(xn, w_ref[owner ^ 2]) + vec[5:6])
    masks = head_masks()
    live = lax.broadcasted_iota(jnp.int32, (8, 1), 0) < LIVE - (ROWS - 8)

    def score(w, g):
        lanes = slice(GROUP * g, GROUP * (g + 1))
        q = q_held[g, pl.ds(w, QUERIES, stride=count), :].astype(BF)
        q_ref[w, :, lanes] = q
        k = k_held[g, pl.ds(w, ROWS, stride=count), :].astype(BF)
        k_ref[w, :, lanes] = k
        return nt(k, spread_low(q))

    def normalize(w, g, s):
        s = jnp.concatenate([s[: ROWS - 8], jnp.where(live, s[ROWS - 8 :], MASKED)], axis=0)
        e = jnp.exp2((s - jnp.max(s, axis=0, keepdims=True)) * (SCALE * LOG2E))
        p = (e * (1.0 / jnp.sum(e, axis=0, keepdims=True))).astype(BF)
        pt_ref[w, g] = p
        return p

    def mix(w, g, p):
        lanes = slice(GROUP * g, GROUP * (g + 1))
        rows = pl.ds(w, ROWS, stride=count)
        v = v_held[g, rows, :].astype(BF)
        v_ref[w, :, lanes] = v
        o_held[g, rows, :] = collect(tn(p, v), masks, ROWS, QUERIES)

    staggered(count, batch, score, normalize, mix)
    mixed = held_rows(o_held, total).astype(BF)
    o_ref[...] = mixed.reshape(LIVE, count, D)
    x1_ref[...] = (x + nn(mixed, w_ref[owner ^ 3]) + vec[6:7]).reshape(LIVE, count, D)


def middle(rows, count, skip=0):
    return pl.BlockSpec((rows, count, D), lambda i: (0, i + skip, 0))


def attn_fwd(owner, patches, region_rows, weights, vec, after, count=16, batch=16):
    windows = patches.shape[1]
    array = jax.ShapeDtypeStruct
    return pl.pallas_call(
        partial(attn_fwd_kernel, count, batch),
        grid=(windows // count,),
        in_specs=[pl.BlockSpec(memory_space=pltpu.SMEM), middle(PATCH, count), block((count, D)), full((4, D, D)),
                  full(vec.shape), pl.BlockSpec(memory_space=pl.ANY)],
        out_specs=[middle(LIVE, count), block((count, QUERIES, D))] + [block((count, ROWS, D))] * 2
        + [middle(LIVE, count), block((count, 4, ROWS, STACK))],
        out_shape=[array((LIVE, windows, D), F32), array((windows, QUERIES, D), BF)]
        + [array((windows, ROWS, D), BF)] * 2
        + [array((LIVE, windows, D), BF), array((windows, 4, ROWS, STACK), BF)],
        scratch_shapes=[pltpu.VMEM((4, count * QUERIES, GROUP), F32)] + [pltpu.VMEM((4, count * ROWS, GROUP), F32)] * 3,
        compiler_params=pltpu.CompilerParams(vmem_limit_bytes=VMEM),
        cost_estimate=cost(16e9),
        name="window_attention_forward",
    )(owner, patches, region_rows, weights, vec, after)


def mlp_kernel(many, sources, cols, steps, lanes, last, *refs):
    x1_ref, pc_ref, *w_refs, vec_ref, b1_ref = refs[:8]
    if last:
        prev_refs = refs[9:11]
        op_ref, dx1_ref, dwa_ref, dwb_ref, dv_ref, db1_ref, acc1, acc2 = refs[11:]
    else:
        prev_refs = ()
        early_ref, op_ref, dx1_ref, dwa_ref, dwb_ref, dv_ref, db1_ref, acc1, acc2 = refs[8:]
    total = many * sources * cols
    step = pl.program_id(0)

    @pl.when(step == 0)
    def _():
        for ref in (dv_ref, db1_ref):
            ref[...] = jnp.zeros_like(ref)

    vec = vec_ref[...]
    gain = vec[2:3]
    x1 = x1_ref[...].reshape(total, D)
    xhat, scale = norm_parts(x1)
    h = (xhat * gain + vec[3:4]).astype(BF)
    for s in range(sources):
        dx1_ref[:, s * cols : (s + 1) * cols] = pc_ref[s].astype(F32)
    dy = dx1_ref[...].reshape(total, D)
    dm = dy.astype(BF)
    ht = h.T
    dmt = dm.T
    y = x1 + vec[7:8]
    dh = jnp.zeros((total, D), F32)
    parts = [(j, slice(c, c + lanes)) for j in range(4) for c in range(0, D, lanes)]

    def activate(j, s):
        u, slope = gelu_parts(nn(h, w_refs[j][0, :, s]) + b1_ref[j : j + 1, s])
        da = slope * nt(dm, w_refs[j][1, s, :])
        db1_ref[j, :, s] += fold(da)
        return u.astype(BF), da.astype(BF)

    def apply(j, s, u, da):
        acc1[j, :, s] = jnp.where(step == 0, 0.0, acc1[j, :, s]) + nn(ht, da)
        acc2[j, :, s] = jnp.where(step == 0, 0.0, acc2[j, :, s]) + nn(dmt, u)
        return nn(u, w_refs[j][1, s, :]), nt(da, w_refs[j][0, :, s])

    held_pair = activate(*parts[0])
    for n in range(1, len(parts) + 1):
        later = activate(*parts[n]) if n < len(parts) else None
        up, down = apply(*parts[n - 1], *held_pair)
        y, dh = y + up, dh + down
        held_pair = later
    y = y.reshape(many, sources * cols, D)

    def put(ref):
        for s in range(sources):
            ref[s] = y[:, s * cols : (s + 1) * cols].astype(BF)

    if last:
        put(op_ref)
    else:
        pl.when(step < steps - 1)(lambda: put(early_ref))
        pl.when(step == steps - 1)(lambda: put(op_ref))
    dy = dx1_ref[...].reshape(total, D)
    dx1_ref[...] = (dy + norm_back(dh, xhat, scale, gain)).reshape(dx1_ref.shape)
    dv_ref[0] += fold(dh * xhat)
    dv_ref[1] += fold(dh)
    dv_ref[2] += fold(dy)

    @pl.when(step == steps - 1)
    def _():
        for refs_out, first in ((dwa_ref, 0), (dwb_ref, 1)):
            for n, acc in enumerate((acc1, acc2)):
                for m in range(2):
                    piece = acc[first + 2 * m]
                    for prev in prev_refs[first : first + 1]:
                        piece = piece + prev[2 * m + n].astype(F32)
                    refs_out[2 * m + n] = piece.astype(BF)


def mlp(x1, first_position, cot, weights, vec, bias_first, prev=(), many=10, lanes=256):
    sources, positions, cols, _ = cot.shape
    windows = sources * cols
    steps = positions // many
    skip = first_position // many
    some = lambda place: pl.BlockSpec((sources, many, cols, D), lambda i: (0, place(i), 0, 0))
    array = jax.ShapeDtypeStruct
    matrices = full((4, D, D))
    rows = lambda count: array((sources, count, cols, D), BF)
    late = (LIVE - positions if not prev else positions) + many
    outs = [some(lambda i: i + 1)] if prev else [some(lambda i: jnp.minimum(i, steps - 2)), some(lambda i: 0)]
    shapes = [rows(late)] if prev else [rows(positions - many), rows(late)]
    return pl.pallas_call(
        partial(mlp_kernel, many, sources, cols, steps, lanes, len(prev) > 0),
        grid=(steps,),
        in_specs=[pl.BlockSpec((many, windows, D), lambda i: (i + skip, 0, 0)), some(lambda i: i)]
        + [full((2, D, D))] * 4 + [full(vec.shape), full((4, D))]
        + ([pl.BlockSpec(memory_space=pl.ANY)] + [matrices] * 2 if prev else []),
        out_specs=outs + [block((many, windows, D)), matrices, matrices, full((3, 8, D)), full((4, 8, D))],
        out_shape=shapes + [array((positions, windows, D), F32), array((4, D, D), BF),
                            array((4, D, D), BF), array((3, 8, D), F32), array((4, 8, D), F32)],
        scratch_shapes=[pltpu.VMEM((4, D, D), F32), pltpu.VMEM((4, D, D), F32)],
        input_output_aliases={8: 0} if prev else {},
        compiler_params=pltpu.CompilerParams(vmem_limit_bytes=VMEM),
        cost_estimate=cost(4e9 * steps),
        name="mlp_forward_backward",
    )(x1, cot, *weights, vec, bias_first, *prev)


def attn_bwd_kernel(count, batch, chunks, more, owner_ref, *refs):
    p_ref, r_ref = refs[:2]
    refs = refs[:3] + refs[4:]
    dx1_refs = refs[3 : 3 + chunks]
    q_ref, k_ref, v_ref, o_ref, pt_ref, w_ref, vec_ref = refs[3 + chunks : 10 + chunks]
    owner = owner_ref[0, 0]
    prev_refs = refs[10 + chunks : 14 + chunks] if more else ()
    dp_ref, dr_ref, dw_ref, dv_ref, dq_held, dk_held, dvv_held, do_held = refs[10 + chunks + len(prev_refs) :]
    total = count * LIVE

    @pl.when(pl.program_id(0) == 0)
    def _():
        dw_ref[...] = prev_refs[2][...] if more else jnp.zeros_like(dw_ref)
        dv_ref[...] = prev_refs[3][...] if more else jnp.zeros_like(dv_ref)
        do_held[:, total:] = jnp.zeros((4, count * (QUERIES - LIVE), GROUP), F32)

    vec = vec_ref[...]
    gain = vec[0:1]
    dx1 = jnp.concatenate([ref[...] for ref in dx1_refs], axis=0).reshape(total, D)
    gb = dx1.astype(BF)
    hold(do_held, total, nt(gb, w_ref[owner ^ 3]))
    masks = head_masks()

    def grad(w, g):
        lanes = slice(GROUP * g, GROUP * (g + 1))
        do_wide = spread_low(do_held[g, pl.ds(w, QUERIES, stride=count), :].astype(BF))
        dvv_held[g, pl.ds(w, ROWS, stride=count), :] = nn(pt_ref[w, g], do_wide)
        return nt(v_ref[w, :, lanes], do_wide)

    def score(w, g, grad):
        p = pt_ref[w, g].astype(F32)
        both = p * grad
        return (both - p * jnp.sum(both, axis=0, keepdims=True)).astype(BF)

    def finish(w, g, ds):
        lanes = slice(GROUP * g, GROUP * (g + 1))
        rows = pl.ds(w, ROWS, stride=count)
        dk_held[g, rows, :] = nn(ds, spread_low(q_ref[w, :, lanes])) * SCALE
        dq_held[g, rows, :] = collect(tn(ds, k_ref[w, :, lanes]), masks, ROWS, QUERIES) * SCALE

    staggered(count, batch, grad, score, finish)
    x = jnp.concatenate([p_ref[...].astype(F32), r_ref[...][None]], axis=0).reshape(total, D)
    xhat, scale = norm_parts(x)
    xn = (xhat * gain + vec[1:2]).astype(BF)
    dq_wide = held_rows(dq_held, total)
    dv_wide = held_rows(dvv_held, total)
    dq = dq_wide.astype(BF)
    dk = held_rows(dk_held, total).astype(BF)
    dv = dv_wide.astype(BF)
    dn = nt(dq, w_ref[owner ^ 0]) + nt(dk, w_ref[owner ^ 1]) + nt(dv, w_ref[owner ^ 2])
    dx = (dx1 + norm_back(dn, xhat, scale, gain)).reshape(LIVE, count, D)
    dp_ref[...] = dx[:PATCH].astype(BF)
    dr_ref[...] = dx[PATCH]
    xt = xn.T
    dw_ref[0] += nn(xt, dq)
    dw_ref[1] += nn(xt, dk)
    dw_ref[2] += nn(xt, dv)
    dw_ref[3] += nn(o_ref[...].reshape(total, D).T, gb)
    dv_ref[0] += fold(dn * xhat)
    dv_ref[1] += fold(dn)
    dv_ref[2] += fold(dq_wide)
    dv_ref[3] += fold(dv_wide)
    dv_ref[4] += fold(dx1)


def attn_bwd(owner, patches, region_rows, dx1_parts, saved, weights, vec, start, windows, after, prev=(), count=16, batch=16):
    skip = start // count
    array = jax.ShapeDtypeStruct
    sums = [full((4, D, D)), full((5, 8, D))]
    anywhere = pl.BlockSpec(memory_space=pl.ANY)
    rows = pl.BlockSpec((count, D), lambda i: (i + skip, 0))
    before = 12 + len(dx1_parts)
    return pl.pallas_call(
        partial(attn_bwd_kernel, count, batch, len(dx1_parts), len(prev) > 0),
        grid=(windows // count,),
        in_specs=[pl.BlockSpec(memory_space=pltpu.SMEM), middle(PATCH, count, skip), rows, anywhere, anywhere]
        + [middle(part.shape[0], count, skip) for part in dx1_parts]
        + [pl.BlockSpec((count, r, D), lambda i: (i + skip, 0, 0)) for r in (QUERIES, ROWS, ROWS)]
        + [middle(LIVE, count, skip), pl.BlockSpec((count, 4, ROWS, STACK), lambda i: (i + skip, 0, 0, 0))]
        + [full((4, D, D)), full(vec.shape)] + ([anywhere] * 2 + sums)[: len(prev)],
        out_specs=[middle(PATCH, count, skip), rows] + sums,
        out_shape=[array(patches.shape, BF), array(region_rows.shape, F32),
                   array((4, D, D), F32), array((5, 8, D), F32)],
        scratch_shapes=[pltpu.VMEM((4, count * ROWS, GROUP), F32)] * 3 + [pltpu.VMEM((4, count * QUERIES, GROUP), F32)],
        input_output_aliases={before: 0, before + 1: 1} if prev else {},
        compiler_params=pltpu.CompilerParams(vmem_limit_bytes=VMEM),
        cost_estimate=cost(12e9),
        name="window_attention_backward",
    )(owner, patches, region_rows, *after, *dx1_parts, *saved, weights, vec, *prev)


def regional_fwd_kernel(owner_ref, canvas_ref, band_ref, ids_ref, band_ids_ref, w_ref, vec_ref,
                        r1_ref, mixed_ref, level_ref, q_ref, k_ref, v_ref):
    vec = vec_ref[...]
    owner = owner_ref[0, 0]
    xhat, _ = norm_parts(canvas_ref[...].astype(F32))
    low = (xhat * vec[0:1] + vec[1:2]).astype(BF)
    q_ref[...] = (nn(low, w_ref[owner ^ 0]) + vec[4:5]).astype(BF)
    k_ref[...] = nn(low, w_ref[owner ^ 1]).astype(BF)
    v_ref[...] = (nn(low, w_ref[owner ^ 2]) + vec[5:6]).astype(BF)
    band = band_ref[...].astype(F32)
    rows = band.shape[0]
    xhat, _ = norm_parts(band)
    q = nn((xhat * vec[0:1] + vec[1:2]).astype(BF), w_ref[owner ^ 0]) + vec[4:5]
    masks = head_masks()
    same = ids_ref[...] == band_ids_ref[...]
    scores, probs = [], []
    for g in range(4):
        lanes = slice(GROUP * g, GROUP * (g + 1))
        scores.append(nt(k_ref[:, lanes], spread(q[:, lanes], masks)))
    for g, s in enumerate(scores):
        s = jnp.where(same, s, MASKED)
        peak = jnp.max(s, axis=0, keepdims=True)
        e = jnp.exp((s - peak) * SCALE)
        sums = jnp.sum(e, axis=0, keepdims=True)
        level_ref[g : g + 1] = peak * SCALE + jnp.log(sums)
        probs.append((e * (1.0 / sums)).astype(BF))
    for g, p in enumerate(probs):
        lanes = slice(GROUP * g, GROUP * (g + 1))
        mixed_ref[:, lanes] = collect(tn(p, v_ref[:, lanes]), masks, rows)
    r1_ref[...] = band + nn(mixed_ref[...].astype(BF), w_ref[owner ^ 3]) + vec[6:7]


def in_vmem(kernel, outs, name, *args, after=(), scratch=(), flops=2e9):
    spaces = [pltpu.SMEM if arg.shape == (1, 1) else pltpu.VMEM for arg in args]
    count = len(args)
    return pl.pallas_call(
        lambda *refs: kernel(*refs[:count], *refs[count + len(after) :]),
        in_specs=[pl.BlockSpec(memory_space=space) for space in spaces]
        + [pl.BlockSpec(memory_space=pl.ANY) for _ in after],
        out_specs=[pl.BlockSpec(memory_space=pltpu.VMEM) for _ in outs],
        out_shape=[jax.ShapeDtypeStruct(*out) for out in outs],
        scratch_shapes=list(scratch),
        compiler_params=pltpu.CompilerParams(vmem_limit_bytes=VMEM),
        cost_estimate=cost(flops),
        name=name,
    )(*args, *after)


def payload_kernel(owner_ref, dr_ref, mixed_ref, level_ref, w_ref, grad_ref, extra_ref):
    low = dr_ref[...].astype(BF)
    grad_ref[...] = low
    both = nt(low, w_ref[owner_ref[0, 0] ^ 3]).astype(BF).astype(F32) * mixed_ref[...]
    head = lax.broadcasted_iota(jnp.int32, (D, GROUP), 0) // HEAD_DIM
    lane = lax.broadcasted_iota(jnp.int32, (D, GROUP), 1)
    pick = ((head == lane) | (head + HEADS == lane)).astype(BF)
    high, low_part = halves(both)
    rest = (both - high.astype(F32) - low_part.astype(F32)).astype(BF)
    delta = nn(high, pick) + (nn(low_part, pick) + nn(rest, pick))
    top = delta.astype(BF).astype(F32)
    lane = lax.broadcasted_iota(jnp.int32, (1, GROUP), 1)
    level = level_ref[...]
    level_top = level.astype(BF).astype(F32)
    level_rest = level - level_top
    level_mid = level_rest.astype(BF).astype(F32)
    extra = level_rest - level_mid
    for place, term in ((4, level_mid), (3, level_top), (2, delta - top), (1, top)):
        extra = jnp.where(lane < place * HEADS, term, extra)
    extra_ref[...] = extra.astype(BF)


def regional_bwd_kernel(own_rows, owner_ref, place_ref, q_ref, k_ref, v_ref, canvas_ref, grads_ref, extra_ref, ids_ref,
                        ids_row_ref, ids_own_ref, ids_own_row_ref, mixed_ref, band_grad_ref, dw_ref, w_ref, vec_ref,
                        dr_ref, keep_ref, give_ref, gv_ref, sum_held):
    vec = vec_ref[...]
    owner = owner_ref[0, 0]
    mine = pl.ds(pl.multiple_of(place_ref[0, 0] * own_rows, own_rows), own_rows)
    masks = head_masks()
    grads_own = grads_ref[mine]
    do = nt(grads_ref[...], w_ref[owner ^ 3]).astype(BF).astype(F32)
    do_own = nt(grads_own, w_ref[owner ^ 3]).astype(BF).astype(F32)
    same_own = ids_ref[...] == ids_own_row_ref[...]
    same = ids_own_ref[...] == ids_row_ref[...]
    lanes = [slice(GROUP * g, GROUP * (g + 1)) for g in range(4)]

    def columns(rows):
        term = rows.astype(F32).T
        part = lambda n: term[n * HEADS : (n + 1) * HEADS]
        wide = lambda x: [jnp.concatenate([x[h : h + 1] for h in range(4 * g, 4 * g + 4)], axis=1) for g in range(4)]
        return wide(part(0) + part(1)), wide(part(2) + part(3) + part(4))

    delta, level = columns(extra_ref[...])
    delta_own, level_own = columns(extra_ref[mine])
    first, second = [], []
    dqs, dks, dvs = [], [], []
    for g in range(4):
        q_wide = spread(q_ref[mine, lanes[g]].astype(F32), masks)
        do_wide = spread(do_own[:, lanes[g]], masks)
        first.append((nt(k_ref[:, lanes[g]], q_wide), nt(v_ref[:, lanes[g]], do_wide)))
        q_wide = spread(q_ref[:, lanes[g]].astype(F32), masks)
        do_wide = spread(do[:, lanes[g]], masks)
        second.append((nt(k_ref[mine, lanes[g]], q_wide), nt(v_ref[mine, lanes[g]], do_wide), q_wide, do_wide))
    for g in range(4):
        s, dp = first[g]
        p = jnp.where(same_own, jnp.exp(s * SCALE - level_own[g]), 0.0)
        ds = (p * (dp - delta_own[g])).astype(BF)
        dqs.append(collect(tn(ds, k_ref[:, lanes[g]]), masks, own_rows) * SCALE)
        s, dp, q_wide, do_wide = second[g]
        p = jnp.where(same, jnp.exp(s * SCALE - level[g]), 0.0)
        ds = (p * (dp - delta[g])).astype(BF)
        dvs.append(nn(p.astype(BF), do_wide))
        dks.append(nn(ds, q_wide) * SCALE)
    xhat, scale = norm_parts(canvas_ref[mine].astype(F32))
    low = (xhat * vec[0:1] + vec[1:2]).astype(BF)
    dq_wide, dk_wide, dv_wide = (jnp.concatenate(x, axis=1) for x in (dqs, dks, dvs))
    dq, dk, dv = dq_wide.astype(BF), dk_wide.astype(BF), dv_wide.astype(BF)
    dn = nt(dq, w_ref[owner ^ 0]) + nt(dk, w_ref[owner ^ 1]) + nt(dv, w_ref[owner ^ 2])
    dr_ref[...] = grads_own.astype(F32) + norm_back(dn, xhat, scale, vec[0:1])
    sum_held[0] = dw_ref[0] + tn(low, dq)
    sum_held[1] = dw_ref[1] + tn(low, dk)
    sum_held[2] = dw_ref[2] + tn(low, dv)
    sum_held[3] = dw_ref[3] + tn(mixed_ref[...].astype(BF), band_grad_ref[...])
    for n in range(2):
        keep_ref[n] = sum_held[owner ^ (2 * n)].astype(BF)
        give_ref[n] = sum_held[owner ^ (2 * n + 1)].astype(BF)
    gv_ref[0] = fold(dn * xhat)
    gv_ref[1] = fold(dn)
    gv_ref[2] = fold(dq_wide)
    gv_ref[3] = fold(dv_wide)
    gv_ref[4] = fold(band_grad_ref[...].astype(F32))


def halves(a):
    high = a.astype(BF)
    return high, (a - high.astype(F32)).astype(BF)


def terms(a, passes):
    return (a.astype(BF),) if passes == 1 else halves(a)


def product(a, b, dot=nn):
    if len(a) == 1:
        return dot(a[0], b[0])
    return dot(a[0], b[0]) + (dot(a[0], b[1]) + dot(a[1], b[0]))


def symmetric(a, b, dot=nn):
    half = D // 2
    right = (lambda x: x[half:]) if dot is nt else (lambda x: x[:, half:])
    top = product([x[:half] for x in a], b, dot)
    corner = product([x[half:] for x in a], [right(x) for x in b], dot)
    return jnp.concatenate([top, jnp.concatenate([top[:, half:].T, corner], axis=1)], axis=0)


DIRECT_STEPS = (1, 1, 1, -1, -1)
GRAM_STEPS = (1, 1, 3, 3, 3)
NEAR_ZERO = NS_FIRST + NS_SECOND + NS_THIRD
NEAR_ONE = NS_SECOND + 2.0 * NS_THIRD


def identity():
    rows = lax.broadcasted_iota(jnp.int32, (D, D), 0)
    return rows == lax.broadcasted_iota(jnp.int32, (D, D), 1)


def polynomial(gram, eye, step):
    if step > 0:
        parts = terms(gram, step)
        return NS_FIRST, NS_SECOND * gram + NS_THIRD * symmetric(parts, parts)
    rest = gram - jnp.where(eye, 1.0, 0.0)
    parts = terms(rest, -step)
    return NEAR_ZERO, NEAR_ONE * rest + NS_THIRD * symmetric(parts, parts)


def direct_steps(moment, eye):
    z = moment * (1.0 / (jnp.sqrt(jnp.sum(moment * moment)) + 1e-07))
    for step in DIRECT_STEPS:
        parts = terms(z, abs(step))
        gram = symmetric(parts, parts, nt)
        yield
        scale, poly = polynomial(gram, eye, step)
        yield
        z = scale * z + product(terms(poly, abs(step)), parts)
        yield
    return z


def gram_steps(gram, eye):
    factor = 1.0 / (jnp.sqrt(jnp.sum(jnp.where(eye, gram, 0.0))) + 1e-07)
    gram = gram * (factor * factor)
    steps = None
    for n, passes in enumerate(GRAM_STEPS):
        scale, poly = polynomial(gram, eye, passes)
        yield
        parts = terms(poly, passes)
        if steps is None:
            steps = jnp.where(eye, scale, 0.0) + poly
        else:
            steps = scale * steps + symmetric(parts, terms(steps, passes))
            yield
        if n < len(GRAM_STEPS) - 1:
            half = scale * gram + symmetric(parts, terms(gram, passes))
            yield
            gram = scale * half + symmetric(parts, terms(half, passes))
            yield
    return steps * factor


def in_turns(*chains):
    results = [None] * len(chains)
    running = list(enumerate(chains))
    while running:
        still = []
        for n, chain in running:
            try:
                next(chain)
                still.append((n, chain))
            except StopIteration as stop:
                results[n] = stop.value
        running = still
    return results


def old_grams_kernel(moms_ref, *out_refs):
    for n, out_ref in enumerate(out_refs):
        square, cross = jnp.zeros((D, D), F32), jnp.zeros((D, D), F32)
        for j in range(OPT):
            high, low = halves(moms_ref[j, n])
            if n == 1:
                high, low = high.T, low.T
            square = square + nt(high, high)
            cross = cross + nt(high, low)
        out_ref[...] = square + (cross + cross.T)


def grams_kernel(places, owner_ref, moms_ref, all_ref, mixed1_ref, new1_ref, mixed2_ref, new2_ref, own_ref,
                 squares_ref):
    half = len(places) // 2
    squares = jnp.zeros((8, D), F32)
    for n, (mixed_ref, new_ref) in enumerate(((mixed1_ref, new1_ref), (mixed2_ref, new2_ref))):
        mixed, new = jnp.zeros((D, D), F32), jnp.zeros((D, D), F32)
        mine = places[n * half : (n + 1) * half]
        for j in range(OPT):
            high, low = halves(moms_ref[j, n])
            if n == 1:
                high, low = high.T, low.T
            g = jnp.concatenate([all_ref[d, j] for d in mine], axis=0)
            wide = g.astype(F32)
            squares = squares + fold(wide * wide)
            mixed = mixed + (nt(high, g) + nt(low, g))
            new = new + nt(g, g)
        mixed_ref[...] = mixed + mixed.T
        new_ref[...] = new
        own_ref[n] = jnp.concatenate([all_ref[d, owner_ref[0, 0]] for d in mine], axis=0)
    squares_ref[...] = jnp.full((8, 128), jnp.sum(squares))


def update_kernel(clip_ref, ga_ref, ma_ref, wa_ref, g_ref, m1_ref, m2_ref, w1_ref, w2_ref,
                  old1, mixed1, new1, old2, mixed2, new2, na_ref, newa_ref, n1_ref, new1_ref, n2_ref, new2_ref):
    clip = clip_ref[0, 0]
    eye = identity()
    na_ref[...] = MUON_MOMENTUM * ma_ref[...] + clip * ga_ref[...].astype(F32)
    n1_ref[...] = MUON_MOMENTUM * m1_ref[...] + clip * g_ref[0].astype(F32)
    n2_ref[...] = MUON_MOMENTUM * m2_ref[...] + clip * g_ref[1].astype(F32).T
    a, b, c = MUON_MOMENTUM * MUON_MOMENTUM, MUON_MOMENTUM * clip, clip * clip
    gram1 = a * old1[...] + b * mixed1[...] + c * new1[...]
    gram2 = a * old2[...] + b * mixed2[...] + c * new2[...]
    steps1, steps2, z = in_turns(gram_steps(gram1, eye), gram_steps(gram2, eye), direct_steps(na_ref[...], eye))
    newa_ref[...] = wa_ref[...] * DECAY_KEEP - MUON_RATE * z
    z = product(halves(steps1), halves(n1_ref[...]))
    new1_ref[...] = w1_ref[...] * DECAY_KEEP - MUON_RATE * z
    z = product(halves(n2_ref[...]), halves(steps2))
    new2_ref[...] = w2_ref[...] * DECAY_KEEP - (MUON_RATE * max(1.0, FF / D) ** 0.5) * z


def pair(values, bit):
    return lax.ppermute(values, "opt", [(i, i ^ bit) for i in range(OPT)])


def fence(x, *first):
    here = pl.BlockSpec(memory_space=pl.ANY)
    return pl.pallas_call(
        lambda *refs: None,
        in_specs=[here] * (1 + len(first)),
        out_specs=here,
        out_shape=jax.ShapeDtypeStruct(x.shape, x.dtype),
        input_output_aliases={0: 0},
        cost_estimate=cost(1e3),
        name="fence",
    )(x, *first)


def pieces_of_owners(own):
    mate = pair(own, 1)
    across = pair(own, 2)
    return [own, mate, across, pair(across, 1)]


def share(x, *first):
    copies = jnp.broadcast_to(x[None], (lax.axis_size("dp"),) + x.shape)
    if first:
        copies = fence(copies, *first)
    return lax.all_to_all(copies, "dp", 0, 0, tiled=True)


def swap(x, bit):
    return lax.ppermute(x, "dp", [(i, i ^ bit) for i in range(lax.axis_size("dp"))])


def bits():
    return [1 << n for n in range(lax.axis_size("dp").bit_length() - 1)]


def halving_step(x, bit):
    half = x.shape[0] // 2
    side = (lax.axis_index("dp") // bit) % 2
    give = lax.dynamic_slice_in_dim(x, (1 - side) * half, half, 0).astype(BF)
    return lax.dynamic_slice_in_dim(x, side * half, half, 0), give


def order_of_halves(count):
    width = count.bit_length() - 1
    return [int(format(n, "b").zfill(width)[::-1], 2) if width else 0 for n in range(count)]


def sum_small_over_dp(x):
    for bit in bits():
        x = x + swap(x, bit)
    return x


def split_heads(x):
    return x.reshape(x.shape[0], HEADS, HEAD_DIM)


def regional_forward(canvas, band, same, weights, vec):
    low = lambda x: (norm_parts(x.astype(F32))[0] * vec[0] + vec[1]).astype(BF)
    normed = low(canvas)
    queries = (nn(normed, weights[0]) + vec[4]).astype(BF)
    keys = nn(normed, weights[1]).astype(BF)
    values = (nn(normed, weights[2]) + vec[5]).astype(BF)
    own = (nn(low(band), weights[0]) + vec[4]).astype(BF)
    scores = jnp.einsum("qhd,khd->hqk", split_heads(own), split_heads(keys), preferred_element_type=F32)
    scores = jnp.where(same[None], scores * SCALE, MASKED)
    peak = jnp.max(scores, axis=-1, keepdims=True)
    raised = jnp.exp(scores - peak)
    sums = jnp.sum(raised, axis=-1, keepdims=True)
    probs = (raised / sums).astype(BF)
    mixed = jnp.einsum("hqk,khd->qhd", probs, split_heads(values), preferred_element_type=F32).reshape(own.shape)
    region_rows = band.astype(F32) + nn(mixed.astype(BF), weights[3]) + vec[6]
    return region_rows, mixed, (peak + jnp.log(sums))[:, :, 0], queries, keys, values


def regional_terms(queries, keys, values, grad_mixed, same, level, delta):
    scores = jnp.einsum("qhd,khd->hqk", split_heads(queries), split_heads(keys), preferred_element_type=F32)
    probs = jnp.where(same[None], jnp.exp(scores * SCALE - level[:, :, None]), 0.0)
    grads = jnp.einsum("qhd,khd->hqk", split_heads(grad_mixed), split_heads(values), preferred_element_type=F32)
    return probs.astype(BF), (probs * (grads - delta[:, :, None])).astype(BF)


def regional_backward(queries, keys, values, grads, own, rows, same, level, delta, weights, vec, mixed, band_grad, dw):
    grad_mixed = nt(grads, weights[3]).astype(BF)
    level_own, delta_own = own(level.T).T, own(delta.T).T
    _, scores = regional_terms(own(queries), keys, values, own(grad_mixed), same.T, level_own, delta_own)
    dq = jnp.einsum("hqk,khd->qhd", scores, split_heads(keys), preferred_element_type=F32)
    probs, scores = regional_terms(queries, own(keys), own(values), grad_mixed, same, level, delta)
    dk = jnp.einsum("hqk,qhd->khd", scores, split_heads(queries), preferred_element_type=F32)
    dv = jnp.einsum("hqk,qhd->khd", probs, split_heads(grad_mixed), preferred_element_type=F32)
    flat = lambda x: x.reshape(-1, D)
    dq, dk, dv = flat(dq) * SCALE, flat(dk) * SCALE, flat(dv)
    lows = [x.astype(BF) for x in (dq, dk, dv)]
    dn = sum(nt(x, w) for x, w in zip(lows, weights))
    xhat, scale = norm_parts(rows.astype(F32))
    low = (xhat * vec[0] + vec[1]).astype(BF)
    d_regions = own(grads).astype(F32) + norm_back(dn, xhat, scale, vec[0])
    matrices = [dw[j] + tn(low, x) for j, x in enumerate(lows)] + [dw[3] + tn(mixed.astype(BF), band_grad)]
    vectors = [fold(x) for x in (dn * xhat, dn, dq, dv, band_grad.astype(F32))]
    return d_regions, jnp.stack(matrices).astype(BF), jnp.stack(vectors)


def per_device(patches, regions, image_ids, attn_w, mlp_in, mlp_out, vec_params, patch_cot, region_cot,
               attn_mom, mlp_in_mom, mlp_out_mom, adam_first, adam_second):
    dp_size = lax.axis_size("dp")
    dp_index = lax.axis_index("dp")
    opt_index = lax.axis_index("opt")
    _, grid_rows, cols, _, _ = patch_cot.shape
    grid_cols = patches.shape[2]
    tokens = grid_rows * grid_cols
    own_count = grid_rows * cols
    one_kernel = tokens <= 1024
    vec = vec_params
    order = opt_index ^ jnp.arange(OPT)
    move = lambda x: lax.all_to_all(x, "dp", 0, 0, tiled=True)

    attn_low = attn_w[0].astype(BF)
    attn_pieces = jnp.stack(pieces_of_owners(attn_low))
    mlp_w = pieces_of_owners(jnp.stack([mlp_in, mlp_out]).astype(BF))
    owner = opt_index.reshape(1, 1)
    if not one_kernel:
        weights = [lax.dynamic_index_in_dim(attn_pieces, opt_index ^ j, 0, keepdims=False) for j in range(OPT)]
    canvas_blocks = share(regions[0], attn_low)
    canvas = canvas_blocks.reshape(tokens, D)
    by_position = patch_cot[0].transpose(0, 2, 1, 3)
    split = 30
    last = jnp.concatenate([by_position[:, split:], region_cot[0][:, None]], axis=1)
    first_cot = move(fence(by_position[:, :split], canvas))
    bias_first = jnp.take(vec[8:], order, axis=0)

    band_of = lambda x: lax.dynamic_slice_in_dim(x, dp_index, 1, 1).reshape((grid_cols,) + x.shape[3:])
    own_of = lambda x: lax.dynamic_slice_in_dim(x, dp_index * own_count, own_count, 0)
    ids_blocks = image_ids[0].reshape(grid_rows, dp_size, cols).transpose(1, 0, 2)
    ids = ids_blocks.reshape(tokens)
    band_ids, own_ids = band_of(ids_blocks), own_of(ids)
    band = band_of(canvas_blocks)
    if one_kernel:
        repeat = lambda x: jnp.tile(x, 4)[None]
        region_rows, mixed, level, reg_q, reg_k, reg_v = in_vmem(
            regional_fwd_kernel,
            [((grid_cols, D), F32), ((grid_cols, D), F32), ((4, 4 * grid_cols), F32)] + [((tokens, D), BF)] * 3,
            "regional_attention_forward", owner, canvas, band, ids[:, None], repeat(band_ids), attn_pieces, vec)
        level = level.reshape(HEADS, grid_cols)
    else:
        region_rows, mixed, level, reg_q, reg_k, reg_v = regional_forward(
            canvas, band, band_ids[:, None] == ids[None, :], weights, vec)
    level_wide = jnp.tile(level.T, (1, GROUP // HEADS))

    windows = patches[0, 0].transpose(1, 0, 2)
    some = grid_cols // 2
    x1, *saved = attn_fwd(owner, windows, region_rows, attn_pieces, vec, mlp_w[2])
    last_cot = move(fence(last, x1))
    early_out, late_out, dx1_a, *grads_a = mlp(x1, 0, first_cot, mlp_w, vec, bias_first)
    moved_a = move(early_out)
    moms = lax.all_gather(fence(jnp.stack([mlp_in_mom, mlp_out_mom]), x1), "opt", axis=0)
    late_out, dx1_b, *grads_b = mlp(x1, split, last_cot, mlp_w, vec, bias_first, prev=(late_out, *grads_a[:2]))
    near = pair(fence(grads_b[1], moved_a), 1)
    far = (near[2:].astype(F32) + grads_b[0][2:].astype(F32)).astype(BF)
    moved_b = move(fence(late_out, far))
    out_patches = jnp.concatenate([moved_a, moved_b[:, :-1]], axis=1).transpose(0, 2, 1, 3)[None]
    out_regions = moved_b[None, :, -1]

    dx1 = (dx1_a, dx1_b)
    early = attn_bwd(owner, windows, region_rows, dx1, saved, attn_pieces, vec, 0, some, (far, far))
    own_mlp = near[:2].astype(F32) + grads_b[0][:2].astype(F32) + fence(pair(far, 2), early[3]).astype(F32)
    keep, give = halving_step(own_mlp.reshape(2 * D, D), 1)
    d_patches, d_region, d_attn, d_vec_attn = attn_bwd(
        owner, windows, region_rows, dx1, saved, attn_pieces, vec, some, some, (give, moms), prev=early)
    d_patches = d_patches.transpose(1, 0, 2)[None, None]
    gives = []
    band_grad, extra = in_vmem(payload_kernel, [((grid_cols, D), BF), ((grid_cols, GROUP), BF)],
                               "regional_payload", owner, d_region, mixed, level_wide, attn_pieces,
                               after=(give, moved_b))
    taken = fence(swap(give, 1), band_grad)
    for bit in bits()[1:]:
        keep, give = halving_step(keep + taken.astype(F32), bit)
        gives.append(give)
        taken = swap(give, bit)
    payload = share(jnp.concatenate([band_grad, extra], axis=1)).reshape(grid_rows, dp_size, cols, D + GROUP)
    payload = payload.transpose(1, 0, 2, 3).reshape(tokens, D + GROUP)
    grads = payload[:, :D]
    extra = payload[:, D:]
    if one_kernel:
        matrices = ((2, D, D), BF)
        d_regions, keep_attn, give_attn, d_vec_reg = in_vmem(
            partial(regional_bwd_kernel, own_count),
            [((own_count, D), F32), matrices, matrices, ((5, 8, D), F32)],
            "regional_attention_backward", owner, dp_index.reshape(1, 1), reg_q, reg_k, reg_v, canvas, grads, extra,
            ids[:, None], repeat(ids), own_ids[:, None], repeat(own_ids), mixed, band_grad, d_attn, attn_pieces, vec,
            scratch=[pltpu.VMEM((4, D, D), F32)], flops=4e9)
    else:
        part = lambda n: extra[:, n * HEADS : (n + 1) * HEADS].astype(F32)
        delta, level = (part(0) + part(1)).T, (part(2) + part(3) + part(4)).T
        d_regions, grad_attn, d_vec_reg = regional_backward(
            reg_q, reg_k, reg_v, grads, own_of, own_of(canvas), ids[:, None] == own_ids[None, :], level, delta,
            weights, vec, mixed, band_grad, d_attn)
        pick = lambda j: lax.dynamic_index_in_dim(grad_attn, opt_index ^ j, 0, keepdims=False)
        keep_attn, give_attn = jnp.stack([pick(0), pick(2)]), jnp.stack([pick(1), pick(3)])
    d_regions = d_regions.reshape(regions.shape)

    d_vec_attn = jnp.sum(d_vec_attn + d_vec_reg, axis=1)
    d_vec_mlp = jnp.sum(grads_a[2] + grads_b[2], axis=1)
    d_bias_first = jnp.take(jnp.sum(grads_a[3] + grads_b[3], axis=1), order, axis=0)
    grad_vec = jnp.concatenate([d_vec_attn[:2], d_vec_mlp[:2], d_vec_attn[2:], d_vec_mlp[2:], d_bias_first])
    grad_vec = grad_vec + pair(grad_vec, 1)
    grad_vec = grad_vec + pair(grad_vec, 2)
    grad_vec = sum_small_over_dp(grad_vec)

    piece_mlp = (keep + fence(taken, give_attn).astype(F32)).astype(BF)

    old_grams = in_vmem(old_grams_kernel, [((D, D), F32)] * 2, "momentum_grams", moms, after=(d_regions,),
                         flops=8e9)

    near = pair(give_attn, 1)
    far = (near[1].astype(F32) + keep_attn[1].astype(F32)).astype(BF)
    piece_attn = near[0].astype(F32) + keep_attn[0].astype(F32) + pair(far, 2).astype(F32)
    piece_attn = move(piece_attn.astype(BF).reshape(dp_size, D // dp_size, D))
    piece_attn = jnp.sum(fence(piece_attn, grad_vec).astype(F32), axis=0).astype(BF)
    shared_attn = share(piece_attn)
    all_mlp = lax.all_gather(piece_mlp, ("dp", "opt"), axis=0).reshape(dp_size, OPT, -1, D)
    *grams, own_mlp, mlp_squares = in_vmem(partial(grams_kernel, order_of_halves(dp_size)),
                                           [((D, D), F32)] * 4 + [((2, D, D), BF), ((8, 128), F32)], "mlp_grams", owner, moms, all_mlp, flops=4e9)
    grams = [old_grams[0], *grams[:2], old_grams[1], *grams[2:]]
    own_attn = fence(shared_attn, *old_grams).reshape(D, D)

    total = jnp.full((8, 128), jnp.sum(own_attn.astype(F32) ** 2))
    total = total + pair(total, 1)
    total = (total + pair(total, 2))[0, 0] + mlp_squares[0, 0]
    grad_norm = jnp.sqrt(total + jnp.sum(grad_vec * grad_vec))
    clip = jnp.minimum(1.0, CLIP_LIMIT / (grad_norm + 1e-06))
    attn_mom_new, new_attn, first_mom, new_first, second_mom, new_second = in_vmem(
        update_kernel, [((D, D), F32)] * 6, "matrix_updates", clip.reshape(1, 1), own_attn, attn_mom[0], attn_w[0],
        own_mlp, mlp_in_mom, mlp_out_mom, mlp_in, mlp_out, *grams, flops=12e9)
    clipped = clip * grad_vec
    moment_one = BETA_FIRST * adam_first + (1.0 - BETA_FIRST) * clipped
    moment_two = BETA_SECOND * adam_second + (1.0 - BETA_SECOND) * clipped * clipped
    first_hat = moment_one / (1.0 - BETA_FIRST**OPT_STEP)
    second_hat = moment_two / (1.0 - BETA_SECOND**OPT_STEP)
    new_vec = vec_params - ADAM_RATE * first_hat / (jnp.sqrt(second_hat) + ADAM_EPS)
    return (out_patches, out_regions, d_patches, d_regions, new_attn[None], attn_mom_new[None], new_first, first_mom,
            new_second, second_mom, new_vec, moment_one, moment_two, grad_norm)


def solution(mesh):
    canvas = P("opt", None, "dp", None)
    wide = P("opt", None, "dp", None, None)
    bands = P("opt", "dp", None, None, None)
    square, right, down = P("opt", None, None), P(None, "opt"), P("opt", None)
    return jax.shard_map(
        per_device,
        mesh=mesh,
        in_specs=(bands, canvas, square, square, right, down, P(), wide, canvas, square, right, down, P(), P()),
        out_specs=(wide, canvas, bands, canvas, square, square, right, right, down, down, P(), P(), P(), P()),
        check_vma=False,
    )
```

```python
from functools import partial

import jax
import jax.numpy as jnp
from jax import lax
from jax.experimental import pallas as pl
from jax.experimental.pallas import tpu as pltpu
from jax.sharding import PartitionSpec as P

BF = jnp.bfloat16
F32 = jnp.float32

D = 512
HEADS = 16
HEAD_DIM = 32
FF = 2048
PATCH = 49
LIVE = 50
ROWS = 56
GROUP = 128
QUERIES = 64
STACK = 4 * QUERIES
OPT_STEP = 10
OPT = 4

SCALE = HEAD_DIM ** (-0.5)
NORM_EPS = 1e-05
MASKED = -1e30
NS_FIRST = 3.4445
NS_SECOND = -4.775
NS_THIRD = 2.0315
MUON_RATE = 0.5
MUON_MOMENTUM = 0.5
MUON_DECAY = 0.01
ADAM_RATE = 0.5
BETA_FIRST = 0.9
BETA_SECOND = 0.95
ADAM_EPS = 1e-08
CLIP_LIMIT = 1.0
DECAY_KEEP = 1.0 - MUON_RATE * MUON_DECAY
VMEM = 60 * 2**20


def cost(flops):
    return pl.CostEstimate(flops=int(flops), bytes_accessed=10**5, transcendentals=0)

ERF_P = 0.3275911 * 0.5**0.5
ERF = tuple(0.5 * c for c in (0.254829592, -0.284496736, 1.421413741, -1.453152027, 1.061405429))
INV_SQRT_2PI = 0.3989422804014327
LOG2E = 1.4426950408889634


def nn(a, b):
    return lax.dot_general(a, b, (((1,), (0,)), ((), ())), preferred_element_type=F32)


def nt(a, b):
    return lax.dot_general(a, b, (((1,), (1,)), ((), ())), preferred_element_type=F32)


def tn(a, b):
    return lax.dot_general(a, b, (((0,), (0,)), ((), ())), preferred_element_type=F32)


def full(shape):
    return pl.BlockSpec(shape, lambda i: (0,) * len(shape))


def block(shape):
    return pl.BlockSpec(shape, lambda i: (i,) + (0,) * (len(shape) - 1))


def norm_parts(x):
    centre = x - jnp.mean(x, axis=-1, keepdims=True)
    scale = lax.rsqrt(jnp.mean(centre * centre, axis=-1, keepdims=True) + NORM_EPS)
    return centre * scale, scale


def norm_back(grad, xhat, scale, gain):
    inner = grad * gain
    first = jnp.mean(inner, axis=-1, keepdims=True)
    second = jnp.mean(inner * xhat, axis=-1, keepdims=True)
    return scale * (inner - first - xhat * second)


def head_masks():
    lane = lax.broadcasted_iota(jnp.int32, (1, GROUP), 1) // HEAD_DIM
    return [lane == h for h in range(4)]


def spread(rows, masks):
    return jnp.concatenate([jnp.where(m, rows, 0.0) for m in masks], axis=0).astype(BF)


def spread_low(rows):
    lane = lax.broadcasted_iota(jnp.int32, (1, GROUP), 1) // HEAD_DIM
    return jnp.concatenate([rows * (lane == h).astype(F32).astype(BF) for h in range(4)], axis=0)


def collect(stacked, masks, rows, step=None):
    step = step or rows
    out = stacked[:rows]
    for h in range(1, 4):
        out = jnp.where(masks[h], stacked[h * step : h * step + rows], out)
    return out


def staggered(windows, batch, first, second, third):
    steps = [[(w, g) for w in range(n, n + batch) for g in range(4)] for n in range(0, windows, batch)]
    one, two = {}, {}
    for n in range(len(steps) + 2):
        if n < len(steps):
            one.update({unit: first(*unit) for unit in steps[n]})
        if 0 <= n - 1 < len(steps):
            two.update({unit: second(*unit, one.pop(unit)) for unit in steps[n - 1]})
        if 0 <= n - 2:
            for unit in steps[n - 2]:
                third(*unit, two.pop(unit))


def lane_groups(x):
    return [x[:, GROUP * g : GROUP * (g + 1)] for g in range(4)]


def hold(ref, total, x):
    for g, part in enumerate(lane_groups(x)):
        ref[g, :total] = part


def held_rows(ref, total):
    return jnp.concatenate([ref[g, :total] for g in range(4)], axis=1)


def fold(x):
    return jnp.sum(x.reshape(x.shape[0] // 8, 8, x.shape[1]), axis=0)


def gelu_parts(a):
    bell = jnp.exp2(a * a * (-0.5 * LOG2E))
    t = 1.0 / (1.0 + ERF_P * jnp.abs(a))
    tail = ((((ERF[4] * t + ERF[3]) * t + ERF[2]) * t + ERF[1]) * t + ERF[0]) * t * bell
    share = jnp.where(a < 0, tail, 1.0 - tail)
    return a * share, share + a * bell * INV_SQRT_2PI


def attn_fwd_kernel(count, batch, owner_ref, p_ref, r_ref, w_ref, vec_ref, _,
                    x1_ref, q_ref, k_ref, v_ref, o_ref, pt_ref, q_held, k_held, v_held, o_held):
    total = count * LIVE
    owner = owner_ref[0, 0]

    @pl.when(pl.program_id(0) == 0)
    def _():
        for ref in (q_held, k_held, v_held):
            ref[:, total:] = jnp.zeros((4, ref.shape[1] - total, GROUP), F32)

    x = jnp.concatenate([p_ref[...].astype(F32), r_ref[...][None]], axis=0).reshape(total, D)
    vec = vec_ref[...]
    xhat, _ = norm_parts(x)
    xn = (xhat * vec[0:1] + vec[1:2]).astype(BF)
    hold(q_held, total, nn(xn, w_ref[owner ^ 0]) + vec[4:5])
    hold(k_held, total, nn(xn, w_ref[owner ^ 1]))
    hold(v_held, total, nn(xn, w_ref[owner ^ 2]) + vec[5:6])
    masks = head_masks()
    live = lax.broadcasted_iota(jnp.int32, (8, 1), 0) < LIVE - (ROWS - 8)

    def score(w, g):
        lanes = slice(GROUP * g, GROUP * (g + 1))
        q = q_held[g, pl.ds(w, QUERIES, stride=count), :].astype(BF)
        q_ref[w, :, lanes] = q
        k = k_held[g, pl.ds(w, ROWS, stride=count), :].astype(BF)
        k_ref[w, :, lanes] = k
        return nt(k, spread_low(q))

    def normalize(w, g, s):
        s = jnp.concatenate([s[: ROWS - 8], jnp.where(live, s[ROWS - 8 :], MASKED)], axis=0)
        e = jnp.exp2((s - jnp.max(s, axis=0, keepdims=True)) * (SCALE * LOG2E))
        p = (e * (1.0 / jnp.sum(e, axis=0, keepdims=True))).astype(BF)
        pt_ref[w, g] = p
        return p

    def mix(w, g, p):
        lanes = slice(GROUP * g, GROUP * (g + 1))
        rows = pl.ds(w, ROWS, stride=count)
        v = v_held[g, rows, :].astype(BF)
        v_ref[w, :, lanes] = v
        o_held[g, rows, :] = collect(tn(p, v), masks, ROWS, QUERIES)

    staggered(count, batch, score, normalize, mix)
    mixed = held_rows(o_held, total).astype(BF)
    o_ref[...] = mixed.reshape(LIVE, count, D)
    x1_ref[...] = (x + nn(mixed, w_ref[owner ^ 3]) + vec[6:7]).reshape(LIVE, count, D)


def middle(rows, count, skip=0):
    return pl.BlockSpec((rows, count, D), lambda i: (0, i + skip, 0))


def attn_fwd(owner, patches, region_rows, weights, vec, after, count=16, batch=16):
    windows = patches.shape[1]
    array = jax.ShapeDtypeStruct
    return pl.pallas_call(
        partial(attn_fwd_kernel, count, batch),
        grid=(windows // count,),
        in_specs=[pl.BlockSpec(memory_space=pltpu.SMEM), middle(PATCH, count), block((count, D)), full((4, D, D)),
                  full(vec.shape), pl.BlockSpec(memory_space=pl.ANY)],
        out_specs=[middle(LIVE, count), block((count, QUERIES, D))] + [block((count, ROWS, D))] * 2
        + [middle(LIVE, count), block((count, 4, ROWS, STACK))],
        out_shape=[array((LIVE, windows, D), F32), array((windows, QUERIES, D), BF)]
        + [array((windows, ROWS, D), BF)] * 2
        + [array((LIVE, windows, D), BF), array((windows, 4, ROWS, STACK), BF)],
        scratch_shapes=[pltpu.VMEM((4, count * QUERIES, GROUP), F32)] + [pltpu.VMEM((4, count * ROWS, GROUP), F32)] * 3,
        compiler_params=pltpu.CompilerParams(vmem_limit_bytes=VMEM),
        cost_estimate=cost(16e9),
        name="window_attention_forward",
    )(owner, patches, region_rows, weights, vec, after)


def mlp_kernel(many, sources, cols, steps, lanes, last, *refs):
    x1_ref, pc_ref, *w_refs, vec_ref, b1_ref = refs[:8]
    if last:
        prev_refs = refs[9:11]
        op_ref, dx1_ref, dwa_ref, dwb_ref, dv_ref, db1_ref, acc1, acc2 = refs[11:]
    else:
        prev_refs = ()
        early_ref, op_ref, dx1_ref, dwa_ref, dwb_ref, dv_ref, db1_ref, acc1, acc2 = refs[8:]
    total = many * sources * cols
    step = pl.program_id(0)

    @pl.when(step == 0)
    def _():
        for ref in (dv_ref, db1_ref):
            ref[...] = jnp.zeros_like(ref)

    vec = vec_ref[...]
    gain = vec[2:3]
    x1 = x1_ref[...].reshape(total, D)
    xhat, scale = norm_parts(x1)
    h = (xhat * gain + vec[3:4]).astype(BF)
    for s in range(sources):
        dx1_ref[:, s * cols : (s + 1) * cols] = pc_ref[s].astype(F32)
    dy = dx1_ref[...].reshape(total, D)
    dm = dy.astype(BF)
    ht = h.T
    dmt = dm.T
    y = x1 + vec[7:8]
    dh = jnp.zeros((total, D), F32)
    parts = [(j, slice(c, c + lanes)) for j in range(4) for c in range(0, D, lanes)]

    def activate(j, s):
        u, slope = gelu_parts(nn(h, w_refs[j][0, :, s]) + b1_ref[j : j + 1, s])
        da = slope * nt(dm, w_refs[j][1, s, :])
        db1_ref[j, :, s] += fold(da)
        return u.astype(BF), da.astype(BF)

    def apply(j, s, u, da):
        acc1[j, :, s] = jnp.where(step == 0, 0.0, acc1[j, :, s]) + nn(ht, da)
        acc2[j, :, s] = jnp.where(step == 0, 0.0, acc2[j, :, s]) + nn(dmt, u)
        return nn(u, w_refs[j][1, s, :]), nt(da, w_refs[j][0, :, s])

    held_pair = activate(*parts[0])
    for n in range(1, len(parts) + 1):
        later = activate(*parts[n]) if n < len(parts) else None
        up, down = apply(*parts[n - 1], *held_pair)
        y, dh = y + up, dh + down
        held_pair = later
    y = y.reshape(many, sources * cols, D)

    def put(ref):
        for s in range(sources):
            ref[s] = y[:, s * cols : (s + 1) * cols].astype(BF)

    if last:
        put(op_ref)
    else:
        pl.when(step < steps - 1)(lambda: put(early_ref))
        pl.when(step == steps - 1)(lambda: put(op_ref))
    dy = dx1_ref[...].reshape(total, D)
    dx1_ref[...] = (dy + norm_back(dh, xhat, scale, gain)).reshape(dx1_ref.shape)
    dv_ref[0] += fold(dh * xhat)
    dv_ref[1] += fold(dh)
    dv_ref[2] += fold(dy)

    @pl.when(step == steps - 1)
    def _():
        for refs_out, first in ((dwa_ref, 0), (dwb_ref, 1)):
            for n, acc in enumerate((acc1, acc2)):
                for m in range(2):
                    piece = acc[first + 2 * m]
                    for prev in prev_refs[first : first + 1]:
                        piece = piece + prev[2 * m + n].astype(F32)
                    refs_out[2 * m + n] = piece.astype(BF)


def mlp(x1, first_position, cot, weights, vec, bias_first, prev=(), many=10, lanes=256):
    sources, positions, cols, _ = cot.shape
    windows = sources * cols
    steps = positions // many
    skip = first_position // many
    some = lambda place: pl.BlockSpec((sources, many, cols, D), lambda i: (0, place(i), 0, 0))
    array = jax.ShapeDtypeStruct
    matrices = full((4, D, D))
    rows = lambda count: array((sources, count, cols, D), BF)
    late = (LIVE - positions if not prev else positions) + many
    outs = [some(lambda i: i + 1)] if prev else [some(lambda i: jnp.minimum(i, steps - 2)), some(lambda i: 0)]
    shapes = [rows(late)] if prev else [rows(positions - many), rows(late)]
    return pl.pallas_call(
        partial(mlp_kernel, many, sources, cols, steps, lanes, len(prev) > 0),
        grid=(steps,),
        in_specs=[pl.BlockSpec((many, windows, D), lambda i: (i + skip, 0, 0)), some(lambda i: i)]
        + [full((2, D, D))] * 4 + [full(vec.shape), full((4, D))]
        + ([pl.BlockSpec(memory_space=pl.ANY)] + [matrices] * 2 if prev else []),
        out_specs=outs + [block((many, windows, D)), matrices, matrices, full((3, 8, D)), full((4, 8, D))],
        out_shape=shapes + [array((positions, windows, D), F32), array((4, D, D), BF),
                            array((4, D, D), BF), array((3, 8, D), F32), array((4, 8, D), F32)],
        scratch_shapes=[pltpu.VMEM((4, D, D), F32), pltpu.VMEM((4, D, D), F32)],
        input_output_aliases={8: 0} if prev else {},
        compiler_params=pltpu.CompilerParams(vmem_limit_bytes=VMEM),
        cost_estimate=cost(4e9 * steps),
        name="mlp_forward_backward",
    )(x1, cot, *weights, vec, bias_first, *prev)


def attn_bwd_kernel(count, batch, chunks, more, owner_ref, *refs):
    p_ref, r_ref = refs[:2]
    refs = refs[:3] + refs[4:]
    dx1_refs = refs[3 : 3 + chunks]
    q_ref, k_ref, v_ref, o_ref, pt_ref, w_ref, vec_ref = refs[3 + chunks : 10 + chunks]
    owner = owner_ref[0, 0]
    prev_refs = refs[10 + chunks : 14 + chunks] if more else ()
    dp_ref, dr_ref, dw_ref, dv_ref, dq_held, dk_held, dvv_held, do_held = refs[10 + chunks + len(prev_refs) :]
    total = count * LIVE

    @pl.when(pl.program_id(0) == 0)
    def _():
        dw_ref[...] = prev_refs[2][...] if more else jnp.zeros_like(dw_ref)
        dv_ref[...] = prev_refs[3][...] if more else jnp.zeros_like(dv_ref)
        do_held[:, total:] = jnp.zeros((4, count * (QUERIES - LIVE), GROUP), F32)

    vec = vec_ref[...]
    gain = vec[0:1]
    dx1 = jnp.concatenate([ref[...] for ref in dx1_refs], axis=0).reshape(total, D)
    gb = dx1.astype(BF)
    hold(do_held, total, nt(gb, w_ref[owner ^ 3]))
    masks = head_masks()

    def grad(w, g):
        lanes = slice(GROUP * g, GROUP * (g + 1))
        do_wide = spread_low(do_held[g, pl.ds(w, QUERIES, stride=count), :].astype(BF))
        dvv_held[g, pl.ds(w, ROWS, stride=count), :] = nn(pt_ref[w, g], do_wide)
        return nt(v_ref[w, :, lanes], do_wide)

    def score(w, g, grad):
        p = pt_ref[w, g].astype(F32)
        both = p * grad
        return (both - p * jnp.sum(both, axis=0, keepdims=True)).astype(BF)

    def finish(w, g, ds):
        lanes = slice(GROUP * g, GROUP * (g + 1))
        rows = pl.ds(w, ROWS, stride=count)
        dk_held[g, rows, :] = nn(ds, spread_low(q_ref[w, :, lanes])) * SCALE
        dq_held[g, rows, :] = collect(tn(ds, k_ref[w, :, lanes]), masks, ROWS, QUERIES) * SCALE

    staggered(count, batch, grad, score, finish)
    x = jnp.concatenate([p_ref[...].astype(F32), r_ref[...][None]], axis=0).reshape(total, D)
    xhat, scale = norm_parts(x)
    xn = (xhat * gain + vec[1:2]).astype(BF)
    dq_wide = held_rows(dq_held, total)
    dv_wide = held_rows(dvv_held, total)
    dq = dq_wide.astype(BF)
    dk = held_rows(dk_held, total).astype(BF)
    dv = dv_wide.astype(BF)
    dn = nt(dq, w_ref[owner ^ 0]) + nt(dk, w_ref[owner ^ 1]) + nt(dv, w_ref[owner ^ 2])
    dx = (dx1 + norm_back(dn, xhat, scale, gain)).reshape(LIVE, count, D)
    dp_ref[...] = dx[:PATCH].astype(BF)
    dr_ref[...] = dx[PATCH]
    xt = xn.T
    dw_ref[0] += nn(xt, dq)
    dw_ref[1] += nn(xt, dk)
    dw_ref[2] += nn(xt, dv)
    dw_ref[3] += nn(o_ref[...].reshape(total, D).T, gb)
    dv_ref[0] += fold(dn * xhat)
    dv_ref[1] += fold(dn)
    dv_ref[2] += fold(dq_wide)
    dv_ref[3] += fold(dv_wide)
    dv_ref[4] += fold(dx1)


def attn_bwd(owner, patches, region_rows, dx1_parts, saved, weights, vec, start, windows, after, prev=(), count=16, batch=16):
    skip = start // count
    array = jax.ShapeDtypeStruct
    sums = [full((4, D, D)), full((5, 8, D))]
    anywhere = pl.BlockSpec(memory_space=pl.ANY)
    rows = pl.BlockSpec((count, D), lambda i: (i + skip, 0))
    before = 12 + len(dx1_parts)
    return pl.pallas_call(
        partial(attn_bwd_kernel, count, batch, len(dx1_parts), len(prev) > 0),
        grid=(windows // count,),
        in_specs=[pl.BlockSpec(memory_space=pltpu.SMEM), middle(PATCH, count, skip), rows, anywhere, anywhere]
        + [middle(part.shape[0], count, skip) for part in dx1_parts]
        + [pl.BlockSpec((count, r, D), lambda i: (i + skip, 0, 0)) for r in (QUERIES, ROWS, ROWS)]
        + [middle(LIVE, count, skip), pl.BlockSpec((count, 4, ROWS, STACK), lambda i: (i + skip, 0, 0, 0))]
        + [full((4, D, D)), full(vec.shape)] + ([anywhere] * 2 + sums)[: len(prev)],
        out_specs=[middle(PATCH, count, skip), rows] + sums,
        out_shape=[array(patches.shape, BF), array(region_rows.shape, F32),
                   array((4, D, D), F32), array((5, 8, D), F32)],
        scratch_shapes=[pltpu.VMEM((4, count * ROWS, GROUP), F32)] * 3 + [pltpu.VMEM((4, count * QUERIES, GROUP), F32)],
        input_output_aliases={before: 0, before + 1: 1} if prev else {},
        compiler_params=pltpu.CompilerParams(vmem_limit_bytes=VMEM),
        cost_estimate=cost(12e9),
        name="window_attention_backward",
    )(owner, patches, region_rows, *after, *dx1_parts, *saved, weights, vec, *prev)


def regional_fwd_kernel(owner_ref, canvas_ref, band_ref, ids_ref, band_ids_ref, w_ref, vec_ref,
                        r1_ref, mixed_ref, level_ref, q_ref, k_ref, v_ref):
    vec = vec_ref[...]
    owner = owner_ref[0, 0]
    xhat, _ = norm_parts(canvas_ref[...].astype(F32))
    low = (xhat * vec[0:1] + vec[1:2]).astype(BF)
    q_ref[...] = (nn(low, w_ref[owner ^ 0]) + vec[4:5]).astype(BF)
    k_ref[...] = nn(low, w_ref[owner ^ 1]).astype(BF)
    v_ref[...] = (nn(low, w_ref[owner ^ 2]) + vec[5:6]).astype(BF)
    band = band_ref[...].astype(F32)
    rows = band.shape[0]
    xhat, _ = norm_parts(band)
    q = nn((xhat * vec[0:1] + vec[1:2]).astype(BF), w_ref[owner ^ 0]) + vec[4:5]
    masks = head_masks()
    same = ids_ref[...] == band_ids_ref[...]
    scores, probs = [], []
    for g in range(4):
        lanes = slice(GROUP * g, GROUP * (g + 1))
        scores.append(nt(k_ref[:, lanes], spread(q[:, lanes], masks)))
    for g, s in enumerate(scores):
        s = jnp.where(same, s, MASKED)
        peak = jnp.max(s, axis=0, keepdims=True)
        e = jnp.exp((s - peak) * SCALE)
        sums = jnp.sum(e, axis=0, keepdims=True)
        level_ref[g : g + 1] = peak * SCALE + jnp.log(sums)
        probs.append((e * (1.0 / sums)).astype(BF))
    for g, p in enumerate(probs):
        lanes = slice(GROUP * g, GROUP * (g + 1))
        mixed_ref[:, lanes] = collect(tn(p, v_ref[:, lanes]), masks, rows)
    r1_ref[...] = band + nn(mixed_ref[...].astype(BF), w_ref[owner ^ 3]) + vec[6:7]


def in_vmem(kernel, outs, name, *args, after=(), scratch=(), flops=2e9):
    spaces = [pltpu.SMEM if arg.shape == (1, 1) else pltpu.VMEM for arg in args]
    count = len(args)
    return pl.pallas_call(
        lambda *refs: kernel(*refs[:count], *refs[count + len(after) :]),
        in_specs=[pl.BlockSpec(memory_space=space) for space in spaces]
        + [pl.BlockSpec(memory_space=pl.ANY) for _ in after],
        out_specs=[pl.BlockSpec(memory_space=pltpu.VMEM) for _ in outs],
        out_shape=[jax.ShapeDtypeStruct(*out) for out in outs],
        scratch_shapes=list(scratch),
        compiler_params=pltpu.CompilerParams(vmem_limit_bytes=VMEM),
        cost_estimate=cost(flops),
        name=name,
    )(*args, *after)


def payload_kernel(owner_ref, dr_ref, mixed_ref, level_ref, w_ref, grad_ref, extra_ref):
    low = dr_ref[...].astype(BF)
    grad_ref[...] = low
    both = nt(low, w_ref[owner_ref[0, 0] ^ 3]).astype(BF).astype(F32) * mixed_ref[...]
    head = lax.broadcasted_iota(jnp.int32, (D, GROUP), 0) // HEAD_DIM
    lane = lax.broadcasted_iota(jnp.int32, (D, GROUP), 1)
    pick = ((head == lane) | (head + HEADS == lane)).astype(BF)
    high, low_part = halves(both)
    rest = (both - high.astype(F32) - low_part.astype(F32)).astype(BF)
    delta = nn(high, pick) + (nn(low_part, pick) + nn(rest, pick))
    top = delta.astype(BF).astype(F32)
    lane = lax.broadcasted_iota(jnp.int32, (1, GROUP), 1)
    level = level_ref[...]
    level_top = level.astype(BF).astype(F32)
    level_rest = level - level_top
    level_mid = level_rest.astype(BF).astype(F32)
    extra = level_rest - level_mid
    for place, term in ((4, level_mid), (3, level_top), (2, delta - top), (1, top)):
        extra = jnp.where(lane < place * HEADS, term, extra)
    extra_ref[...] = extra.astype(BF)


def regional_bwd_kernel(own_rows, owner_ref, place_ref, q_ref, k_ref, v_ref, canvas_ref, grads_ref, extra_ref, ids_ref,
                        ids_row_ref, ids_own_ref, ids_own_row_ref, mixed_ref, band_grad_ref, dw_ref, w_ref, vec_ref,
                        dr_ref, keep_ref, give_ref, gv_ref, sum_held):
    vec = vec_ref[...]
    owner = owner_ref[0, 0]
    mine = pl.ds(pl.multiple_of(place_ref[0, 0] * own_rows, own_rows), own_rows)
    masks = head_masks()
    grads_own = grads_ref[mine]
    do = nt(grads_ref[...], w_ref[owner ^ 3]).astype(BF).astype(F32)
    do_own = nt(grads_own, w_ref[owner ^ 3]).astype(BF).astype(F32)
    same_own = ids_ref[...] == ids_own_row_ref[...]
    same = ids_own_ref[...] == ids_row_ref[...]
    lanes = [slice(GROUP * g, GROUP * (g + 1)) for g in range(4)]

    def columns(rows):
        term = rows.astype(F32).T
        part = lambda n: term[n * HEADS : (n + 1) * HEADS]
        wide = lambda x: [jnp.concatenate([x[h : h + 1] for h in range(4 * g, 4 * g + 4)], axis=1) for g in range(4)]
        return wide(part(0) + part(1)), wide(part(2) + part(3) + part(4))

    delta, level = columns(extra_ref[...])
    delta_own, level_own = columns(extra_ref[mine])
    first, second = [], []
    dqs, dks, dvs = [], [], []
    for g in range(4):
        q_wide = spread(q_ref[mine, lanes[g]].astype(F32), masks)
        do_wide = spread(do_own[:, lanes[g]], masks)
        first.append((nt(k_ref[:, lanes[g]], q_wide), nt(v_ref[:, lanes[g]], do_wide)))
        q_wide = spread(q_ref[:, lanes[g]].astype(F32), masks)
        do_wide = spread(do[:, lanes[g]], masks)
        second.append((nt(k_ref[mine, lanes[g]], q_wide), nt(v_ref[mine, lanes[g]], do_wide), q_wide, do_wide))
    for g in range(4):
        s, dp = first[g]
        p = jnp.where(same_own, jnp.exp(s * SCALE - level_own[g]), 0.0)
        ds = (p * (dp - delta_own[g])).astype(BF)
        dqs.append(collect(tn(ds, k_ref[:, lanes[g]]), masks, own_rows) * SCALE)
        s, dp, q_wide, do_wide = second[g]
        p = jnp.where(same, jnp.exp(s * SCALE - level[g]), 0.0)
        ds = (p * (dp - delta[g])).astype(BF)
        dvs.append(nn(p.astype(BF), do_wide))
        dks.append(nn(ds, q_wide) * SCALE)
    xhat, scale = norm_parts(canvas_ref[mine].astype(F32))
    low = (xhat * vec[0:1] + vec[1:2]).astype(BF)
    dq_wide, dk_wide, dv_wide = (jnp.concatenate(x, axis=1) for x in (dqs, dks, dvs))
    dq, dk, dv = dq_wide.astype(BF), dk_wide.astype(BF), dv_wide.astype(BF)
    dn = nt(dq, w_ref[owner ^ 0]) + nt(dk, w_ref[owner ^ 1]) + nt(dv, w_ref[owner ^ 2])
    dr_ref[...] = grads_own.astype(F32) + norm_back(dn, xhat, scale, vec[0:1])
    sum_held[0] = dw_ref[0] + tn(low, dq)
    sum_held[1] = dw_ref[1] + tn(low, dk)
    sum_held[2] = dw_ref[2] + tn(low, dv)
    sum_held[3] = dw_ref[3] + tn(mixed_ref[...].astype(BF), band_grad_ref[...])
    for n in range(2):
        keep_ref[n] = sum_held[owner ^ (2 * n)].astype(BF)
        give_ref[n] = sum_held[owner ^ (2 * n + 1)].astype(BF)
    gv_ref[0] = fold(dn * xhat)
    gv_ref[1] = fold(dn)
    gv_ref[2] = fold(dq_wide)
    gv_ref[3] = fold(dv_wide)
    gv_ref[4] = fold(band_grad_ref[...].astype(F32))


def halves(a):
    high = a.astype(BF)
    return high, (a - high.astype(F32)).astype(BF)


def terms(a, passes):
    return (a.astype(BF),) if passes == 1 else halves(a)


def product(a, b, dot=nn):
    if len(a) == 1:
        return dot(a[0], b[0])
    return dot(a[0], b[0]) + (dot(a[0], b[1]) + dot(a[1], b[0]))


def symmetric(a, b, dot=nn):
    half = D // 2
    right = (lambda x: x[half:]) if dot is nt else (lambda x: x[:, half:])
    top = product([x[:half] for x in a], b, dot)
    corner = product([x[half:] for x in a], [right(x) for x in b], dot)
    return jnp.concatenate([top, jnp.concatenate([top[:, half:].T, corner], axis=1)], axis=0)


DIRECT_STEPS = (1, 1, 1, -1, -1)
GRAM_STEPS = (1, 1, 3, 3, 3)
NEAR_ZERO = NS_FIRST + NS_SECOND + NS_THIRD
NEAR_ONE = NS_SECOND + 2.0 * NS_THIRD


def identity():
    rows = lax.broadcasted_iota(jnp.int32, (D, D), 0)
    return rows == lax.broadcasted_iota(jnp.int32, (D, D), 1)


def polynomial(gram, eye, step):
    if step > 0:
        parts = terms(gram, step)
        return NS_FIRST, NS_SECOND * gram + NS_THIRD * symmetric(parts, parts)
    rest = gram - jnp.where(eye, 1.0, 0.0)
    parts = terms(rest, -step)
    return NEAR_ZERO, NEAR_ONE * rest + NS_THIRD * symmetric(parts, parts)


def direct_steps(moment, eye):
    z = moment * (1.0 / (jnp.sqrt(jnp.sum(moment * moment)) + 1e-07))
    for step in DIRECT_STEPS:
        parts = terms(z, abs(step))
        gram = symmetric(parts, parts, nt)
        yield
        scale, poly = polynomial(gram, eye, step)
        yield
        z = scale * z + product(terms(poly, abs(step)), parts)
        yield
    return z


def gram_steps(gram, eye):
    factor = 1.0 / (jnp.sqrt(jnp.sum(jnp.where(eye, gram, 0.0))) + 1e-07)
    gram = gram * (factor * factor)
    steps = None
    for n, passes in enumerate(GRAM_STEPS):
        scale, poly = polynomial(gram, eye, passes)
        yield
        parts = terms(poly, passes)
        if steps is None:
            steps = jnp.where(eye, scale, 0.0) + poly
        else:
            steps = scale * steps + symmetric(parts, terms(steps, passes))
            yield
        if n < len(GRAM_STEPS) - 1:
            half = scale * gram + symmetric(parts, terms(gram, passes))
            yield
            gram = scale * half + symmetric(parts, terms(half, passes))
            yield
    return steps * factor


def in_turns(*chains):
    results = [None] * len(chains)
    running = list(enumerate(chains))
    while running:
        still = []
        for n, chain in running:
            try:
                next(chain)
                still.append((n, chain))
            except StopIteration as stop:
                results[n] = stop.value
        running = still
    return results


def old_grams_kernel(moms_ref, *out_refs):
    for n, out_ref in enumerate(out_refs):
        square, cross = jnp.zeros((D, D), F32), jnp.zeros((D, D), F32)
        for j in range(OPT):
            high, low = halves(moms_ref[j, n])
            if n == 1:
                high, low = high.T, low.T
            square = square + nt(high, high)
            cross = cross + nt(high, low)
        out_ref[...] = square + (cross + cross.T)


def grams_kernel(places, owner_ref, moms_ref, all_ref, mixed1_ref, new1_ref, mixed2_ref, new2_ref, own_ref,
                 squares_ref):
    half = len(places) // 2
    squares = jnp.zeros((8, D), F32)
    for n, (mixed_ref, new_ref) in enumerate(((mixed1_ref, new1_ref), (mixed2_ref, new2_ref))):
        mixed, new = jnp.zeros((D, D), F32), jnp.zeros((D, D), F32)
        mine = places[n * half : (n + 1) * half]
        for j in range(OPT):
            high, low = halves(moms_ref[j, n])
            if n == 1:
                high, low = high.T, low.T
            g = jnp.concatenate([all_ref[d, j] for d in mine], axis=0)
            wide = g.astype(F32)
            squares = squares + fold(wide * wide)
            mixed = mixed + (nt(high, g) + nt(low, g))
            new = new + nt(g, g)
        mixed_ref[...] = mixed + mixed.T
        new_ref[...] = new
        own_ref[n] = jnp.concatenate([all_ref[d, owner_ref[0, 0]] for d in mine], axis=0)
    squares_ref[...] = jnp.full((8, 128), jnp.sum(squares))


def update_kernel(clip_ref, ga_ref, ma_ref, wa_ref, g_ref, m1_ref, m2_ref, w1_ref, w2_ref,
                  old1, mixed1, new1, old2, mixed2, new2, na_ref, newa_ref, n1_ref, new1_ref, n2_ref, new2_ref):
    clip = clip_ref[0, 0]
    eye = identity()
    na_ref[...] = MUON_MOMENTUM * ma_ref[...] + clip * ga_ref[...].astype(F32)
    n1_ref[...] = MUON_MOMENTUM * m1_ref[...] + clip * g_ref[0].astype(F32)
    n2_ref[...] = MUON_MOMENTUM * m2_ref[...] + clip * g_ref[1].astype(F32).T
    a, b, c = MUON_MOMENTUM * MUON_MOMENTUM, MUON_MOMENTUM * clip, clip * clip
    gram1 = a * old1[...] + b * mixed1[...] + c * new1[...]
    gram2 = a * old2[...] + b * mixed2[...] + c * new2[...]
    steps1, steps2, z = in_turns(gram_steps(gram1, eye), gram_steps(gram2, eye), direct_steps(na_ref[...], eye))
    newa_ref[...] = wa_ref[...] * DECAY_KEEP - MUON_RATE * z
    z = product(halves(steps1), halves(n1_ref[...]))
    new1_ref[...] = w1_ref[...] * DECAY_KEEP - MUON_RATE * z
    z = product(halves(n2_ref[...]), halves(steps2))
    new2_ref[...] = w2_ref[...] * DECAY_KEEP - (MUON_RATE * max(1.0, FF / D) ** 0.5) * z


def pair(values, bit):
    return lax.ppermute(values, "opt", [(i, i ^ bit) for i in range(OPT)])


def fence(x, *first):
    here = pl.BlockSpec(memory_space=pl.ANY)
    return pl.pallas_call(
        lambda *refs: None,
        in_specs=[here] * (1 + len(first)),
        out_specs=here,
        out_shape=jax.ShapeDtypeStruct(x.shape, x.dtype),
        input_output_aliases={0: 0},
        cost_estimate=cost(1e3),
        name="fence",
    )(x, *first)


def pieces_of_owners(own):
    mate = pair(own, 1)
    across = pair(own, 2)
    return [own, mate, across, pair(across, 1)]


def share(x, *first):
    copies = jnp.broadcast_to(x[None], (lax.axis_size("dp"),) + x.shape)
    if first:
        copies = fence(copies, *first)
    return lax.all_to_all(copies, "dp", 0, 0, tiled=True)


def swap(x, bit):
    return lax.ppermute(x, "dp", [(i, i ^ bit) for i in range(lax.axis_size("dp"))])


def bits():
    return [1 << n for n in range(lax.axis_size("dp").bit_length() - 1)]


def halving_step(x, bit):
    half = x.shape[0] // 2
    side = (lax.axis_index("dp") // bit) % 2
    give = lax.dynamic_slice_in_dim(x, (1 - side) * half, half, 0).astype(BF)
    return lax.dynamic_slice_in_dim(x, side * half, half, 0), give


def order_of_halves(count):
    width = count.bit_length() - 1
    return [int(format(n, "b").zfill(width)[::-1], 2) if width else 0 for n in range(count)]


def sum_small_over_dp(x):
    for bit in bits():
        x = x + swap(x, bit)
    return x


def split_heads(x):
    return x.reshape(x.shape[0], HEADS, HEAD_DIM)


def regional_forward(canvas, band, same, weights, vec):
    low = lambda x: (norm_parts(x.astype(F32))[0] * vec[0] + vec[1]).astype(BF)
    normed = low(canvas)
    queries = (nn(normed, weights[0]) + vec[4]).astype(BF)
    keys = nn(normed, weights[1]).astype(BF)
    values = (nn(normed, weights[2]) + vec[5]).astype(BF)
    own = (nn(low(band), weights[0]) + vec[4]).astype(BF)
    scores = jnp.einsum("qhd,khd->hqk", split_heads(own), split_heads(keys), preferred_element_type=F32)
    scores = jnp.where(same[None], scores * SCALE, MASKED)
    peak = jnp.max(scores, axis=-1, keepdims=True)
    raised = jnp.exp(scores - peak)
    sums = jnp.sum(raised, axis=-1, keepdims=True)
    probs = (raised / sums).astype(BF)
    mixed = jnp.einsum("hqk,khd->qhd", probs, split_heads(values), preferred_element_type=F32).reshape(own.shape)
    region_rows = band.astype(F32) + nn(mixed.astype(BF), weights[3]) + vec[6]
    return region_rows, mixed, (peak + jnp.log(sums))[:, :, 0], queries, keys, values


def regional_terms(queries, keys, values, grad_mixed, same, level, delta):
    scores = jnp.einsum("qhd,khd->hqk", split_heads(queries), split_heads(keys), preferred_element_type=F32)
    probs = jnp.where(same[None], jnp.exp(scores * SCALE - level[:, :, None]), 0.0)
    grads = jnp.einsum("qhd,khd->hqk", split_heads(grad_mixed), split_heads(values), preferred_element_type=F32)
    return probs.astype(BF), (probs * (grads - delta[:, :, None])).astype(BF)


def regional_backward(queries, keys, values, grads, own, rows, same, level, delta, weights, vec, mixed, band_grad, dw):
    grad_mixed = nt(grads, weights[3]).astype(BF)
    level_own, delta_own = own(level.T).T, own(delta.T).T
    _, scores = regional_terms(own(queries), keys, values, own(grad_mixed), same.T, level_own, delta_own)
    dq = jnp.einsum("hqk,khd->qhd", scores, split_heads(keys), preferred_element_type=F32)
    probs, scores = regional_terms(queries, own(keys), own(values), grad_mixed, same, level, delta)
    dk = jnp.einsum("hqk,qhd->khd", scores, split_heads(queries), preferred_element_type=F32)
    dv = jnp.einsum("hqk,qhd->khd", probs, split_heads(grad_mixed), preferred_element_type=F32)
    flat = lambda x: x.reshape(-1, D)
    dq, dk, dv = flat(dq) * SCALE, flat(dk) * SCALE, flat(dv)
    lows = [x.astype(BF) for x in (dq, dk, dv)]
    dn = sum(nt(x, w) for x, w in zip(lows, weights))
    xhat, scale = norm_parts(rows.astype(F32))
    low = (xhat * vec[0] + vec[1]).astype(BF)
    d_regions = own(grads).astype(F32) + norm_back(dn, xhat, scale, vec[0])
    matrices = [dw[j] + tn(low, x) for j, x in enumerate(lows)] + [dw[3] + tn(mixed.astype(BF), band_grad)]
    vectors = [fold(x) for x in (dn * xhat, dn, dq, dv, band_grad.astype(F32))]
    return d_regions, jnp.stack(matrices).astype(BF), jnp.stack(vectors)


def per_device(patches, regions, image_ids, attn_w, mlp_in, mlp_out, vec_params, patch_cot, region_cot,
               attn_mom, mlp_in_mom, mlp_out_mom, adam_first, adam_second):
    dp_size = lax.axis_size("dp")
    dp_index = lax.axis_index("dp")
    opt_index = lax.axis_index("opt")
    _, grid_rows, cols, _, _ = patch_cot.shape
    grid_cols = patches.shape[2]
    tokens = grid_rows * grid_cols
    own_count = grid_rows * cols
    one_kernel = tokens <= 1024
    vec = vec_params
    order = opt_index ^ jnp.arange(OPT)
    move = lambda x: lax.all_to_all(x, "dp", 0, 0, tiled=True)

    attn_low = attn_w[0].astype(BF)
    attn_pieces = jnp.stack(pieces_of_owners(attn_low))
    mlp_w = pieces_of_owners(jnp.stack([mlp_in, mlp_out]).astype(BF))
    owner = opt_index.reshape(1, 1)
    if not one_kernel:
        weights = [lax.dynamic_index_in_dim(attn_pieces, opt_index ^ j, 0, keepdims=False) for j in range(OPT)]
    canvas_blocks = share(regions[0], attn_low)
    canvas = canvas_blocks.reshape(tokens, D)
    by_position = patch_cot[0].transpose(0, 2, 1, 3)
    split = 30
    last = jnp.concatenate([by_position[:, split:], region_cot[0][:, None]], axis=1)
    first_cot = move(fence(by_position[:, :split], canvas))
    bias_first = jnp.take(vec[8:], order, axis=0)

    band_of = lambda x: lax.dynamic_slice_in_dim(x, dp_index, 1, 1).reshape((grid_cols,) + x.shape[3:])
    own_of = lambda x: lax.dynamic_slice_in_dim(x, dp_index * own_count, own_count, 0)
    ids_blocks = image_ids[0].reshape(grid_rows, dp_size, cols).transpose(1, 0, 2)
    ids = ids_blocks.reshape(tokens)
    band_ids, own_ids = band_of(ids_blocks), own_of(ids)
    band = band_of(canvas_blocks)
    if one_kernel:
        repeat = lambda x: jnp.tile(x, 4)[None]
        region_rows, mixed, level, reg_q, reg_k, reg_v = in_vmem(
            regional_fwd_kernel,
            [((grid_cols, D), F32), ((grid_cols, D), F32), ((4, 4 * grid_cols), F32)] + [((tokens, D), BF)] * 3,
            "regional_attention_forward", owner, canvas, band, ids[:, None], repeat(band_ids), attn_pieces, vec)
        level = level.reshape(HEADS, grid_cols)
    else:
        region_rows, mixed, level, reg_q, reg_k, reg_v = regional_forward(
            canvas, band, band_ids[:, None] == ids[None, :], weights, vec)
    level_wide = jnp.tile(level.T, (1, GROUP // HEADS))

    windows = patches[0, 0].transpose(1, 0, 2)
    some = grid_cols // 2
    x1, *saved = attn_fwd(owner, windows, region_rows, attn_pieces, vec, mlp_w[2])
    last_cot = move(fence(last, x1))
    early_out, late_out, dx1_a, *grads_a = mlp(x1, 0, first_cot, mlp_w, vec, bias_first)
    moved_a = move(early_out)
    moms = lax.all_gather(fence(jnp.stack([mlp_in_mom, mlp_out_mom]), x1), "opt", axis=0)
    late_out, dx1_b, *grads_b = mlp(x1, split, last_cot, mlp_w, vec, bias_first, prev=(late_out, *grads_a[:2]))
    near = pair(fence(grads_b[1], moved_a), 1)
    far = (near[2:].astype(F32) + grads_b[0][2:].astype(F32)).astype(BF)
    moved_b = move(fence(late_out, far))
    out_patches = jnp.concatenate([moved_a, moved_b[:, :-1]], axis=1).transpose(0, 2, 1, 3)[None]
    out_regions = moved_b[None, :, -1]

    dx1 = (dx1_a, dx1_b)
    early = attn_bwd(owner, windows, region_rows, dx1, saved, attn_pieces, vec, 0, some, (far, far))
    own_mlp = near[:2].astype(F32) + grads_b[0][:2].astype(F32) + fence(pair(far, 2), early[3]).astype(F32)
    keep, give = halving_step(own_mlp.reshape(2 * D, D), 1)
    d_patches, d_region, d_attn, d_vec_attn = attn_bwd(
        owner, windows, region_rows, dx1, saved, attn_pieces, vec, some, some, (give, moms), prev=early)
    d_patches = d_patches.transpose(1, 0, 2)[None, None]
    gives = []
    old_grams = in_vmem(old_grams_kernel, [((D, D), F32)] * 2, "momentum_grams", moms, after=(d_vec_attn,),
                         flops=4e9)

    band_grad, extra = in_vmem(payload_kernel, [((grid_cols, D), BF), ((grid_cols, GROUP), BF)],
                               "regional_payload", owner, d_region, mixed, level_wide, attn_pieces,
                               after=(give, moved_b))
    taken = fence(swap(give, 1), band_grad)
    for bit in bits()[1:]:
        keep, give = halving_step(keep + taken.astype(F32), bit)
        gives.append(give)
        taken = swap(give, bit)
    payload = share(jnp.concatenate([band_grad, extra], axis=1)).reshape(grid_rows, dp_size, cols, D + GROUP)
    payload = payload.transpose(1, 0, 2, 3).reshape(tokens, D + GROUP)
    grads = payload[:, :D]
    extra = payload[:, D:]
    if one_kernel:
        matrices = ((2, D, D), BF)
        d_regions, keep_attn, give_attn, d_vec_reg = in_vmem(
            partial(regional_bwd_kernel, own_count),
            [((own_count, D), F32), matrices, matrices, ((5, 8, D), F32)],
            "regional_attention_backward", owner, dp_index.reshape(1, 1), reg_q, reg_k, reg_v, canvas, grads, extra,
            ids[:, None], repeat(ids), own_ids[:, None], repeat(own_ids), mixed, band_grad, d_attn, attn_pieces, vec,
            after=tuple(old_grams), scratch=[pltpu.VMEM((4, D, D), F32)], flops=4e9)
    else:
        part = lambda n: extra[:, n * HEADS : (n + 1) * HEADS].astype(F32)
        delta, level = (part(0) + part(1)).T, (part(2) + part(3) + part(4)).T
        d_regions, grad_attn, d_vec_reg = regional_backward(
            reg_q, reg_k, reg_v, grads, own_of, own_of(canvas), ids[:, None] == own_ids[None, :], level, delta,
            weights, vec, mixed, band_grad, d_attn)
        pick = lambda j: lax.dynamic_index_in_dim(grad_attn, opt_index ^ j, 0, keepdims=False)
        keep_attn, give_attn = jnp.stack([pick(0), pick(2)]), jnp.stack([pick(1), pick(3)])
    d_regions = d_regions.reshape(regions.shape)

    d_vec_attn = jnp.sum(d_vec_attn + d_vec_reg, axis=1)
    d_vec_mlp = jnp.sum(grads_a[2] + grads_b[2], axis=1)
    d_bias_first = jnp.take(jnp.sum(grads_a[3] + grads_b[3], axis=1), order, axis=0)
    grad_vec = jnp.concatenate([d_vec_attn[:2], d_vec_mlp[:2], d_vec_attn[2:], d_vec_mlp[2:], d_bias_first])
    grad_vec = grad_vec + pair(grad_vec, 1)
    vec_over_opt = grad_vec + pair(grad_vec, 2)
    grad_vec = sum_small_over_dp(vec_over_opt)

    piece_mlp = (keep + fence(taken, give_attn).astype(F32)).astype(BF)

    near = pair(give_attn, 1)
    far = (near[1].astype(F32) + keep_attn[1].astype(F32)).astype(BF)
    piece_attn = near[0].astype(F32) + keep_attn[0].astype(F32) + fence(pair(far, 2), vec_over_opt).astype(F32)
    piece_attn = move(piece_attn.astype(BF).reshape(dp_size, D // dp_size, D))
    piece_attn = jnp.sum(fence(piece_attn, grad_vec).astype(F32), axis=0).astype(BF)
    shared_attn = share(piece_attn)
    all_mlp = lax.all_gather(piece_mlp, ("dp", "opt"), axis=0).reshape(dp_size, OPT, -1, D)
    *grams, own_mlp, mlp_squares = in_vmem(partial(grams_kernel, order_of_halves(dp_size)),
                                           [((D, D), F32)] * 4 + [((2, D, D), BF), ((8, 128), F32)], "mlp_grams", owner, moms, all_mlp, flops=4e9)
    grams = [old_grams[0], *grams[:2], old_grams[1], *grams[2:]]
    own_attn = fence(shared_attn, *old_grams).reshape(D, D)

    total = fence(jnp.full((8, 128), jnp.sum(piece_attn.astype(F32) ** 2)), *old_grams)
    total = total + pair(total, 1)
    total = total + pair(total, 2)
    for bit in bits():
        if bit == bits()[-1]:
            total = fence(total, mlp_squares)
        total = total + swap(total, bit)
    total = total[0, 0] + mlp_squares[0, 0]
    grad_norm = jnp.sqrt(total + jnp.sum(grad_vec * grad_vec))
    clip = jnp.minimum(1.0, CLIP_LIMIT / (grad_norm + 1e-06))
    attn_mom_new, new_attn, first_mom, new_first, second_mom, new_second = in_vmem(
        update_kernel, [((D, D), F32)] * 6, "matrix_updates", clip.reshape(1, 1), own_attn, attn_mom[0], attn_w[0],
        own_mlp, mlp_in_mom, mlp_out_mom, mlp_in, mlp_out, *grams, flops=12e9)
    clipped = clip * grad_vec
    moment_one = BETA_FIRST * adam_first + (1.0 - BETA_FIRST) * clipped
    moment_two = BETA_SECOND * adam_second + (1.0 - BETA_SECOND) * clipped * clipped
    first_hat = moment_one / (1.0 - BETA_FIRST**OPT_STEP)
    second_hat = moment_two / (1.0 - BETA_SECOND**OPT_STEP)
    new_vec = vec_params - ADAM_RATE * first_hat / (jnp.sqrt(second_hat) + ADAM_EPS)
    return (out_patches, out_regions, d_patches, d_regions, new_attn[None], attn_mom_new[None], new_first, first_mom,
            new_second, second_mom, new_vec, moment_one, moment_two, grad_norm)


def solution(mesh):
    canvas = P("opt", None, "dp", None)
    wide = P("opt", None, "dp", None, None)
    bands = P("opt", "dp", None, None, None)
    square, right, down = P("opt", None, None), P(None, "opt"), P("opt", None)
    return jax.shard_map(
        per_device,
        mesh=mesh,
        in_specs=(bands, canvas, square, square, right, down, P(), wide, canvas, square, right, down, P(), P()),
        out_specs=(wide, canvas, bands, canvas, square, square, right, right, down, down, P(), P(), P(), P()),
        check_vma=False,
    )
```

```python
from functools import partial

import jax
import jax.numpy as jnp
from jax import lax
from jax.experimental import pallas as pl
from jax.experimental.pallas import tpu as pltpu
from jax.sharding import PartitionSpec as P

BF = jnp.bfloat16
F32 = jnp.float32

D = 512
HEADS = 16
HEAD_DIM = 32
FF = 2048
PATCH = 49
LIVE = 50
ROWS = 56
GROUP = 128
QUERIES = 64
STACK = 4 * QUERIES
OPT_STEP = 10
OPT = 4

SCALE = HEAD_DIM ** (-0.5)
NORM_EPS = 1e-05
MASKED = -1e30
NS_FIRST = 3.4445
NS_SECOND = -4.775
NS_THIRD = 2.0315
MUON_RATE = 0.5
MUON_MOMENTUM = 0.5
MUON_DECAY = 0.01
ADAM_RATE = 0.5
BETA_FIRST = 0.9
BETA_SECOND = 0.95
ADAM_EPS = 1e-08
CLIP_LIMIT = 1.0
DECAY_KEEP = 1.0 - MUON_RATE * MUON_DECAY
VMEM = 60 * 2**20


def cost(flops):
    return pl.CostEstimate(flops=int(flops), bytes_accessed=10**5, transcendentals=0)

ERF_P = 0.3275911 * 0.5**0.5
ERF = tuple(0.5 * c for c in (0.254829592, -0.284496736, 1.421413741, -1.453152027, 1.061405429))
INV_SQRT_2PI = 0.3989422804014327
LOG2E = 1.4426950408889634


def nn(a, b):
    return lax.dot_general(a, b, (((1,), (0,)), ((), ())), preferred_element_type=F32)


def nt(a, b):
    return lax.dot_general(a, b, (((1,), (1,)), ((), ())), preferred_element_type=F32)


def tn(a, b):
    return lax.dot_general(a, b, (((0,), (0,)), ((), ())), preferred_element_type=F32)


def full(shape):
    return pl.BlockSpec(shape, lambda i: (0,) * len(shape))


def block(shape):
    return pl.BlockSpec(shape, lambda i: (i,) + (0,) * (len(shape) - 1))


def norm_parts(x):
    centre = x - jnp.mean(x, axis=-1, keepdims=True)
    scale = lax.rsqrt(jnp.mean(centre * centre, axis=-1, keepdims=True) + NORM_EPS)
    return centre * scale, scale


def norm_back(grad, xhat, scale, gain):
    inner = grad * gain
    first = jnp.mean(inner, axis=-1, keepdims=True)
    second = jnp.mean(inner * xhat, axis=-1, keepdims=True)
    return scale * (inner - first - xhat * second)


def head_masks():
    lane = lax.broadcasted_iota(jnp.int32, (1, GROUP), 1) // HEAD_DIM
    return [lane == h for h in range(4)]


def spread(rows, masks):
    return jnp.concatenate([jnp.where(m, rows, 0.0) for m in masks], axis=0).astype(BF)


def spread_low(rows):
    lane = lax.broadcasted_iota(jnp.int32, (1, GROUP), 1) // HEAD_DIM
    return jnp.concatenate([rows * (lane == h).astype(F32).astype(BF) for h in range(4)], axis=0)


def collect(stacked, masks, rows, step=None):
    step = step or rows
    out = stacked[:rows]
    for h in range(1, 4):
        out = jnp.where(masks[h], stacked[h * step : h * step + rows], out)
    return out


def staggered(windows, batch, first, second, third):
    steps = [[(w, g) for w in range(n, n + batch) for g in range(4)] for n in range(0, windows, batch)]
    one, two = {}, {}
    for n in range(len(steps) + 2):
        if n < len(steps):
            one.update({unit: first(*unit) for unit in steps[n]})
        if 0 <= n - 1 < len(steps):
            two.update({unit: second(*unit, one.pop(unit)) for unit in steps[n - 1]})
        if 0 <= n - 2:
            for unit in steps[n - 2]:
                third(*unit, two.pop(unit))


def lane_groups(x):
    return [x[:, GROUP * g : GROUP * (g + 1)] for g in range(4)]


def hold(ref, total, x):
    for g, part in enumerate(lane_groups(x)):
        ref[g, :total] = part


def held_rows(ref, total):
    return jnp.concatenate([ref[g, :total] for g in range(4)], axis=1)


def fold(x):
    return jnp.sum(x.reshape(x.shape[0] // 8, 8, x.shape[1]), axis=0)


def gelu_parts(a):
    bell = jnp.exp2(a * a * (-0.5 * LOG2E))
    t = 1.0 / (1.0 + ERF_P * jnp.abs(a))
    tail = ((((ERF[4] * t + ERF[3]) * t + ERF[2]) * t + ERF[1]) * t + ERF[0]) * t * bell
    share = jnp.where(a < 0, tail, 1.0 - tail)
    return a * share, share + a * bell * INV_SQRT_2PI


def attn_fwd_kernel(count, batch, owner_ref, p_ref, r_ref, w_ref, vec_ref, _,
                    x1_ref, q_ref, k_ref, v_ref, o_ref, pt_ref, q_held, k_held, v_held, o_held):
    total = count * LIVE
    owner = owner_ref[0, 0]

    @pl.when(pl.program_id(0) == 0)
    def _():
        for ref in (q_held, k_held, v_held):
            ref[:, total:] = jnp.zeros((4, ref.shape[1] - total, GROUP), F32)

    x = jnp.concatenate([p_ref[...].astype(F32), r_ref[...][None]], axis=0).reshape(total, D)
    vec = vec_ref[...]
    xhat, _ = norm_parts(x)
    xn = (xhat * vec[0:1] + vec[1:2]).astype(BF)
    hold(q_held, total, nn(xn, w_ref[0]) + vec[4:5])
    hold(k_held, total, nn(xn, w_ref[1]))
    hold(v_held, total, nn(xn, w_ref[2]) + vec[5:6])
    masks = head_masks()
    live = lax.broadcasted_iota(jnp.int32, (8, 1), 0) < LIVE - (ROWS - 8)

    def score(w, g):
        lanes = slice(GROUP * g, GROUP * (g + 1))
        q = q_held[g, pl.ds(w, QUERIES, stride=count), :].astype(BF)
        q_ref[w, :, lanes] = q
        k = k_held[g, pl.ds(w, ROWS, stride=count), :].astype(BF)
        k_ref[w, :, lanes] = k
        return nt(k, spread_low(q))

    def normalize(w, g, s):
        s = jnp.concatenate([s[: ROWS - 8], jnp.where(live, s[ROWS - 8 :], MASKED)], axis=0)
        e = jnp.exp2((s - jnp.max(s, axis=0, keepdims=True)) * (SCALE * LOG2E))
        p = (e * (1.0 / jnp.sum(e, axis=0, keepdims=True))).astype(BF)
        pt_ref[w, g] = p
        return p

    def mix(w, g, p):
        lanes = slice(GROUP * g, GROUP * (g + 1))
        rows = pl.ds(w, ROWS, stride=count)
        v = v_held[g, rows, :].astype(BF)
        v_ref[w, :, lanes] = v
        o_held[g, rows, :] = collect(tn(p, v), masks, ROWS, QUERIES)

    staggered(count, batch, score, normalize, mix)
    mixed = held_rows(o_held, total).astype(BF)
    o_ref[...] = mixed.reshape(LIVE, count, D)
    x1_ref[...] = (x + nn(mixed, w_ref[3]) + vec[6:7]).reshape(LIVE, count, D)


def middle(rows, count, skip=0):
    return pl.BlockSpec((rows, count, D), lambda i: (0, i + skip, 0))


def attn_fwd(owner, patches, region_rows, weights, vec, after, count=16, batch=16):
    windows = patches.shape[1]
    array = jax.ShapeDtypeStruct
    return pl.pallas_call(
        partial(attn_fwd_kernel, count, batch),
        grid=(windows // count,),
        in_specs=[pl.BlockSpec(memory_space=pltpu.SMEM), middle(PATCH, count), block((count, D)), full((4, D, D)),
                  full(vec.shape), pl.BlockSpec(memory_space=pl.ANY)],
        out_specs=[middle(LIVE, count), block((count, QUERIES, D))] + [block((count, ROWS, D))] * 2
        + [middle(LIVE, count), block((count, 4, ROWS, STACK))],
        out_shape=[array((LIVE, windows, D), F32), array((windows, QUERIES, D), BF)]
        + [array((windows, ROWS, D), BF)] * 2
        + [array((LIVE, windows, D), BF), array((windows, 4, ROWS, STACK), BF)],
        scratch_shapes=[pltpu.VMEM((4, count * QUERIES, GROUP), F32)] + [pltpu.VMEM((4, count * ROWS, GROUP), F32)] * 3,
        compiler_params=pltpu.CompilerParams(vmem_limit_bytes=VMEM),
        cost_estimate=cost(16e9),
        name="window_attention_forward",
    )(owner, patches, region_rows, weights, vec, after)


def mlp_kernel(many, sources, cols, steps, lanes, last, *refs):
    x1_ref, pc_ref, *w_refs, vec_ref, b1_ref = refs[:8]
    if last:
        prev_refs = refs[9:11]
        op_ref, dx1_ref, dwa_ref, dwb_ref, dv_ref, db1_ref, acc1, acc2 = refs[11:]
    else:
        prev_refs = ()
        early_ref, op_ref, dx1_ref, dwa_ref, dwb_ref, dv_ref, db1_ref, acc1, acc2 = refs[8:]
    total = many * sources * cols
    step = pl.program_id(0)

    @pl.when(step == 0)
    def _():
        for ref in (dv_ref, db1_ref):
            ref[...] = jnp.zeros_like(ref)

    vec = vec_ref[...]
    gain = vec[2:3]
    x1 = x1_ref[...].reshape(total, D)
    xhat, scale = norm_parts(x1)
    h = (xhat * gain + vec[3:4]).astype(BF)
    for s in range(sources):
        dx1_ref[:, s * cols : (s + 1) * cols] = pc_ref[s].astype(F32)
    dy = dx1_ref[...].reshape(total, D)
    dm = dy.astype(BF)
    ht = h.T
    dmt = dm.T
    y = x1 + vec[7:8]
    dh = jnp.zeros((total, D), F32)
    parts = [(j, slice(c, c + lanes)) for j in range(4) for c in range(0, D, lanes)]

    def activate(j, s):
        u, slope = gelu_parts(nn(h, w_refs[j][0, :, s]) + b1_ref[j : j + 1, s])
        da = slope * nt(dm, w_refs[j][1, s, :])
        db1_ref[j, :, s] += fold(da)
        return u.astype(BF), da.astype(BF)

    def apply(j, s, u, da):
        acc1[j, :, s] = jnp.where(step == 0, 0.0, acc1[j, :, s]) + nn(ht, da)
        acc2[j, :, s] = jnp.where(step == 0, 0.0, acc2[j, :, s]) + nn(dmt, u)
        return nn(u, w_refs[j][1, s, :]), nt(da, w_refs[j][0, :, s])

    held_pair = activate(*parts[0])
    for n in range(1, len(parts) + 1):
        later = activate(*parts[n]) if n < len(parts) else None
        up, down = apply(*parts[n - 1], *held_pair)
        y, dh = y + up, dh + down
        held_pair = later
    y = y.reshape(many, sources * cols, D)

    def put(ref):
        for s in range(sources):
            ref[s] = y[:, s * cols : (s + 1) * cols].astype(BF)

    if last:
        put(op_ref)
    else:
        pl.when(step < steps - 1)(lambda: put(early_ref))
        pl.when(step == steps - 1)(lambda: put(op_ref))
    dy = dx1_ref[...].reshape(total, D)
    dx1_ref[...] = (dy + norm_back(dh, xhat, scale, gain)).reshape(dx1_ref.shape)
    dv_ref[0] += fold(dh * xhat)
    dv_ref[1] += fold(dh)
    dv_ref[2] += fold(dy)

    @pl.when(step == steps - 1)
    def _():
        for refs_out, first in ((dwa_ref, 0), (dwb_ref, 1)):
            for n, acc in enumerate((acc1, acc2)):
                for m in range(2):
                    piece = acc[first + 2 * m]
                    for prev in prev_refs[first : first + 1]:
                        piece = piece + prev[2 * m + n].astype(F32)
                    refs_out[2 * m + n] = piece.astype(BF)


def mlp(x1, first_position, cot, weights, vec, bias_first, prev=(), many=10, lanes=256):
    sources, positions, cols, _ = cot.shape
    windows = sources * cols
    steps = positions // many
    skip = first_position // many
    some = lambda place: pl.BlockSpec((sources, many, cols, D), lambda i: (0, place(i), 0, 0))
    array = jax.ShapeDtypeStruct
    matrices = full((4, D, D))
    rows = lambda count: array((sources, count, cols, D), BF)
    late = (LIVE - positions if not prev else positions) + many
    outs = [some(lambda i: i + 1)] if prev else [some(lambda i: jnp.minimum(i, steps - 2)), some(lambda i: 0)]
    shapes = [rows(late)] if prev else [rows(positions - many), rows(late)]
    return pl.pallas_call(
        partial(mlp_kernel, many, sources, cols, steps, lanes, len(prev) > 0),
        grid=(steps,),
        in_specs=[pl.BlockSpec((many, windows, D), lambda i: (i + skip, 0, 0)), some(lambda i: i)]
        + [full((2, D, D))] * 4 + [full(vec.shape), full((4, D))]
        + ([pl.BlockSpec(memory_space=pl.ANY)] + [matrices] * 2 if prev else []),
        out_specs=outs + [block((many, windows, D)), matrices, matrices, full((3, 8, D)), full((4, 8, D))],
        out_shape=shapes + [array((positions, windows, D), F32), array((4, D, D), BF),
                            array((4, D, D), BF), array((3, 8, D), F32), array((4, 8, D), F32)],
        scratch_shapes=[pltpu.VMEM((4, D, D), F32), pltpu.VMEM((4, D, D), F32)],
        input_output_aliases={8: 0} if prev else {},
        compiler_params=pltpu.CompilerParams(vmem_limit_bytes=VMEM),
        cost_estimate=cost(4e9 * steps),
        name="mlp_forward_backward",
    )(x1, cot, *weights, vec, bias_first, *prev)


def attn_bwd_kernel(count, batch, chunks, more, owner_ref, *refs):
    p_ref, r_ref = refs[:2]
    refs = refs[:3] + refs[4:]
    dx1_refs = refs[3 : 3 + chunks]
    q_ref, k_ref, v_ref, o_ref, pt_ref, w_ref, vec_ref = refs[3 + chunks : 10 + chunks]
    owner = owner_ref[0, 0]
    prev_refs = refs[10 + chunks : 14 + chunks] if more else ()
    dp_ref, dr_ref, dw_ref, dv_ref, dq_held, dk_held, dvv_held, do_held = refs[10 + chunks + len(prev_refs) :]
    total = count * LIVE

    @pl.when(pl.program_id(0) == 0)
    def _():
        dw_ref[...] = prev_refs[2][...] if more else jnp.zeros_like(dw_ref)
        dv_ref[...] = prev_refs[3][...] if more else jnp.zeros_like(dv_ref)
        do_held[:, total:] = jnp.zeros((4, count * (QUERIES - LIVE), GROUP), F32)

    vec = vec_ref[...]
    gain = vec[0:1]
    dx1 = jnp.concatenate([ref[...] for ref in dx1_refs], axis=0).reshape(total, D)
    gb = dx1.astype(BF)
    hold(do_held, total, nt(gb, w_ref[3]))
    masks = head_masks()

    def grad(w, g):
        lanes = slice(GROUP * g, GROUP * (g + 1))
        do_wide = spread_low(do_held[g, pl.ds(w, QUERIES, stride=count), :].astype(BF))
        dvv_held[g, pl.ds(w, ROWS, stride=count), :] = nn(pt_ref[w, g], do_wide)
        return nt(v_ref[w, :, lanes], do_wide)

    def score(w, g, grad):
        p = pt_ref[w, g].astype(F32)
        both = p * grad
        return (both - p * jnp.sum(both, axis=0, keepdims=True)).astype(BF)

    def finish(w, g, ds):
        lanes = slice(GROUP * g, GROUP * (g + 1))
        rows = pl.ds(w, ROWS, stride=count)
        dk_held[g, rows, :] = nn(ds, spread_low(q_ref[w, :, lanes])) * SCALE
        dq_held[g, rows, :] = collect(tn(ds, k_ref[w, :, lanes]), masks, ROWS, QUERIES) * SCALE

    staggered(count, batch, grad, score, finish)
    x = jnp.concatenate([p_ref[...].astype(F32), r_ref[...][None]], axis=0).reshape(total, D)
    xhat, scale = norm_parts(x)
    xn = (xhat * gain + vec[1:2]).astype(BF)
    dq_wide = held_rows(dq_held, total)
    dv_wide = held_rows(dvv_held, total)
    dq = dq_wide.astype(BF)
    dk = held_rows(dk_held, total).astype(BF)
    dv = dv_wide.astype(BF)
    dn = nt(dq, w_ref[0]) + nt(dk, w_ref[1]) + nt(dv, w_ref[2])
    dx = (dx1 + norm_back(dn, xhat, scale, gain)).reshape(LIVE, count, D)
    dp_ref[...] = dx[:PATCH].astype(BF)
    dr_ref[...] = dx[PATCH]
    xt = xn.T
    dw_ref[0] += nn(xt, dq)
    dw_ref[1] += nn(xt, dk)
    dw_ref[2] += nn(xt, dv)
    dw_ref[3] += nn(o_ref[...].reshape(total, D).T, gb)
    dv_ref[0] += fold(dn * xhat)
    dv_ref[1] += fold(dn)
    dv_ref[2] += fold(dq_wide)
    dv_ref[3] += fold(dv_wide)
    dv_ref[4] += fold(dx1)


def attn_bwd(owner, patches, region_rows, dx1_parts, saved, weights, vec, start, windows, after, prev=(), count=16, batch=16):
    skip = start // count
    array = jax.ShapeDtypeStruct
    sums = [full((4, D, D)), full((5, 8, D))]
    anywhere = pl.BlockSpec(memory_space=pl.ANY)
    rows = pl.BlockSpec((count, D), lambda i: (i + skip, 0))
    before = 12 + len(dx1_parts)
    return pl.pallas_call(
        partial(attn_bwd_kernel, count, batch, len(dx1_parts), len(prev) > 0),
        grid=(windows // count,),
        in_specs=[pl.BlockSpec(memory_space=pltpu.SMEM), middle(PATCH, count, skip), rows, anywhere, anywhere]
        + [middle(part.shape[0], count, skip) for part in dx1_parts]
        + [pl.BlockSpec((count, r, D), lambda i: (i + skip, 0, 0)) for r in (QUERIES, ROWS, ROWS)]
        + [middle(LIVE, count, skip), pl.BlockSpec((count, 4, ROWS, STACK), lambda i: (i + skip, 0, 0, 0))]
        + [full((4, D, D)), full(vec.shape)] + ([anywhere] * 2 + sums)[: len(prev)],
        out_specs=[middle(PATCH, count, skip), rows] + sums,
        out_shape=[array(patches.shape, BF), array(region_rows.shape, F32),
                   array((4, D, D), F32), array((5, 8, D), F32)],
        scratch_shapes=[pltpu.VMEM((4, count * ROWS, GROUP), F32)] * 3 + [pltpu.VMEM((4, count * QUERIES, GROUP), F32)],
        input_output_aliases={before: 0, before + 1: 1} if prev else {},
        compiler_params=pltpu.CompilerParams(vmem_limit_bytes=VMEM),
        cost_estimate=cost(12e9),
        name="window_attention_backward",
    )(owner, patches, region_rows, *after, *dx1_parts, *saved, weights, vec, *prev)


def regional_fwd_kernel(owner_ref, canvas_ref, band_ref, ids_ref, band_ids_ref, own_ref, mate_ref, across_ref, last_ref,
                        vec_ref, r1_ref, mixed_ref, level_ref, q_ref, k_ref, v_ref, w_ref):
    vec = vec_ref[...]
    owner = owner_ref[0, 0]
    for n, piece in enumerate((own_ref, mate_ref, across_ref, last_ref)):
        w_ref[owner ^ n] = piece[...]
    xhat, _ = norm_parts(canvas_ref[...].astype(F32))
    low = (xhat * vec[0:1] + vec[1:2]).astype(BF)
    q_ref[...] = (nn(low, w_ref[0]) + vec[4:5]).astype(BF)
    k_ref[...] = nn(low, w_ref[1]).astype(BF)
    v_ref[...] = (nn(low, w_ref[2]) + vec[5:6]).astype(BF)
    band = band_ref[...].astype(F32)
    rows = band.shape[0]
    xhat, _ = norm_parts(band)
    q = nn((xhat * vec[0:1] + vec[1:2]).astype(BF), w_ref[0]) + vec[4:5]
    masks = head_masks()
    same = ids_ref[...] == band_ids_ref[...]
    scores, probs = [], []
    for g in range(4):
        lanes = slice(GROUP * g, GROUP * (g + 1))
        scores.append(nt(k_ref[:, lanes], spread(q[:, lanes], masks)))
    for g, s in enumerate(scores):
        s = jnp.where(same, s, MASKED)
        peak = jnp.max(s, axis=0, keepdims=True)
        e = jnp.exp((s - peak) * SCALE)
        sums = jnp.sum(e, axis=0, keepdims=True)
        level_ref[g : g + 1] = peak * SCALE + jnp.log(sums)
        probs.append((e * (1.0 / sums)).astype(BF))
    for g, p in enumerate(probs):
        lanes = slice(GROUP * g, GROUP * (g + 1))
        mixed_ref[:, lanes] = collect(tn(p, v_ref[:, lanes]), masks, rows)
    r1_ref[...] = band + nn(mixed_ref[...].astype(BF), w_ref[3]) + vec[6:7]


def in_vmem(kernel, outs, name, *args, after=(), scratch=(), flops=2e9, in_hbm=()):
    spaces = [pltpu.SMEM if arg.shape == (1, 1) else pltpu.VMEM for arg in args]
    spaces = [pl.ANY if n in in_hbm else space for n, space in enumerate(spaces)]
    count = len(args)
    return pl.pallas_call(
        lambda *refs: kernel(*refs[:count], *refs[count + len(after) :]),
        in_specs=[pl.BlockSpec(memory_space=space) for space in spaces]
        + [pl.BlockSpec(memory_space=pl.ANY) for _ in after],
        out_specs=[pl.BlockSpec(memory_space=pltpu.VMEM) for _ in outs],
        out_shape=[jax.ShapeDtypeStruct(*out) for out in outs],
        scratch_shapes=list(scratch),
        compiler_params=pltpu.CompilerParams(vmem_limit_bytes=VMEM),
        cost_estimate=cost(flops),
        name=name,
    )(*args, *after)


def payload_kernel(owner_ref, dr_ref, mixed_ref, level_ref, w_ref, grad_ref, extra_ref):
    low = dr_ref[...].astype(BF)
    grad_ref[...] = low
    both = nt(low, w_ref[3]).astype(BF).astype(F32) * mixed_ref[...]
    head = lax.broadcasted_iota(jnp.int32, (D, GROUP), 0) // HEAD_DIM
    lane = lax.broadcasted_iota(jnp.int32, (D, GROUP), 1)
    pick = ((head == lane) | (head + HEADS == lane)).astype(BF)
    high, low_part = halves(both)
    rest = (both - high.astype(F32) - low_part.astype(F32)).astype(BF)
    delta = nn(high, pick) + (nn(low_part, pick) + nn(rest, pick))
    top = delta.astype(BF).astype(F32)
    lane = lax.broadcasted_iota(jnp.int32, (1, GROUP), 1)
    level = level_ref[...]
    level_top = level.astype(BF).astype(F32)
    level_rest = level - level_top
    level_mid = level_rest.astype(BF).astype(F32)
    extra = level_rest - level_mid
    for place, term in ((4, level_mid), (3, level_top), (2, delta - top), (1, top)):
        extra = jnp.where(lane < place * HEADS, term, extra)
    extra_ref[...] = extra.astype(BF)


def regional_bwd_kernel(own_rows, owner_ref, place_ref, q_ref, k_ref, v_ref, canvas_ref, grads_ref, extra_ref, ids_ref,
                        ids_row_ref, ids_own_ref, ids_own_row_ref, mixed_ref, band_grad_ref, dw_ref, w_ref, vec_ref,
                        dr_ref, keep_ref, give_ref, gv_ref, sum_held):
    vec = vec_ref[...]
    owner = owner_ref[0, 0]
    mine = pl.ds(pl.multiple_of(place_ref[0, 0] * own_rows, own_rows), own_rows)
    masks = head_masks()
    grads_own = grads_ref[mine]
    do = nt(grads_ref[...], w_ref[3]).astype(BF).astype(F32)
    do_own = nt(grads_own, w_ref[3]).astype(BF).astype(F32)
    same_own = ids_ref[...] == ids_own_row_ref[...]
    same = ids_own_ref[...] == ids_row_ref[...]
    lanes = [slice(GROUP * g, GROUP * (g + 1)) for g in range(4)]

    def columns(rows):
        term = rows.astype(F32).T
        part = lambda n: term[n * HEADS : (n + 1) * HEADS]
        wide = lambda x: [jnp.concatenate([x[h : h + 1] for h in range(4 * g, 4 * g + 4)], axis=1) for g in range(4)]
        return wide(part(0) + part(1)), wide(part(2) + part(3) + part(4))

    delta, level = columns(extra_ref[...])
    delta_own, level_own = columns(extra_ref[mine])
    first, second = [], []
    dqs, dks, dvs = [], [], []
    for g in range(4):
        q_wide = spread(q_ref[mine, lanes[g]].astype(F32), masks)
        do_wide = spread(do_own[:, lanes[g]], masks)
        first.append((nt(k_ref[:, lanes[g]], q_wide), nt(v_ref[:, lanes[g]], do_wide)))
        q_wide = spread(q_ref[:, lanes[g]].astype(F32), masks)
        do_wide = spread(do[:, lanes[g]], masks)
        second.append((nt(k_ref[mine, lanes[g]], q_wide), nt(v_ref[mine, lanes[g]], do_wide), q_wide, do_wide))
    for g in range(4):
        s, dp = first[g]
        p = jnp.where(same_own, jnp.exp(s * SCALE - level_own[g]), 0.0)
        ds = (p * (dp - delta_own[g])).astype(BF)
        dqs.append(collect(tn(ds, k_ref[:, lanes[g]]), masks, own_rows) * SCALE)
        s, dp, q_wide, do_wide = second[g]
        p = jnp.where(same, jnp.exp(s * SCALE - level[g]), 0.0)
        ds = (p * (dp - delta[g])).astype(BF)
        dvs.append(nn(p.astype(BF), do_wide))
        dks.append(nn(ds, q_wide) * SCALE)
    xhat, scale = norm_parts(canvas_ref[mine].astype(F32))
    low = (xhat * vec[0:1] + vec[1:2]).astype(BF)
    dq_wide, dk_wide, dv_wide = (jnp.concatenate(x, axis=1) for x in (dqs, dks, dvs))
    dq, dk, dv = dq_wide.astype(BF), dk_wide.astype(BF), dv_wide.astype(BF)
    dn = nt(dq, w_ref[0]) + nt(dk, w_ref[1]) + nt(dv, w_ref[2])
    dr_ref[...] = grads_own.astype(F32) + norm_back(dn, xhat, scale, vec[0:1])
    sum_held[0] = dw_ref[0] + tn(low, dq)
    sum_held[1] = dw_ref[1] + tn(low, dk)
    sum_held[2] = dw_ref[2] + tn(low, dv)
    sum_held[3] = dw_ref[3] + tn(mixed_ref[...].astype(BF), band_grad_ref[...])
    for n in range(2):
        keep_ref[n] = sum_held[owner ^ (2 * n)].astype(BF)
        give_ref[n] = sum_held[owner ^ (2 * n + 1)].astype(BF)
    gv_ref[0] = fold(dn * xhat)
    gv_ref[1] = fold(dn)
    gv_ref[2] = fold(dq_wide)
    gv_ref[3] = fold(dv_wide)
    gv_ref[4] = fold(band_grad_ref[...].astype(F32))


def halves(a):
    high = a.astype(BF)
    return high, (a - high.astype(F32)).astype(BF)


def terms(a, passes):
    return (a.astype(BF),) if passes == 1 else halves(a)


def product(a, b, dot=nn):
    if len(a) == 1:
        return dot(a[0], b[0])
    return dot(a[0], b[0]) + (dot(a[0], b[1]) + dot(a[1], b[0]))


def symmetric(a, b, dot=nn):
    half = D // 2
    right = (lambda x: x[half:]) if dot is nt else (lambda x: x[:, half:])
    top = product([x[:half] for x in a], b, dot)
    corner = product([x[half:] for x in a], [right(x) for x in b], dot)
    return jnp.concatenate([top, jnp.concatenate([top[:, half:].T, corner], axis=1)], axis=0)


DIRECT_STEPS = (1, 1, 1, -1, -1)
GRAM_STEPS = (1, 1, 3, 3, 3)
NEAR_ZERO = NS_FIRST + NS_SECOND + NS_THIRD
NEAR_ONE = NS_SECOND + 2.0 * NS_THIRD


def identity():
    rows = lax.broadcasted_iota(jnp.int32, (D, D), 0)
    return rows == lax.broadcasted_iota(jnp.int32, (D, D), 1)


def polynomial(gram, eye, step):
    if step > 0:
        parts = terms(gram, step)
        return NS_FIRST, NS_SECOND * gram + NS_THIRD * symmetric(parts, parts)
    rest = gram - jnp.where(eye, 1.0, 0.0)
    parts = terms(rest, -step)
    return NEAR_ZERO, NEAR_ONE * rest + NS_THIRD * symmetric(parts, parts)


def direct_steps(moment, eye):
    z = moment * (1.0 / (jnp.sqrt(jnp.sum(moment * moment)) + 1e-07))
    for step in DIRECT_STEPS:
        parts = terms(z, abs(step))
        gram = symmetric(parts, parts, nt)
        yield
        scale, poly = polynomial(gram, eye, step)
        yield
        z = scale * z + product(terms(poly, abs(step)), parts)
        yield
    return z


def gram_steps(gram, eye):
    factor = 1.0 / (jnp.sqrt(jnp.sum(jnp.where(eye, gram, 0.0))) + 1e-07)
    gram = gram * (factor * factor)
    steps = None
    for n, passes in enumerate(GRAM_STEPS):
        scale, poly = polynomial(gram, eye, passes)
        yield
        parts = terms(poly, passes)
        if steps is None:
            steps = jnp.where(eye, scale, 0.0) + poly
        else:
            steps = scale * steps + symmetric(parts, terms(steps, passes))
            yield
        if n < len(GRAM_STEPS) - 1:
            half = scale * gram + symmetric(parts, terms(gram, passes))
            yield
            gram = scale * half + symmetric(parts, terms(half, passes))
            yield
    return steps * factor


def in_turns(*chains):
    results = [None] * len(chains)
    running = list(enumerate(chains))
    while running:
        still = []
        for n, chain in running:
            try:
                next(chain)
                still.append((n, chain))
            except StopIteration as stop:
                results[n] = stop.value
        running = still
    return results


def old_grams_kernel(moms_ref, *out_refs):
    for n, out_ref in enumerate(out_refs):
        square, cross = jnp.zeros((D, D), F32), jnp.zeros((D, D), F32)
        for j in range(OPT):
            high, low = halves(moms_ref[j, n])
            if n == 1:
                high, low = high.T, low.T
            square = square + nt(high, high)
            cross = cross + nt(high, low)
        out_ref[...] = square + (cross + cross.T)


def grams_kernel(places, owner_ref, moms_ref, all_ref, mixed1_ref, new1_ref, mixed2_ref, new2_ref, own_ref,
                 squares_ref, moms_held, all_held, moms_sems, all_sems):
    half = len(places) // 2
    squares = jnp.zeros((8, D), F32)
    all_copies = [pltpu.make_async_copy(all_ref.at[:, j], all_held.at[:, j], all_sems.at[j]) for j in range(OPT)]
    moms_copies = [[pltpu.make_async_copy(moms_ref.at[j, n], moms_held.at[j, n], moms_sems.at[j, n])
                    for n in range(2)] for j in range(OPT)]
    for j in range(OPT):
        all_copies[j].start()
        moms_copies[j][0].start()
    for j in range(OPT):
        moms_copies[j][1].start()
    for n, (mixed_ref, new_ref) in enumerate(((mixed1_ref, new1_ref), (mixed2_ref, new2_ref))):
        mixed, new = jnp.zeros((D, D), F32), jnp.zeros((D, D), F32)
        mine = places[n * half : (n + 1) * half]
        for j in range(OPT):
            if n == 0:
                all_copies[j].wait()
            moms_copies[j][n].wait()
            high, low = halves(moms_held[j, n])
            if n == 1:
                high, low = high.T, low.T
            g = jnp.concatenate([all_held[d, j] for d in mine], axis=0)
            wide = g.astype(F32)
            squares = squares + fold(wide * wide)
            mixed = mixed + (nt(high, g) + nt(low, g))
            new = new + nt(g, g)
        mixed_ref[...] = mixed + mixed.T
        new_ref[...] = new
        own_ref[n] = jnp.concatenate([all_held[d, owner_ref[0, 0]] for d in mine], axis=0)
    squares_ref[...] = jnp.full((8, 128), jnp.sum(squares))


def update_kernel(total_ref, squares_ref, gv_ref, vec_ref, first_ref, second_ref, ga_ref, ma_ref, wa_ref, g_ref, m1_ref, m2_ref, w1_ref, w2_ref,
                  old1, mixed1, new1, old2, mixed2, new2, na_ref, newa_ref, n1_ref, new1_ref, n2_ref, new2_ref,
                  norm_ref, newv_ref, one_ref, two_ref):
    gv = gv_ref[...]
    norm = jnp.sqrt(jnp.max(total_ref[...]) + jnp.max(squares_ref[...]) + jnp.sum(gv * gv))
    clip = jnp.minimum(1.0, CLIP_LIMIT / (norm + 1e-06))
    norm_ref[...] = jnp.full((8, 128), norm)
    clipped = clip * gv
    one = BETA_FIRST * first_ref[...] + (1.0 - BETA_FIRST) * clipped
    two = BETA_SECOND * second_ref[...] + (1.0 - BETA_SECOND) * clipped * clipped
    one_ref[...] = one
    two_ref[...] = two
    first_hat = one / (1.0 - BETA_FIRST**OPT_STEP)
    second_hat = two / (1.0 - BETA_SECOND**OPT_STEP)
    newv_ref[...] = vec_ref[...] - ADAM_RATE * first_hat / (jnp.sqrt(second_hat) + ADAM_EPS)
    eye = identity()
    na_ref[...] = MUON_MOMENTUM * ma_ref[...] + clip * ga_ref[...].astype(F32)
    n1_ref[...] = MUON_MOMENTUM * m1_ref[...] + clip * g_ref[0].astype(F32)
    n2_ref[...] = MUON_MOMENTUM * m2_ref[...] + clip * g_ref[1].astype(F32).T
    a, b, c = MUON_MOMENTUM * MUON_MOMENTUM, MUON_MOMENTUM * clip, clip * clip
    gram1 = a * old1[...] + b * mixed1[...] + c * new1[...]
    gram2 = a * old2[...] + b * mixed2[...] + c * new2[...]
    steps1, steps2, z = in_turns(gram_steps(gram1, eye), gram_steps(gram2, eye), direct_steps(na_ref[...], eye))
    newa_ref[...] = wa_ref[...] * DECAY_KEEP - MUON_RATE * z
    z = product(halves(steps1), halves(n1_ref[...]))
    new1_ref[...] = w1_ref[...] * DECAY_KEEP - MUON_RATE * z
    z = product(halves(n2_ref[...]), halves(steps2))
    new2_ref[...] = w2_ref[...] * DECAY_KEEP - (MUON_RATE * max(1.0, FF / D) ** 0.5) * z


def pair(values, bit):
    return lax.ppermute(values, "opt", [(i, i ^ bit) for i in range(OPT)])


def fence(x, *first):
    here = pl.BlockSpec(memory_space=pl.ANY)
    return pl.pallas_call(
        lambda *refs: None,
        in_specs=[here] * (1 + len(first)),
        out_specs=here,
        out_shape=jax.ShapeDtypeStruct(x.shape, x.dtype),
        input_output_aliases={0: 0},
        cost_estimate=cost(1e3),
        name="fence",
    )(x, *first)


def pieces_of_owners(own):
    mate = pair(own, 1)
    across = pair(own, 2)
    return [own, mate, across, pair(across, 1)]


def share(x, *first):
    copies = jnp.broadcast_to(x[None], (lax.axis_size("dp"),) + x.shape)
    if first:
        copies = fence(copies, *first)
    return lax.all_to_all(copies, "dp", 0, 0, tiled=True)


def swap(x, bit):
    return lax.ppermute(x, "dp", [(i, i ^ bit) for i in range(lax.axis_size("dp"))])


def bits():
    return [1 << n for n in range(lax.axis_size("dp").bit_length() - 1)]


def halving_step(x, bit):
    half = x.shape[0] // 2
    side = (lax.axis_index("dp") // bit) % 2
    give = lax.dynamic_slice_in_dim(x, (1 - side) * half, half, 0).astype(BF)
    return lax.dynamic_slice_in_dim(x, side * half, half, 0), give


def order_of_halves(count):
    width = count.bit_length() - 1
    return [int(format(n, "b").zfill(width)[::-1], 2) if width else 0 for n in range(count)]


def sum_small_over_dp(x):
    for bit in bits():
        x = x + swap(x, bit)
    return x


def split_heads(x):
    return x.reshape(x.shape[0], HEADS, HEAD_DIM)


def regional_forward(canvas, band, same, weights, vec):
    low = lambda x: (norm_parts(x.astype(F32))[0] * vec[0] + vec[1]).astype(BF)
    normed = low(canvas)
    queries = (nn(normed, weights[0]) + vec[4]).astype(BF)
    keys = nn(normed, weights[1]).astype(BF)
    values = (nn(normed, weights[2]) + vec[5]).astype(BF)
    own = (nn(low(band), weights[0]) + vec[4]).astype(BF)
    scores = jnp.einsum("qhd,khd->hqk", split_heads(own), split_heads(keys), preferred_element_type=F32)
    scores = jnp.where(same[None], scores * SCALE, MASKED)
    peak = jnp.max(scores, axis=-1, keepdims=True)
    raised = jnp.exp(scores - peak)
    sums = jnp.sum(raised, axis=-1, keepdims=True)
    probs = (raised / sums).astype(BF)
    mixed = jnp.einsum("hqk,khd->qhd", probs, split_heads(values), preferred_element_type=F32).reshape(own.shape)
    region_rows = band.astype(F32) + nn(mixed.astype(BF), weights[3]) + vec[6]
    return region_rows, mixed, (peak + jnp.log(sums))[:, :, 0], queries, keys, values


def regional_terms(queries, keys, values, grad_mixed, same, level, delta):
    scores = jnp.einsum("qhd,khd->hqk", split_heads(queries), split_heads(keys), preferred_element_type=F32)
    probs = jnp.where(same[None], jnp.exp(scores * SCALE - level[:, :, None]), 0.0)
    grads = jnp.einsum("qhd,khd->hqk", split_heads(grad_mixed), split_heads(values), preferred_element_type=F32)
    return probs.astype(BF), (probs * (grads - delta[:, :, None])).astype(BF)


def regional_backward(queries, keys, values, grads, own, rows, same, level, delta, weights, vec, mixed, band_grad, dw):
    grad_mixed = nt(grads, weights[3]).astype(BF)
    level_own, delta_own = own(level.T).T, own(delta.T).T
    _, scores = regional_terms(own(queries), keys, values, own(grad_mixed), same.T, level_own, delta_own)
    dq = jnp.einsum("hqk,khd->qhd", scores, split_heads(keys), preferred_element_type=F32)
    probs, scores = regional_terms(queries, own(keys), own(values), grad_mixed, same, level, delta)
    dk = jnp.einsum("hqk,qhd->khd", scores, split_heads(queries), preferred_element_type=F32)
    dv = jnp.einsum("hqk,qhd->khd", probs, split_heads(grad_mixed), preferred_element_type=F32)
    flat = lambda x: x.reshape(-1, D)
    dq, dk, dv = flat(dq) * SCALE, flat(dk) * SCALE, flat(dv)
    lows = [x.astype(BF) for x in (dq, dk, dv)]
    dn = sum(nt(x, w) for x, w in zip(lows, weights))
    xhat, scale = norm_parts(rows.astype(F32))
    low = (xhat * vec[0] + vec[1]).astype(BF)
    d_regions = own(grads).astype(F32) + norm_back(dn, xhat, scale, vec[0])
    matrices = [dw[j] + tn(low, x) for j, x in enumerate(lows)] + [dw[3] + tn(mixed.astype(BF), band_grad)]
    vectors = [fold(x) for x in (dn * xhat, dn, dq, dv, band_grad.astype(F32))]
    return d_regions, jnp.stack(matrices).astype(BF), jnp.stack(vectors)


def per_device(patches, regions, image_ids, attn_w, mlp_in, mlp_out, vec_params, patch_cot, region_cot,
               attn_mom, mlp_in_mom, mlp_out_mom, adam_first, adam_second):
    dp_size = lax.axis_size("dp")
    dp_index = lax.axis_index("dp")
    opt_index = lax.axis_index("opt")
    _, grid_rows, cols, _, _ = patch_cot.shape
    grid_cols = patches.shape[2]
    tokens = grid_rows * grid_cols
    own_count = grid_rows * cols
    one_kernel = tokens <= 1024
    vec = vec_params
    order = opt_index ^ jnp.arange(OPT)
    move = lambda x: lax.all_to_all(x, "dp", 0, 0, tiled=True)

    attn_low = attn_w[0].astype(BF)
    attn_pieces = pieces_of_owners(attn_low)
    mlp_w = pieces_of_owners(jnp.stack([mlp_in, mlp_out]).astype(BF))
    owner = opt_index.reshape(1, 1)
    canvas_blocks = share(regions[0], attn_low)
    canvas = canvas_blocks.reshape(tokens, D)
    by_position = patch_cot[0].transpose(0, 2, 1, 3)
    split = 30
    last = jnp.concatenate([by_position[:, split:], region_cot[0][:, None]], axis=1)
    first_cot = move(fence(by_position[:, :split], canvas))
    bias_first = jnp.take(vec[8:], order, axis=0)

    band_of = lambda x: lax.dynamic_slice_in_dim(x, dp_index, 1, 1).reshape((grid_cols,) + x.shape[3:])
    own_of = lambda x: lax.dynamic_slice_in_dim(x, dp_index * own_count, own_count, 0)
    ids_blocks = image_ids[0].reshape(grid_rows, dp_size, cols).transpose(1, 0, 2)
    ids = ids_blocks.reshape(tokens)
    band_ids, own_ids = band_of(ids_blocks), own_of(ids)
    band = band_of(canvas_blocks)
    if one_kernel:
        repeat = lambda x: jnp.tile(x, 4)[None]
        region_rows, mixed, level, reg_q, reg_k, reg_v, weights = in_vmem(
            regional_fwd_kernel,
            [((grid_cols, D), F32), ((grid_cols, D), F32), ((4, 4 * grid_cols), F32)] + [((tokens, D), BF)] * 3
            + [((4, D, D), BF)],
            "regional_attention_forward", owner, canvas, band, ids[:, None], repeat(band_ids), *attn_pieces, vec,
            after=(mlp_w[1],))
        level = level.reshape(HEADS, grid_cols)
    else:
        weights = jnp.take(jnp.stack(attn_pieces), order, axis=0)
        region_rows, mixed, level, reg_q, reg_k, reg_v = regional_forward(
            canvas, band, band_ids[:, None] == ids[None, :], weights, vec)
    level_wide = jnp.tile(level.T, (1, GROUP // HEADS))

    windows = patches[0, 0].transpose(1, 0, 2)
    some = grid_cols // 2
    x1, *saved = attn_fwd(owner, windows, region_rows, weights, vec, mlp_w[2])
    last_cot = move(fence(last, x1))
    early_out, late_out, dx1_a, *grads_a = mlp(x1, 0, first_cot, mlp_w, vec, bias_first)
    moved_a = move(early_out)
    moms = lax.all_gather(fence(jnp.stack([mlp_in_mom, mlp_out_mom]), x1), "opt", axis=0)
    late_out, dx1_b, *grads_b = mlp(x1, split, last_cot, mlp_w, vec, bias_first, prev=(late_out, *grads_a[:2]))
    near = pair(fence(grads_b[1], moved_a), 1)
    far = (near[2:].astype(F32) + grads_b[0][2:].astype(F32)).astype(BF)
    moved_b = move(fence(late_out, far))
    out_patches = jnp.concatenate([moved_a, moved_b[:, :-1]], axis=1).transpose(0, 2, 1, 3)[None]
    out_regions = moved_b[None, :, -1]

    dx1 = (dx1_a, dx1_b)
    early = attn_bwd(owner, windows, region_rows, dx1, saved, weights, vec, 0, some, (far, far))
    own_mlp = near[:2].astype(F32) + grads_b[0][:2].astype(F32) + fence(pair(far, 2), early[3]).astype(F32)
    keep, give = halving_step(own_mlp.reshape(2 * D, D), 1)
    d_patches, d_region, d_attn, d_vec_attn = attn_bwd(
        owner, windows, region_rows, dx1, saved, weights, vec, some, some, (give, moms), prev=early)
    d_patches = d_patches.transpose(1, 0, 2)[None, None]
    gives = []
    old_grams = in_vmem(old_grams_kernel, [((D, D), F32)] * 2, "momentum_grams", moms, after=(d_vec_attn,),
                         flops=4e9)

    band_grad, extra = in_vmem(payload_kernel, [((grid_cols, D), BF), ((grid_cols, GROUP), BF)],
                               "regional_payload", owner, d_region, mixed, level_wide, weights,
                               after=(give, moved_b))
    taken = fence(swap(give, 1), band_grad)
    for bit in bits()[1:]:
        keep, give = halving_step(keep + taken.astype(F32), bit)
        gives.append(give)
        taken = swap(give, bit)
    payload = share(jnp.concatenate([band_grad, extra], axis=1)).reshape(grid_rows, dp_size, cols, D + GROUP)
    payload = payload.transpose(1, 0, 2, 3).reshape(tokens, D + GROUP)
    grads = payload[:, :D]
    extra = payload[:, D:]
    if one_kernel:
        matrices = ((2, D, D), BF)
        d_regions, keep_attn, give_attn, d_vec_reg = in_vmem(
            partial(regional_bwd_kernel, own_count),
            [((own_count, D), F32), matrices, matrices, ((5, 8, D), F32)],
            "regional_attention_backward", owner, dp_index.reshape(1, 1), reg_q, reg_k, reg_v, canvas, grads, extra,
            ids[:, None], repeat(ids), own_ids[:, None], repeat(own_ids), mixed, band_grad, d_attn, weights, vec,
            after=tuple(old_grams), scratch=[pltpu.VMEM((4, D, D), F32)], flops=4e9)
    else:
        part = lambda n: extra[:, n * HEADS : (n + 1) * HEADS].astype(F32)
        delta, level = (part(0) + part(1)).T, (part(2) + part(3) + part(4)).T
        d_regions, grad_attn, d_vec_reg = regional_backward(
            reg_q, reg_k, reg_v, grads, own_of, own_of(canvas), ids[:, None] == own_ids[None, :], level, delta,
            weights, vec, mixed, band_grad, d_attn)
        pick = lambda j: lax.dynamic_index_in_dim(grad_attn, opt_index ^ j, 0, keepdims=False)
        keep_attn, give_attn = jnp.stack([pick(0), pick(2)]), jnp.stack([pick(1), pick(3)])
    d_regions = d_regions.reshape(regions.shape)

    d_vec_attn = jnp.sum(d_vec_attn + d_vec_reg, axis=1)
    d_vec_mlp = jnp.sum(grads_a[2] + grads_b[2], axis=1)
    d_bias_first = jnp.take(jnp.sum(grads_a[3] + grads_b[3], axis=1), order, axis=0)
    grad_vec = jnp.concatenate([d_vec_attn[:2], d_vec_mlp[:2], d_vec_attn[2:], d_vec_mlp[2:], d_bias_first])
    grad_vec = grad_vec + pair(grad_vec, 1)
    vec_over_opt = grad_vec + pair(grad_vec, 2)
    grad_vec = sum_small_over_dp(vec_over_opt)

    piece_mlp = (keep + fence(taken, give_attn).astype(F32)).astype(BF)

    near = pair(give_attn, 1)
    far = (near[1].astype(F32) + keep_attn[1].astype(F32)).astype(BF)
    piece_attn = near[0].astype(F32) + keep_attn[0].astype(F32) + fence(pair(far, 2), vec_over_opt).astype(F32)
    piece_attn = move(piece_attn.astype(BF).reshape(dp_size, D // dp_size, D))
    piece_attn = jnp.sum(fence(piece_attn, grad_vec).astype(F32), axis=0).astype(BF)
    shared_attn = share(piece_attn)
    all_mlp = lax.all_gather(piece_mlp, ("dp", "opt"), axis=0).reshape(dp_size, OPT, -1, D)
    *grams, own_mlp, mlp_squares = in_vmem(
        partial(grams_kernel, order_of_halves(dp_size)), [((D, D), F32)] * 4 + [((2, D, D), BF), ((8, 128), F32)], "mlp_grams",
        owner, moms, all_mlp, flops=4e9, in_hbm=(1, 2),
        scratch=[pltpu.VMEM(moms.shape, F32), pltpu.VMEM(all_mlp.shape, BF), pltpu.SemaphoreType.DMA((OPT, 2)),
                 pltpu.SemaphoreType.DMA((OPT,))])
    grams = [old_grams[0], *grams[:2], old_grams[1], *grams[2:]]
    own_attn = fence(shared_attn, *old_grams).reshape(D, D)

    total = fence(jnp.full((8, 128), jnp.sum(piece_attn.astype(F32) ** 2)), *old_grams)
    total = total + pair(total, 1)
    total = total + pair(total, 2)
    for bit in bits():
        if bit == bits()[-1]:
            total = fence(total, mlp_squares)
        total = total + swap(total, bit)
    vectors = (vec.shape, F32)
    (attn_mom_new, new_attn, first_mom, new_first, second_mom, new_second, norm, new_vec, moment_one,
     moment_two) = in_vmem(
        update_kernel, [((D, D), F32)] * 6 + [((8, 128), F32)] + [vectors] * 3, "updates", total, mlp_squares, grad_vec,
        vec, adam_first, adam_second, own_attn, attn_mom[0], attn_w[0], own_mlp, mlp_in_mom, mlp_out_mom, mlp_in,
        mlp_out, *grams, flops=12e9)
    return (out_patches, out_regions, d_patches, d_regions, new_attn[None], attn_mom_new[None], new_first, first_mom,
            new_second, second_mom, new_vec, moment_one, moment_two, norm[0, 0])


def solution(mesh):
    canvas = P("opt", None, "dp", None)
    wide = P("opt", None, "dp", None, None)
    bands = P("opt", "dp", None, None, None)
    square, right, down = P("opt", None, None), P(None, "opt"), P("opt", None)
    return jax.shard_map(
        per_device,
        mesh=mesh,
        in_specs=(bands, canvas, square, square, right, down, P(), wide, canvas, square, right, down, P(), P()),
        out_specs=(wide, canvas, bands, canvas, square, square, right, right, down, down, P(), P(), P(), P()),
        check_vma=False,
    )
```
